32 devices in a mesh: dp: 8 (over z, x), mp: 4 (over y, core).
Axes of the slice: x: 2, y: 2, z: 4, core: 2. Of those that a mesh axis runs over, the one named last changes fastest.
Arguments:
- patch_rows: bfloat16 [4096, 768], P('dp'), may hold values from -6 to 6
- patches: int32 [64], replicated, may hold values from 100 to 256, as said below
- visible: int32 [64, 64], replicated, may hold values from -1 to 255, as said below
- owner: int32 [64], replicated, may hold values from 0 to 7, as said below
- qkv_weight: bfloat16 [768, 2304], P(None, 'mp'), may hold values from -0.21875 to 0.21875
- query_bias: bfloat16 [768], P('mp'), may hold values from -3 to 3
- value_bias: bfloat16 [768], P('mp'), may hold values from -3 to 3
- out_weight: bfloat16 [768, 768], P('mp'), may hold values from -1.25 to 1.25
- out_bias: bfloat16 [768], replicated, may hold values from -2 to 2
- first_gain: bfloat16 [768], replicated, may hold values from 0.5 to 1.5
- first_shift: bfloat16 [768], replicated, may hold values from -2 to 2
- second_gain: bfloat16 [768], replicated, may hold values from 0.5 to 1.5
- second_shift: bfloat16 [768], replicated, may hold values from -2 to 2
- up_weight: bfloat16 [768, 3072], P(None, 'mp'), may hold values from -0.21875 to 0.21875
- up_bias: bfloat16 [3072], P('mp'), may hold values from -2 to 2
- down_weight: bfloat16 [3072, 768], P('mp'), may hold values from -0.109375 to 0.109375
- down_bias: bfloat16 [768], replicated, may hold values from -2 to 2
- proj_weight: bfloat16 [768, 512], P(None, 'mp'), may hold values from -0.21875 to 0.21875
- proj_bias: bfloat16 [512], P('mp'), may hold values from -2 to 2
- mask_token: bfloat16 [512], P('mp'), may hold values from -3 to 3
- decoder_pos: bfloat16 [256, 512], P(None, 'mp'), may hold values from -3 to 3
- grid_cotangent: bfloat16 [64, 256, 512], P('dp', None, 'mp'), may hold values from -6 to 6
Outputs:
- grids: bfloat16 [64, 256, 512], P('dp', None, 'mp')
- input_grad: bfloat16 [4096, 768], P(('dp', 'mp'))
- qkv_weight_grad: float32 [768, 2304], P('dp', 'mp')
- query_bias_grad: float32 [768], P('mp')
- value_bias_grad: float32 [768], P('mp')
- out_weight_grad: float32 [768, 768], P('mp', 'dp')
- out_bias_grad: float32 [768], replicated
- first_gain_grad: float32 [768], replicated
- first_shift_grad: float32 [768], replicated
- second_gain_grad: float32 [768], replicated
- second_shift_grad: float32 [768], replicated
- up_weight_grad: float32 [768, 3072], P('dp', 'mp')
- up_bias_grad: float32 [3072], P('mp')
- down_weight_grad: float32 [3072, 768], P('mp', 'dp')
- down_bias_grad: float32 [768], replicated
- proj_weight_grad: float32 [768, 512], P('dp', 'mp')
- proj_bias_grad: float32 [512], P('mp')
- mask_token_grad: float32 [512], P('mp')
- decoder_pos_grad: float32 [256, 512], P('dp', 'mp')
The draws below stay inside these ranges and needn't reach their ends.
Inputs may be any that keep to these rules, and one draw needn't show every extreme that they name: Every entry is 100, 196 or 256 (grids of 10, 14 or 16 patches a side); the first image has 100 and the second 256. `visible`: row g holds patches_g / 4 distinct positions below patches_g in its first entries and -1 in the rest. `owner`: the 8 images of each index of dp name every index of dp exactly once.
All inputs are finite; a program needn't handle non-finite values.
Results may differ from the reference program's by a relative error of at most 0.024.
Values may be sent and summed in bfloat16 or wider, within the bound.
No kernel may reach another device: no remote copies, remote signals or barrier semaphores. Data moves between devices by JAX's collectives and lax.ppermute only.
A program may use at most 192 MiB of HBM per device.

```python
import math
import jax
import jax.numpy as jnp
from jax import lax

D = 768
HEADS = 12
HEAD_DIM = 64
FF = 3072
DEC = 512
GRID = 256
VIS = 64
IMG_DEV = 8
IMAGES = 64
SLOTS = 4096
N_DP = 8


def grid_cells(key):
    picked = jax.random.randint(key, (IMAGES,), 0, 3)
    picked = picked.at[0].set(0).at[1].set(2)
    return (100 + 96 * (picked >= 1) + 60 * (picked >= 2)).astype(jnp.int32)


def draw_patches(key, part):
    return grid_cells(key)


def draw_visible(key, part):
    sizes = grid_cells(key)
    key = jax.random.fold_in(key, 2)
    places = jnp.arange(GRID)
    ranking = jax.random.randint(key, (IMAGES, GRID), 0, 2 ** 20) + jnp.where(places[None, :] >= sizes[:, None], 2 ** 21, 0)
    ordering = jnp.argsort(ranking, axis=1, stable=True)[:, :VIS].astype(jnp.int32)
    slot_ids = jnp.arange(VIS)
    return jnp.where(slot_ids[None, :] < (sizes // 4)[:, None], ordering, -1).astype(jnp.int32)


def draw_owner(key, part):
    key = jax.random.fold_in(key, 3)
    block_keys = jax.random.split(key, IMAGES // IMG_DEV)
    orders = jax.vmap(lambda block_key: jax.random.permutation(block_key, IMG_DEV))(block_keys)
    return orders.reshape(IMAGES).astype(jnp.int32)


def steps_of(own_key, extent, cuts, smallest, high):
    def one(axis_at, blocks):
        draws = jax.random.uniform(jax.random.fold_in(jax.random.fold_in(own_key, 6), axis_at), (blocks,), jnp.float32, smallest / len(cuts), high / len(cuts))
        return jnp.repeat(jnp.exp(draws), extent[axis_at] // blocks).reshape((-1,) + (1,) * (len(extent) - axis_at - 1))

    level = one(*cuts[0])
    for cut in cuts[1:]:
        level = level * one(*cut)
    return level


def bell_draw(key, dims, scale, most, pieces=(), kind=jnp.bfloat16):
    array = scale * jax.random.normal(key, dims, jnp.float32)
    if pieces:
        array = array * steps_of(key, dims, pieces, -0.22, 0.18)
    return jnp.clip(array, -most, most).astype(kind)


def setup_inputs(seed: int = 0) -> dict:
    keys = jax.random.split(jax.random.key(seed), 23)
    patch_rows = bell_draw(keys[0], (SLOTS, D), 1.0, 6.0, ((0, 8),))
    patches = draw_patches(jax.random.fold_in(keys[22], 71), 0)
    visible = draw_visible(jax.random.fold_in(keys[22], 71), 0)
    owner = draw_owner(jax.random.fold_in(keys[22], 71), 0)
    qkv_weight = bell_draw(keys[4], (D, 3 * D), D ** -0.5, 0.21875, ((1, 4),))
    query_bias = bell_draw(keys[5], (D,), 0.5, 3.0, ((0, 4),))
    value_bias = bell_draw(keys[6], (D,), 0.5, 3.0, ((0, 4),))
    out_weight = bell_draw(keys[7], (D, D), (D // 32) ** -0.5, 1.25, ((0, 4),))
    out_bias = bell_draw(keys[8], (D,), 0.3, 2.0)
    first_gain = jnp.clip(1.0 + 0.1 * jax.random.normal(keys[9], (D,), jnp.float32), 0.5, 1.5).astype(jnp.bfloat16)
    first_shift = bell_draw(keys[10], (D,), 0.3, 2.0)
    second_gain = jnp.clip(1.0 + 0.1 * jax.random.normal(keys[11], (D,), jnp.float32), 0.5, 1.5).astype(jnp.bfloat16)
    second_shift = bell_draw(keys[12], (D,), 0.3, 2.0)
    up_weight = bell_draw(keys[13], (D, FF), D ** -0.5, 0.21875, ((1, 4),))
    up_bias = bell_draw(keys[14], (FF,), 0.3, 2.0, ((0, 4),))
    down_weight = bell_draw(keys[15], (FF, D), FF ** -0.5, 0.109375, ((0, 4),))
    down_bias = bell_draw(keys[16], (D,), 0.3, 2.0)
    proj_weight = bell_draw(keys[17], (D, DEC), D ** -0.5, 0.21875, ((1, 4),))
    proj_bias = bell_draw(keys[18], (DEC,), 0.3, 2.0, ((0, 4),))
    mask_token = bell_draw(keys[19], (DEC,), 0.5, 3.0, ((0, 4),))
    decoder_pos = bell_draw(keys[20], (GRID, DEC), 0.5, 3.0, ((1, 4),))
    grid_cotangent = bell_draw(keys[21], (IMAGES, GRID, DEC), 1.0, 6.0, ((0, 8), (2, 4)))
    return dict(patch_rows=patch_rows, patches=patches, visible=visible, owner=owner, qkv_weight=qkv_weight, query_bias=query_bias, value_bias=value_bias, out_weight=out_weight, out_bias=out_bias, first_gain=first_gain, first_shift=first_shift, second_gain=second_gain, second_shift=second_shift, up_weight=up_weight, up_bias=up_bias, down_weight=down_weight, down_bias=down_bias, proj_weight=proj_weight, proj_bias=proj_bias, mask_token=mask_token, decoder_pos=decoder_pos, grid_cotangent=grid_cotangent)


epsilon = 1e-06
highest = lax.Precision.HIGHEST
grid_sides = (10, 14, 16)

@jax.custom_vjp
def low(v):
    return lax.optimization_barrier(v.astype(jnp.bfloat16)).astype(jnp.float32)

@jax.custom_vjp
def low_back(v):
    return v

def low_keep(v):
    return (low(v), None)

def low_pass(kept, grad):
    return (grad,)

def back_keep(v):
    return (v, None)

def back_low(kept, grad):
    return (low(grad),)
low.defvjp(low_keep, low_pass)
low_back.defvjp(back_keep, back_low)

def layer_norm(inputs, norm_gain, norm_shift):
    center = inputs - lax.optimization_barrier(jnp.mean(inputs, axis=-1, keepdims=True))
    spread = lax.optimization_barrier(jnp.mean(center * center, axis=-1, keepdims=True))
    return center * lax.rsqrt(spread + epsilon) * norm_gain + norm_shift

def interp_table(side_cells, grid_edge):
    places = jnp.arange(grid_edge)
    numerator = (2 * places + 1) * grid_edge - side_cells
    lower_cell = numerator // (2 * side_cells)
    upper_share = numerator.astype(jnp.float32) / (2 * side_cells) - lower_cell.astype(jnp.float32)
    first_cell = jnp.clip(lower_cell, 0, grid_edge - 1)
    second_cell = jnp.clip(lower_cell + 1, 0, grid_edge - 1)
    columns = jnp.arange(grid_edge)
    lerp_rows = (1.0 - upper_share)[:, None] * (columns[None, :] == first_cell[:, None]) + upper_share[:, None] * (columns[None, :] == second_cell[:, None])
    return lerp_rows[:side_cells]

def spread_table(table_pos, side_cells):
    grid_edge = math.isqrt(GRID)
    lerp_rows = interp_table(side_cells, grid_edge)
    pos_cube = table_pos.reshape(grid_edge, grid_edge, -1)
    full_grid = jnp.einsum('ia,jb,abc->ijc', lerp_rows, lerp_rows, pos_cube, precision=highest)
    flat_rows = full_grid.reshape(side_cells * side_cells, -1)
    return jnp.pad(flat_rows, ((0, GRID - side_cells * side_cells), (0, 0)))

def fill_grids(encoded, visible, patches, mask_token, table_pos):
    places = jnp.arange(GRID)
    onehot = (visible[:, None, :] == places[None, :, None]).astype(jnp.float32)
    seen_mask = lax.optimization_barrier(jnp.sum(onehot, axis=2))
    valid_mask = (places[None, :] < patches[:, None]).astype(jnp.float32)
    placed = jnp.einsum('spk,skc->spc', onehot, encoded, precision=highest)
    layouts = [spread_table(table_pos, side_cells) for side_cells in grid_sides]
    position = jnp.where((patches == 100)[:, None, None], layouts[0], jnp.where((patches == 196)[:, None, None], layouts[1], layouts[2]))
    return placed + (valid_mask - seen_mask)[:, :, None] * mask_token + position

def forward(weights, group_rows, visible, patches):
    qkv_weight, query_bias, value_bias, out_weight, out_bias, first_gain, first_shift, second_gain, second_shift, up_weight, up_bias, down_weight, down_bias, proj_weight, proj_bias, mask_token, decoder_pos = weights
    images = group_rows.shape[0] // VIS
    act_one = low(layer_norm(group_rows, first_gain, first_shift))
    mixed_cols = jnp.dot(act_one, qkv_weight, precision=highest).reshape(images, VIS, HEADS, 3, HEAD_DIM)
    queries = low(low_back(mixed_cols[:, :, :, 0] + query_bias.reshape(HEADS, HEAD_DIM)))
    key_rows = low(low_back(mixed_cols[:, :, :, 1]))
    value_rows = low(low_back(mixed_cols[:, :, :, 2] + value_bias.reshape(HEADS, HEAD_DIM)))
    scores = low_back(jnp.einsum('sqhd,skhd->shqk', queries, key_rows, precision=highest) * HEAD_DIM ** (-0.5))
    live_keys = jnp.arange(VIS)[None, :] < (patches // 4)[:, None]
    scores = jnp.where(live_keys[:, None, None, :], scores, -1e+30)
    row_top = lax.optimization_barrier(jnp.max(scores, axis=-1, keepdims=True))
    raised = jnp.exp(scores - row_top)
    attn_probs = raised / lax.optimization_barrier(jnp.sum(raised, axis=-1, keepdims=True))
    attended = jnp.einsum('shqk,skhd->sqhd', low(attn_probs), value_rows, precision=highest)
    attended = low(low_back(attended.reshape(-1, HEADS * HEAD_DIM)))
    hidden = group_rows + low_back(jnp.dot(attended, out_weight, precision=highest)) + out_bias
    act_two = low(layer_norm(hidden, second_gain, second_shift))
    up_pre = low_back(jnp.dot(act_two, up_weight, precision=highest) + up_bias)
    activated = low(jax.nn.gelu(up_pre, approximate=False))
    encoder_out = hidden + low_back(jnp.dot(activated, down_weight, precision=highest)) + down_bias
    encoded = low(jnp.dot(low(encoder_out), proj_weight, precision=highest) + proj_bias)
    return fill_grids(encoded.reshape(images, VIS, -1), visible, patches, mask_token, decoder_pos)

def reference(patch_rows, patches, visible, owner, qkv_weight, query_bias, value_bias, out_weight, out_bias, first_gain, first_shift, second_gain, second_shift, up_weight, up_bias, down_weight, down_bias, proj_weight, proj_bias, mask_token, decoder_pos, grid_cotangent):
    weights = jax.tree.map(lambda weight_in: weight_in.astype(jnp.float32), (qkv_weight, query_bias, value_bias, out_weight, out_bias, first_gain, first_shift, second_gain, second_shift, up_weight, up_bias, down_weight, down_bias, proj_weight, proj_bias, mask_token, decoder_pos))
    per_group = min(IMAGES, 64)
    groups = IMAGES // per_group
    image_ids = jnp.arange(IMAGES, dtype=jnp.int32)
    slot_ids = (owner * N_DP + image_ids // IMG_DEV).astype(jnp.int32)
    row_blocks = patch_rows.astype(jnp.float32).reshape(groups, per_group * VIS, D)

    def accumulate(totals, group_data):
        group_rows, group_visible, group_patches, group_slots = group_data
        grid_values, pullback = jax.vjp(lambda params, inputs: forward(params, inputs, group_visible, group_patches), weights, group_rows)
        cotangent = grid_cotangent[group_slots].astype(jnp.float32)
        weight_grads, input_grads = pullback(cotangent)
        totals = jax.tree.map(lambda left_sum, right_sum: left_sum + right_sum, totals, weight_grads)
        return (totals, (grid_values.astype(jnp.bfloat16), input_grads.astype(jnp.bfloat16)))
    start_totals = jax.tree.map(jnp.zeros_like, weights)
    totals, (grid_blocks, input_blocks) = lax.scan(accumulate, start_totals, (row_blocks, visible.reshape(groups, per_group, VIS), patches.reshape(groups, per_group), slot_ids.reshape(groups, per_group)))
    inverse = jnp.zeros((IMAGES,), jnp.int32).at[slot_ids].set(image_ids)
    grid_out = grid_blocks.reshape(IMAGES, GRID, DEC)[inverse]
    input_grad = input_blocks.reshape(SLOTS, D)
    return (grid_out, input_grad, totals[0], totals[1], totals[2], totals[3], totals[4], totals[5], totals[6], totals[7], totals[8], totals[9], totals[10], totals[11], totals[12], totals[13], totals[14], totals[15], totals[16])
```

```python
from functools import partial
import math

import jax
import jax.numpy as jnp
from jax import lax
from jax.sharding import PartitionSpec as P

HEAD_DIM = 64
GRID = 256
VIS = 64


epsilon = 1e-06
highest = lax.Precision.HIGHEST
grid_sides = (10, 14, 16)


def layer_norm(inputs, norm_gain, norm_shift):
    center = inputs - jnp.mean(inputs, axis=-1, keepdims=True)
    spread = jnp.mean(center * center, axis=-1, keepdims=True)
    return center * lax.rsqrt(spread + epsilon) * norm_gain + norm_shift


def interp_table(side_cells, grid_edge):
    places = jnp.arange(grid_edge)
    numerator = (2 * places + 1) * grid_edge - side_cells
    lower_cell = numerator // (2 * side_cells)
    upper_share = numerator.astype(jnp.float32) / (2 * side_cells) - lower_cell.astype(jnp.float32)
    first_cell = jnp.clip(lower_cell, 0, grid_edge - 1)
    second_cell = jnp.clip(lower_cell + 1, 0, grid_edge - 1)
    columns = jnp.arange(grid_edge)
    lerp_rows = (1.0 - upper_share)[:, None] * (
        columns[None, :] == first_cell[:, None]
    ) + upper_share[:, None] * (columns[None, :] == second_cell[:, None])
    return lerp_rows[:side_cells]


def spread_table(table_pos, side_cells):
    grid_edge = math.isqrt(GRID)
    lerp_rows = interp_table(side_cells, grid_edge)
    pos_cube = table_pos.reshape(grid_edge, grid_edge, -1)
    full_grid = jnp.einsum("ia,jb,abc->ijc", lerp_rows, lerp_rows, pos_cube, precision=highest)
    flat_rows = full_grid.reshape(side_cells * side_cells, -1)
    return jnp.pad(flat_rows, ((0, GRID - side_cells * side_cells), (0, 0)))


def spread_back(grad_rows, side_cells):
    grid_edge = math.isqrt(GRID)
    lerp_rows = interp_table(side_cells, grid_edge)
    grad_cube = grad_rows[: side_cells * side_cells].reshape(side_cells, side_cells, -1)
    return jnp.einsum("ia,jb,ijc->abc", lerp_rows, lerp_rows, grad_cube, precision=highest).reshape(
        GRID, -1
    )


def matmul(left_op, right_op, pattern):
    return jnp.einsum(pattern, left_op, right_op, preferred_element_type=jnp.float32)


def swap(value, axis, bit):
    count = lax.axis_size(axis)
    return lax.ppermute(value, axis, [(i, i ^ bit) for i in range(count)])


def low_add(left, right):
    return (left.astype(jnp.float32) + right.astype(jnp.float32)).astype(jnp.bfloat16)


def pair_sum(partial_sum, index):
    half = partial_sum.shape[0] // 2
    upper = (index & 1) == 1
    first, second = partial_sum[:half], partial_sum[half:]
    kept = jnp.where(upper, second, first)
    total = low_add(kept, swap(jnp.where(upper, first, second), "mp", 1))
    bit = 2
    while bit < lax.axis_size("mp"):
        total = low_add(total, swap(total, "mp", bit))
        bit *= 2
    other = swap(total, "mp", 1)
    return jnp.concatenate([jnp.where(upper, other, total), jnp.where(upper, total, other)])


def scatter_sum(blocks, index):
    bit = 1
    count = blocks.shape[0]
    blocks = blocks.astype(jnp.bfloat16)
    while bit < count:
        parted = blocks.reshape(-1, 2, *blocks.shape[1:])
        upper = (index & bit) != 0
        kept = jnp.where(upper, parted[:, 1], parted[:, 0])
        sent = jnp.where(upper, parted[:, 0], parted[:, 1])
        blocks = low_add(kept, swap(sent, "dp", bit))
        bit *= 2
    return blocks[0].astype(jnp.float32)


def local(
    patch_rows,
    patches,
    visible,
    owner,
    qkv_weight,
    query_bias,
    value_bias,
    out_weight,
    out_bias,
    first_gain,
    first_shift,
    second_gain,
    second_shift,
    up_weight,
    up_bias,
    down_weight,
    down_bias,
    proj_weight,
    proj_bias,
    mask_token,
    decoder_pos,
    grid_cotangent,
):
    low_type = jnp.bfloat16
    wide_type = jnp.float32
    data_ranks = lax.axis_size("dp")
    model_parts = lax.axis_size("mp")
    data_index = lax.axis_index("dp")
    model_index = lax.axis_index("mp")
    row_count = patch_rows.shape[0]
    image_count = row_count // VIS
    local_heads = qkv_weight.shape[1] // (3 * HEAD_DIM)
    share_rows = row_count // model_parts

    def combine(partial_sum):
        return pair_sum(partial_sum.astype(jnp.bfloat16), model_index).astype(jnp.float32)

    residual_in = patch_rows.astype(wide_type)
    normed_one, norm_one_back = jax.vjp(
        layer_norm, residual_in, first_gain.astype(wide_type), first_shift.astype(wide_type)
    )
    act_one = normed_one.astype(low_type)
    mixed_cols = matmul(act_one, qkv_weight, "rd,dc->rc").reshape(
        image_count, VIS, local_heads, 3, HEAD_DIM
    )
    queries = (
        mixed_cols[:, :, :, 0] + query_bias.astype(wide_type).reshape(local_heads, HEAD_DIM)
    ).astype(low_type)
    key_rows = mixed_cols[:, :, :, 1].astype(low_type)
    value_rows = (
        mixed_cols[:, :, :, 2] + value_bias.astype(wide_type).reshape(local_heads, HEAD_DIM)
    ).astype(low_type)
    own_patches = lax.dynamic_slice_in_dim(patches, data_index * image_count, image_count, 0)
    live_keys = (jnp.arange(VIS)[None, :] < (own_patches // 4)[:, None])[:, None, None, :]
    scale_factor = HEAD_DIM ** (-0.5)

    def score_block():
        raw_scores = matmul(queries, key_rows, "sqhd,skhd->shqk") * scale_factor
        return jnp.where(live_keys, raw_scores, -1e30)

    scores = score_block()
    row_top = jnp.max(scores, axis=-1, keepdims=True)
    raised = jnp.exp(scores - row_top)
    row_total = jnp.sum(raised, axis=-1, keepdims=True)
    log_total = row_top + jnp.log(row_total)
    prob_low = (raised / row_total).astype(low_type)
    attended = (
        matmul(prob_low, value_rows, "shqk,skhd->sqhd")
        .reshape(row_count, local_heads * HEAD_DIM)
        .astype(low_type)
    )
    hidden = (
        residual_in
        + combine(matmul(attended, out_weight, "rh,hd->rd"))
        + out_bias.astype(wide_type)
    )
    normed_two, norm_two_back = jax.vjp(
        layer_norm, hidden, second_gain.astype(wide_type), second_shift.astype(wide_type)
    )
    act_two = normed_two.astype(low_type)
    up_pre = matmul(act_two, up_weight, "rd,df->rf") + up_bias.astype(wide_type)
    activated, gelu_back = jax.vjp(partial(jax.nn.gelu, approximate=False), up_pre)
    acted_low = activated.astype(low_type)
    encoder_out = (
        hidden + combine(matmul(acted_low, down_weight, "rf,fd->rd")) + down_bias.astype(wide_type)
    )
    out_low = encoder_out.astype(low_type)
    encoded = (
        (matmul(out_low, proj_weight, "rd,dc->rc") + proj_bias.astype(wide_type))
        .astype(low_type)
        .reshape(image_count, VIS, -1)
    )
    own_owner = lax.dynamic_slice_in_dim(owner, data_index * image_count, image_count, 0)
    image_slots = jnp.arange(image_count)
    peer_match = own_owner[None, :] == jnp.arange(data_ranks)[:, None]
    sender_order = jnp.sum(jnp.where(peer_match, image_slots[None, :], 0), axis=1)
    arrived = lax.all_to_all(encoded[sender_order], "dp", split_axis=0, concat_axis=0, tiled=True)
    owner_table = owner.reshape(data_ranks, image_count)
    source_match = owner_table == data_index
    source_image = jnp.arange(data_ranks) * image_count + jnp.sum(
        jnp.where(source_match, image_slots[None, :], 0), axis=1
    )
    slot_visible = visible[source_image]
    slot_patches = patches[source_image]
    places = jnp.arange(GRID)
    onehot = (slot_visible[:, None, :] == places[None, :, None]).astype(low_type)
    seen_mask = jnp.sum(onehot.astype(wide_type), axis=2)
    valid_mask = (places[None, :] < slot_patches[:, None]).astype(wide_type)
    fill_mask = valid_mask - seen_mask
    table_pos = decoder_pos.astype(wide_type)
    layouts = [spread_table(table_pos, side_cells) for side_cells in grid_sides]
    position = jnp.where(
        (slot_patches == 100)[:, None, None],
        layouts[0],
        jnp.where((slot_patches == 196)[:, None, None], layouts[1], layouts[2]),
    )
    placed = matmul(onehot, arrived, "spk,skc->spc")
    grid_out = (placed + fill_mask[:, :, None] * mask_token.astype(wide_type) + position).astype(
        low_type
    )
    mask_grad = matmul(fill_mask.astype(low_type), grid_cotangent, "sp,spc->c")
    pos_grad = jnp.zeros(decoder_pos.shape, wide_type)
    for side_cells in grid_sides:
        chosen = (slot_patches == side_cells * side_cells).astype(low_type)
        pos_grad = pos_grad + spread_back(matmul(chosen, grid_cotangent, "s,spc->pc"), side_cells)
    back_rows = matmul(onehot, grid_cotangent, "spk,spc->skc").astype(low_type)
    returned = lax.all_to_all(back_rows, "dp", split_axis=0, concat_axis=0, tiled=True)
    enc_grad = returned[own_owner].reshape(row_count, -1)
    proj_bias_grad = jnp.sum(enc_grad, axis=0, dtype=wide_type)
    proj_weight_grad = matmul(out_low, enc_grad, "rd,rc->dc")
    out_grad = combine(matmul(enc_grad, proj_weight, "rc,dc->rd"))
    down_bias_grad = jnp.sum(out_grad, axis=0)
    down_low = out_grad.astype(low_type)
    down_weight_grad = matmul(acted_low, down_low, "rf,rd->fd")
    (up_grad,) = gelu_back(matmul(down_low, down_weight, "rd,fd->rf"))
    up_low = up_grad.astype(low_type)
    up_bias_grad = jnp.sum(up_low, axis=0, dtype=wide_type)
    up_weight_grad = matmul(act_two, up_low, "rd,rf->df")
    norm_two_grad = combine(matmul(up_low, up_weight, "rf,df->rd"))
    hidden_part, second_gain_grad, second_shift_grad = norm_two_back(norm_two_grad)
    hidden_grad = out_grad + hidden_part
    out_bias_grad = jnp.sum(hidden_grad, axis=0)
    attn_low = hidden_grad.astype(low_type)
    out_weight_grad = matmul(attended, attn_low, "rh,rd->hd")
    attended_grad = (
        matmul(attn_low, out_weight, "rd,hd->rh")
        .astype(low_type)
        .reshape(image_count, VIS, local_heads, HEAD_DIM)
    )
    value_low = matmul(prob_low, attended_grad, "shqk,sqhd->skhd").astype(low_type)
    recomputed = jnp.exp(score_block() - log_total)
    prob_grad = matmul(attended_grad, value_rows, "sqhd,skhd->shqk")
    score_low = (
        recomputed * (prob_grad - jnp.sum(recomputed * prob_grad, axis=-1, keepdims=True))
    ).astype(low_type)
    query_low = (matmul(score_low, key_rows, "shqk,skhd->sqhd") * scale_factor).astype(low_type)
    key_low = (matmul(score_low, queries, "shqk,sqhd->skhd") * scale_factor).astype(low_type)
    query_bias_grad = jnp.sum(query_low, axis=(0, 1), dtype=wide_type).reshape(-1)
    value_bias_grad = jnp.sum(value_low, axis=(0, 1), dtype=wide_type).reshape(-1)
    qkv_grad = jnp.stack((query_low, key_low, value_low), axis=3).reshape(row_count, -1)
    qkv_weight_grad = matmul(act_one, qkv_grad, "rd,rc->dc")
    norm_one_grad = combine(matmul(qkv_grad, qkv_weight, "rc,dc->rd"))
    input_part, first_gain_grad, first_shift_grad = norm_one_back(norm_one_grad)
    input_grad = hidden_grad + input_part
    input_grad = lax.dynamic_slice_in_dim(input_grad, model_index * share_rows, share_rows, 0)
    blocks = jnp.concatenate(
        [
            down_weight_grad.T.reshape(data_ranks, -1, down_weight.shape[0]),
            up_weight_grad.reshape(data_ranks, -1, up_weight.shape[1]),
            proj_weight_grad.reshape(data_ranks, -1, proj_weight.shape[1]),
            out_weight_grad.T.reshape(data_ranks, -1, out_weight.shape[0]),
            qkv_weight_grad.reshape(data_ranks, -1, qkv_weight.shape[1]),
        ],
        axis=2,
    )
    summed = scatter_sum(blocks, data_index)
    widths = (
        down_weight.shape[0],
        up_weight.shape[1],
        proj_weight.shape[1],
        out_weight.shape[0],
        qkv_weight.shape[1],
    )
    pieces = []
    offset = 0
    for width in widths:
        pieces.append(summed[:, offset : offset + width])
        offset += width
    down_weight_grad, up_weight_grad, proj_weight_grad, out_weight_grad, qkv_weight_grad = pieces
    down_weight_grad = down_weight_grad.T
    out_weight_grad = out_weight_grad.T
    pos_grad = scatter_sum(pos_grad.reshape(data_ranks, -1, pos_grad.shape[1]), data_index)
    vectors = (
        query_bias_grad,
        value_bias_grad,
        up_bias_grad,
        proj_bias_grad,
        mask_grad,
        first_gain_grad,
        first_shift_grad,
        second_gain_grad,
        second_shift_grad,
        out_bias_grad,
        down_bias_grad,
    )
    packed = jnp.concatenate(vectors)
    bit = 1
    while bit < data_ranks:
        packed = packed + swap(packed, "dp", bit)
        bit *= 2
    pieces = []
    offset = 0
    for vector in vectors:
        pieces.append(packed[offset : offset + vector.shape[0]])
        offset += vector.shape[0]
    (
        query_bias_grad,
        value_bias_grad,
        up_bias_grad,
        proj_bias_grad,
        mask_grad,
        first_gain_grad,
        first_shift_grad,
        second_gain_grad,
        second_shift_grad,
        out_bias_grad,
        down_bias_grad,
    ) = pieces
    return (
        grid_out,
        input_grad.astype(low_type),
        qkv_weight_grad,
        query_bias_grad,
        value_bias_grad,
        out_weight_grad,
        out_bias_grad,
        first_gain_grad,
        first_shift_grad,
        second_gain_grad,
        second_shift_grad,
        up_weight_grad,
        up_bias_grad,
        down_weight_grad,
        down_bias_grad,
        proj_weight_grad,
        proj_bias_grad,
        mask_grad,
        pos_grad,
    )


def solution(mesh):
    return jax.shard_map(
        local,
        mesh=mesh,
        in_specs=(
            P("dp", None),
            P(),
            P(),
            P(),
            P(None, "mp"),
            P("mp"),
            P("mp"),
            P("mp", None),
            P(),
            P(),
            P(),
            P(),
            P(),
            P(None, "mp"),
            P("mp"),
            P("mp", None),
            P(),
            P(None, "mp"),
            P("mp"),
            P("mp"),
            P(None, "mp"),
            P("dp", None, "mp"),
        ),
        out_specs=(
            P("dp", None, "mp"),
            P(("dp", "mp"), None),
            P("dp", "mp"),
            P("mp"),
            P("mp"),
            P("mp", "dp"),
            P(),
            P(),
            P(),
            P(),
            P(),
            P("dp", "mp"),
            P("mp"),
            P("mp", "dp"),
            P(),
            P("dp", "mp"),
            P("mp"),
            P("mp"),
            P("dp", "mp"),
        ),
        check_vma=False,
    )
```

```python
import math

import jax
import jax.numpy as jnp
import numpy as np
from jax import lax
from jax.experimental import pallas as pl
from jax.experimental.pallas import tpu as pltpu
from jax.sharding import PartitionSpec as P

HEAD_DIM = 64
GRID = 256
VIS = 64
PAIR = 2 * VIS
CHUNK = 512
LANES = 128

epsilon = 1e-06
low_type = jnp.bfloat16
wide_type = jnp.float32
scale_factor = HEAD_DIM ** (-0.5)

VMEM = pl.BlockSpec(memory_space=pltpu.VMEM)
SMEM = pl.BlockSpec(memory_space=pltpu.SMEM)


def grid_tables():
    grid_edge = math.isqrt(GRID)
    tables = []
    for side_cells in (10, 14):
        places = np.arange(side_cells)
        centers = ((2 * places + 1) * grid_edge - side_cells) / (2 * side_cells)
        lower = np.floor(centers).astype(np.int64)
        share = centers - lower
        lerp = np.zeros((side_cells, grid_edge))
        lerp[places, np.clip(lower, 0, grid_edge - 1)] += 1.0 - share
        lerp[places, np.clip(lower + 1, 0, grid_edge - 1)] += share
        table = np.zeros((GRID, GRID))
        table[: side_cells * side_cells] = np.kron(lerp, lerp)
        tables.append(table)
    return np.stack(tables).astype(np.float32)


def split_low(value):
    high = value.astype(low_type)
    return high, (value - high.astype(wide_type)).astype(low_type)


def dot(left, right):
    return lax.dot_general(left, right, (((1,), (0,)), ((), ())), preferred_element_type=wide_type)


def dot_right_t(left, right):
    return lax.dot_general(left, right, (((1,), (1,)), ((), ())), preferred_element_type=wide_type)


def dot_left_t(left, right):
    return lax.dot_general(left, right, (((0,), (0,)), ((), ())), preferred_element_type=wide_type)


def normalized(value):
    center = value - jnp.mean(value, axis=-1, keepdims=True)
    spread = lax.rsqrt(jnp.mean(center * center, axis=-1, keepdims=True) + epsilon)
    return center * spread, spread


def norm_back(grad, normed, spread, gain):
    scaled = grad * gain
    mean_one = jnp.mean(scaled, axis=-1, keepdims=True)
    mean_two = jnp.mean(scaled * normed, axis=-1, keepdims=True)
    return spread * (scaled - mean_one - normed * mean_two)


def row_sum(value):
    return jnp.sum(value, axis=0, keepdims=True)


def over_rows(total, size, body):
    size = min(size, total)
    if total == size:
        body(0, size)
        return

    def step(i, carry):
        body(pl.multiple_of(i * size, size), size)
        return carry

    lax.fori_loop(0, total // size, step, 0)


def call(kernel, outs, args, specs, scratch=(), flops=0, nbytes=0, out_specs=None):
    return pl.pallas_call(
        kernel,
        out_shape=tuple(jax.ShapeDtypeStruct(shape, kind) for shape, kind in outs),
        in_specs=list(specs),
        out_specs=tuple(VMEM for _ in outs) if out_specs is None else out_specs,
        scratch_shapes=list(scratch),
        compiler_params=pltpu.CompilerParams(vmem_limit_bytes=56 * 2**20),
        cost_estimate=pl.CostEstimate(flops=flops, bytes_accessed=nbytes, transcendentals=0),
    )(*args)


def cotangent_kernel(
    count, images, where_ref, owner_ref, patches_ref, visible_ref, cot_ref, table_high_ref, table_low_ref,
    send_ref, source_ref, mask_ref, sums_ref,
):
    me = where_ref[0]
    share = GRID // count
    cells = lax.broadcasted_iota(jnp.int32, (GRID, VIS), 0)
    cell_column = lax.broadcasted_iota(jnp.int32, (GRID, 1), 0)
    sums_ref[...] = jnp.zeros_like(sums_ref)
    mask_ref[...] = jnp.zeros_like(mask_ref)

    def one_slot(slot):
        def find(i, found):
            return jnp.where(owner_ref[slot * images + i] == me, slot * images + i, found)

        source = lax.fori_loop(0, images, find, slot * images)
        source_ref[slot] = source
        seen = visible_ref[pl.ds(source, 1), :] == cells
        cot = cot_ref[slot]
        send_ref[slot, :VIS, :] = dot_left_t(seen.astype(low_type), cot).astype(low_type)
        size = patches_ref[source]
        wide = cot.astype(wide_type)
        fill = (cell_column < size).astype(wide_type) - jnp.sum(
            seen.astype(wide_type), axis=1, keepdims=True
        )
        mask_ref[...] += row_sum(fill * wide)
        side = (size >= 196).astype(jnp.int32) + (size >= 256).astype(jnp.int32)
        sums_ref[side] += wide

    if count <= 8:
        for slot in range(count):
            one_slot(slot)
    else:
        lax.fori_loop(0, count, lambda slot, carry: (one_slot(slot), carry)[1], 0)
    total = sums_ref[2]
    for side in range(2):
        high, low = split_low(sums_ref[side])
        total += (
            dot(table_high_ref[side], high) + dot(table_high_ref[side], low) + dot(table_low_ref[side], high)
        )
    total = total.astype(low_type)
    for block in range(count):
        send_ref[block, VIS : VIS + share, :] = total[block * share : (block + 1) * share]


def enter_kernel(rows_ref, gain_ref, shift_ref, weight_ref, bias_ref, act_ref, qkv_ref):
    def body(start, size):
        rows = pl.ds(start, size)
        normed, _ = normalized(rows_ref[rows, :].astype(wide_type))
        act = (normed * gain_ref[...] + shift_ref[...]).astype(low_type)
        act_ref[rows, :] = act
        qkv_ref[rows, :] = (dot(act, weight_ref[...]) + bias_ref[...]).astype(low_type)

    over_rows(rows_ref.shape[0], CHUNK, body)


def attention_kernel(
    images, heads, where_ref, patches_ref, qkv_ref, weight_ref, prob_ref, attended_ref, keep_ref, sent_ref
):
    first_image = where_ref[0] * images
    row_half = lax.broadcasted_iota(jnp.int32, (PAIR, PAIR), 0) // VIS
    lane = lax.broadcasted_iota(jnp.int32, (PAIR, PAIR), 1)

    def body(start, size):
        for pair in range(size // PAIR):
            rows = pl.ds(start + pair * PAIR, PAIR)
            image = first_image + (start + pair * PAIR) // VIS
            limits = [patches_ref[image + i] // 4 for i in range(2)]
            last = jnp.where(row_half == 0, limits[0], VIS + limits[1])
            live = jnp.logical_and(lane >= row_half * VIS, lane < last)
            for head in range(heads):
                base = head * 3 * HEAD_DIM
                queries = qkv_ref[rows, base : base + HEAD_DIM]
                key_rows = qkv_ref[rows, base + HEAD_DIM : base + 2 * HEAD_DIM]
                value_rows = qkv_ref[rows, base + 2 * HEAD_DIM : base + 3 * HEAD_DIM]
                scores = jnp.where(live, dot_right_t(queries, key_rows) * scale_factor, -1e30)
                raised = jnp.exp(scores - jnp.max(scores, axis=-1, keepdims=True))
                probs = (raised / jnp.sum(raised, axis=-1, keepdims=True)).astype(low_type)
                prob_ref[rows, head * PAIR : (head + 1) * PAIR] = probs
                attended_ref[rows, head * HEAD_DIM : (head + 1) * HEAD_DIM] = dot(
                    probs, value_rows
                ).astype(low_type)

    over_rows(qkv_ref.shape[0], CHUNK, body)
    halves(where_ref[1] & 1, attended_ref, weight_ref, keep_ref, sent_ref, dot)


def halves(upper, left_ref, weight_ref, keep_ref, sent_ref, product):
    half = keep_ref.shape[0]
    for out_ref, which in ((sent_ref, 1 - upper), (keep_ref, upper)):

        def body(start, size, out_ref=out_ref, which=which):
            rows = pl.ds(pl.multiple_of(which * half + start, size), size)
            out_ref[pl.ds(start, size), :] = product(left_ref[rows, :], weight_ref[...]).astype(
                out_ref.dtype
            )

        over_rows(half, CHUNK, body)


def back_kernel(images, where_ref, owner_ref, back_ref, weight_ref, enc_ref, keep_ref, sent_ref):
    base = where_ref[0] * images
    for image in range(images):
        enc_ref[image * VIS : (image + 1) * VIS, :] = back_ref[owner_ref[base + image], :VIS, :]
    halves(where_ref[1] & 1, enc_ref, weight_ref, keep_ref, sent_ref, dot_right_t)


def gathered(upper, own_ref, other_ref, out_ref):
    half = own_ref.shape[0]
    out_ref[pl.ds(pl.multiple_of(upper * half, half), half), :] = own_ref[...]
    out_ref[pl.ds(pl.multiple_of((1 - upper) * half, half), half), :] = other_ref[...]


def forward_back_kernel(
    where_ref, rows_ref, sum_ref, sum_other_ref, grad_ref, grad_other_ref, vec_ref, up_ref, up_bias_ref, down_ref,
    hidden_ref, act_ref, acted_ref, up_low_ref, down_low_ref, bias_ref, keep_ref, sent_ref, fkeep_ref, fsent_ref,
    sums_ref,
):
    upper = where_ref[1] & 1
    gathered(upper, sum_ref, sum_other_ref, sums_ref)
    gathered(upper, grad_ref, grad_other_ref, down_low_ref)
    out_bias, gain, shift = vec_ref[2:3, :], vec_ref[3:4, :], vec_ref[4:5, :]

    def body(start, size):
        rows = pl.ds(start, size)
        hidden = rows_ref[rows, :].astype(wide_type) + sums_ref[rows, :].astype(wide_type) + out_bias
        hidden_ref[rows, :] = hidden
        normed, _ = normalized(hidden)
        act = (normed * gain + shift).astype(low_type)
        act_ref[rows, :] = act
        up_pre = dot(act, up_ref[...]) + up_bias_ref[...]
        cdf = 0.5 + 0.5 * lax.erf(up_pre * math.sqrt(0.5))
        acted_ref[rows, :] = (up_pre * cdf).astype(low_type)
        slope = cdf + up_pre * jnp.exp(-0.5 * up_pre * up_pre) * (1.0 / math.sqrt(2.0 * math.pi))
        up_low_ref[rows, :] = (dot_right_t(down_low_ref[rows, :], down_ref[...]) * slope).astype(low_type)

    over_rows(rows_ref.shape[0], 256, body)
    bias_ref[0:1, :] = row_sum(down_low_ref[...].astype(wide_type))
    bias_ref[1:2, :] = row_sum(up_low_ref[...].astype(wide_type))
    halves(upper, up_low_ref, up_ref, keep_ref, sent_ref, dot_right_t)
    halves(upper, acted_ref, down_ref, fkeep_ref, fsent_ref, dot)


def part_blocks(lower_bit, wide_ref, parts, keep_ref, sent_ref, first_tile):
    share = keep_ref.shape[2]
    for out_ref, which in ((sent_ref, 1 - lower_bit), (keep_ref, lower_bit)):
        for block in range(keep_ref.shape[0]):
            rows = pl.ds(pl.multiple_of((2 * block + which) * share, 8), share)
            for tile in range(parts):
                out_ref[block, first_tile + tile] = wide_ref[
                    rows, tile * LANES : (tile + 1) * LANES
                ].astype(out_ref.dtype)


def early_grads_kernel(where_ref, act_ref, up_low_ref, acted_ref, down_low_ref, keep_ref, sent_ref, wide_ref):
    lower_bit = where_ref[0] & 1
    tiles = wide_ref.shape[1] // LANES
    wide_ref[...] = dot_left_t(act_ref[...], up_low_ref[...])
    part_blocks(lower_bit, wide_ref, tiles, keep_ref, sent_ref, 0)
    wide_ref[...] = dot_left_t(down_low_ref[...], acted_ref[...])
    part_blocks(lower_bit, wide_ref, tiles, keep_ref, sent_ref, tiles)


def attention_back_kernel(
    heads, where_ref, sum_ref, sum_other_ref, hidden_ref, down_low_ref, vec_ref, weight_ref, qkv_ref, prob_ref,
    attended_ref, grads_ref, own_ref, weight_grad_ref, bias_ref, sums_ref, grad_ref, low_ref,
):
    gathered(where_ref[1] & 1, sum_ref, sum_other_ref, sums_ref)
    gain = vec_ref[3:4, :]
    bias_ref[...] = jnp.zeros_like(bias_ref)

    def body(start, size):
        rows = pl.ds(start, size)
        normed, spread = normalized(hidden_ref[rows, :])
        grad = sums_ref[rows, :].astype(wide_type)
        bias_ref[0:1, :] += row_sum(grad * normed)
        bias_ref[1:2, :] += row_sum(grad)
        hidden_grad = down_low_ref[rows, :].astype(wide_type) + norm_back(grad, normed, spread, gain)
        grad_ref[rows, :] = hidden_grad
        bias_ref[2:3, :] += row_sum(hidden_grad)
        attn_low = hidden_grad.astype(low_type)
        low_ref[rows, :] = attn_low
        attended_grad = dot_right_t(attn_low, weight_ref[...]).astype(low_type)
        for pair in range(size // PAIR):
            pair_rows = pl.ds(start + pair * PAIR, PAIR)
            for head in range(heads):
                base = head * 3 * HEAD_DIM
                queries = qkv_ref[pair_rows, base : base + HEAD_DIM]
                key_rows = qkv_ref[pair_rows, base + HEAD_DIM : base + 2 * HEAD_DIM]
                value_rows = qkv_ref[pair_rows, base + 2 * HEAD_DIM : base + 3 * HEAD_DIM]
                probs = prob_ref[pair_rows, head * PAIR : (head + 1) * PAIR]
                grad_rows = attended_grad[
                    pair * PAIR : (pair + 1) * PAIR, head * HEAD_DIM : (head + 1) * HEAD_DIM
                ]
                value_low = dot_left_t(probs, grad_rows).astype(low_type)
                prob_grad = dot_right_t(grad_rows, value_rows)
                wide_probs = probs.astype(wide_type)
                weighted = wide_probs * prob_grad
                score_low = (
                    weighted - wide_probs * jnp.sum(weighted, axis=-1, keepdims=True)
                ).astype(low_type)
                query_low = (dot(score_low, key_rows) * scale_factor).astype(low_type)
                key_low = (dot_left_t(score_low, queries) * scale_factor).astype(low_type)
                grads_ref[pair_rows, base : base + HEAD_DIM] = query_low
                grads_ref[pair_rows, base + HEAD_DIM : base + 2 * HEAD_DIM] = key_low
                grads_ref[pair_rows, base + 2 * HEAD_DIM : base + 3 * HEAD_DIM] = value_low

    over_rows(hidden_ref.shape[0], CHUNK, body)
    share = own_ref.shape[0]
    own_ref[...] = grad_ref[pl.ds(pl.multiple_of(where_ref[1] * share, share), share), :]
    weight_grad_ref[...] = dot_left_t(low_ref[...], attended_ref[...])


def late_grads_kernel(where_ref, act_ref, grads_ref, out_grad_ref, keep_ref, sent_ref, bias_ref, wide_ref):
    columns = grads_ref.shape[1]
    heads_columns = out_grad_ref.shape[1]
    bias_ref[...] = row_sum(grads_ref[...].astype(wide_type))
    wide_ref[:, :heads_columns] = out_grad_ref[...]
    wide_ref[:, heads_columns : heads_columns + columns] = dot_left_t(act_ref[...], grads_ref[...])
    part_blocks(
        where_ref[0] & 1, wide_ref, wide_ref.shape[1] // LANES, keep_ref, sent_ref, 0
    )


def input_part_kernel(
    where_ref, rows_ref, grads_ref, weight_ref, keep_ref, sent_ref, bias_ref, part_ref
):
    lower_bit = where_ref[1] & 1
    bias_ref[...] = jnp.zeros_like(bias_ref)

    def body(start, size):
        rows = pl.ds(start, size)
        grad = dot_right_t(grads_ref[rows, :], weight_ref[...])
        part_ref[rows, :] = grad
        normed, _ = normalized(rows_ref[rows, :].astype(wide_type))
        bias_ref[0:1, :] += row_sum(grad * normed)
        bias_ref[1:2, :] += row_sum(grad)

    over_rows(rows_ref.shape[0], CHUNK, body)
    share = keep_ref.shape[1]
    for out_ref, which in ((sent_ref, 1 - lower_bit), (keep_ref, lower_bit)):
        for block in range(keep_ref.shape[0]):
            rows = pl.ds(pl.multiple_of((2 * block + which) * share, share), share)
            out_ref[block] = part_ref[rows, :].astype(low_type)


def input_grad_kernel(where_ref, rows_ref, keep_ref, other_ref, own_ref, gain_ref, out_ref):
    share = out_ref.shape[0]
    rows = pl.ds(pl.multiple_of(where_ref[1] * share, share), share)
    normed, spread = normalized(rows_ref[rows, :].astype(wide_type))
    grad = keep_ref[...].astype(wide_type) + other_ref[...].astype(wide_type)
    out_ref[...] = (own_ref[...] + norm_back(grad, normed, spread, gain_ref[...])).astype(low_type)


def encoded_kernel(
    images, where_ref, owner_ref, hidden_ref, sum_ref, sum_other_ref, vec_ref, weight_ref, bias_ref, enc_ref,
    send_ref, bias_grad_ref, sums_ref, low_ref, wide_ref,
):
    gathered(where_ref[1] & 1, sum_ref, sum_other_ref, sums_ref)
    down_bias = vec_ref[5:6, :]
    base = where_ref[0] * images
    bias_grad_ref[...] = row_sum(enc_ref[...].astype(wide_type))

    def body(start, size):
        rows = pl.ds(start, size)
        out_low = (
            hidden_ref[rows, :] + sums_ref[rows, :].astype(wide_type) + down_bias
        ).astype(low_type)
        low_ref[rows, :] = out_low
        encoded = (dot(out_low, weight_ref[...]) + bias_ref[...]).astype(low_type)
        for image in range(size // VIS):
            send_ref[owner_ref[base + start // VIS + image], :VIS, :] = encoded[
                image * VIS : (image + 1) * VIS
            ]

    over_rows(hidden_ref.shape[0], CHUNK, body)
    wide_ref[...] = dot_left_t(low_ref[...], enc_ref[...])
    count = send_ref.shape[0]
    share = wide_ref.shape[0] // count
    for block in range(count):
        send_ref[block, VIS : VIS + share, :] = wide_ref[block * share : (block + 1) * share, :].astype(
            low_type
        )


def grids_kernel(
    source_ref, patches_ref, visible_ref, arrived_ref, mask_ref, pos_ref, table_high_ref, table_low_ref,
    grids_ref, weight_grad_ref, layout_ref,
):
    count = grids_ref.shape[0]
    share = weight_grad_ref.shape[0]
    cells = lax.broadcasted_iota(jnp.int32, (GRID, VIS), 0)
    cell_column = lax.broadcasted_iota(jnp.int32, (GRID, 1), 0)
    table = pos_ref[...]
    for side in range(2):
        layout_ref[side] = dot(table_high_ref[side], table) + dot(table_low_ref[side], table)
    layout_ref[2] = table.astype(wide_type)
    mask_row = mask_ref[...]

    def one_slot(slot):
        source = source_ref[slot]
        seen = visible_ref[pl.ds(source, 1), :] == cells
        size = patches_ref[source]
        fill = (cell_column < size).astype(wide_type) - jnp.sum(
            seen.astype(wide_type), axis=1, keepdims=True
        )
        side = (size >= 196).astype(jnp.int32) + (size >= 256).astype(jnp.int32)
        placed = dot(seen.astype(low_type), arrived_ref[slot, :VIS, :])
        grids_ref[slot] = (placed + fill * mask_row + layout_ref[side]).astype(low_type)

    if count <= 8:
        for slot in range(count):
            one_slot(slot)
    else:
        lax.fori_loop(0, count, lambda slot, carry: (one_slot(slot), carry)[1], 0)
    total = arrived_ref[0, VIS : VIS + share, :].astype(wide_type)
    for block in range(1, count):
        total += arrived_ref[block, VIS : VIS + share, :].astype(wide_type)
    weight_grad_ref[...] = total


def early_out_kernel(keep_ref, other_ref, up_ref, down_ref):
    tiles = keep_ref.shape[0] // 2
    for tile in range(2 * tiles):
        total = keep_ref[tile].astype(wide_type) + other_ref[tile].astype(wide_type)
        if tile < tiles:
            up_ref[:, tile * LANES : (tile + 1) * LANES] = total
        else:
            down_ref[(tile - tiles) * LANES : (tile - tiles + 1) * LANES, :] = total.T


def late_out_kernel(keep_ref, other_ref, out_ref, qkv_ref, wide_ref):
    tiles = keep_ref.shape[0]
    for tile in range(tiles):
        wide_ref[:, tile * LANES : (tile + 1) * LANES] = keep_ref[tile].astype(wide_type) + other_ref[
            tile
        ].astype(wide_type)
    columns = out_ref.shape[0]
    wide_out = -(-columns // LANES) * LANES
    out_ref[...] = wide_ref[:, :wide_out].T[:columns]
    qkv_ref[...] = wide_ref[:, columns:]


VECTOR_ROWS = 48


def vectors_kernel(
    mask_ref, proj_ref, down_up_ref, second_ref, qkv_ref, first_ref, first_other_ref, out_ref, rows_ref
):
    heads = qkv_ref.shape[1] // (3 * HEAD_DIM)
    qkv = qkv_ref[...]
    first = first_ref[...] + first_other_ref[...]
    empty = jnp.zeros((1, 2 * LANES - heads * HEAD_DIM), wide_type)
    spread = []
    for part in (0, 2):
        spread += [
            qkv[:, (3 * head + part) * HEAD_DIM : (3 * head + part + 1) * HEAD_DIM] for head in range(heads)
        ] + [empty]
    heads_row = jnp.concatenate(spread, axis=1)
    row = 0
    for value in (
        heads_row, down_up_ref[1:2, :], proj_ref[...], mask_ref[...], first[0:1], first[1:2],
        second_ref[0:1, :], second_ref[1:2, :], second_ref[2:3, :], down_up_ref[0:1, :],
    ):
        for tile in range(value.shape[1] // LANES):
            rows_ref[row : row + 1, :] = value[:, tile * LANES : (tile + 1) * LANES]
            row += 1
    for block in range(out_ref.shape[0]):
        out_ref[block] = rows_ref[...]


def vectors_sum_kernel(rows_ref, out_ref):
    total = rows_ref[0]
    for block in range(1, rows_ref.shape[0]):
        total += rows_ref[block]
    out_ref[...] = total


def swap(value, axis, bit):
    count = lax.axis_size(axis)
    return lax.ppermute(value, axis, [(i, i ^ bit) for i in range(count)])


def low_add(left, right):
    return (left.astype(wide_type) + right.astype(wide_type)).astype(low_type)


def model_sum(keep, sent):
    total = low_add(keep, swap(sent, "mp", 1))
    bit = 2
    while bit < lax.axis_size("mp"):
        total = low_add(total, swap(total, "mp", bit))
        bit *= 2
    return total, swap(total, "mp", 1)


def data_scatter(keep, sent, index):
    received = swap(sent, "dp", 1)
    bit = 2
    while keep.shape[0] > 1:
        blocks = low_add(keep, received)
        parted = blocks.reshape(-1, 2, *blocks.shape[1:])
        upper = (index & bit) != 0
        keep = jnp.where(upper, parted[:, 1], parted[:, 0])
        received = swap(jnp.where(upper, parted[:, 0], parted[:, 1]), "dp", bit)
        bit *= 2
    return keep[0], received[0]


def local(
    patch_rows, patches, visible, owner, qkv_weight, query_bias, value_bias, out_weight, out_bias, first_gain,
    first_shift, second_gain, second_shift, up_weight, up_bias, down_weight, down_bias, proj_weight, proj_bias,
    mask_token, decoder_pos, grid_cotangent,
):
    count = lax.axis_size("dp")
    parts = lax.axis_size("mp")
    data_index = lax.axis_index("dp")
    model_index = lax.axis_index("mp")
    where = jnp.stack([data_index, model_index]).astype(jnp.int32)
    rows, width = patch_rows.shape
    images = rows // VIS
    heads = qkv_weight.shape[1] // (3 * HEAD_DIM)
    units = up_weight.shape[1]
    columns = proj_weight.shape[1]
    share = width // count
    pos_share = GRID // count
    half = rows // 2
    pad = -(-share // 16) * 16
    pos_pad = -(-pos_share // 16) * 16

    tables = grid_tables()
    table_high = tables.astype(low_type)
    table_low = (tables - table_high.astype(np.float32)).astype(low_type)
    turned_high = jnp.asarray(np.ascontiguousarray(table_high.transpose(0, 2, 1)))
    turned_low = jnp.asarray(np.ascontiguousarray(table_low.transpose(0, 2, 1)))
    table_high, table_low = jnp.asarray(table_high), jnp.asarray(table_low)

    vec = jnp.stack(
        [first_gain, first_shift, out_bias, second_gain, second_shift, down_bias]
    ).astype(wide_type)
    nothing = jnp.zeros((heads, HEAD_DIM), wide_type)
    qkv_bias = jnp.stack(
        [
            query_bias.astype(wide_type).reshape(heads, HEAD_DIM),
            nothing,
            value_bias.astype(wide_type).reshape(heads, HEAD_DIM),
        ],
        axis=1,
    ).reshape(1, -1)
    up_bias_row = up_bias.astype(wide_type).reshape(1, -1)
    proj_bias_row = proj_bias.astype(wide_type).reshape(1, -1)
    mask_row = mask_token.astype(wide_type).reshape(1, -1)

    def low(*shape):
        return (shape, low_type)

    def wide(*shape):
        return (shape, wide_type)

    back_send, source, mask_grad = call(
        lambda *refs: cotangent_kernel(count, images, *refs),
        [low(count, VIS + pos_pad, columns), ((count,), jnp.int32), wide(1, columns)],
        (where, owner, patches, visible, grid_cotangent, turned_high, turned_low),
        (SMEM, SMEM, SMEM, VMEM, VMEM, VMEM, VMEM),
        scratch=[pltpu.VMEM((3, GRID, columns), wide_type)],
        out_specs=(VMEM, SMEM, VMEM),
        flops=10**8,
        nbytes=2 * 10**6,
    )
    returned = lax.all_to_all(back_send, "dp", split_axis=0, concat_axis=0, tiled=True)

    act_one, qkv = call(
        enter_kernel,
        [low(rows, width), low(rows, qkv_weight.shape[1])],
        (patch_rows, vec[0:1], vec[1:2], qkv_weight, qkv_bias),
        (VMEM,) * 5,
        flops=10**9,
        nbytes=3 * 10**6,
    )

    enc_grad, grad_keep, grad_sent = call(
        lambda *refs: back_kernel(images, *refs),
        [low(rows, columns), low(half, width), low(half, width)],
        (where, owner, returned, proj_weight),
        (SMEM, SMEM, VMEM, VMEM),
        flops=10**8,
        nbytes=10**6,
    )
    grad_sum, grad_other = model_sum(grad_keep, grad_sent)

    probs, attended, keep, sent = call(
        lambda *refs: attention_kernel(images, heads, *refs),
        [low(rows, heads * PAIR), low(rows, heads * HEAD_DIM), low(half, width), low(half, width)],
        (where, patches, qkv, out_weight),
        (SMEM, SMEM, VMEM, VMEM),
        flops=10**9,
        nbytes=3 * 10**6,
    )
    attn_sum, attn_other = model_sum(keep, sent)

    hidden, act_two, acted, up_low, down_low, bias_grads, keep, sent, fkeep, fsent = call(
        forward_back_kernel,
        [
            wide(rows, width), low(rows, width), low(rows, units), low(rows, units), low(rows, width),
            wide(2, width), low(half, width), low(half, width), low(half, width), low(half, width),
        ],
        (where, patch_rows, attn_sum, attn_other, grad_sum, grad_other, vec, up_weight, up_bias_row, down_weight),
        (SMEM,) + (VMEM,) * 9,
        scratch=[pltpu.VMEM((rows, width), low_type)],
        flops=3 * 10**9,
        nbytes=10**7,
    )
    second_sum, second_other = model_sum(keep, sent)
    out_sum, out_other = model_sum(fkeep, fsent)

    early_keep, early_sent = call(
        early_grads_kernel,
        [low(count // 2, 2 * units // LANES, share, LANES)] * 2,
        (where, act_two, up_low, acted, down_low),
        (SMEM,) + (VMEM,) * 4,
        scratch=[pltpu.VMEM((width, units), wide_type)],
        flops=2 * 10**9,
        nbytes=5 * 10**6,
    )
    early_keep, early_other = data_scatter(early_keep, early_sent, data_index)

    grads, own_grad, out_weight_grad, second_grads = call(
        lambda *refs: attention_back_kernel(heads, *refs),
        [low(rows, qkv_weight.shape[1]), wide(rows // parts, width), wide(width, heads * HEAD_DIM), wide(3, width)],
        (where, second_sum, second_other, hidden, down_low, vec, out_weight, qkv, probs, attended),
        (SMEM,) + (VMEM,) * 9,
        scratch=[
            pltpu.VMEM((rows, width), low_type),
            pltpu.VMEM((rows, width), wide_type),
            pltpu.VMEM((rows, width), low_type),
        ],
        flops=2 * 10**9,
        nbytes=8 * 10**6,
    )
    late_columns = qkv_weight.shape[1] + heads * HEAD_DIM
    late_keep, late_sent, qkv_bias_grad = call(
        late_grads_kernel,
        [low(count // 2, late_columns // LANES, share, LANES)] * 2 + [wide(1, qkv_weight.shape[1])],
        (where, act_one, grads, out_weight_grad),
        (SMEM,) + (VMEM,) * 3,
        scratch=[pltpu.VMEM((width, late_columns), wide_type)],
        flops=10**9,
        nbytes=4 * 10**6,
    )
    late_keep, late_other = data_scatter(late_keep, late_sent, data_index)

    in_keep, in_sent, first_grads = call(
        input_part_kernel,
        [low(parts // 2, rows // parts, width)] * 2 + [wide(2, width)],
        (where, patch_rows, grads, qkv_weight),
        (SMEM,) + (VMEM,) * 3,
        scratch=[pltpu.VMEM((rows, width), wide_type)],
        flops=10**9,
        nbytes=4 * 10**6,
    )
    received = swap(in_sent, "mp", 1)
    bit = 2
    while in_keep.shape[0] > 1:
        blocks = low_add(in_keep, received)
        parted = blocks.reshape(-1, 2, *blocks.shape[1:])
        upper = (model_index & bit) != 0
        in_keep = jnp.where(upper, parted[:, 1], parted[:, 0])
        received = swap(jnp.where(upper, parted[:, 0], parted[:, 1]), "mp", bit)
        bit *= 2
    bit = 1
    while 2 * bit < parts:
        first_grads = first_grads + swap(first_grads, "mp", bit)
        bit *= 2
    first_other = swap(first_grads, "mp", bit)

    (input_grad,) = call(
        input_grad_kernel,
        [low(rows // parts, width)],
        (where, patch_rows, in_keep[0], received[0], own_grad, vec[0:1]),
        (SMEM,) + (VMEM,) * 5,
        flops=10**7,
        nbytes=2 * 10**6,
    )

    send, proj_bias_grad = call(
        lambda *refs: encoded_kernel(images, *refs),
        [low(count, VIS + pad, columns), wide(1, columns)],
        (where, owner, hidden, out_sum, out_other, vec, proj_weight, proj_bias_row, enc_grad),
        (SMEM, SMEM) + (VMEM,) * 7,
        scratch=[
            pltpu.VMEM((rows, width), low_type),
            pltpu.VMEM((rows, width), low_type),
            pltpu.VMEM((width, columns), wide_type),
        ],
        flops=3 * 10**8,
        nbytes=4 * 10**6,
    )
    arrived = lax.all_to_all(send, "dp", split_axis=0, concat_axis=0, tiled=True)
    grids, proj_weight_grad = call(
        grids_kernel,
        [low(count, GRID, columns), wide(share, columns)],
        (source, patches, visible, arrived, mask_row, decoder_pos, table_high, table_low),
        (SMEM, SMEM) + (VMEM,) * 6,
        scratch=[pltpu.VMEM((3, GRID, columns), wide_type)],
        flops=10**8,
        nbytes=2 * 10**6,
    )

    (vector_rows,) = call(
        vectors_kernel,
        [wide(count, VECTOR_ROWS, LANES)],
        (mask_grad, proj_bias_grad, bias_grads, second_grads, qkv_bias_grad, first_grads, first_other),
        (VMEM,) * 7,
        scratch=[pltpu.VMEM((VECTOR_ROWS, LANES), wide_type)],
        nbytes=10**6,
    )
    vector_rows = lax.all_to_all(vector_rows, "dp", split_axis=0, concat_axis=0, tiled=True)
    (vectors,) = call(vectors_sum_kernel, [wide(VECTOR_ROWS, LANES)], (vector_rows,), (VMEM,), nbytes=10**6)
    flat = vectors.reshape(-1)
    pos_grad = jnp.sum(returned[:, VIS : VIS + pos_share, :].astype(wide_type), axis=0)

    up_weight_grad, down_weight_grad = call(
        early_out_kernel,
        [wide(share, units), wide(units, share)],
        (early_keep, early_other),
        (VMEM,) * 2,
        nbytes=2 * 10**6,
    )
    out_weight_grad, qkv_weight_grad = call(
        late_out_kernel,
        [wide(heads * HEAD_DIM, share), wide(share, qkv_weight.shape[1])],
        (late_keep, late_other),
        (VMEM,) * 2,
        scratch=[pltpu.VMEM((share, late_columns), wide_type)],
        nbytes=10**6,
    )

    tile = LANES
    head_columns = heads * HEAD_DIM
    return (
        grids,
        input_grad,
        qkv_weight_grad,
        flat[:head_columns],
        flat[2 * tile : 2 * tile + head_columns],
        out_weight_grad,
        flat[36 * tile : 42 * tile],
        flat[12 * tile : 18 * tile],
        flat[18 * tile : 24 * tile],
        flat[24 * tile : 30 * tile],
        flat[30 * tile : 36 * tile],
        up_weight_grad,
        flat[4 * tile : 10 * tile],
        down_weight_grad,
        flat[42 * tile : 48 * tile],
        proj_weight_grad,
        flat[10 * tile : 11 * tile],
        flat[11 * tile : 12 * tile],
        pos_grad,
    )


def solution(mesh):
    return jax.shard_map(
        local,
        mesh=mesh,
        in_specs=(
            P("dp", None), P(), P(), P(), P(None, "mp"), P("mp"), P("mp"), P("mp", None), P(), P(), P(), P(), P(),
            P(None, "mp"), P("mp"), P("mp", None), P(), P(None, "mp"), P("mp"), P("mp"), P(None, "mp"),
            P("dp", None, "mp"),
        ),
        out_specs=(
            P("dp", None, "mp"), P(("dp", "mp"), None), P("dp", "mp"), P("mp"), P("mp"), P("mp", "dp"), P(), P(),
            P(), P(), P(), P("dp", "mp"), P("mp"), P("mp", "dp"), P(), P("dp", "mp"), P("mp"), P("mp"),
            P("dp", "mp"),
        ),
        check_vma=False,
    )
```

```python
import math

import jax
import jax.numpy as jnp
import numpy as np
from jax import lax
from jax.experimental import pallas as pl
from jax.experimental.pallas import tpu as pltpu
from jax.sharding import PartitionSpec as P

HEAD_DIM = 64
GRID = 256
VIS = 64
PAIR = 2 * VIS
CHUNK = 512
LANES = 128

epsilon = 1e-06
low_type = jnp.bfloat16
wide_type = jnp.float32
scale_factor = HEAD_DIM ** (-0.5)

VMEM = pl.BlockSpec(memory_space=pltpu.VMEM)
SMEM = pl.BlockSpec(memory_space=pltpu.SMEM)
ANY = pl.BlockSpec(memory_space=pl.ANY)
PINNED_ROWS = 512


def grid_tables():
    grid_edge = math.isqrt(GRID)
    tables = []
    for side_cells in (10, 14):
        places = np.arange(side_cells)
        centers = ((2 * places + 1) * grid_edge - side_cells) / (2 * side_cells)
        lower = np.floor(centers).astype(np.int64)
        share = centers - lower
        lerp = np.zeros((side_cells, grid_edge))
        lerp[places, np.clip(lower, 0, grid_edge - 1)] += 1.0 - share
        lerp[places, np.clip(lower + 1, 0, grid_edge - 1)] += share
        table = np.zeros((GRID, GRID))
        table[: side_cells * side_cells] = np.kron(lerp, lerp)
        tables.append(table)
    return np.stack(tables).astype(np.float32)


def split_low(value):
    high = value.astype(low_type)
    return high, (value - high.astype(wide_type)).astype(low_type)


def dot(left, right):
    return lax.dot_general(left, right, (((1,), (0,)), ((), ())), preferred_element_type=wide_type)


def dot_right_t(left, right):
    return lax.dot_general(left, right, (((1,), (1,)), ((), ())), preferred_element_type=wide_type)


def dot_left_t(left, right):
    return lax.dot_general(left, right, (((0,), (0,)), ((), ())), preferred_element_type=wide_type)


def normalized(value):
    center = value - jnp.mean(value, axis=-1, keepdims=True)
    spread = lax.rsqrt(jnp.mean(center * center, axis=-1, keepdims=True) + epsilon)
    return center * spread, spread


def norm_back(grad, normed, spread, gain):
    scaled = grad * gain
    mean_one = jnp.mean(scaled, axis=-1, keepdims=True)
    mean_two = jnp.mean(scaled * normed, axis=-1, keepdims=True)
    return spread * (scaled - mean_one - normed * mean_two)


def row_sum(value):
    return jnp.sum(value, axis=0, keepdims=True)


def over_rows(total, size, body):
    size = min(size, total)
    if total == size:
        body(0, size)
        return

    def step(i, carry):
        body(pl.multiple_of(i * size, size), size)
        return carry

    lax.fori_loop(0, total // size, step, 0)


def size_of(shape, kind):
    return math.prod(shape) * jnp.dtype(kind).itemsize


class Order:
    def __init__(self, pinned):
        self.pinned = pinned
        self.last = None
        self.held = []

    def keep(self, value):
        if not self.pinned:
            return value
        value = pltpu.with_memory_space_constraint(value, pltpu.VMEM)
        self.held.append(value)
        return value

    def __call__(self, kernel, outs, args, specs=None, scratch=(), out_specs=None, final=False):
        args = tuple(args)
        specs = [VMEM] * len(args) if specs is None else list(specs)
        count = len(args)
        needed = sum(size_of(ref.shape, ref.dtype) for ref in scratch)
        needed += sum(
            size_of(arg.shape, arg.dtype) for arg in args if not any(arg is held for held in self.held)
        )
        out_specs = [VMEM] * len(outs) if out_specs is None else list(out_specs)
        shapes = []
        for (shape, kind), spec in zip(outs, out_specs):
            if self.pinned and not final and spec is VMEM:
                shapes.append(pltpu.VMEM(shape, kind))
            else:
                shapes.append(jax.ShapeDtypeStruct(shape, kind))
                needed += size_of(shape, kind)
        body = kernel
        if self.last is not None:
            args += (self.last,)
            specs.append(ANY)

            def body(*refs):
                kernel(*refs[:count], *refs[count + 1 :])

        results = pl.pallas_call(
            body,
            out_shape=tuple(shapes),
            in_specs=specs,
            out_specs=tuple(out_specs),
            scratch_shapes=list(scratch),
            compiler_params=pltpu.CompilerParams(
                vmem_limit_bytes=min(needed + needed // 4 + 10 * 2**20, 60 * 2**20)
            ),
            cost_estimate=pl.CostEstimate(flops=1000, bytes_accessed=1000, transcendentals=0),
        )(*args)
        self.held += [
            result
            for result, shape in zip(results, shapes)
            if not isinstance(shape, jax.ShapeDtypeStruct)
        ]
        if not final:
            self.last = results[0]
        return results


def find_sources(count, images, me, owner_ref, source_ref):
    for slot in range(count):

        def find(i, found, slot=slot):
            return jnp.where(owner_ref[slot * images + i] == me, slot * images + i, found)

        source_ref[slot] = lax.fori_loop(0, images, find, slot * images, unroll=images <= 8)


def over_slots(count, one_slot):
    if count <= 8:
        for slot in range(count):
            one_slot(slot)
    else:
        lax.fori_loop(0, count, lambda slot, carry: (one_slot(slot), carry)[1], 0)


def side_of(size):
    return (size >= 196).astype(jnp.int32) + (size >= 256).astype(jnp.int32)


def cotangent_kernel(count, images, where_ref, owner_ref, visible_ref, cot_ref, send_ref, source_ref):
    find_sources(count, images, where_ref[0], owner_ref, source_ref)
    cells = lax.broadcasted_iota(jnp.int32, (GRID, VIS), 0)

    def one_slot(slot):
        seen = visible_ref[pl.ds(source_ref[slot], 1), :] == cells
        send_ref[slot] = dot_left_t(seen.astype(low_type), cot_ref[slot]).astype(low_type)

    over_slots(count, one_slot)


def position_kernel(
    count, source_ref, patches_ref, visible_ref, cot_ref, turned_high_ref, turned_low_ref, table_high_ref,
    table_low_ref, pos_ref, send_ref, mask_ref, layout_ref, sums_ref,
):
    share = GRID // count
    cells = lax.broadcasted_iota(jnp.int32, (GRID, VIS), 0)
    cell_column = lax.broadcasted_iota(jnp.int32, (GRID, 1), 0)
    sums_ref[...] = jnp.zeros_like(sums_ref)
    mask_ref[...] = jnp.zeros_like(mask_ref)

    def one_slot(slot):
        source = source_ref[slot]
        size = patches_ref[source]
        seen = visible_ref[pl.ds(source, 1), :] == cells
        fill = (cell_column < size).astype(wide_type) - jnp.sum(
            seen.astype(wide_type), axis=1, keepdims=True
        )
        wide = cot_ref[slot].astype(wide_type)
        mask_ref[...] += row_sum(fill * wide)
        sums_ref[side_of(size)] += wide

    over_slots(count, one_slot)
    total = sums_ref[2]
    for side in range(2):
        high, low = split_low(sums_ref[side])
        total += (
            dot(turned_high_ref[side], high) + dot(turned_high_ref[side], low) + dot(turned_low_ref[side], high)
        )
    send_ref[...] = jnp.zeros_like(send_ref)
    total = total.astype(low_type)
    for block in range(count):
        send_ref[block, :share, :] = total[block * share : (block + 1) * share]
    table = pos_ref[...]
    for side in range(2):
        layout_ref[side] = dot(table_high_ref[side], table) + dot(table_low_ref[side], table)
    layout_ref[2] = table.astype(wide_type)


def wide_row(ref):
    return ref[...].astype(wide_type).reshape(1, ref.shape[0])


def enter_kernel(rows_ref, gain_ref, shift_ref, weight_ref, query_ref, value_ref, act_ref, qkv_ref):
    gain, shift = wide_row(gain_ref), wide_row(shift_ref)
    query, value = wide_row(query_ref), wide_row(value_ref)
    nothing = jnp.zeros((1, HEAD_DIM), wide_type)
    pieces = []
    for start in range(0, query.shape[1], HEAD_DIM):
        pieces += [query[:, start : start + HEAD_DIM], nothing, value[:, start : start + HEAD_DIM]]
    bias = jnp.concatenate(pieces, axis=1)

    def body(start, size):
        rows = pl.ds(start, size)
        normed, _ = normalized(rows_ref[rows, :].astype(wide_type))
        act = (normed * gain + shift).astype(low_type)
        act_ref[rows, :] = act
        qkv_ref[rows, :] = (dot_right_t(act, weight_ref[...]) + bias).astype(low_type)

    over_rows(rows_ref.shape[0], CHUNK, body)


def attention_kernel(
    images, heads, where_ref, patches_ref, qkv_ref, weight_ref, keep_ref, sent_ref, prob_ref, attended_ref
):
    first_image = where_ref[0] * images
    row_half = lax.broadcasted_iota(jnp.int32, (PAIR, PAIR), 0) // VIS
    lane = lax.broadcasted_iota(jnp.int32, (PAIR, PAIR), 1)

    def body(start, size):
        for pair in range(size // PAIR):
            rows = pl.ds(start + pair * PAIR, PAIR)
            image = first_image + (start + pair * PAIR) // VIS
            limits = [patches_ref[image + i] // 4 for i in range(2)]
            last = jnp.where(row_half == 0, limits[0], VIS + limits[1])
            live = jnp.logical_and(lane >= row_half * VIS, lane < last)
            for head in range(heads):
                base = head * 3 * HEAD_DIM
                queries = qkv_ref[rows, base : base + HEAD_DIM]
                key_rows = qkv_ref[rows, base + HEAD_DIM : base + 2 * HEAD_DIM]
                value_rows = qkv_ref[rows, base + 2 * HEAD_DIM : base + 3 * HEAD_DIM]
                scores = jnp.where(live, dot_right_t(queries, key_rows) * scale_factor, -1e30)
                raised = jnp.exp(scores - jnp.max(scores, axis=-1, keepdims=True))
                probs = (raised / jnp.sum(raised, axis=-1, keepdims=True)).astype(low_type)
                prob_ref[rows, head * PAIR : (head + 1) * PAIR] = probs
                attended_ref[rows, head * HEAD_DIM : (head + 1) * HEAD_DIM] = dot(
                    probs, value_rows
                ).astype(low_type)

    over_rows(qkv_ref.shape[0], CHUNK, body)
    halves(where_ref[1] & 1, attended_ref, weight_ref, keep_ref, sent_ref, dot)


def halves(upper, left_ref, weight_ref, keep_ref, sent_ref, product):
    half = keep_ref.shape[0]
    for out_ref, which in ((sent_ref, 1 - upper), (keep_ref, upper)):

        def body(start, size, out_ref=out_ref, which=which):
            rows = pl.ds(pl.multiple_of(which * half + start, size), size)
            out_ref[pl.ds(start, size), :] = product(left_ref[rows, :], weight_ref[...]).astype(
                out_ref.dtype
            )

        over_rows(half, CHUNK, body)


def both_halves(upper, half, body):
    for source, which in enumerate((upper, 1 - upper)):

        def one(start, size, source=source, which=which):
            body(source, pl.ds(pl.multiple_of(which * half + start, size), size), pl.ds(start, size), size)

        over_rows(half, 256, one)


def back_kernel(images, where_ref, owner_ref, back_ref, weight_ref, keep_ref, sent_ref, enc_ref):
    base = where_ref[0] * images
    for image in range(images):
        enc_ref[image * VIS : (image + 1) * VIS, :] = back_ref[owner_ref[base + image]]
    halves(where_ref[1] & 1, enc_ref, weight_ref, keep_ref, sent_ref, dot_right_t)


def add_kernel(left_ref, right_ref, out_ref):
    out_ref[...] = (left_ref[...].astype(wide_type) + right_ref[...].astype(wide_type)).astype(low_type)


def forward_back_kernel(
    where_ref, rows_ref, sum_ref, sum_other_ref, grad_ref, grad_other_ref, out_bias_ref, gain_ref, shift_ref,
    up_ref, up_bias_ref, down_ref,
    keep_ref, sent_ref, hidden_ref, act_ref, acted_ref, up_low_ref, down_low_ref, bias_ref,
):
    upper = where_ref[1] & 1
    out_bias, gain, shift, up_bias = (
        wide_row(ref) for ref in (out_bias_ref, gain_ref, shift_ref, up_bias_ref)
    )

    def body(source, rows, part, size):
        total = (sum_ref, sum_other_ref)[source][part, :].astype(wide_type)
        hidden = rows_ref[rows, :].astype(wide_type) + total + out_bias
        hidden_ref[rows, :] = hidden
        normed, _ = normalized(hidden)
        act = (normed * gain + shift).astype(low_type)
        act_ref[rows, :] = act
        down_low = (grad_ref, grad_other_ref)[source][part, :]
        down_low_ref[rows, :] = down_low
        up_pre = dot(act, up_ref[...]) + up_bias
        cdf = 0.5 + 0.5 * lax.erf(up_pre * math.sqrt(0.5))
        acted_ref[rows, :] = (up_pre * cdf).astype(low_type)
        slope = cdf + up_pre * jnp.exp(-0.5 * up_pre * up_pre) * (1.0 / math.sqrt(2.0 * math.pi))
        up_low_ref[rows, :] = (dot_right_t(down_low, down_ref[...]) * slope).astype(low_type)

    both_halves(upper, sum_ref.shape[0], body)
    halves(upper, up_low_ref, up_ref, keep_ref, sent_ref, dot_right_t)
    bias_ref[0:1, :] = row_sum(down_low_ref[...].astype(wide_type))
    bias_ref[1:2, :] = row_sum(up_low_ref[...].astype(wide_type))


def part_blocks(lower_bit, wide_ref, parts, keep_ref, sent_ref, first_tile):
    share = keep_ref.shape[2]
    for out_ref, which in ((sent_ref, 1 - lower_bit), (keep_ref, lower_bit)):
        for block in range(keep_ref.shape[0]):
            rows = pl.ds(pl.multiple_of((2 * block + which) * share, 8), share)
            for tile in range(parts):
                out_ref[block, first_tile + tile] = wide_ref[
                    rows, tile * LANES : (tile + 1) * LANES
                ].astype(out_ref.dtype)


def early_grads_kernel(where_ref, act_ref, up_low_ref, acted_ref, down_low_ref, keep_ref, sent_ref, wide_ref):
    lower_bit = where_ref[0] & 1
    tiles = wide_ref.shape[1] // LANES
    wide_ref[...] = dot_left_t(act_ref[...], up_low_ref[...])
    part_blocks(lower_bit, wide_ref, tiles, keep_ref, sent_ref, 0)
    wide_ref[...] = dot_left_t(down_low_ref[...], acted_ref[...])
    part_blocks(lower_bit, wide_ref, tiles, keep_ref, sent_ref, tiles)


def forward_part_kernel(where_ref, acted_ref, down_ref, keep_ref, sent_ref):
    halves(where_ref[1] & 1, acted_ref, down_ref, keep_ref, sent_ref, dot)


def attention_back_kernel(
    heads, where_ref, sum_ref, sum_other_ref, hidden_ref, down_low_ref, gain_ref, weight_ref, qkv_ref, prob_ref,
    grads_ref, attn_low_ref, own_ref, bias_ref, grad_ref,
):
    gain = wide_row(gain_ref)
    bias_ref[...] = jnp.zeros_like(bias_ref)

    def body(source, rows, part, size):
        normed, spread = normalized(hidden_ref[rows, :])
        grad = (sum_ref, sum_other_ref)[source][part, :].astype(wide_type)
        bias_ref[0:1, :] += row_sum(grad * normed)
        bias_ref[1:2, :] += row_sum(grad)
        hidden_grad = down_low_ref[rows, :].astype(wide_type) + norm_back(grad, normed, spread, gain)
        grad_ref[rows, :] = hidden_grad
        bias_ref[2:3, :] += row_sum(hidden_grad)
        attn_low = hidden_grad.astype(low_type)
        attn_low_ref[rows, :] = attn_low
        attended_grad = dot_right_t(attn_low, weight_ref[...]).astype(low_type)
        for pair in range(size // PAIR):
            pair_rows = pl.ds(rows.start + pair * PAIR, PAIR)
            for head in range(heads):
                base = head * 3 * HEAD_DIM
                queries = qkv_ref[pair_rows, base : base + HEAD_DIM]
                key_rows = qkv_ref[pair_rows, base + HEAD_DIM : base + 2 * HEAD_DIM]
                value_rows = qkv_ref[pair_rows, base + 2 * HEAD_DIM : base + 3 * HEAD_DIM]
                probs = prob_ref[pair_rows, head * PAIR : (head + 1) * PAIR]
                grad_rows = attended_grad[
                    pair * PAIR : (pair + 1) * PAIR, head * HEAD_DIM : (head + 1) * HEAD_DIM
                ]
                value_low = dot_left_t(probs, grad_rows).astype(low_type)
                prob_grad = dot_right_t(grad_rows, value_rows)
                wide_probs = probs.astype(wide_type)
                weighted = wide_probs * prob_grad
                score_low = (
                    weighted - wide_probs * jnp.sum(weighted, axis=-1, keepdims=True)
                ).astype(low_type)
                query_low = (dot(score_low, key_rows) * scale_factor).astype(low_type)
                key_low = (dot_left_t(score_low, queries) * scale_factor).astype(low_type)
                grads_ref[pair_rows, base : base + HEAD_DIM] = query_low
                grads_ref[pair_rows, base + HEAD_DIM : base + 2 * HEAD_DIM] = key_low
                grads_ref[pair_rows, base + 2 * HEAD_DIM : base + 3 * HEAD_DIM] = value_low

    both_halves(where_ref[1] & 1, sum_ref.shape[0], body)
    share = own_ref.shape[0]
    own_ref[...] = grad_ref[pl.ds(pl.multiple_of(where_ref[1] * share, share), share), :]


def late_grads_kernel(
    where_ref, act_ref, grads_ref, attn_low_ref, attended_ref, keep_ref, sent_ref, bias_ref, wide_ref
):
    columns = grads_ref.shape[1]
    first = attended_ref.shape[1]
    wide_ref[:, :first] = dot_left_t(attn_low_ref[...], attended_ref[...])
    wide_ref[:, first : first + columns] = dot_left_t(act_ref[...], grads_ref[...])
    part_blocks(where_ref[0] & 1, wide_ref, wide_ref.shape[1] // LANES, keep_ref, sent_ref, 0)
    bias_ref[...] = row_sum(grads_ref[...].astype(wide_type))


EXTRA = 16


def put_extra(ref, start, gain, shift):
    rows = []
    for value in (gain, shift):
        rows += list(split_low(value))
    rows.append(jnp.zeros((EXTRA - 4, gain.shape[1]), low_type))
    ref[start : start + EXTRA, :] = jnp.concatenate(rows, axis=0)


def get_extra(ref, start):
    rows = ref[start : start + EXTRA, :].astype(wide_type)
    return rows[0:1] + rows[1:2], rows[2:3] + rows[3:4]


def input_part_kernel(where_ref, rows_ref, grads_ref, weight_ref, keep_ref, sent_ref, part_ref, bias_ref):
    lower_bit = where_ref[1] & 1
    bias_ref[...] = jnp.zeros_like(bias_ref)

    def body(start, size):
        rows = pl.ds(start, size)
        grad = dot(grads_ref[rows, :], weight_ref[...])
        part_ref[rows, :] = grad
        normed, _ = normalized(rows_ref[rows, :].astype(wide_type))
        bias_ref[0:1, :] += row_sum(grad * normed)
        bias_ref[1:2, :] += row_sum(grad)

    over_rows(rows_ref.shape[0], CHUNK, body)
    size = keep_ref.shape[0] - EXTRA
    share = size // (lax.axis_size("mp") // 2)
    for out_ref, which in ((sent_ref, 1 - lower_bit), (keep_ref, lower_bit)):
        for block in range(size // share):
            rows = pl.ds(pl.multiple_of((2 * block + which) * share, share), share)
            out_ref[block * share : (block + 1) * share, :] = part_ref[rows, :].astype(low_type)
        put_extra(out_ref, size, bias_ref[0:1, :], bias_ref[1:2, :])


def input_halve_kernel(bit, where_ref, keep_ref, other_ref, next_keep_ref, next_sent_ref, total_ref):
    upper = (where_ref[1] >> bit) & 1
    half = next_keep_ref.shape[0] - EXTRA
    size = 2 * half
    share = total_ref.shape[0] - size
    total_ref[:size, :] = keep_ref[:size, :].astype(wide_type) + other_ref[:size, :].astype(wide_type)
    own, other = get_extra(keep_ref, size), get_extra(other_ref, size)
    for out_ref, which in ((next_sent_ref, 1 - upper), (next_keep_ref, upper)):
        for block in range(half // share):
            rows = pl.ds(pl.multiple_of((2 * block + which) * share, share), share)
            out_ref[block * share : (block + 1) * share, :] = total_ref[rows, :].astype(low_type)
        put_extra(out_ref, half, own[0] + other[0], own[1] + other[1])


def input_grad_kernel(where_ref, rows_ref, keep_ref, other_ref, own_ref, gain_ref, out_ref):
    share = out_ref.shape[0]
    rows = pl.ds(pl.multiple_of(where_ref[1] * share, share), share)
    normed, spread = normalized(rows_ref[rows, :].astype(wide_type))
    grad = keep_ref[:share, :].astype(wide_type) + other_ref[:share, :].astype(wide_type)
    out_ref[...] = (own_ref[...] + norm_back(grad, normed, spread, wide_row(gain_ref))).astype(low_type)


VECTOR_ROWS = 48


def vector_rows(heads, mask_ref, down_up_ref, second_ref, qkv_ref, proj, gain, shift, rows_ref):
    qkv = qkv_ref[...]
    empty = jnp.zeros((1, 2 * LANES - heads * HEAD_DIM), wide_type)
    spread = []
    for part in (0, 2):
        spread += [
            qkv[:, (3 * head + part) * HEAD_DIM : (3 * head + part + 1) * HEAD_DIM] for head in range(heads)
        ] + [empty]
    row = 0
    for value in (
        jnp.concatenate(spread, axis=1), down_up_ref[1:2, :], proj, mask_ref[...], gain, shift,
        second_ref[0:1, :], second_ref[1:2, :], second_ref[2:3, :], down_up_ref[0:1, :],
    ):
        for tile in range(value.shape[1] // LANES):
            rows_ref[row : row + 1, :] = value[:, tile * LANES : (tile + 1) * LANES]
            row += 1


def encoded_kernel(
    images, heads, pad, where_ref, owner_ref, hidden_ref, sum_ref, sum_other_ref, down_bias_ref, weight_ref,
    bias_ref, enc_ref, mask_ref, down_up_ref, second_ref, qkv_ref, first_ref, first_other_ref,
    send_ref, low_ref, wide_ref, rows_ref,
):
    down_bias, bias = wide_row(down_bias_ref), wide_row(bias_ref)
    base = where_ref[0] * images

    def body(source, rows, part, size):
        total = (sum_ref, sum_other_ref)[source][part, :].astype(wide_type)
        out_low = (hidden_ref[rows, :] + total + down_bias).astype(low_type)
        low_ref[rows, :] = out_low
        encoded = (dot(out_low, weight_ref[...]) + bias).astype(low_type)
        for image in range(size // VIS):
            send_ref[owner_ref[base + rows.start // VIS + image], :VIS, :] = encoded[
                image * VIS : (image + 1) * VIS
            ]

    both_halves(where_ref[1] & 1, sum_ref.shape[0], body)
    wide_ref[...] = dot_left_t(low_ref[...], enc_ref[...])
    count = send_ref.shape[0]
    share = wide_ref.shape[0] // count
    own = get_extra(first_ref, first_ref.shape[0] - EXTRA)
    other = get_extra(first_other_ref, first_ref.shape[0] - EXTRA)
    proj = row_sum(enc_ref[...].astype(wide_type))
    vector_rows(
        heads, mask_ref, down_up_ref, second_ref, qkv_ref, proj, own[0] + other[0], own[1] + other[1], rows_ref
    )
    for block in range(count):
        send_ref[block, VIS : VIS + share, :] = wide_ref[block * share : (block + 1) * share, :].astype(
            low_type
        )
        if pad > share:
            send_ref[block, VIS + share : VIS + pad, :] = jnp.zeros((pad - share, LANES), low_type)
        send_ref[block, VIS + pad :, :] = rows_ref[...].astype(low_type)


def grids_kernel(
    pad, heads, source_ref, patches_ref, visible_ref, arrived_ref, mask_ref, layout_ref, moved_ref, grids_ref,
    weight_grad_ref, pos_grad_ref, *refs
):
    *vector_refs, rows_ref = refs
    count = grids_ref.shape[0]
    share = weight_grad_ref.shape[0]
    cells = lax.broadcasted_iota(jnp.int32, (GRID, VIS), 0)
    cell_column = lax.broadcasted_iota(jnp.int32, (GRID, 1), 0)
    mask_row = wide_row(mask_ref)

    def one_slot(slot):
        source = source_ref[slot]
        seen = visible_ref[pl.ds(source, 1), :] == cells
        size = patches_ref[source]
        fill = (cell_column < size).astype(wide_type) - jnp.sum(
            seen.astype(wide_type), axis=1, keepdims=True
        )
        placed = dot(seen.astype(low_type), arrived_ref[slot, :VIS, :])
        grids_ref[slot] = (placed + fill * mask_row + layout_ref[side_of(size)]).astype(low_type)

    over_slots(count, one_slot)

    def summed(ref, start, size):
        total = ref[0, start : start + size, :].astype(wide_type)
        for block in range(1, count):
            total += ref[block, start : start + size, :].astype(wide_type)
        return total

    weight_grad_ref[...] = summed(arrived_ref, VIS, share)
    pos_grad_ref[...] = summed(moved_ref, 0, pos_grad_ref.shape[0])
    rows_ref[...] = summed(arrived_ref, VIS + pad, VECTOR_ROWS)
    row = 0
    for ref in vector_refs:
        size = ref.shape[0]
        for tile in range(-(-size // LANES)):
            width = min(LANES, size - tile * LANES)
            ref[tile * LANES : tile * LANES + width] = rows_ref[row, :width]
            row += 1


def halve_kernel(bit, where_ref, keep_ref, other_ref, next_keep_ref, next_sent_ref):
    upper = (where_ref[0] >> bit) & 1
    for out_ref, which in ((next_sent_ref, 1 - upper), (next_keep_ref, upper)):
        for block in range(next_keep_ref.shape[0]):
            at = 2 * block + which
            out_ref[block] = (keep_ref[at].astype(wide_type) + other_ref[at].astype(wide_type)).astype(
                low_type
            )


def early_out_kernel(keep_ref, other_ref, up_ref, down_ref):
    tiles = keep_ref.shape[1] // 2
    for tile in range(2 * tiles):
        out_ref = up_ref if tile < tiles else down_ref
        at = (tile % tiles) * LANES
        out_ref[:, at : at + LANES] = keep_ref[0, tile].astype(wide_type) + other_ref[0, tile].astype(
            wide_type
        )


def late_out_kernel(keep_ref, other_ref, out_ref, qkv_ref, wide_ref):
    for tile in range(keep_ref.shape[1]):
        wide_ref[:, tile * LANES : (tile + 1) * LANES] = keep_ref[0, tile].astype(wide_type) + other_ref[
            0, tile
        ].astype(wide_type)
    columns = out_ref.shape[0]
    wide_out = -(-columns // LANES) * LANES
    out_ref[...] = wide_ref[:, :wide_out].T[:columns]
    qkv_ref[...] = wide_ref[:, columns:]


def swap(value, axis, bit):
    count = lax.axis_size(axis)
    return lax.ppermute(value, axis, [(i, i ^ bit) for i in range(count)])


def local(
    patch_rows, patches, visible, owner, qkv_weight, query_bias, value_bias, out_weight, out_bias, first_gain,
    first_shift, second_gain, second_shift, up_weight, up_bias, down_weight, down_bias, proj_weight, proj_bias,
    mask_token, decoder_pos, grid_cotangent,
):
    count = lax.axis_size("dp")
    parts = lax.axis_size("mp")
    where = jnp.stack([lax.axis_index("dp"), lax.axis_index("mp")]).astype(jnp.int32)
    rows, width = patch_rows.shape
    images = rows // VIS
    heads = qkv_weight.shape[1] // (3 * HEAD_DIM)
    head_columns = heads * HEAD_DIM
    qkv_columns = qkv_weight.shape[1]
    units = up_weight.shape[1]
    columns = proj_weight.shape[1]
    share = width // count
    pos_share = GRID // count
    half = rows // 2
    own_rows = rows // parts
    pad = -(-share // 16) * 16
    pos_pad = -(-pos_share // 16) * 16
    run = Order(rows <= PINNED_ROWS)

    tables = grid_tables()
    table_high = tables.astype(low_type)
    table_low = (tables - table_high.astype(np.float32)).astype(low_type)
    turned_high = jnp.asarray(np.ascontiguousarray(table_high.transpose(0, 2, 1)))
    turned_low = jnp.asarray(np.ascontiguousarray(table_low.transpose(0, 2, 1)))
    table_high, table_low = jnp.asarray(table_high), jnp.asarray(table_low)
    qkv_weight_t = qkv_weight.T

    def low(*shape):
        return (shape, low_type)

    def wide(*shape):
        return (shape, wide_type)

    def moved(value, axis, bit):
        return run.keep(swap(value, axis, bit))

    def spread(value):
        return run.keep(lax.all_to_all(value, "dp", split_axis=0, concat_axis=0, tiled=True))

    def model_steps(keep, sent):
        received = moved(sent, "mp", 1)
        yield
        (total,) = run(add_kernel, [low(half, width)], (keep, received))
        bit = 2
        while bit < parts:
            received = moved(total, "mp", bit)
            yield
            (total,) = run(add_kernel, [low(half, width)], (total, received))
            bit *= 2
        return total, moved(total, "mp", 1)

    def data_steps(keep, sent):
        received = moved(sent, "dp", 1)
        yield
        bit = 1
        while keep.shape[0] > 1:
            shape = (keep.shape[0] // 2,) + keep.shape[1:]
            keep, sent = run(
                lambda *refs, bit=bit: halve_kernel(bit, *refs),
                [low(*shape)] * 2,
                (where, keep, received),
                (SMEM, VMEM, VMEM),
            )
            received = moved(sent, "dp", 2**bit)
            yield
            bit += 1
        return keep, received

    def finish(steps):
        while True:
            try:
                next(steps)
            except StopIteration as stop:
                return stop.value

    back_send, source = run(
        lambda *refs: cotangent_kernel(count, images, *refs),
        [low(count, VIS, columns), ((count,), jnp.int32)],
        (where, owner, visible, grid_cotangent),
        (SMEM, SMEM, VMEM, VMEM),
        out_specs=(VMEM, SMEM),
    )
    returned = spread(back_send)
    act_one, qkv = run(
        enter_kernel,
        [low(rows, width), low(rows, qkv_columns)],
        (patch_rows, first_gain, first_shift, qkv_weight_t, query_bias, value_bias),
    )
    grad_keep, grad_sent, enc_grad = run(
        lambda *refs: back_kernel(images, *refs),
        [low(half, width), low(half, width), low(rows, columns)],
        (where, owner, returned, proj_weight),
        (SMEM, SMEM, VMEM, VMEM),
    )
    grad_steps = model_steps(grad_keep, grad_sent)
    next(grad_steps)
    next(grad_steps)
    keep, sent, probs, attended = run(
        lambda *refs: attention_kernel(images, heads, *refs),
        [low(half, width), low(half, width), low(rows, heads * PAIR), low(rows, head_columns)],
        (where, patches, qkv, out_weight),
        (SMEM, SMEM, VMEM, VMEM),
    )
    attn_steps = model_steps(keep, sent)
    next(attn_steps)
    next(attn_steps)
    grad_sum, grad_other = finish(grad_steps)
    pos_send, mask_grad, layouts = run(
        lambda *refs: position_kernel(count, *refs),
        [low(count, pos_pad, columns), wide(1, columns), wide(3, GRID, columns)],
        (source, patches, visible, grid_cotangent, turned_high, turned_low, table_high, table_low, decoder_pos),
        (SMEM, SMEM) + (VMEM,) * 7,
        scratch=[pltpu.VMEM((3, GRID, columns), wide_type)],
    )
    pos_moved = spread(pos_send)
    attn_sum, attn_other = finish(attn_steps)

    keep, sent, hidden, act_two, acted, up_low, down_low, bias_grads = run(
        forward_back_kernel,
        [
            low(half, width), low(half, width), wide(rows, width), low(rows, width), low(rows, units),
            low(rows, units), low(rows, width), wide(2, width),
        ],
        (
            where, patch_rows, attn_sum, attn_other, grad_sum, grad_other, out_bias, second_gain, second_shift,
            up_weight, up_bias, down_weight,
        ),
        (SMEM,) + (VMEM,) * 11,
    )
    second_steps = model_steps(keep, sent)
    next(second_steps)
    next(second_steps)
    early_keep, early_sent = run(
        early_grads_kernel,
        [low(count // 2, 2 * units // LANES, share, LANES)] * 2,
        (where, act_two, up_low, acted, down_low),
        (SMEM,) + (VMEM,) * 4,
        scratch=[pltpu.VMEM((width, units), wide_type)],
    )
    early_steps = data_steps(early_keep, early_sent)
    next(early_steps)
    keep, sent = run(
        forward_part_kernel,
        [low(half, width), low(half, width)],
        (where, acted, down_weight),
        (SMEM, VMEM, VMEM),
    )
    out_steps = model_steps(keep, sent)
    next(out_steps)
    second_sum, second_other = finish(second_steps)
    next(out_steps)
    grads, attn_low, own_grad, second_grads = run(
        lambda *refs: attention_back_kernel(heads, *refs),
        [low(rows, qkv_columns), low(rows, width), wide(own_rows, width), wide(3, width)],
        (where, second_sum, second_other, hidden, down_low, second_gain, out_weight, qkv, probs),
        (SMEM,) + (VMEM,) * 8,
        scratch=[pltpu.VMEM((rows, width), wide_type)],
    )
    late_columns = qkv_columns + head_columns
    late_keep, late_sent, qkv_bias_grad = run(
        late_grads_kernel,
        [low(count // 2, late_columns // LANES, share, LANES)] * 2 + [wide(1, qkv_columns)],
        (where, act_one, grads, attn_low, attended),
        (SMEM,) + (VMEM,) * 4,
        scratch=[pltpu.VMEM((width, late_columns), wide_type)],
    )
    late_steps = data_steps(late_keep, late_sent)
    next(late_steps)
    in_keep, in_sent = run(
        input_part_kernel,
        [low(half + EXTRA, width)] * 2,
        (where, patch_rows, grads, qkv_weight_t),
        (SMEM,) + (VMEM,) * 3,
        scratch=[pltpu.VMEM((rows, width), wide_type), pltpu.VMEM((2, width), wide_type)],
    )
    in_other = moved(in_sent, "mp", 1)
    out_sum, out_other = finish(out_steps)
    bit = 1
    size = half
    while 2**bit < parts:
        in_keep, in_sent = run(
            lambda *refs, bit=bit: input_halve_kernel(bit, *refs),
            [low(size // 2 + EXTRA, width)] * 2,
            (where, in_keep, in_other),
            (SMEM, VMEM, VMEM),
            scratch=[pltpu.VMEM((size + own_rows, width), wide_type)],
        )
        in_other = moved(in_sent, "mp", 2**bit)
        size //= 2
        bit += 1
    (send,) = run(
        lambda *refs: encoded_kernel(images, heads, pad, *refs),
        [low(count, VIS + pad + VECTOR_ROWS, columns)],
        (
            where, owner, hidden, out_sum, out_other, down_bias, proj_weight, proj_bias, enc_grad, mask_grad,
            bias_grads, second_grads, qkv_bias_grad, in_keep, in_other,
        ),
        (SMEM, SMEM) + (VMEM,) * 13,
        scratch=[
            pltpu.VMEM((rows, width), low_type),
            pltpu.VMEM((width, columns), wide_type),
            pltpu.VMEM((VECTOR_ROWS, LANES), wide_type),
        ],
    )
    arrived = spread(send)
    next(early_steps)
    (input_grad,) = run(
        input_grad_kernel,
        [low(own_rows, width)],
        (where, patch_rows, in_keep, in_other, own_grad, first_gain),
        (SMEM,) + (VMEM,) * 5,
        final=True,
    )
    next(late_steps)
    early_keep, early_other = finish(early_steps)
    late_keep, late_other = finish(late_steps)
    vector_sizes = [
        head_columns, head_columns, units, columns, columns, width, width, width, width, width, width
    ]
    (
        grids, proj_weight_grad, pos_grad, query_bias_grad, value_bias_grad, up_bias_grad, proj_bias_grad,
        mask_grad, first_gain_grad, first_shift_grad, second_gain_grad, second_shift_grad, out_bias_grad,
        down_bias_grad,
    ) = run(
        lambda *refs: grids_kernel(pad, heads, *refs),
        [low(count, GRID, columns), wide(share, columns), wide(pos_share, columns)]
        + [wide(size) for size in vector_sizes],
        (source, patches, visible, arrived, mask_token, layouts, pos_moved),
        (SMEM, SMEM) + (VMEM,) * 5,
        scratch=[pltpu.VMEM((VECTOR_ROWS, LANES), wide_type)],
        final=True,
    )
    up_weight_grad, down_weight_grad = run(
        early_out_kernel, [wide(share, units), wide(share, units)], (early_keep, early_other), final=True
    )
    out_weight_grad, qkv_weight_grad = run(
        late_out_kernel,
        [wide(head_columns, share), wide(share, qkv_columns)],
        (late_keep, late_other),
        scratch=[pltpu.VMEM((share, late_columns), wide_type)],
        final=True,
    )
    return (
        grids, input_grad, qkv_weight_grad, query_bias_grad, value_bias_grad, out_weight_grad, out_bias_grad,
        first_gain_grad, first_shift_grad, second_gain_grad, second_shift_grad, up_weight_grad, up_bias_grad,
        down_weight_grad.T, down_bias_grad, proj_weight_grad, proj_bias_grad, mask_grad, pos_grad,
    )


def solution(mesh):
    return jax.shard_map(
        local,
        mesh=mesh,
        in_specs=(
            P("dp", None), P(), P(), P(), P(None, "mp"), P("mp"), P("mp"), P("mp", None), P(), P(), P(), P(), P(),
            P(None, "mp"), P("mp"), P("mp", None), P(), P(None, "mp"), P("mp"), P("mp"), P(None, "mp"),
            P("dp", None, "mp"),
        ),
        out_specs=(
            P("dp", None, "mp"), P(("dp", "mp"), None), P("dp", "mp"), P("mp"), P("mp"), P("mp", "dp"), P(), P(),
            P(), P(), P(), P("dp", "mp"), P("mp"), P("mp", "dp"), P(), P("dp", "mp"), P("mp"), P("mp"),
            P("dp", "mp"),
        ),
        check_vma=False,
    )
```

```python
import math

import jax
import jax.numpy as jnp
import numpy as np
from jax import lax
from jax.experimental import pallas as pl
from jax.experimental.pallas import tpu as pltpu
from jax.sharding import PartitionSpec as P

HEAD_DIM = 64
GRID = 256
VIS = 64
PAIR = 2 * VIS
CHUNK = 512
LANES = 128

epsilon = 1e-06
low_type = jnp.bfloat16
wide_type = jnp.float32
scale_factor = HEAD_DIM ** (-0.5)

VMEM = pl.BlockSpec(memory_space=pltpu.VMEM)
SMEM = pl.BlockSpec(memory_space=pltpu.SMEM)
ANY = pl.BlockSpec(memory_space=pl.ANY)
PINNED_ROWS = 512


def grid_tables():
    grid_edge = math.isqrt(GRID)
    tables = []
    for side_cells in (10, 14):
        places = np.arange(side_cells)
        centers = ((2 * places + 1) * grid_edge - side_cells) / (2 * side_cells)
        lower = np.floor(centers).astype(np.int64)
        share = centers - lower
        lerp = np.zeros((side_cells, grid_edge))
        lerp[places, np.clip(lower, 0, grid_edge - 1)] += 1.0 - share
        lerp[places, np.clip(lower + 1, 0, grid_edge - 1)] += share
        table = np.zeros((GRID, GRID))
        table[: side_cells * side_cells] = np.kron(lerp, lerp)
        tables.append(table)
    return np.stack(tables).astype(np.float32)


def split_low(value):
    high = value.astype(low_type)
    return high, (value - high.astype(wide_type)).astype(low_type)


def dot(left, right):
    return lax.dot_general(left, right, (((1,), (0,)), ((), ())), preferred_element_type=wide_type)


def dot_right_t(left, right):
    return lax.dot_general(left, right, (((1,), (1,)), ((), ())), preferred_element_type=wide_type)


def dot_left_t(left, right):
    return lax.dot_general(left, right, (((0,), (0,)), ((), ())), preferred_element_type=wide_type)


def normalized(value):
    center = value - jnp.mean(value, axis=-1, keepdims=True)
    spread = lax.rsqrt(jnp.mean(center * center, axis=-1, keepdims=True) + epsilon)
    return center * spread, spread


def norm_back(grad, normed, spread, gain):
    scaled = grad * gain
    mean_one = jnp.mean(scaled, axis=-1, keepdims=True)
    mean_two = jnp.mean(scaled * normed, axis=-1, keepdims=True)
    return spread * (scaled - mean_one - normed * mean_two)


def row_sum(value):
    return jnp.sum(value, axis=0, keepdims=True)


def over_rows(total, size, body):
    size = min(size, total)
    if total <= 2 * size:
        for start in range(0, total, size):
            body(start, size)
        return

    def step(i, carry):
        body(pl.multiple_of(i * size, size), size)
        return carry

    lax.fori_loop(0, total // size, step, 0)


def size_of(shape, kind):
    return math.prod(shape) * jnp.dtype(kind).itemsize


RATE = 10**9
COST_SHARE = 20.0


class Order:
    def __init__(self, pinned):
        self.pinned = pinned
        self.last = None
        self.near = []
        self.far = []

    def keep(self, value):
        if self.pinned:
            self.near.append((value, pltpu.VMEM))
        return value

    def leave(self, *values):
        self.far += values

    def placed(self, value):
        for near, space in self.near:
            if value is near:
                return pltpu.with_memory_space_constraint(value, space)
        if any(value is far for far in self.far):
            return pltpu.with_memory_space_constraint(value, pltpu.HBM)
        return value

    def __call__(
        self, kernel, outs, args, specs=None, scratch=(), out_specs=None, final=False, stage=(), cost=1.0
    ):
        args = tuple(args)
        specs = [VMEM] * len(args) if specs is None else list(specs)
        out_specs = [VMEM] * len(outs) if out_specs is None else list(out_specs)
        count, results_count = len(args), len(outs)
        staged = list(stage) if self.pinned else []
        self.leave(*staged)
        needed = sum(size_of(ref.shape, ref.dtype) for ref in scratch)
        needed += sum(
            size_of(arg.shape, arg.dtype) for arg in args if not any(arg is near for near, _ in self.near)
        )
        shapes = []
        for (shape, kind), spec in zip(outs, out_specs):
            if self.pinned and not final:
                shapes.append((pltpu.SMEM if spec is SMEM else pltpu.VMEM)(shape, kind))
            else:
                shapes.append(jax.ShapeDtypeStruct(shape, kind))
                needed += size_of(shape, kind)
        tail = len(staged)
        args += tuple(staged)
        specs += [ANY] * tail
        skipped = 0
        if self.last is not None:
            args += (self.last,)
            specs.append(ANY)
            skipped = 1

        def body(*refs):
            own, sources, refs = refs[:count], refs[count : count + tail], refs[count + tail + skipped :]
            results, targets, refs = (
                refs[:results_count], refs[results_count : results_count + tail], refs[results_count + tail :]
            )
            copies = []
            if tail:
                *refs, sems = refs
                copies = [
                    pltpu.make_async_copy(source, target, sems.at[at])
                    for at, (source, target) in enumerate(zip(sources, targets))
                ]
            for copy in copies:
                copy.start()
            kernel(*own, *results, *refs)
            for copy in copies:
                copy.wait()

        results = pl.pallas_call(
            body,
            out_shape=tuple(shapes) + tuple(pltpu.VMEM(array.shape, array.dtype) for array in staged),
            in_specs=specs,
            out_specs=tuple(out_specs) + (VMEM,) * tail,
            scratch_shapes=list(scratch) + ([pltpu.SemaphoreType.DMA((tail,))] if tail else []),
            compiler_params=pltpu.CompilerParams(
                vmem_limit_bytes=min(needed + needed // 4 + 10 * 2**20, 60 * 2**20)
            ),
            cost_estimate=pl.CostEstimate(
                flops=int(cost * RATE * COST_SHARE), bytes_accessed=0, transcendentals=0
            ),
        )(*(self.placed(arg) for arg in args))
        if self.pinned and not final:
            for result, spec in zip(results, out_specs + [VMEM] * tail):
                self.near.append((result, pltpu.SMEM if spec is SMEM else pltpu.VMEM))
        if not final:
            self.last = results[0]
        if stage and not self.pinned:
            return (*results, *stage)
        return results


class Info:
    def __init__(self, count):
        self.count = count
        self.size = 2 + 5 * count

    def dp(self, ref):
        return ref[0]

    def mp(self, ref):
        return ref[1]

    def owner(self, ref, image):
        return ref[2 + image]

    def live(self, ref, image):
        return ref[2 + self.count + image]

    def source(self, ref, slot):
        return ref[2 + 2 * self.count + slot]

    def cells(self, ref, slot):
        return ref[2 + 3 * self.count + slot]

    def image(self, ref, owner):
        return ref[2 + 4 * self.count + owner]


def fill_info(count, where_ref, owner_ref, patches_ref, info_ref):
    me = where_ref[0]
    info_ref[0] = me
    info_ref[1] = where_ref[1]

    def one(at):
        own = me * count + at
        info_ref[2 + at] = owner_ref[own]
        info_ref[2 + 4 * count + owner_ref[own]] = at
        info_ref[2 + count + at] = patches_ref[own] // 4

        def find(i, found):
            return jnp.where(owner_ref[at * count + i] == me, at * count + i, found)

        source = lax.fori_loop(0, count, find, at * count, unroll=count <= 8)
        info_ref[2 + 2 * count + at] = source
        info_ref[2 + 3 * count + at] = patches_ref[source]

    over_slots(count, one)


def over_slots(count, one_slot):
    if count <= 8:
        for slot in range(count):
            one_slot(slot)
    else:
        lax.fori_loop(0, count, lambda slot, carry: (one_slot(slot), carry)[1], 0)


def side_of(size):
    return (size >= 196).astype(jnp.int32) + (size >= 256).astype(jnp.int32)


def block_at(rest, place, bit):
    low = rest & ((1 << place) - 1)
    return ((rest - low) << 1) + (bit << place) + low


class Exchange:
    def __init__(self, count, bits, block, moved=0, shared=0):
        self.count, self.bits, self.block, self.moved, self.shared = count, bits, block, moved, shared

    def blocks(self, step):
        return self.count >> (step + 1)

    def place(self, step):
        bit = self.bits[step]
        return bit - sum(done < bit for done in self.bits[:step])

    def moved_at(self, step):
        return self.blocks(step) * self.block

    def shared_at(self, step):
        return self.moved_at(step) + self.count // 2 * self.moved

    def rows(self, step):
        return self.shared_at(step) + self.shared

    def own_bit(self, step, info_ref):
        return (info_ref[0] >> self.bits[step]) & 1

    def targets(self, step, info_ref, keep_ref, sent_ref):
        own = self.own_bit(step, info_ref)
        place = self.place(step)
        for ref, which in ((sent_ref, 1 - own), (keep_ref, own)):
            yield ref, [block_at(block, place, which) for block in range(self.blocks(step))]

    def kernel(self, step, parts, info_ref, *refs):
        *from_refs, next_keep_ref, next_sent_ref = refs
        pairs = list(zip(parts, from_refs[::2], from_refs[1::2]))
        sources = 1 << (step - 1)
        rests = self.blocks(step - 1)
        for ref, indices in self.targets(step, info_ref, next_keep_ref, next_sent_ref):
            first, moved_at, shared_at = 0, self.moved_at(step), self.shared_at(step)
            for part, keep_ref, other_ref in pairs:
                for block, index in enumerate(indices if part.block else ()):
                    rows = pl.ds(pl.multiple_of(index * part.block, 16), part.block)
                    at = block * self.block + first
                    ref[at : at + part.block, :] = (
                        keep_ref[rows, :].astype(wide_type) + other_ref[rows, :].astype(wide_type)
                    ).astype(low_type)
                first += part.block
                for from_ref in (keep_ref, other_ref) if part.moved else ():
                    for source in range(sources):
                        for index in indices:
                            rows = part.moved_at(step - 1) + (source * rests + index) * part.moved
                            ref[moved_at : moved_at + part.moved, :] = from_ref[
                                pl.ds(pl.multiple_of(rows, 16), part.moved), :
                            ]
                            moved_at += part.moved
                if part.shared:
                    at = part.shared_at(step - 1)
                    rows = slice(at, at + part.shared)
                    ref[shared_at : shared_at + part.shared, :] = (
                        keep_ref[rows, :].astype(wide_type) + other_ref[rows, :].astype(wide_type)
                    ).astype(low_type)

    def arrived(self, keep_ref, other_ref):
        last = len(self.bits) - 1
        sources = 1 << last
        for half, ref in enumerate((keep_ref, other_ref)):
            for source in range(sources):
                relative = 0
                for step, bit in enumerate(self.bits):
                    relative |= (((source + half * sources) >> step) & 1) << bit
                yield relative, ref, self.moved_at(last) + source * self.moved

    def total(self, keep_ref, other_ref, start, size):
        rows = slice(start, start + size)
        return keep_ref[rows, :].astype(wide_type) + other_ref[rows, :].astype(wide_type)

    def shared_total(self, keep_ref, other_ref):
        return self.total(keep_ref, other_ref, self.shared_at(len(self.bits) - 1), self.shared)


def cotangent_kernel(
    info, exchange, where_ref, owner_ref, patches_ref, visible_ref, cot_ref, keep_ref, sent_ref, info_ref, seen_ref,
    turned_ref,
):
    count = info.count
    fill_info(count, where_ref, owner_ref, patches_ref, info_ref)

    def take(slot):
        seen_ref[pl.ds(slot, 1), :] = visible_ref[pl.ds(info.source(info_ref, slot), 1), :]

    over_slots(count, take)
    turned_ref[...] = seen_ref[...].astype(wide_type).T
    cells = lax.broadcasted_iota(jnp.int32, (VIS, GRID), 1).astype(wide_type)
    own = exchange.own_bit(0, info_ref)
    place = exchange.place(0)
    for slot in range(count):
        onehot = (turned_ref[:, slot : slot + 1] == cells).astype(wide_type).astype(low_type)
        rows = dot(onehot, cot_ref[slot]).astype(low_type)
        rest = (slot & ((1 << place) - 1)) | ((slot >> (place + 1)) << place)
        kept = ((slot >> place) & 1) == own

        @pl.when(kept)
        def _(rest=rest, rows=rows):
            keep_ref[rest * VIS : (rest + 1) * VIS, :] = rows

        @pl.when(jnp.logical_not(kept))
        def _(rest=rest, rows=rows):
            sent_ref[rest * VIS : (rest + 1) * VIS, :] = rows


def position_kernel(
    info, info_ref, visible_ref, cot_ref, turned_high_ref, turned_low_ref, table_high_ref, table_low_ref, pos_ref,
    grad_ref, mask_ref, layout_ref, sums_ref,
):
    cells = lax.broadcasted_iota(jnp.int32, (GRID, VIS), 0)
    cell_column = lax.broadcasted_iota(jnp.int32, (GRID, 1), 0)
    sums_ref[...] = jnp.zeros_like(sums_ref)
    mask_ref[...] = jnp.zeros_like(mask_ref)

    def one_slot(slot):
        size = info.cells(info_ref, slot)
        seen = visible_ref[pl.ds(slot, 1), :] == cells
        fill = (cell_column < size).astype(wide_type) - jnp.sum(
            seen.astype(wide_type), axis=1, keepdims=True
        )
        wide = cot_ref[slot].astype(wide_type)
        mask_ref[...] += row_sum(fill * wide)
        sums_ref[side_of(size)] += wide

    over_slots(info.count, one_slot)
    total = sums_ref[2]
    for side in range(2):
        high, low = split_low(sums_ref[side])
        total += (
            dot(turned_high_ref[side], high) + dot(turned_high_ref[side], low) + dot(turned_low_ref[side], high)
        )
    grad_ref[...] = total
    table = pos_ref[...]
    for side in range(2):
        layout_ref[side] = dot(table_high_ref[side], table) + dot(table_low_ref[side], table)
    layout_ref[2] = table.astype(wide_type)


def wide_row(ref):
    return ref[...].astype(wide_type).reshape(1, ref.shape[0])


def enter_kernel(
    rows_ref, gain_ref, shift_ref, weight_ref, query_ref, value_ref, out_ref, proj_ref, weights_ref, act_ref, qkv_ref
):
    weights_ref[: out_ref.shape[0], :] = out_ref[...]
    weights_ref[out_ref.shape[0] :, :] = proj_ref[...].astype(wide_type).T.astype(low_type)
    gain, shift = wide_row(gain_ref), wide_row(shift_ref)
    query, value = wide_row(query_ref), wide_row(value_ref)
    nothing = jnp.zeros((1, HEAD_DIM), wide_type)
    pieces = []
    for start in range(0, query.shape[1], HEAD_DIM):
        pieces += [query[:, start : start + HEAD_DIM], nothing, value[:, start : start + HEAD_DIM]]
    bias = jnp.concatenate(pieces, axis=1)

    def body(start, size):
        rows = pl.ds(start, size)
        normed, _ = normalized(rows_ref[rows, :].astype(wide_type))
        act = (normed * gain + shift).astype(low_type)
        act_ref[rows, :] = act
        qkv_ref[rows, :] = (dot_right_t(act, weight_ref[...]) + bias).astype(low_type)

    over_rows(rows_ref.shape[0], CHUNK, body)


PACKED = 256


def attention_kernel(info, heads, first, info_ref, qkv_ref, packed_ref, prob_ref, attended_ref):
    row_half = lax.broadcasted_iota(jnp.int32, (PAIR, PAIR), 0) // VIS
    lane = lax.broadcasted_iota(jnp.int32, (PAIR, PAIR), 1)
    columns = heads * HEAD_DIM
    full = columns // LANES * LANES
    rest = PACKED * (columns - full) // LANES

    def body(start, size):
        for pair in range(size // PAIR):
            rows = pl.ds(start + pair * PAIR, PAIR)
            from_rows = pl.ds(first + start + pair * PAIR, PAIR)
            image = (first + start + pair * PAIR) // VIS
            limits = [info.live(info_ref, image + i) for i in range(2)]
            last = jnp.where(row_half == 0, limits[0], VIS + limits[1])
            live = jnp.logical_and(lane >= row_half * VIS, lane < last)
            for head in range(heads):
                base = head * 3 * HEAD_DIM
                queries = qkv_ref[from_rows, base : base + HEAD_DIM]
                key_rows = qkv_ref[from_rows, base + HEAD_DIM : base + 2 * HEAD_DIM]
                value_rows = qkv_ref[from_rows, base + 2 * HEAD_DIM : base + 3 * HEAD_DIM]
                scores = jnp.where(live, dot_right_t(queries, key_rows) * scale_factor, -1e30)
                raised = jnp.exp(scores - jnp.max(scores, axis=-1, keepdims=True))
                probs = (raised / jnp.sum(raised, axis=-1, keepdims=True)).astype(low_type)
                prob_ref[rows, head * PAIR : (head + 1) * PAIR] = probs
                attended_ref[rows, head * HEAD_DIM : (head + 1) * HEAD_DIM] = dot(
                    probs, value_rows
                ).astype(low_type)
        at = start // PACKED * (full // LANES * PACKED + rest)
        rows = pl.ds(start, PACKED)
        for tile in range(full // LANES):
            packed_ref[pl.ds(at, PACKED), :] = attended_ref[rows, tile * LANES : (tile + 1) * LANES]
            at += PACKED
        pieces = [
            attended_ref[pl.ds(start + piece * rest, rest), full:].astype(wide_type)
            for piece in range(PACKED // rest)
        ]
        packed_ref[pl.ds(at, rest), :] = jnp.concatenate(pieces, axis=1).astype(low_type)

    over_rows(prob_ref.shape[0], PACKED, body)


def packed_product(packed_ref, weight_ref, start, columns):
    full = columns // LANES * LANES
    width = columns - full
    rest = PACKED * width // LANES
    at = start // PACKED * (full // LANES * PACKED + rest)
    total = None
    for tile in range(full // LANES):
        part = dot(packed_ref[pl.ds(at, PACKED), :], weight_ref[tile * LANES : (tile + 1) * LANES, :])
        total = part if total is None else total + part
        at += PACKED
    rows = packed_ref[pl.ds(at, rest), :].astype(wide_type)
    left = jnp.concatenate(
        [rows[:, piece * width : (piece + 1) * width] for piece in range(PACKED // rest)], axis=0
    ).astype(low_type)
    return total + dot(left, weight_ref[full:columns, :])


def halves(upper, left_ref, weight_ref, keep_ref, sent_ref, product):
    half = keep_ref.shape[0]
    for out_ref, which in ((sent_ref, 1 - upper), (keep_ref, upper)):

        def body(start, size, out_ref=out_ref, which=which):
            rows = pl.ds(pl.multiple_of(which * half + start, size), size)
            out_ref[pl.ds(start, size), :] = product(left_ref[rows, :], weight_ref[...]).astype(
                out_ref.dtype
            )

        over_rows(half, CHUNK, body)


def both_halves(upper, half, body):
    for source, which in enumerate((upper, 1 - upper)):

        def one(start, size, source=source, which=which):
            body(source, pl.ds(pl.multiple_of(which * half + start, size), size), pl.ds(start, size), size)

        over_rows(half, 256, one)


def back_kernel(info, exchange, info_ref, back_ref, back_other_ref, enc_ref):
    for relative, ref, start in exchange.arrived(back_ref, back_other_ref):
        image = info.image(info_ref, info_ref[0] ^ relative)
        enc_ref[pl.ds(pl.multiple_of(image * VIS, VIS), VIS), :] = ref[start : start + VIS, :]


def paired_sum(sums):
    while len(sums) > 1:
        sums = [left + right for left, right in zip(sums[::2], sums[1::2])]
    return sums[0]


def add_kernel(left_ref, right_ref, out_ref):
    out_ref[...] = (left_ref[...].astype(wide_type) + right_ref[...].astype(wide_type)).astype(low_type)


def forward_kernel(
    parts, proj_columns, rows_ref, out_bias_ref, gain_ref, shift_ref, up_ref, up_bias_ref, *refs
):
    attended_refs = (refs[:parts], refs[parts : 2 * parts])
    weight_refs = refs[2 * parts : 3 * parts]
    hidden_ref, act_ref, acted_ref, slope_ref = refs[3 * parts :]
    columns = weight_refs[0].shape[0] - proj_columns
    half = rows_ref.shape[0] // 2
    out_bias, gain, shift, up_bias = (
        wide_row(ref) for ref in (out_bias_ref, gain_ref, shift_ref, up_bias_ref)
    )

    def body(which, start, size):
        rows = pl.ds(which * half + start, size)
        total = paired_sum(
            [
                packed_product(attended_ref, weight_ref, start, columns)
                for attended_ref, weight_ref in zip(attended_refs[which], weight_refs)
            ]
        )
        hidden = rows_ref[rows, :].astype(wide_type) + total + out_bias
        hidden_ref[rows, :] = hidden
        normed, _ = normalized(hidden)
        act = (normed * gain + shift).astype(low_type)
        act_ref[rows, :] = act
        up_pre = dot(act, up_ref[...]) + up_bias
        cdf = 0.5 + 0.5 * lax.erf(up_pre * math.sqrt(0.5))
        acted_ref[rows, :] = (up_pre * cdf).astype(low_type)
        slope_ref[rows, :] = cdf + up_pre * jnp.exp(-0.5 * up_pre * up_pre) * (
            1.0 / math.sqrt(2.0 * math.pi)
        )

    for which in range(2):
        over_rows(half, PACKED, lambda start, size, which=which: body(which, start, size))


def forward_part_kernel(info_ref, acted_ref, down_ref, keep_ref, sent_ref):
    halves(info_ref[1] & 1, acted_ref, down_ref, keep_ref, sent_ref, dot)


def forward_grad_kernel(parts, first, info_ref, slope_ref, up_ref, down_ref, *refs):
    enc_refs, weight_refs = refs[:parts], refs[parts : 2 * parts]
    keep_ref, sent_ref, up_low_ref, down_low_ref, bias_ref = refs[2 * parts :]
    bias_ref[...] = jnp.zeros_like(bias_ref)

    def body(start, size):
        rows = pl.ds(start, size)
        out_grad = paired_sum(
            [
                dot(enc_ref[rows, :], weight_ref[first:, :])
                for enc_ref, weight_ref in zip(enc_refs, weight_refs)
            ]
        )
        bias_ref[0:1, :] += row_sum(out_grad)
        down_low = out_grad.astype(low_type)
        down_low_ref[rows, :] = down_low
        up_low_ref[rows, :] = (dot_right_t(down_low, down_ref[...]) * slope_ref[rows, :]).astype(low_type)

    over_rows(slope_ref.shape[0], 256, body)
    halves(info_ref[1] & 1, up_low_ref, up_ref, keep_ref, sent_ref, dot_right_t)
    bias_ref[1:2, :] = row_sum(up_low_ref[...].astype(wide_type))


def put_blocks(exchange, info_ref, keep_ref, sent_ref, wide_ref, pad, first=0):
    share = wide_ref.shape[0] // exchange.count
    for ref, indices in exchange.targets(0, info_ref, keep_ref, sent_ref):
        for block, index in enumerate(indices):
            rows = pl.ds(pl.multiple_of(index * share, 8), share)
            for tile in range(wide_ref.shape[1] // LANES):
                at = block * exchange.block + first + tile * pad
                ref[at : at + share, :] = wide_ref[rows, tile * LANES : (tile + 1) * LANES].astype(low_type)


def weight_grad_kernel(exchange, pad, info_ref, left_ref, right_ref, *refs):
    *pos_refs, keep_ref, sent_ref, wide_ref = refs
    wide_ref[...] = dot_left_t(left_ref[...], right_ref[...])
    put_blocks(exchange, info_ref, keep_ref, sent_ref, wide_ref, pad)
    for pos_ref in pos_refs:
        put_blocks(exchange, info_ref, keep_ref, sent_ref, pos_ref, 0, wide_ref.shape[1] // LANES * pad)


def attention_back_kernel(
    heads, info_ref, sum_ref, sum_other_ref, hidden_ref, down_low_ref, gain_ref, weight_ref, qkv_ref, prob_ref,
    prob_last_ref, grads_ref, attn_low_ref, own_ref, bias_ref, grad_ref, probs_ref,
):
    gain = wide_row(gain_ref)
    bias_ref[...] = jnp.zeros_like(bias_ref)
    probs_ref[: prob_ref.shape[0], :] = prob_ref[...]
    probs_ref[prob_ref.shape[0] :, :] = prob_last_ref[...]

    def body(source, rows, part, size):
        normed, spread = normalized(hidden_ref[rows, :])
        grad = (sum_ref, sum_other_ref)[source][part, :].astype(wide_type)
        bias_ref[0:1, :] += row_sum(grad * normed)
        bias_ref[1:2, :] += row_sum(grad)
        hidden_grad = down_low_ref[rows, :].astype(wide_type) + norm_back(grad, normed, spread, gain)
        grad_ref[rows, :] = hidden_grad
        bias_ref[2:3, :] += row_sum(hidden_grad)
        attn_low = hidden_grad.astype(low_type)
        attn_low_ref[rows, :] = attn_low
        attended_grad = dot_right_t(attn_low, weight_ref[...]).astype(low_type)
        for pair in range(size // PAIR):
            pair_rows = pl.ds(rows.start + pair * PAIR, PAIR)
            for head in range(heads):
                base = head * 3 * HEAD_DIM
                queries = qkv_ref[pair_rows, base : base + HEAD_DIM]
                key_rows = qkv_ref[pair_rows, base + HEAD_DIM : base + 2 * HEAD_DIM]
                value_rows = qkv_ref[pair_rows, base + 2 * HEAD_DIM : base + 3 * HEAD_DIM]
                probs = probs_ref[pair_rows, head * PAIR : (head + 1) * PAIR]
                grad_rows = attended_grad[
                    pair * PAIR : (pair + 1) * PAIR, head * HEAD_DIM : (head + 1) * HEAD_DIM
                ]
                value_low = dot_left_t(probs, grad_rows).astype(low_type)
                prob_grad = dot_right_t(grad_rows, value_rows)
                wide_probs = probs.astype(wide_type)
                weighted = wide_probs * prob_grad
                score_low = (
                    weighted - wide_probs * jnp.sum(weighted, axis=-1, keepdims=True)
                ).astype(low_type)
                query_low = (dot(score_low, key_rows) * scale_factor).astype(low_type)
                key_low = (dot_left_t(score_low, queries) * scale_factor).astype(low_type)
                grads_ref[pair_rows, base : base + HEAD_DIM] = query_low
                grads_ref[pair_rows, base + HEAD_DIM : base + 2 * HEAD_DIM] = key_low
                grads_ref[pair_rows, base + 2 * HEAD_DIM : base + 3 * HEAD_DIM] = value_low

    both_halves(info_ref[1] & 1, sum_ref.shape[0], body)
    share = own_ref.shape[0]
    own_ref[...] = grad_ref[pl.ds(pl.multiple_of(info_ref[1] * share, share), share), :]


def late_grads_kernel(
    exchange, pad, info_ref, act_ref, grads_ref, attn_low_ref, first_ref, last_ref, keep_ref, sent_ref, bias_ref,
    wide_ref,
):
    columns = grads_ref.shape[1]
    half, first = first_ref.shape
    wide_ref[:, :first] = dot_left_t(attn_low_ref[:half, :], first_ref[...]) + dot_left_t(
        attn_low_ref[half:, :], last_ref[...]
    )
    wide_ref[:, first : first + columns] = dot_left_t(act_ref[...], grads_ref[...])
    put_blocks(exchange, info_ref, keep_ref, sent_ref, wide_ref, pad)
    bias_ref[...] = row_sum(grads_ref[...].astype(wide_type))


EXTRA = 16


def put_extra(ref, start, gain, shift):
    rows = []
    for value in (gain, shift):
        rows += list(split_low(value))
    rows.append(jnp.zeros((EXTRA - 4, gain.shape[1]), low_type))
    ref[start : start + EXTRA, :] = jnp.concatenate(rows, axis=0)


def get_extra(ref, start):
    rows = ref[start : start + EXTRA, :].astype(wide_type)
    return rows[0:1] + rows[1:2], rows[2:3] + rows[3:4]


def input_part_kernel(info_ref, rows_ref, grads_ref, weight_ref, keep_ref, sent_ref, part_ref, bias_ref):
    lower_bit = info_ref[1] & 1
    bias_ref[...] = jnp.zeros_like(bias_ref)

    def body(start, size):
        rows = pl.ds(start, size)
        grad = dot(grads_ref[rows, :], weight_ref[...])
        part_ref[rows, :] = grad
        normed, _ = normalized(rows_ref[rows, :].astype(wide_type))
        bias_ref[0:1, :] += row_sum(grad * normed)
        bias_ref[1:2, :] += row_sum(grad)

    over_rows(rows_ref.shape[0], CHUNK, body)
    size = keep_ref.shape[0] - EXTRA
    share = size // (lax.axis_size("mp") // 2)
    for out_ref, which in ((sent_ref, 1 - lower_bit), (keep_ref, lower_bit)):
        for block in range(size // share):
            rows = pl.ds(pl.multiple_of((2 * block + which) * share, share), share)
            out_ref[block * share : (block + 1) * share, :] = part_ref[rows, :].astype(low_type)
        put_extra(out_ref, size, bias_ref[0:1, :], bias_ref[1:2, :])


def input_halve_kernel(bit, info_ref, keep_ref, other_ref, next_keep_ref, next_sent_ref, total_ref):
    upper = (info_ref[1] >> bit) & 1
    half = next_keep_ref.shape[0] - EXTRA
    size = 2 * half
    share = total_ref.shape[0] - size
    total_ref[:size, :] = keep_ref[:size, :].astype(wide_type) + other_ref[:size, :].astype(wide_type)
    own, other = get_extra(keep_ref, size), get_extra(other_ref, size)
    for out_ref, which in ((next_sent_ref, 1 - upper), (next_keep_ref, upper)):
        for block in range(half // share):
            rows = pl.ds(pl.multiple_of((2 * block + which) * share, share), share)
            out_ref[block * share : (block + 1) * share, :] = total_ref[rows, :].astype(low_type)
        put_extra(out_ref, half, own[0] + other[0], own[1] + other[1])


def input_grad_kernel(info_ref, rows_ref, keep_ref, other_ref, own_ref, gain_ref, out_ref):
    share = out_ref.shape[0]
    rows = pl.ds(pl.multiple_of(info_ref[1] * share, share), share)
    normed, spread = normalized(rows_ref[rows, :].astype(wide_type))
    grad = keep_ref[:share, :].astype(wide_type) + other_ref[:share, :].astype(wide_type)
    out_ref[...] = (own_ref[...] + norm_back(grad, normed, spread, wide_row(gain_ref))).astype(low_type)


VECTOR_ROWS = 48


def put_rows(values, rows_ref):
    row = 0
    for value in values:
        for tile in range(value.shape[1] // LANES):
            rows_ref[row : row + 1, :] = value[:, tile * LANES : (tile + 1) * LANES]
            row += 1


def take_rows(rows_ref, refs):
    row = 0
    for ref in refs:
        size = ref.shape[0]
        for tile in range(-(-size // LANES)):
            width = min(LANES, size - tile * LANES)
            ref[tile * LANES : tile * LANES + width] = rows_ref[row, :width]
            row += 1


def encoded_kernel(
    info, exchange, heads, info_ref, hidden_ref, sum_ref, sum_other_ref, down_bias_ref, weight_ref, bias_ref, enc_ref,
    mask_ref, grads_ref, second_ref, qkv_ref, first_ref, first_other_ref, keep_ref, sent_ref, low_ref, wide_ref,
    encoded_ref, rows_ref,
):
    down_bias, bias = wide_row(down_bias_ref), wide_row(bias_ref)

    def body(source, rows, part, size):
        total = (sum_ref, sum_other_ref)[source][part, :].astype(wide_type)
        out_low = (hidden_ref[rows, :] + total + down_bias).astype(low_type)
        low_ref[rows, :] = out_low
        encoded_ref[rows, :] = (dot(out_low, weight_ref[...]) + bias).astype(low_type)

    both_halves(info_ref[1] & 1, sum_ref.shape[0], body)
    wide_ref[...] = dot_left_t(low_ref[...], enc_ref[...])
    put_blocks(exchange, info_ref, keep_ref, sent_ref, wide_ref, 0)
    for ref, indices in exchange.targets(0, info_ref, keep_ref, sent_ref):
        at = exchange.moved_at(0)
        for index in indices:
            image = info.image(info_ref, index)
            ref[at : at + VIS, :] = encoded_ref[pl.ds(pl.multiple_of(image * VIS, VIS), VIS), :]
            at += VIS
    qkv = qkv_ref[...]
    empty = jnp.zeros((1, 2 * LANES - heads * HEAD_DIM), wide_type)
    spread = []
    for part in (0, 2):
        spread += [
            qkv[:, (3 * head + part) * HEAD_DIM : (3 * head + part + 1) * HEAD_DIM] for head in range(heads)
        ] + [empty]
    own = get_extra(first_ref, first_ref.shape[0] - EXTRA)
    other = get_extra(first_other_ref, first_ref.shape[0] - EXTRA)
    put_rows(
        (
            jnp.concatenate(spread, axis=1), grads_ref[1:2, :], row_sum(enc_ref[...].astype(wide_type)),
            mask_ref[...], own[0] + other[0], own[1] + other[1], second_ref[0:1, :], second_ref[1:2, :],
            second_ref[2:3, :], grads_ref[0:1, :],
        ),
        rows_ref,
    )
    for ref in (keep_ref, sent_ref):
        ref[exchange.shared_at(0) :, :] = rows_ref[...].astype(low_type)


def late_out_kernel(
    info, exchange, pad, info_ref, seen_ref, keep_ref, other_ref, mask_ref, layout_ref, grids_ref, out_ref, qkv_ref,
    proj_ref, *refs
):
    *vector_refs, wide_ref, rows_ref = refs
    cells = lax.broadcasted_iota(jnp.int32, (GRID, VIS), 0)
    cell_column = lax.broadcasted_iota(jnp.int32, (GRID, 1), 0)
    mask_row = wide_row(mask_ref)
    for relative, ref, start in exchange.arrived(keep_ref, other_ref):
        slot = info_ref[0] ^ relative
        seen = seen_ref[pl.ds(slot, 1), :] == cells
        size = info.cells(info_ref, slot)
        fill = (cell_column < size).astype(wide_type) - jnp.sum(
            seen.astype(wide_type), axis=1, keepdims=True
        )
        placed = dot(seen.astype(low_type), ref[start : start + VIS, :])
        grids_ref[slot] = (placed + fill * mask_row + layout_ref[side_of(size)]).astype(low_type)
    share = proj_ref.shape[0]
    tiles = wide_ref.shape[1] // LANES
    for tile in range(tiles):
        wide_ref[:, tile * LANES : (tile + 1) * LANES] = exchange.total(keep_ref, other_ref, tile * pad, share)
    columns = out_ref.shape[0]
    wide_out = -(-columns // LANES) * LANES
    out_ref[...] = wide_ref[:, :wide_out].T[:columns]
    qkv_ref[...] = wide_ref[:, columns:]
    proj_ref[...] = exchange.total(keep_ref, other_ref, tiles * pad, share)
    rows_ref[...] = exchange.shared_total(keep_ref, other_ref)
    take_rows(rows_ref, vector_refs)


def early_out_kernel(exchange, pad, keep_ref, other_ref, out_ref, *pos_refs):
    tiles = out_ref.shape[1] // LANES
    for tile in range(tiles):
        out_ref[:, tile * LANES : (tile + 1) * LANES] = exchange.total(
            keep_ref, other_ref, tile * pad, out_ref.shape[0]
        )
    for pos_ref in pos_refs:
        pos_ref[...] = exchange.total(keep_ref, other_ref, tiles * pad, pos_ref.shape[0])


def swap(value, axis, bit):
    count = lax.axis_size(axis)
    return lax.ppermute(value, axis, [(i, i ^ bit) for i in range(count)])


def local(
    patch_rows, patches, visible, owner, qkv_weight, query_bias, value_bias, out_weight, out_bias, first_gain,
    first_shift, second_gain, second_shift, up_weight, up_bias, down_weight, down_bias, proj_weight, proj_bias,
    mask_token, decoder_pos, grid_cotangent,
):
    count = lax.axis_size("dp")
    parts = lax.axis_size("mp")
    where = jnp.stack([lax.axis_index("dp"), lax.axis_index("mp")]).astype(jnp.int32)
    rows, width = patch_rows.shape
    images = rows // VIS
    heads = qkv_weight.shape[1] // (3 * HEAD_DIM)
    head_columns = heads * HEAD_DIM
    qkv_columns = qkv_weight.shape[1]
    units = up_weight.shape[1]
    columns = proj_weight.shape[1]
    share = width // count
    pos_share = GRID // count
    half = rows // 2
    own_rows = rows // parts
    pads = (-(-share // 16) * 16, -(-pos_share // 16) * 16)
    run = Order(rows <= PINNED_ROWS)

    tables = grid_tables()
    table_high = tables.astype(low_type)
    table_low = (tables - table_high.astype(np.float32)).astype(low_type)
    turned_high = jnp.asarray(np.ascontiguousarray(table_high.transpose(0, 2, 1)))
    turned_low = jnp.asarray(np.ascontiguousarray(table_low.transpose(0, 2, 1)))
    table_high, table_low = jnp.asarray(table_high), jnp.asarray(table_low)
    qkv_weight_t = qkv_weight.T
    run.leave(owner, visible, patches, grid_cotangent)
    info = Info(count)
    bits = tuple(range(count.bit_length() - 1))
    late_columns = qkv_columns + head_columns
    turned = (1, 0) + bits[2:]
    back_exchange = Exchange(count, bits, 0, moved=VIS)
    up_exchange = Exchange(count, bits, units // LANES * pads[0] + pads[1])
    down_exchange = Exchange(count, turned, units // LANES * pads[0])
    late_exchange = Exchange(count, turned, late_columns // LANES * pads[0])
    last_exchange = Exchange(count, turned, pads[0], moved=VIS, shared=VECTOR_ROWS)
    joint_exchange = Exchange(
        count, turned, late_exchange.block + last_exchange.block, moved=VIS, shared=VECTOR_ROWS
    )

    def low(*shape):
        return (shape, low_type)

    def wide(*shape):
        return (shape, wide_type)

    def moved(value, axis, bit):
        return run.keep(swap(value, axis, bit))

    def model_steps(keep, sent):
        received = moved(sent, "mp", 1)
        yield
        (total,) = run(add_kernel, [low(half, width)], (keep, received), cost=0.6)
        bit = 2
        while bit < parts:
            received = moved(total, "mp", bit)
            yield
            (total,) = run(add_kernel, [low(half, width)], (total, received), cost=0.6)
            bit *= 2
        other = moved(total, "mp", 1)
        yield
        return total, other

    def model_gather(value):
        values = {0: value}
        bit = parts // 2
        while bit:
            values.update({other | bit: moved(values[other], "mp", bit) for other in tuple(values)})
            bit //= 2
        return tuple(values[at] for at in range(parts))

    def data_step(step, exchange, pairs):
        keep, sent = run(
            lambda *refs: exchange.kernel(step, [part for part, _, _ in pairs], *refs),
            [low(exchange.rows(step), LANES)] * 2,
            (facts,) + tuple(array for _, *arrays in pairs for array in arrays),
            (SMEM,) + (VMEM,) * (2 * len(pairs)),
            cost=1.2,
        )
        return keep, moved(sent, "dp", 2 ** exchange.bits[step])

    def data_steps(exchange, keep, sent):
        received = moved(sent, "dp", 2 ** exchange.bits[0])
        yield keep, received
        for step in range(1, len(exchange.bits)):
            keep, received = data_step(step, exchange, [(exchange, keep, received)])
            yield keep, received

    def finish_pair(steps):
        *_, last = steps
        return last

    def finish(steps):
        while True:
            try:
                next(steps)
            except StopIteration as stop:
                return stop.value

    (
        back_keep, back_sent, facts, seen, patch_rows, qkv_weight_t, first_gain, first_shift, query_bias, value_bias,
        out_weight, proj_weight,
    ) = run(
        lambda *refs: cotangent_kernel(info, back_exchange, *refs),
        [
            low(back_exchange.rows(0), columns), low(back_exchange.rows(0), columns), ((info.size,), jnp.int32),
            ((count, VIS), jnp.int32),
        ],
        (where, owner, patches, visible, grid_cotangent),
        (SMEM, SMEM, SMEM, VMEM, VMEM),
        out_specs=(VMEM, VMEM, SMEM, VMEM),
        scratch=[pltpu.VMEM((VIS, count), wide_type)],
        stage=(
            patch_rows, qkv_weight_t, first_gain, first_shift, query_bias, value_bias, out_weight, proj_weight
        ),
        cost=3.0,
    )
    back_steps = data_steps(back_exchange, back_keep, back_sent)
    next(back_steps)
    weights, act_one, qkv = run(
        enter_kernel,
        [low(head_columns + columns, width), low(rows, width), low(rows, qkv_columns)],
        (
            patch_rows, first_gain, first_shift, qkv_weight_t, query_bias, value_bias, out_weight, proj_weight
        ),
        cost=1.2,
    )
    weights = model_gather(weights)
    next(back_steps)
    packed_rows = half * head_columns // LANES
    packed, first_probs, first_attended, out_bias, second_gain, second_shift, up_weight, up_bias = run(
        lambda *refs: attention_kernel(info, heads, 0, *refs),
        [low(packed_rows, LANES), low(half, heads * PAIR), low(half, head_columns)],
        (facts, qkv),
        (SMEM, VMEM),
        stage=(out_bias, second_gain, second_shift, up_weight, up_bias),
        cost=2.8,
    )
    first_all = model_gather(packed)
    back_own, back_other = finish_pair(back_steps)
    packed, last_probs, last_attended, down_weight, down_bias, proj_bias = run(
        lambda *refs: attention_kernel(info, heads, half, *refs),
        [low(packed_rows, LANES), low(half, heads * PAIR), low(half, head_columns)],
        (facts, qkv),
        (SMEM, VMEM),
        stage=(down_weight, down_bias, proj_bias),
        cost=2.5,
    )
    last_all = model_gather(packed)
    (enc_grad,) = run(
        lambda *refs: back_kernel(info, back_exchange, *refs),
        [low(rows, columns)],
        (facts, back_own, back_other),
        (SMEM, VMEM, VMEM),
        cost=0.4,
    )
    enc_all = model_gather(enc_grad)
    (
        hidden, act_two, acted, slope, turned_high, turned_low, table_high, table_low, decoder_pos, grid_cotangent
    ) = run(
        lambda *refs: forward_kernel(parts, columns, *refs),
        [wide(rows, width), low(rows, width), low(rows, units), wide(rows, units)],
        (patch_rows, out_bias, second_gain, second_shift, up_weight, up_bias) + first_all + last_all + weights,
        stage=(turned_high, turned_low, table_high, table_low, decoder_pos, grid_cotangent),
        cost=2.6,
    )
    keep, sent, up_low, down_low, bias_grads = run(
        lambda *refs: forward_grad_kernel(parts, head_columns, *refs),
        [low(half, width), low(half, width), low(rows, units), low(rows, width), wide(2, width)],
        (facts, slope, up_weight, down_weight) + enc_all + weights,
        (SMEM,) + (VMEM,) * (3 + 2 * parts),
        cost=2.0,
    )
    second_steps = model_steps(keep, sent)
    next(second_steps)
    keep, sent = run(
        forward_part_kernel,
        [low(half, width), low(half, width)],
        (facts, acted, down_weight),
        (SMEM, VMEM, VMEM),
        cost=0.7,
    )
    next(second_steps)
    out_steps = model_steps(keep, sent)
    next(out_steps)

    def weight_grad(exchange, left, right, *pos):
        keep, sent = run(
            lambda *refs: weight_grad_kernel(exchange, pads[0], *refs),
            [low(exchange.rows(0), LANES)] * 2,
            (facts, left, right) + pos,
            (SMEM,) + (VMEM,) * (2 + len(pos)),
            scratch=[pltpu.VMEM((width, right.shape[1]), wide_type)],
            cost=1.9,
        )
        steps = data_steps(exchange, keep, sent)
        next(steps)
        return steps

    down_steps = weight_grad(down_exchange, down_low, acted)
    pos_grad_own, mask_grad, layouts = run(
        lambda *refs: position_kernel(info, *refs),
        [wide(GRID, columns), wide(1, columns), wide(3, GRID, columns)],
        (facts, seen, grid_cotangent, turned_high, turned_low, table_high, table_low, decoder_pos),
        (SMEM,) + (VMEM,) * 7,
        scratch=[pltpu.VMEM((3, GRID, columns), wide_type)],
        cost=1.0,
    )
    up_steps = weight_grad(up_exchange, act_two, up_low, pos_grad_own)
    next(second_steps)
    next(out_steps)
    second_sum, second_other = finish(second_steps)
    grads, attn_low, own_grad, second_grads = run(
        lambda *refs: attention_back_kernel(heads, *refs),
        [low(rows, qkv_columns), low(rows, width), wide(own_rows, width), wide(3, width)],
        (
            facts, second_sum, second_other, hidden, down_low, second_gain, out_weight, qkv, first_probs, last_probs
        ),
        (SMEM,) + (VMEM,) * 9,
        scratch=[pltpu.VMEM((rows, width), wide_type), pltpu.VMEM((rows, heads * PAIR), low_type)],
        cost=5.5,
    )
    in_keep, in_sent = run(
        input_part_kernel,
        [low(half + EXTRA, width)] * 2,
        (facts, patch_rows, grads, qkv_weight_t),
        (SMEM,) + (VMEM,) * 3,
        scratch=[pltpu.VMEM((rows, width), wide_type), pltpu.VMEM((2, width), wide_type)],
        cost=2.0,
    )
    in_other = moved(in_sent, "mp", 1)
    keep, sent, qkv_bias_grad = run(
        lambda *refs: late_grads_kernel(late_exchange, pads[0], *refs),
        [low(late_exchange.rows(0), LANES)] * 2 + [wide(1, qkv_columns)],
        (facts, act_one, grads, attn_low, first_attended, last_attended),
        (SMEM,) + (VMEM,) * 5,
        scratch=[pltpu.VMEM((width, late_columns), wide_type)],
        cost=2.5,
    )
    late_keep, late_other = next(data_steps(late_exchange, keep, sent))
    bit = 1
    size = half
    while 2**bit < parts:
        in_keep, in_sent = run(
            lambda *refs, bit=bit: input_halve_kernel(bit, *refs),
            [low(size // 2 + EXTRA, width)] * 2,
            (facts, in_keep, in_other),
            (SMEM, VMEM, VMEM),
            scratch=[pltpu.VMEM((size + own_rows, width), wide_type)],
            cost=1.1,
        )
        in_other = moved(in_sent, "mp", 2**bit)
        size //= 2
        bit += 1
    next(out_steps)
    next(down_steps)
    out_sum, out_other = finish(out_steps)
    keep, sent = run(
        lambda *refs: encoded_kernel(info, last_exchange, heads, *refs),
        [low(last_exchange.rows(0), LANES)] * 2,
        (
            facts, hidden, out_sum, out_other, down_bias, proj_weight, proj_bias, enc_grad, mask_grad, bias_grads,
            second_grads, qkv_bias_grad, in_keep, in_other,
        ),
        (SMEM,) + (VMEM,) * 13,
        scratch=[
            pltpu.VMEM((rows, width), low_type),
            pltpu.VMEM((width, columns), wide_type),
            pltpu.VMEM((rows, columns), low_type),
            pltpu.VMEM((VECTOR_ROWS, LANES), wide_type),
        ],
        cost=2.2,
    )
    last_keep, last_other = next(data_steps(last_exchange, keep, sent))
    next(up_steps)
    (input_grad,) = run(
        input_grad_kernel,
        [low(own_rows, width)],
        (facts, patch_rows, in_keep, in_other, own_grad, first_gain),
        (SMEM,) + (VMEM,) * 5,
        final=True,
        cost=0.8,
    )
    late_keep, late_other = data_step(
        1, joint_exchange, [(late_exchange, late_keep, late_other), (last_exchange, last_keep, last_other)]
    )
    down_keep, down_other = finish_pair(down_steps)
    up_keep, up_other = finish_pair(up_steps)
    for step in range(2, len(bits)):
        late_keep, late_other = data_step(step, joint_exchange, [(joint_exchange, late_keep, late_other)])
    (down_weight_grad,) = run(
        lambda *refs: early_out_kernel(down_exchange, pads[0], *refs),
        [wide(share, units)],
        (down_keep, down_other),
        final=True,
        cost=0.8,
    )
    up_weight_grad, pos_grad = run(
        lambda *refs: early_out_kernel(up_exchange, pads[0], *refs),
        [wide(share, units), wide(pos_share, columns)],
        (up_keep, up_other),
        final=True,
        cost=0.8,
    )
    (
        grids, out_weight_grad, qkv_weight_grad, proj_weight_grad, query_bias_grad, value_bias_grad, up_bias_grad,
        proj_bias_grad, mask_token_grad, first_gain_grad, first_shift_grad, second_gain_grad, second_shift_grad,
        out_bias_grad, down_bias_grad,
    ) = run(
        lambda *refs: late_out_kernel(info, joint_exchange, pads[0], *refs),
        [
            low(count, GRID, columns), wide(head_columns, share), wide(share, qkv_columns), wide(share, columns)
        ]
        + [wide(size) for size in (head_columns, head_columns, units, columns, columns) + (width,) * 6],
        (facts, seen, late_keep, late_other, mask_token, layouts),
        (SMEM,) + (VMEM,) * 5,
        scratch=[pltpu.VMEM((share, late_columns), wide_type), pltpu.VMEM((VECTOR_ROWS, LANES), wide_type)],
        final=True,
        cost=2.5,
    )
    return (
        grids, input_grad, qkv_weight_grad, query_bias_grad, value_bias_grad, out_weight_grad, out_bias_grad,
        first_gain_grad, first_shift_grad, second_gain_grad, second_shift_grad, up_weight_grad, up_bias_grad,
        down_weight_grad.T, down_bias_grad, proj_weight_grad, proj_bias_grad, mask_token_grad, pos_grad,
    )


def solution(mesh):
    return jax.shard_map(
        local,
        mesh=mesh,
        in_specs=(
            P("dp", None), P(), P(), P(), P(None, "mp"), P("mp"), P("mp"), P("mp", None), P(), P(), P(), P(), P(),
            P(None, "mp"), P("mp"), P("mp", None), P(), P(None, "mp"), P("mp"), P("mp"), P(None, "mp"),
            P("dp", None, "mp"),
        ),
        out_specs=(
            P("dp", None, "mp"), P(("dp", "mp"), None), P("dp", "mp"), P("mp"), P("mp"), P("mp", "dp"), P(), P(),
            P(), P(), P(), P("dp", "mp"), P("mp"), P("mp", "dp"), P(), P("dp", "mp"), P("mp"), P("mp"),
            P("dp", "mp"),
        ),
        check_vma=False,
    )
```

```python
import math

import jax
import jax.numpy as jnp
import numpy as np
from jax import lax
from jax.experimental import pallas as pl
from jax.experimental.pallas import tpu as pltpu
from jax.sharding import PartitionSpec as P

HEAD_DIM = 64
GRID = 256
VIS = 64
CHUNK = 512
LANES = 128

epsilon = 1e-06
low_type = jnp.bfloat16
wide_type = jnp.float32
scale_factor = HEAD_DIM ** (-0.5)

VMEM = pl.BlockSpec(memory_space=pltpu.VMEM)
SMEM = pl.BlockSpec(memory_space=pltpu.SMEM)
ANY = pl.BlockSpec(memory_space=pl.ANY)
PINNED_ROWS = 512


def grid_tables():
    grid_edge = math.isqrt(GRID)
    tables = []
    for side_cells in (10, 14):
        places = np.arange(side_cells)
        centers = ((2 * places + 1) * grid_edge - side_cells) / (2 * side_cells)
        lower = np.floor(centers).astype(np.int64)
        share = centers - lower
        lerp = np.zeros((side_cells, grid_edge))
        lerp[places, np.clip(lower, 0, grid_edge - 1)] += 1.0 - share
        lerp[places, np.clip(lower + 1, 0, grid_edge - 1)] += share
        table = np.zeros((GRID, GRID))
        table[: side_cells * side_cells] = np.kron(lerp, lerp)
        tables.append(table)
    return np.stack(tables).astype(np.float32)


def split_low(value):
    high = value.astype(low_type)
    return high, (value - high.astype(wide_type)).astype(low_type)


def dot(left, right):
    return lax.dot_general(left, right, (((1,), (0,)), ((), ())), preferred_element_type=wide_type)


def dot_right_t(left, right):
    return lax.dot_general(left, right, (((1,), (1,)), ((), ())), preferred_element_type=wide_type)


def dot_left_t(left, right):
    return lax.dot_general(left, right, (((0,), (0,)), ((), ())), preferred_element_type=wide_type)


def normalized(value):
    center = value - jnp.mean(value, axis=-1, keepdims=True)
    spread = lax.rsqrt(jnp.mean(center * center, axis=-1, keepdims=True) + epsilon)
    return center * spread, spread


def norm_back(grad, normed, spread, gain):
    scaled = grad * gain
    mean_one = jnp.mean(scaled, axis=-1, keepdims=True)
    mean_two = jnp.mean(scaled * normed, axis=-1, keepdims=True)
    return spread * (scaled - mean_one - normed * mean_two)


def row_sum(value):
    return jnp.sum(value, axis=0, keepdims=True)


def over_rows(total, size, body):
    size = min(size, total)
    if total <= 2 * size:
        for start in range(0, total, size):
            body(start, size)
        return

    def step(i, carry):
        body(pl.multiple_of(i * size, size), size)
        return carry

    lax.fori_loop(0, total // size, step, 0)


def size_of(shape, kind):
    return math.prod(shape) * jnp.dtype(kind).itemsize


RATE = 10**9
COST_SHARE = 1.0
BYTES = 0


class Order:
    def __init__(self, pinned):
        self.pinned = pinned
        self.last = None
        self.near = []
        self.far = []
        self.share = COST_SHARE

    def keep(self, value):
        if self.pinned:
            self.near.append((value, pltpu.VMEM))
        return value

    def leave(self, *values):
        self.far += values

    def placed(self, value):
        for near, space in self.near:
            if value is near:
                return pltpu.with_memory_space_constraint(value, space)
        if any(value is far for far in self.far):
            return pltpu.with_memory_space_constraint(value, pltpu.HBM)
        return value

    def __call__(
        self, kernel, outs, args, specs=None, scratch=(), out_specs=None, final=False, stage=(), cost=1.0
    ):
        args = tuple(args)
        specs = [VMEM] * len(args) if specs is None else list(specs)
        out_specs = [VMEM] * len(outs) if out_specs is None else list(out_specs)
        count, results_count = len(args), len(outs)
        staged = list(stage) if self.pinned else []
        self.leave(*staged)
        needed = sum(size_of(ref.shape, ref.dtype) for ref in scratch)
        needed += sum(
            size_of(arg.shape, arg.dtype) for arg in args if not any(arg is near for near, _ in self.near)
        )
        shapes = []
        for (shape, kind), spec in zip(outs, out_specs):
            if self.pinned and not final:
                shapes.append((pltpu.SMEM if spec is SMEM else pltpu.VMEM)(shape, kind))
            else:
                shapes.append(jax.ShapeDtypeStruct(shape, kind))
                needed += size_of(shape, kind)
        tail = len(staged)
        args += tuple(staged)
        specs += [ANY] * tail
        skipped = 0
        if self.last is not None:
            args += (self.last,)
            specs.append(ANY)
            skipped = 1

        def body(*refs):
            own, sources, refs = refs[:count], refs[count : count + tail], refs[count + tail + skipped :]
            results, targets, refs = (
                refs[:results_count], refs[results_count : results_count + tail], refs[results_count + tail :]
            )
            copies = []
            if tail:
                *refs, sems = refs
                copies = [
                    pltpu.make_async_copy(source, target, sems.at[at])
                    for at, (source, target) in enumerate(zip(sources, targets))
                ]
            for copy in copies:
                copy.start()
            kernel(*own, *results, *refs)
            for copy in copies:
                copy.wait()

        results = pl.pallas_call(
            body,
            out_shape=tuple(shapes) + tuple(pltpu.VMEM(array.shape, array.dtype) for array in staged),
            in_specs=specs,
            out_specs=tuple(out_specs) + (VMEM,) * tail,
            scratch_shapes=list(scratch) + ([pltpu.SemaphoreType.DMA((tail,))] if tail else []),
            compiler_params=pltpu.CompilerParams(
                vmem_limit_bytes=min(needed + needed // 4 + 10 * 2**20, 60 * 2**20)
            ),
            cost_estimate=pl.CostEstimate(
                flops=int(cost * RATE * self.share), bytes_accessed=int(cost * BYTES), transcendentals=0
            ),
        )(*(self.placed(arg) for arg in args))
        if self.pinned and not final:
            for result, spec in zip(results, out_specs + [VMEM] * tail):
                self.near.append((result, pltpu.SMEM if spec is SMEM else pltpu.VMEM))
        if not final:
            self.last = results[0]
        if stage and not self.pinned:
            return (*results, *stage)
        return results


class Info:
    def __init__(self, count):
        self.count = count
        self.size = 2 + 5 * count

    def dp(self, ref):
        return ref[0]

    def mp(self, ref):
        return ref[1]

    def owner(self, ref, image):
        return ref[2 + image]

    def live(self, ref, image):
        return ref[2 + self.count + image]

    def source(self, ref, slot):
        return ref[2 + 2 * self.count + slot]

    def cells(self, ref, slot):
        return ref[2 + 3 * self.count + slot]

    def image(self, ref, owner):
        return ref[2 + 4 * self.count + owner]


def fill_info(count, where_ref, owner_ref, patches_ref, info_ref):
    me = where_ref[0]
    info_ref[0] = me
    info_ref[1] = where_ref[1]

    def one(at):
        own = me * count + at
        info_ref[2 + at] = owner_ref[own]
        info_ref[2 + 4 * count + owner_ref[own]] = at
        info_ref[2 + count + at] = patches_ref[own] // 4

        def find(i, found):
            return jnp.where(owner_ref[at * count + i] == me, at * count + i, found)

        source = lax.fori_loop(0, count, find, at * count, unroll=count <= 8)
        info_ref[2 + 2 * count + at] = source
        info_ref[2 + 3 * count + at] = patches_ref[source]

    over_slots(count, one)


def over_slots(count, one_slot):
    if count <= 8:
        for slot in range(count):
            one_slot(slot)
    else:
        lax.fori_loop(0, count, lambda slot, carry: (one_slot(slot), carry)[1], 0)


def side_of(size):
    return (size >= 196).astype(jnp.int32) + (size >= 256).astype(jnp.int32)


def block_at(rest, place, bit):
    low = rest & ((1 << place) - 1)
    return ((rest - low) << 1) + (bit << place) + low


class Exchange:
    def __init__(self, count, bits, block, moved=0, shared=0):
        self.count, self.bits, self.block, self.moved, self.shared = count, bits, block, moved, shared

    def blocks(self, step):
        return self.count >> (step + 1)

    def place(self, step):
        bit = self.bits[step]
        return bit - sum(done < bit for done in self.bits[:step])

    def moved_at(self, step):
        return self.blocks(step) * self.block

    def shared_at(self, step):
        return self.moved_at(step) + self.count // 2 * self.moved

    def rows(self, step):
        return self.shared_at(step) + self.shared

    def own_bit(self, step, info_ref):
        return (info_ref[0] >> self.bits[step]) & 1

    def targets(self, step, info_ref, keep_ref, sent_ref):
        own = self.own_bit(step, info_ref)
        place = self.place(step)
        for ref, which in ((sent_ref, 1 - own), (keep_ref, own)):
            yield ref, [block_at(block, place, which) for block in range(self.blocks(step))]

    def kernel(self, step, parts, info_ref, *refs):
        *from_refs, next_keep_ref, next_sent_ref = refs
        pairs = list(zip(parts, from_refs[::2], from_refs[1::2]))
        sources = 1 << (step - 1)
        rests = self.blocks(step - 1)
        for ref, indices in self.targets(step, info_ref, next_keep_ref, next_sent_ref):
            first, moved_at, shared_at = 0, self.moved_at(step), self.shared_at(step)
            for part, keep_ref, other_ref in pairs:
                for block, index in enumerate(indices if part.block else ()):
                    rows = pl.ds(pl.multiple_of(index * part.block, 16), part.block)
                    at = block * self.block + first
                    ref[at : at + part.block, :] = (
                        keep_ref[rows, :].astype(wide_type) + other_ref[rows, :].astype(wide_type)
                    ).astype(low_type)
                first += part.block
                for from_ref in (keep_ref, other_ref) if part.moved else ():
                    for source in range(sources):
                        for index in indices:
                            rows = part.moved_at(step - 1) + (source * rests + index) * part.moved
                            ref[moved_at : moved_at + part.moved, :] = from_ref[
                                pl.ds(pl.multiple_of(rows, 16), part.moved), :
                            ]
                            moved_at += part.moved
                if part.shared:
                    at = part.shared_at(step - 1)
                    rows = slice(at, at + part.shared)
                    ref[shared_at : shared_at + part.shared, :] = (
                        keep_ref[rows, :].astype(wide_type) + other_ref[rows, :].astype(wide_type)
                    ).astype(low_type)

    def arrived(self, keep_ref, other_ref):
        last = len(self.bits) - 1
        sources = 1 << last
        for half, ref in enumerate((keep_ref, other_ref)):
            for source in range(sources):
                relative = 0
                for step, bit in enumerate(self.bits):
                    relative |= (((source + half * sources) >> step) & 1) << bit
                yield relative, ref, self.moved_at(last) + source * self.moved

    def total(self, keep_ref, other_ref, start, size):
        rows = slice(start, start + size)
        return keep_ref[rows, :].astype(wide_type) + other_ref[rows, :].astype(wide_type)

    def shared_total(self, keep_ref, other_ref):
        return self.total(keep_ref, other_ref, self.shared_at(len(self.bits) - 1), self.shared)


def cotangent_kernel(
    info, exchange, where_ref, owner_ref, patches_ref, visible_ref, cot_ref, keep_ref, sent_ref, info_ref, seen_ref,
    turned_ref,
):
    count = info.count
    fill_info(count, where_ref, owner_ref, patches_ref, info_ref)

    def take(slot):
        seen_ref[pl.ds(slot, 1), :] = visible_ref[pl.ds(info.source(info_ref, slot), 1), :]

    over_slots(count, take)
    turned_ref[...] = seen_ref[...].astype(wide_type).T
    cells = lax.broadcasted_iota(jnp.int32, (VIS, GRID), 1).astype(wide_type)
    own = exchange.own_bit(0, info_ref)
    place = exchange.place(0)
    for slot in range(count):
        onehot = (turned_ref[:, slot : slot + 1] == cells).astype(wide_type).astype(low_type)
        rows = dot(onehot, cot_ref[slot]).astype(low_type)
        rest = (slot & ((1 << place) - 1)) | ((slot >> (place + 1)) << place)
        kept = ((slot >> place) & 1) == own

        @pl.when(kept)
        def _(rest=rest, rows=rows):
            keep_ref[rest * VIS : (rest + 1) * VIS, :] = rows

        @pl.when(jnp.logical_not(kept))
        def _(rest=rest, rows=rows):
            sent_ref[rest * VIS : (rest + 1) * VIS, :] = rows


def position_kernel(
    info, info_ref, visible_ref, cot_ref, turned_high_ref, turned_low_ref, table_high_ref, table_low_ref, pos_ref,
    grad_ref, mask_ref, layout_ref, sums_ref,
):
    cells = lax.broadcasted_iota(jnp.int32, (GRID, VIS), 0)
    cell_column = lax.broadcasted_iota(jnp.int32, (GRID, 1), 0)
    sums_ref[...] = jnp.zeros_like(sums_ref)
    mask_ref[...] = jnp.zeros_like(mask_ref)

    def one_slot(slot):
        size = info.cells(info_ref, slot)
        seen = visible_ref[pl.ds(slot, 1), :] == cells
        fill = (cell_column < size).astype(wide_type) - jnp.sum(
            seen.astype(wide_type), axis=1, keepdims=True
        )
        wide = cot_ref[slot].astype(wide_type)
        mask_ref[...] += row_sum(fill * wide)
        sums_ref[side_of(size)] += wide

    over_slots(info.count, one_slot)
    total = sums_ref[2]
    for side in range(2):
        high, low = split_low(sums_ref[side])
        total += (
            dot(turned_high_ref[side], high) + dot(turned_high_ref[side], low) + dot(turned_low_ref[side], high)
        )
    grad_ref[...] = total
    table = pos_ref[...]
    for side in range(2):
        layout_ref[side] = dot(table_high_ref[side], table) + dot(table_low_ref[side], table)
    layout_ref[2] = table.astype(wide_type)


def wide_row(ref):
    return ref[...].astype(wide_type).reshape(1, ref.shape[0])


def enter_kernel(
    rows_ref, gain_ref, shift_ref, weight_ref, query_ref, value_ref, act_ref, qkv_ref
):
    gain, shift = wide_row(gain_ref), wide_row(shift_ref)
    query, value = wide_row(query_ref), wide_row(value_ref)
    nothing = jnp.zeros((1, HEAD_DIM), wide_type)
    pieces = []
    for start in range(0, query.shape[1], HEAD_DIM):
        pieces += [query[:, start : start + HEAD_DIM], nothing, value[:, start : start + HEAD_DIM]]
    bias = jnp.concatenate(pieces, axis=1)

    def body(start, size):
        rows = pl.ds(start, size)
        normed, _ = normalized(rows_ref[rows, :].astype(wide_type))
        act = (normed * gain + shift).astype(low_type)
        act_ref[rows, :] = act
        qkv_ref[rows, :] = (dot_right_t(act, weight_ref[...]) + bias).astype(low_type)

    over_rows(rows_ref.shape[0], CHUNK, body)


BLOCK = 4 * VIS


def attention_kernel(info, heads, first, info_ref, qkv_ref, packed_ref, prob_ref, attended_ref):
    key_image = lax.broadcasted_iota(jnp.int32, (BLOCK, BLOCK), 0) // VIS
    key_slot = lax.broadcasted_iota(jnp.int32, (BLOCK, BLOCK), 0) % VIS
    own_image = key_image == lax.broadcasted_iota(jnp.int32, (BLOCK, BLOCK), 1) // VIS
    columns = heads * HEAD_DIM
    full = columns // LANES * LANES
    rest = BLOCK * (columns - full) // LANES

    def body(start, size):
        rows = pl.ds(start, size)
        from_rows = pl.ds(first + start, size)
        limit = jnp.zeros((size, size), jnp.int32)
        for image in range(size // VIS):
            limit = jnp.where(key_image == image, info.live(info_ref, (first + start) // VIS + image), limit)
        live = jnp.logical_and(own_image, key_slot < limit)
        for head in range(heads):
            base = head * 3 * HEAD_DIM
            queries = qkv_ref[from_rows, base : base + HEAD_DIM]
            key_rows = qkv_ref[from_rows, base + HEAD_DIM : base + 2 * HEAD_DIM]
            value_rows = qkv_ref[from_rows, base + 2 * HEAD_DIM : base + 3 * HEAD_DIM]
            scores = jnp.where(live, dot_right_t(key_rows, queries) * scale_factor, -1e30)
            raised = jnp.exp(scores - jnp.max(scores, axis=0, keepdims=True))
            probs = (raised / jnp.sum(raised, axis=0, keepdims=True)).astype(low_type)
            prob_ref[rows, head * BLOCK : (head + 1) * BLOCK] = probs
            attended_ref[rows, head * HEAD_DIM : (head + 1) * HEAD_DIM] = dot_left_t(
                probs, value_rows
            ).astype(low_type)
        at = start // BLOCK * (full // LANES * BLOCK + rest)
        for tile in range(full // LANES):
            packed_ref[pl.ds(at, BLOCK), :] = attended_ref[rows, tile * LANES : (tile + 1) * LANES]
            at += BLOCK
        pieces = [
            attended_ref[pl.ds(start + piece * rest, rest), full:].astype(wide_type)
            for piece in range(BLOCK // rest)
        ]
        packed_ref[pl.ds(at, rest), :] = jnp.concatenate(pieces, axis=1).astype(low_type)

    over_rows(prob_ref.shape[0], BLOCK, body)


def unpack(own, packed_refs, start, columns, out_ref):
    full = columns // LANES * LANES
    width = columns - full
    rest = BLOCK * width // LANES
    at = start // BLOCK * (full // LANES * BLOCK + rest)
    count = len(packed_refs)
    for tile in range(full // LANES):
        for relative, ref in enumerate(packed_refs):
            lane = (tile * count + (own ^ relative)) * LANES
            out_ref[:, pl.ds(pl.multiple_of(lane, LANES), LANES)] = ref[pl.ds(at, BLOCK), :]
        at += BLOCK
    lane = full * count
    for other in range(0, count, LANES // width):
        pieces = []
        for part in range(other, other + LANES // width):
            rows = None
            for relative, ref in enumerate(packed_refs):
                here = ref[pl.ds(at, rest), :].astype(wide_type)
                rows = here if rows is None else jnp.where((own ^ relative) == part, here, rows)
            pieces.append(
                jnp.concatenate(
                    [rows[:, piece * width : (piece + 1) * width] for piece in range(BLOCK // rest)], axis=0
                )
            )
        out_ref[:, lane : lane + LANES] = jnp.concatenate(pieces, axis=1).astype(low_type)
        lane += LANES


def weights_kernel(parts, info_ref, *refs):
    out_refs, proj_refs, (out_ref, proj_ref) = refs[:parts], refs[parts : 2 * parts], refs[2 * parts :]
    own = info_ref[1]
    columns = out_refs[0].shape[0]
    full = columns // LANES * LANES
    width = columns - full
    for relative, (out_part_ref, proj_part_ref) in enumerate(zip(out_refs, proj_refs)):
        part = own ^ relative
        for tile in range(full // LANES):
            at = pl.multiple_of((tile * parts + part) * LANES, LANES)
            out_ref[pl.ds(at, LANES), :] = out_part_ref[tile * LANES : (tile + 1) * LANES, :]
        at = pl.multiple_of(full * parts + part * width, 16)
        out_ref[pl.ds(at, width), :] = out_part_ref[full:, :]
        size = proj_part_ref.shape[1]
        proj_ref[:, pl.ds(pl.multiple_of(part * size, LANES), size)] = proj_part_ref[...]


def halves(upper, left_ref, weight_ref, keep_ref, sent_ref, product):
    half = keep_ref.shape[0]
    for out_ref, which in ((sent_ref, 1 - upper), (keep_ref, upper)):

        def body(start, size, out_ref=out_ref, which=which):
            rows = pl.ds(pl.multiple_of(which * half + start, size), size)
            out_ref[pl.ds(start, size), :] = product(left_ref[rows, :], weight_ref[...]).astype(
                out_ref.dtype
            )

        over_rows(half, CHUNK, body)


def both_halves(upper, half, body):
    for source, which in enumerate((upper, 1 - upper)):

        def one(start, size, source=source, which=which):
            body(source, pl.ds(pl.multiple_of(which * half + start, size), size), pl.ds(start, size), size)

        over_rows(half, 256, one)


def back_kernel(info, exchange, info_ref, back_ref, back_other_ref, enc_ref):
    for relative, ref, start in exchange.arrived(back_ref, back_other_ref):
        image = info.image(info_ref, info_ref[0] ^ relative)
        enc_ref[pl.ds(pl.multiple_of(image * VIS, VIS), VIS), :] = ref[start : start + VIS, :]


def add_kernel(left_ref, right_ref, out_ref):
    out_ref[...] = (left_ref[...].astype(wide_type) + right_ref[...].astype(wide_type)).astype(low_type)


def forward_kernel(
    parts, columns, info_ref, rows_ref, out_bias_ref, gain_ref, shift_ref, up_ref, up_bias_ref, weight_ref, *refs
):
    attended_refs = (refs[:parts], refs[parts : 2 * parts])
    hidden_ref, act_ref, acted_ref, slope_ref, all_ref = refs[2 * parts :]
    half = rows_ref.shape[0] // 2
    out_bias, gain, shift, up_bias = (
        wide_row(ref) for ref in (out_bias_ref, gain_ref, shift_ref, up_bias_ref)
    )

    def body(which, start, size):
        rows = pl.ds(which * half + start, size)
        unpack(info_ref[1], attended_refs[which], start, columns, all_ref)
        total = dot(all_ref[...], weight_ref[...])
        hidden = rows_ref[rows, :].astype(wide_type) + total + out_bias
        hidden_ref[rows, :] = hidden
        normed, _ = normalized(hidden)
        act = (normed * gain + shift).astype(low_type)
        act_ref[rows, :] = act
        up_pre = dot(act, up_ref[...]) + up_bias
        cdf = 0.5 + 0.5 * lax.erf(up_pre * math.sqrt(0.5))
        acted_ref[rows, :] = (up_pre * cdf).astype(low_type)
        slope_ref[rows, :] = cdf + up_pre * jnp.exp(-0.5 * up_pre * up_pre) * (
            1.0 / math.sqrt(2.0 * math.pi)
        )

    for which in range(2):
        over_rows(half, BLOCK, lambda start, size, which=which: body(which, start, size))


def forward_part_kernel(info_ref, acted_ref, down_ref, keep_ref, sent_ref):
    halves(info_ref[1] & 1, acted_ref, down_ref, keep_ref, sent_ref, dot)


def forward_grad_kernel(
    parts, own, info_ref, slope_ref, up_ref, down_ref, weight_ref, *refs
):
    enc_refs = refs[:parts]
    part_ref, up_low_ref, down_low_ref, bias_ref, all_ref = refs[parts:]
    upper = info_ref[1] & 1
    half = part_ref.shape[0]
    first = (upper if own else 1 - upper) * half
    bias_ref[...] = jnp.zeros_like(bias_ref)

    def body(start, size):
        from_rows = pl.ds(pl.multiple_of(first + start, size), size)
        rows = pl.ds(start, size)
        for relative, enc_ref in enumerate(enc_refs):
            columns = enc_ref.shape[1]
            lane = pl.multiple_of((info_ref[1] ^ relative) * columns, LANES)
            all_ref[:, pl.ds(lane, columns)] = enc_ref[from_rows, :]
        out_grad = dot_right_t(all_ref[...], weight_ref[...])
        down_low = out_grad.astype(low_type)
        down_low_ref[rows, :] = down_low
        up_low = dot_right_t(down_low, down_ref[...]) * slope_ref[from_rows, :]
        up_low_ref[rows, :] = up_low.astype(low_type)
        bias_ref[0:1, :] += row_sum(out_grad)
        bias_ref[1:2, :] += row_sum(up_low_ref[rows, :].astype(wide_type))
        part_ref[rows, :] = dot_right_t(up_low_ref[rows, :], up_ref[...]).astype(low_type)

    over_rows(half, BLOCK, body)


def put_blocks(exchange, info_ref, keep_ref, sent_ref, wide_ref, pad, first=0):
    share = wide_ref.shape[0] // exchange.count
    for ref, indices in exchange.targets(0, info_ref, keep_ref, sent_ref):
        for block, index in enumerate(indices):
            rows = pl.ds(pl.multiple_of(index * share, 8), share)
            for tile in range(wide_ref.shape[1] // LANES):
                at = block * exchange.block + first + tile * pad
                ref[at : at + share, :] = wide_ref[rows, tile * LANES : (tile + 1) * LANES].astype(low_type)


def halves_of(info_ref, refs):
    if len(refs) == 2:
        return refs[0][...], refs[1][...]
    half = refs[0].shape[0] // 2
    upper = info_ref[1] & 1
    return tuple(
        refs[0][pl.ds(pl.multiple_of(which * half, half), half), :] for which in (upper, 1 - upper)
    )


def early_grads_kernel(
    exchanges, pad, info_ref, low_ref, low_other_ref, acted_ref, act_ref, up_ref, up_other_ref, down_keep_ref,
    down_sent_ref, up_keep_ref, up_sent_ref, wide_ref,
):
    left, right = halves_of(info_ref, (low_ref, low_other_ref)), halves_of(info_ref, (acted_ref,))
    wide_ref[...] = dot_left_t(left[0], right[0]) + dot_left_t(left[1], right[1])
    put_blocks(exchanges[0], info_ref, down_keep_ref, down_sent_ref, wide_ref, pad)
    left, right = halves_of(info_ref, (act_ref,)), halves_of(info_ref, (up_ref, up_other_ref))
    wide_ref[...] = dot_left_t(left[0], right[0]) + dot_left_t(left[1], right[1])
    put_blocks(exchanges[1], info_ref, up_keep_ref, up_sent_ref, wide_ref, pad)


def attention_back_kernel(
    heads, info_ref, sum_ref, sum_other_ref, hidden_ref, low_ref, low_other_ref, gain_ref, weight_ref, qkv_ref,
    prob_ref, prob_last_ref, grads_ref, attn_low_ref, own_ref, bias_ref, grad_ref, probs_ref,
):
    gain = wide_row(gain_ref)
    bias_ref[...] = jnp.zeros_like(bias_ref)
    half = prob_ref.shape[0]
    probs_ref[:half, :] = prob_ref[...]
    probs_ref[half:, :] = prob_last_ref[...]

    def body(source, rows, part, size):
        normed, spread = normalized(hidden_ref[rows, :])
        grad = (sum_ref, sum_other_ref)[source][part, :].astype(wide_type)
        bias_ref[0:1, :] += row_sum(grad * normed)
        bias_ref[1:2, :] += row_sum(grad)
        down_low = (low_ref, low_other_ref)[source][part, :].astype(wide_type)
        hidden_grad = down_low + norm_back(grad, normed, spread, gain)
        grad_ref[rows, :] = hidden_grad
        bias_ref[2:3, :] += row_sum(hidden_grad)
        attn_low = hidden_grad.astype(low_type)
        attn_low_ref[rows, :] = attn_low
        attended_grad = dot_right_t(attn_low, weight_ref[...]).astype(low_type)
        for head in range(heads):
            base = head * 3 * HEAD_DIM
            queries = qkv_ref[rows, base : base + HEAD_DIM]
            key_rows = qkv_ref[rows, base + HEAD_DIM : base + 2 * HEAD_DIM]
            value_rows = qkv_ref[rows, base + 2 * HEAD_DIM : base + 3 * HEAD_DIM]
            probs = probs_ref[rows, head * BLOCK : (head + 1) * BLOCK]
            grad_rows = attended_grad[:, head * HEAD_DIM : (head + 1) * HEAD_DIM]
            value_low = dot(probs, grad_rows).astype(low_type)
            prob_grad = dot_right_t(value_rows, grad_rows)
            wide_probs = probs.astype(wide_type)
            weighted = wide_probs * prob_grad
            score_low = (
                weighted - wide_probs * jnp.sum(weighted, axis=0, keepdims=True)
            ).astype(low_type)
            query_low = (dot_left_t(score_low, key_rows) * scale_factor).astype(low_type)
            key_low = (dot(score_low, queries) * scale_factor).astype(low_type)
            grads_ref[rows, base : base + HEAD_DIM] = query_low
            grads_ref[rows, base + HEAD_DIM : base + 2 * HEAD_DIM] = key_low
            grads_ref[rows, base + 2 * HEAD_DIM : base + 3 * HEAD_DIM] = value_low

    both_halves(info_ref[1] & 1, sum_ref.shape[0], body)
    share = own_ref.shape[0]
    own_ref[...] = grad_ref[pl.ds(pl.multiple_of(info_ref[1] * share, share), share), :]


def views(ref, sizes):
    starts = [sum(sizes[:at]) for at in range(len(sizes))]
    return [ref.at[pl.ds(start, size), :] for start, size in zip(starts, sizes)]


def step_kernel(moves, sizes, info_ref, *refs):
    parted = [None if size is None else views(ref, size) for ref, size in zip(refs, sizes)]
    for exchange, step, sources, kept, (sent, place) in moves:
        pairs = []
        for _, keep, (came, at) in sources:
            pairs += [refs[keep], parted[came][at]]
        exchange.kernel(step, [part for part, _, _ in sources], info_ref, *pairs, refs[kept], parted[sent][place])


def late_grads_kernel(
    exchanges, pad, middle, info_ref, act_ref, grads_ref, attn_low_ref, first_ref, last_ref, keep_ref, sent_ref,
    turned_keep_ref, turned_sent_ref, bias_ref, wide_ref,
):
    columns = grads_ref.shape[1]
    half, first = first_ref.shape
    wide_ref[:, :first] = dot_left_t(attn_low_ref[:half, :], first_ref[...]) + dot_left_t(
        attn_low_ref[half:, :], last_ref[...]
    )
    wide_ref[:, first : first + columns] = dot_left_t(act_ref[...], grads_ref[...])
    put_blocks(exchanges[0], info_ref, keep_ref, sent_ref, wide_ref.at[:, pl.ds(0, middle)], pad)
    put_blocks(
        exchanges[1], info_ref, turned_keep_ref, turned_sent_ref,
        wide_ref.at[:, pl.ds(middle, wide_ref.shape[1] - middle)], pad,
    )
    bias_ref[...] = row_sum(grads_ref[...].astype(wide_type))


EXTRA = 16


def put_extra(ref, start, gain, shift):
    rows = []
    for value in (gain, shift):
        rows += list(split_low(value))
    rows.append(jnp.zeros((EXTRA - 4, gain.shape[1]), low_type))
    ref[start : start + EXTRA, :] = jnp.concatenate(rows, axis=0)


def get_extra(ref, start):
    rows = ref[start : start + EXTRA, :].astype(wide_type)
    return rows[0:1] + rows[1:2], rows[2:3] + rows[3:4]


def norm_kernel(rows_ref, normed_ref):
    def body(start, size):
        rows = pl.ds(start, size)
        normed_ref[rows, :] = normalized(rows_ref[rows, :].astype(wide_type))[0].astype(low_type)

    over_rows(rows_ref.shape[0], CHUNK, body)


def input_part_kernel(info_ref, normed_ref, grads_ref, weight_ref, keep_ref, sent_ref, part_ref, bias_ref):
    lower_bit = info_ref[1] & 1
    bias_ref[...] = jnp.zeros_like(bias_ref)

    def body(start, size):
        rows = pl.ds(start, size)
        grad = dot(grads_ref[rows, :], weight_ref[...])
        part_ref[rows, :] = grad
        bias_ref[0:1, :] += row_sum(grad * normed_ref[rows, :].astype(wide_type))
        bias_ref[1:2, :] += row_sum(grad)

    over_rows(normed_ref.shape[0], CHUNK, body)
    size = keep_ref.shape[0] - EXTRA
    share = size // (lax.axis_size("mp") // 2)
    for out_ref, which in ((sent_ref, 1 - lower_bit), (keep_ref, lower_bit)):
        for block in range(size // share):
            rows = pl.ds(pl.multiple_of((2 * block + which) * share, share), share)
            out_ref[block * share : (block + 1) * share, :] = part_ref[rows, :].astype(low_type)
        put_extra(out_ref, size, bias_ref[0:1, :], bias_ref[1:2, :])


def input_halve_kernel(bit, info_ref, keep_ref, other_ref, next_keep_ref, next_sent_ref, total_ref):
    upper = (info_ref[1] >> bit) & 1
    half = next_keep_ref.shape[0] - EXTRA
    size = 2 * half
    share = total_ref.shape[0] - size
    total_ref[:size, :] = keep_ref[:size, :].astype(wide_type) + other_ref[:size, :].astype(wide_type)
    own, other = get_extra(keep_ref, size), get_extra(other_ref, size)
    for out_ref, which in ((next_sent_ref, 1 - upper), (next_keep_ref, upper)):
        for block in range(half // share):
            rows = pl.ds(pl.multiple_of((2 * block + which) * share, share), share)
            out_ref[block * share : (block + 1) * share, :] = total_ref[rows, :].astype(low_type)
        put_extra(out_ref, half, own[0] + other[0], own[1] + other[1])


def input_grad_kernel(info_ref, rows_ref, keep_ref, other_ref, own_ref, gain_ref, out_ref):
    share = out_ref.shape[0]
    rows = pl.ds(pl.multiple_of(info_ref[1] * share, share), share)
    normed, spread = normalized(rows_ref[rows, :].astype(wide_type))
    grad = keep_ref[:share, :].astype(wide_type) + other_ref[:share, :].astype(wide_type)
    out_ref[...] = (own_ref[...] + norm_back(grad, normed, spread, wide_row(gain_ref))).astype(low_type)


VECTOR_ROWS = 48


def put_rows(values, rows_ref):
    row = 0
    for value in values:
        for tile in range(value.shape[1] // LANES):
            rows_ref[row : row + 1, :] = value[:, tile * LANES : (tile + 1) * LANES]
            row += 1


def take_rows(rows_ref, refs):
    row = 0
    for ref in refs:
        size = ref.shape[0]
        for tile in range(-(-size // LANES)):
            width = min(LANES, size - tile * LANES)
            ref[tile * LANES : tile * LANES + width] = rows_ref[row, :width]
            row += 1


def encoded_kernel(
    info_ref, hidden_ref, sum_ref, sum_other_ref, down_bias_ref, weight_ref, bias_ref, enc_ref, encoded_ref, wide_ref,
    low_ref,
):
    down_bias, bias = wide_row(down_bias_ref), wide_row(bias_ref)

    def body(source, rows, part, size):
        total = (sum_ref, sum_other_ref)[source][part, :].astype(wide_type)
        out_low = (hidden_ref[rows, :] + total + down_bias).astype(low_type)
        low_ref[rows, :] = out_low
        encoded_ref[rows, :] = (dot(out_low, weight_ref[...]) + bias).astype(low_type)

    both_halves(info_ref[1] & 1, sum_ref.shape[0], body)
    wide_ref[...] = dot_left_t(low_ref[...], enc_ref[...])


def last_kernel(
    info, exchange, heads, pad, info_ref, encoded_ref, wide_ref, enc_ref, pos_ref, mask_ref, grads_ref, grads_other_ref,
    second_ref, qkv_ref, first_ref, first_other_ref, keep_ref, sent_ref, rows_ref,
):
    put_blocks(exchange, info_ref, keep_ref, sent_ref, wide_ref, 0)
    put_blocks(exchange, info_ref, keep_ref, sent_ref, pos_ref, 0, pad)
    for ref, indices in exchange.targets(0, info_ref, keep_ref, sent_ref):
        at = exchange.moved_at(0)
        for index in indices:
            image = info.image(info_ref, index)
            ref[at : at + VIS, :] = encoded_ref[pl.ds(pl.multiple_of(image * VIS, VIS), VIS), :]
            at += VIS
    qkv, early = qkv_ref[...], grads_ref[...] + grads_other_ref[...]
    empty = jnp.zeros((1, 2 * LANES - heads * HEAD_DIM), wide_type)
    spread = []
    for part in (0, 2):
        spread += [
            qkv[:, (3 * head + part) * HEAD_DIM : (3 * head + part + 1) * HEAD_DIM] for head in range(heads)
        ] + [empty]
    own = get_extra(first_ref, first_ref.shape[0] - EXTRA)
    other = get_extra(first_other_ref, first_ref.shape[0] - EXTRA)
    put_rows(
        (
            jnp.concatenate(spread, axis=1), early[1:2], row_sum(enc_ref[...].astype(wide_type)), mask_ref[...],
            own[0] + other[0], own[1] + other[1], second_ref[0:1, :], second_ref[1:2, :], second_ref[2:3, :],
            early[0:1],
        ),
        rows_ref,
    )
    for ref in (keep_ref, sent_ref):
        ref[exchange.shared_at(0) :, :] = rows_ref[...].astype(low_type)


def late_out_kernel(
    info, exchange, turned_exchange, pad, middle, sizes, info_ref, seen_ref, keep_ref, turned_ref, came_ref, mask_ref,
    layout_ref, grids_ref, out_ref, qkv_ref, proj_ref, pos_ref, *refs
):
    *vector_refs, wide_ref, rows_ref = refs
    other_ref, turned_other_ref = views(came_ref, sizes)
    cells = lax.broadcasted_iota(jnp.int32, (GRID, VIS), 0)
    cell_column = lax.broadcasted_iota(jnp.int32, (GRID, 1), 0)
    mask_row = wide_row(mask_ref)
    for relative, ref, start in exchange.arrived(keep_ref, other_ref):
        slot = info_ref[0] ^ relative
        seen = seen_ref[pl.ds(slot, 1), :] == cells
        size = info.cells(info_ref, slot)
        fill = (cell_column < size).astype(wide_type) - jnp.sum(
            seen.astype(wide_type), axis=1, keepdims=True
        )
        placed = dot(seen.astype(low_type), ref[start : start + VIS, :])
        grids_ref[slot] = (placed + fill * mask_row + layout_ref[side_of(size)]).astype(low_type)
    share = proj_ref.shape[0]
    tiles = wide_ref.shape[1] // LANES
    for tile in range(tiles):
        here = (exchange, keep_ref, other_ref, tile) if tile < middle else (
            turned_exchange, turned_ref, turned_other_ref, tile - middle
        )
        wide_ref[:, tile * LANES : (tile + 1) * LANES] = here[0].total(here[1], here[2], here[3] * pad, share)
    columns = out_ref.shape[0]
    wide_out = -(-columns // LANES) * LANES
    out_ref[...] = wide_ref[:, :wide_out].T[:columns]
    qkv_ref[...] = wide_ref[:, columns:]
    proj_ref[...] = exchange.total(keep_ref, other_ref, middle * pad, share)
    pos_ref[...] = exchange.total(keep_ref, other_ref, (middle + 1) * pad, pos_ref.shape[0])
    rows_ref[...] = exchange.shared_total(keep_ref, other_ref)
    take_rows(rows_ref, vector_refs)


def early_out_kernel(exchanges, pad, *refs):
    for exchange, keep_ref, other_ref, out_ref in zip(exchanges, refs[:2], refs[2:4], refs[4:]):
        for tile in range(out_ref.shape[1] // LANES):
            out_ref[:, tile * LANES : (tile + 1) * LANES] = exchange.total(
                keep_ref, other_ref, tile * pad, out_ref.shape[0]
            )


def swap(value, axis, bit):
    count = lax.axis_size(axis)
    return lax.ppermute(value, axis, [(i, i ^ bit) for i in range(count)])


def local(
    patch_rows, patches, visible, owner, qkv_weight, query_bias, value_bias, out_weight, out_bias, first_gain,
    first_shift, second_gain, second_shift, up_weight, up_bias, down_weight, down_bias, proj_weight, proj_bias,
    mask_token, decoder_pos, grid_cotangent,
):
    count = lax.axis_size("dp")
    parts = lax.axis_size("mp")
    where = jnp.stack([lax.axis_index("dp"), lax.axis_index("mp")]).astype(jnp.int32)
    rows, width = patch_rows.shape
    images = rows // VIS
    heads = qkv_weight.shape[1] // (3 * HEAD_DIM)
    head_columns = heads * HEAD_DIM
    qkv_columns = qkv_weight.shape[1]
    units = up_weight.shape[1]
    columns = proj_weight.shape[1]
    share = width // count
    pos_share = GRID // count
    half = rows // 2
    own_rows = rows // parts
    pads = (-(-share // 16) * 16, -(-pos_share // 16) * 16)
    run = Order(rows <= PINNED_ROWS)

    tables = grid_tables()
    table_high = tables.astype(low_type)
    table_low = (tables - table_high.astype(np.float32)).astype(low_type)
    turned_high = jnp.asarray(np.ascontiguousarray(table_high.transpose(0, 2, 1)))
    turned_low = jnp.asarray(np.ascontiguousarray(table_low.transpose(0, 2, 1)))
    table_high, table_low = jnp.asarray(table_high), jnp.asarray(table_low)
    qkv_weight_t = qkv_weight.T
    run.leave(owner, visible, patches, grid_cotangent, turned_high, turned_low, table_high, table_low, decoder_pos)
    info = Info(count)
    bits = tuple(range(count.bit_length() - 1))
    late_columns = qkv_columns + head_columns
    turned = (1, 0) + bits[2:]
    back_exchange = Exchange(count, bits, 0, moved=VIS)
    far = (0, 2, 1) + bits[3:]
    up_exchange = Exchange(count, far, units // LANES * pads[0])
    down_exchange = Exchange(count, turned, units // LANES * pads[0])
    tiles = late_columns // LANES
    middle = tiles // 3
    late_exchange = Exchange(count, bits, middle * pads[0])
    turned_exchange = Exchange(count, turned, (tiles - middle) * pads[0])
    last_exchange = Exchange(count, bits, sum(pads), moved=VIS, shared=VECTOR_ROWS)
    joint_exchange = Exchange(
        count, bits, late_exchange.block + last_exchange.block, moved=VIS, shared=VECTOR_ROWS
    )

    def low(*shape):
        return (shape, low_type)

    def wide(*shape):
        return (shape, wide_type)

    def moved(value, axis, bit):
        return run.keep(swap(value, axis, bit))

    def model_steps(keep, received):
        (total,) = run(add_kernel, [low(half, width)], (keep, received), cost=0.6)
        bit = 2
        while bit < parts:
            received = moved(total, "mp", bit)
            yield
            (total,) = run(add_kernel, [low(half, width)], (total, received), cost=0.6)
            bit *= 2
        other = moved(total, "mp", 1)
        yield
        return total, other

    def model_gather(value):
        values = {0: value}
        bit = parts // 2
        while bit:
            values.update({other | bit: moved(values[other], "mp", bit) for other in tuple(values)})
            bit //= 2
        return tuple(values[at] for at in range(parts))

    def data_step(step, exchange, pairs):
        keep, sent = run(
            lambda *refs: exchange.kernel(step, [part for part, _, _ in pairs], *refs),
            [low(exchange.rows(step), LANES)] * 2,
            (facts,) + tuple(array for _, *arrays in pairs for array in arrays),
            (SMEM,) + (VMEM,) * (2 * len(pairs)),
            cost=1.2,
        )
        return keep, moved(sent, "dp", 2 ** exchange.bits[step])

    def data_steps(exchange, keep, sent):
        received = moved(sent, "dp", 2 ** exchange.bits[0])
        yield keep, received
        for step in range(1, len(exchange.bits)):
            keep, received = data_step(step, exchange, [(exchange, keep, received)])
            yield keep, received

    def steps(kept, arrays, moves, sends):
        first = len(kept) + len(arrays)
        sizes = [None] * len(kept) + [size for _, size in arrays] + [None] * len(moves)
        sizes += [size for _, size in sends]
        placed = [
            (exchange, step, sources, first + at, (first + len(moves) + to[0], to[1]))
            for at, (exchange, step, sources, to) in enumerate(moves)
        ]
        results = run(
            lambda *refs: step_kernel(placed, sizes, *refs),
            [low(exchange.rows(step), LANES) for exchange, step, _, _ in moves]
            + [low(sum(size), LANES) for _, size in sends],
            (facts, *kept) + tuple(array for array, _ in arrays),
            (SMEM,) + (VMEM,) * first,
            cost=1.0,
        )
        return results[: len(moves)], [
            moved(sent, "dp", 2**bit) for sent, (bit, _) in zip(results[len(moves) :], sends)
        ]

    def finish_pair(steps):
        *_, last = steps
        return last

    def finish(steps):
        while True:
            try:
                next(steps)
            except StopIteration as stop:
                return stop.value

    out_all = model_gather(out_weight)
    proj_all = model_gather(proj_weight)
    (
        back_keep, back_sent, facts, seen, patch_rows, qkv_weight_t, first_gain, first_shift, query_bias, value_bias,
        out_weight, proj_weight,
    ) = run(
        lambda *refs: cotangent_kernel(info, back_exchange, *refs),
        [
            low(back_exchange.rows(0), columns), low(back_exchange.rows(0), columns), ((info.size,), jnp.int32),
            ((count, VIS), jnp.int32),
        ],
        (where, owner, patches, visible, grid_cotangent),
        (SMEM, SMEM, SMEM, VMEM, VMEM),
        out_specs=(VMEM, VMEM, SMEM, VMEM),
        scratch=[pltpu.VMEM((VIS, count), wide_type)],
        stage=(
            patch_rows, qkv_weight_t, first_gain, first_shift, query_bias, value_bias, out_weight, proj_weight
        ),
        cost=3.0,
    )
    back_steps = data_steps(back_exchange, back_keep, back_sent)
    next(back_steps)
    act_one, qkv = run(
        enter_kernel,
        [low(rows, width), low(rows, qkv_columns)],
        (patch_rows, first_gain, first_shift, qkv_weight_t, query_bias, value_bias),
        cost=1.2,
    )
    next(back_steps)
    packed_rows = half * head_columns // LANES
    packed, first_probs, first_attended, out_bias, second_gain, second_shift, up_weight, up_bias = run(
        lambda *refs: attention_kernel(info, heads, 0, *refs),
        [low(packed_rows, LANES), low(half, heads * BLOCK), low(half, head_columns)],
        (facts, qkv),
        (SMEM, VMEM),
        stage=(out_bias, second_gain, second_shift, up_weight, up_bias),
        cost=2.8,
    )
    first_all = model_gather(packed)
    back_own, back_other = finish_pair(back_steps)
    packed, last_probs, last_attended, down_weight, down_bias, proj_bias = run(
        lambda *refs: attention_kernel(info, heads, half, *refs),
        [low(packed_rows, LANES), low(half, heads * BLOCK), low(half, head_columns)],
        (facts, qkv),
        (SMEM, VMEM),
        stage=(down_weight, down_bias, proj_bias),
        cost=2.5,
    )
    last_all = model_gather(packed)
    out_whole, proj_whole = run(
        lambda *refs: weights_kernel(parts, *refs),
        [low(parts * head_columns, width), low(width, parts * columns)],
        (facts,) + out_all + proj_all,
        (SMEM,) + (VMEM,) * (2 * parts),
        cost=0.0,
    )
    (enc_grad,) = run(
        lambda *refs: back_kernel(info, back_exchange, *refs),
        [low(rows, columns)],
        (facts, back_own, back_other),
        (SMEM, VMEM, VMEM),
        cost=0.4,
    )
    enc_all = model_gather(enc_grad)
    hidden, act_two, acted, slope = run(
        lambda *refs: forward_kernel(parts, head_columns, *refs),
        [wide(rows, width), low(rows, width), low(rows, units), wide(rows, units)],
        (facts, patch_rows, out_bias, second_gain, second_shift, up_weight, up_bias, out_whole)
        + first_all
        + last_all,
        (SMEM,) + (VMEM,) * (7 + 2 * parts),
        scratch=[pltpu.VMEM((BLOCK, parts * head_columns), low_type)],
        cost=2.6,
    )

    def forward_grad(own):
        return run(
            lambda *refs: forward_grad_kernel(parts, own, *refs),
            [low(half, width), low(half, units), low(half, width), wide(2, width)],
            (facts, slope, up_weight, down_weight, proj_whole) + enc_all,
            (SMEM,) + (VMEM,) * (4 + parts),
            scratch=[pltpu.VMEM((BLOCK, parts * columns), low_type)],
            cost=1.2,
        )

    sent, up_low_other, down_low_other, bias_grads_other = forward_grad(False)
    second_other = moved(sent, "mp", 1)
    keep, up_low, down_low, bias_grads = forward_grad(True)
    second_steps = model_steps(keep, second_other)
    next(second_steps)
    keep, sent = run(
        forward_part_kernel,
        [low(half, width), low(half, width)],
        (facts, acted, down_weight),
        (SMEM, VMEM, VMEM),
        cost=0.7,
    )
    out_steps = model_steps(keep, moved(sent, "mp", 1))

    down_keep, down_sent, up_keep, up_sent = run(
        lambda *refs: early_grads_kernel((down_exchange, up_exchange), pads[0], *refs),
        [low(down_exchange.rows(0), LANES)] * 2 + [low(up_exchange.rows(0), LANES)] * 2,
        (facts, down_low, down_low_other, acted, act_two, up_low, up_low_other),
        (SMEM,) + (VMEM,) * 6,
        scratch=[pltpu.VMEM((width, units), wide_type)],
        cost=2.2,
    )
    down_pair = (down_keep, moved(down_sent, "dp", 2 ** turned[0]))
    up_pair = (up_keep, moved(up_sent, "dp", 2 ** bits[0]))
    pos_grad_own, mask_grad, layouts = run(
        lambda *refs: position_kernel(info, *refs),
        [wide(GRID, columns), wide(1, columns), wide(3, GRID, columns)],
        (facts, seen, grid_cotangent, turned_high, turned_low, table_high, table_low, decoder_pos),
        (SMEM,) + (VMEM,) * 7,
        scratch=[pltpu.VMEM((3, GRID, columns), wide_type)],
        cost=20.0,
    )
    next(out_steps)
    next(second_steps)
    second_sum, second_other = finish(second_steps)
    (normed_low,) = run(norm_kernel, [low(rows, width)], (patch_rows,), cost=40.0)
    run.share = 3.0
    grads, attn_low, own_grad, second_grads = run(
        lambda *refs: attention_back_kernel(heads, *refs),
        [low(rows, qkv_columns), low(rows, width), wide(own_rows, width), wide(3, width)],
        (
            facts, second_sum, second_other, hidden, down_low, down_low_other, second_gain, out_weight, qkv,
            first_probs, last_probs,
        ),
        (SMEM,) + (VMEM,) * 10,
        scratch=[pltpu.VMEM((rows, width), wide_type), pltpu.VMEM((rows, heads * BLOCK), low_type)],
        cost=5.5,
    )
    in_keep, in_sent = run(
        input_part_kernel,
        [low(half + EXTRA, width)] * 2,
        (facts, normed_low, grads, qkv_weight_t),
        (SMEM,) + (VMEM,) * 3,
        scratch=[pltpu.VMEM((rows, width), wide_type), pltpu.VMEM((2, width), wide_type)],
        cost=2.0,
    )
    in_other = moved(in_sent, "mp", 1)
    in_other = moved(in_sent, "mp", 1)
    late_keep, late_sent, turned_keep, turned_sent, qkv_bias_grad = run(
        lambda *refs: late_grads_kernel((late_exchange, turned_exchange), pads[0], middle * LANES, *refs),
        [low(late_exchange.rows(0), LANES)] * 2
        + [low(turned_exchange.rows(0), LANES)] * 2
        + [wide(1, qkv_columns)],
        (facts, act_one, grads, attn_low, first_attended, last_attended),
        (SMEM,) + (VMEM,) * 5,
        scratch=[pltpu.VMEM((width, late_columns), wide_type)],
        cost=40.0,
    )
    turned_came = moved(turned_sent, "dp", 2 ** turned[0])
    late_came = moved(late_sent, "dp", 2 ** bits[0])
    bit = 1
    size = half
    while 2**bit < parts:
        in_keep, in_sent = run(
            lambda *refs, bit=bit: input_halve_kernel(bit, *refs),
            [low(size // 2 + EXTRA, width)] * 2,
            (facts, in_keep, in_other),
            (SMEM, VMEM, VMEM),
            scratch=[pltpu.VMEM((size + own_rows, width), wide_type)],
            cost=1.1,
        )
        in_other = moved(in_sent, "mp", 2**bit)
        size //= 2
        bit += 1
    next(out_steps)
    early_sizes = [[exchange.rows(1)] for exchange in (up_exchange, down_exchange)]
    (up_keep, down_keep), (up_came, down_came) = steps(
        (up_pair[0], down_pair[0]),
        ((up_pair[1], [up_exchange.rows(0)]), (down_pair[1], [down_exchange.rows(0)])),
        [
            (up_exchange, 1, [(up_exchange, 0, (2, 0))], (0, 0)),
            (down_exchange, 1, [(down_exchange, 1, (3, 0))], (1, 0)),
        ],
        [(far[1], early_sizes[0]), (turned[1], early_sizes[1])],
    )
    out_sum, out_other = finish(out_steps)
    encoded, proj_grad = run(
        encoded_kernel,
        [low(rows, columns), wide(width, columns)],
        (facts, hidden, out_sum, out_other, down_bias, proj_weight, proj_bias, enc_grad),
        (SMEM,) + (VMEM,) * 7,
        scratch=[pltpu.VMEM((rows, width), low_type)],
        cost=1.0,
    )
    last_keep, last_sent = run(
        lambda *refs: last_kernel(info, last_exchange, heads, pads[0], *refs),
        [low(last_exchange.rows(0), LANES)] * 2,
        (
            facts, encoded, proj_grad, enc_grad, pos_grad_own, mask_grad, bias_grads, bias_grads_other, second_grads,
            qkv_bias_grad, in_keep, in_other,
        ),
        (SMEM,) + (VMEM,) * 11,
        scratch=[pltpu.VMEM((VECTOR_ROWS, LANES), wide_type)],
        cost=0.6,
    )
    last_came = moved(last_sent, "dp", 2 ** bits[0])
    (input_grad,) = run(
        input_grad_kernel,
        [low(own_rows, width)],
        (facts, patch_rows, in_keep, in_other, own_grad, first_gain),
        (SMEM,) + (VMEM,) * 5,
        final=True,
        cost=0.8,
    )

    early = (up_exchange, down_exchange)
    late = (joint_exchange, turned_exchange)
    joint_sizes = [[exchange.rows(1)] for exchange in late]
    (late_keep, turned_keep), late_came = steps(
        (late_keep, last_keep, turned_keep),
        (
            (late_came, [late_exchange.rows(0)]), (last_came, [last_exchange.rows(0)]),
            (turned_came, [turned_exchange.rows(0)]),
        ),
        [
            (joint_exchange, 1, [(late_exchange, 0, (3, 0)), (last_exchange, 1, (4, 0))], (0, 0)),
            (turned_exchange, 1, [(turned_exchange, 2, (5, 0))], (1, 0)),
        ],
        [(bits[1], joint_sizes[0]), (turned[1], joint_sizes[1])],
    )
    old_sizes, early_sizes = early_sizes, [[exchange.rows(2)] for exchange in early]
    (up_keep, down_keep), early_came = steps(
        (up_keep, down_keep),
        ((up_came, old_sizes[0]), (down_came, old_sizes[1])),
        [
            (up_exchange, 2, [(up_exchange, 0, (2, 0))], (0, 0)),
            (down_exchange, 2, [(down_exchange, 1, (3, 0))], (1, 0)),
        ],
        [(far[2], early_sizes[0]), (turned[2], early_sizes[1])],
    )
    last_sizes = [exchange.rows(2) for exchange in late]
    (late_keep, turned_keep), (late_came,) = steps(
        (late_keep, turned_keep),
        ((late_came[0], joint_sizes[0]), (late_came[1], joint_sizes[1])),
        [
            (joint_exchange, 2, [(joint_exchange, 0, (2, 0))], (0, 0)),
            (turned_exchange, 2, [(turned_exchange, 1, (3, 0))], (0, 1)),
        ],
        [(2, last_sizes)],
    )
    for step in range(3, len(bits)):
        old_sizes, early_sizes = early_sizes, [[exchange.rows(step)] for exchange in early]
        (up_keep, down_keep), early_came = steps(
            (up_keep, down_keep),
            ((early_came[0], old_sizes[0]), (early_came[1], old_sizes[1])),
            [(exchange, step, [(exchange, at, (2 + at, 0))], (at, 0)) for at, exchange in enumerate(early)],
            [(step, early_sizes[0]), (step, early_sizes[1])],
        )
        old_sizes, last_sizes = last_sizes, [exchange.rows(step) for exchange in late]
        (late_keep, turned_keep), (late_came,) = steps(
            (late_keep, turned_keep),
            ((late_came, old_sizes),),
            [(exchange, step, [(exchange, at, (2, at))], (0, at)) for at, exchange in enumerate(late)],
            [(step, last_sizes)],
        )
    up_weight_grad, down_weight_grad = run(
        lambda *refs: early_out_kernel(early, pads[0], *refs),
        [wide(share, units)] * 2,
        (up_keep, down_keep, *early_came),
        final=True,
        cost=1.0,
    )
    (
        grids, out_weight_grad, qkv_weight_grad, proj_weight_grad, pos_grad, query_bias_grad, value_bias_grad,
        up_bias_grad, proj_bias_grad, mask_token_grad, first_gain_grad, first_shift_grad, second_gain_grad,
        second_shift_grad, out_bias_grad, down_bias_grad,
    ) = run(
        lambda *refs: late_out_kernel(info, joint_exchange, turned_exchange, pads[0], middle, last_sizes, *refs),
        [
            low(count, GRID, columns), wide(head_columns, share), wide(share, qkv_columns), wide(share, columns),
            wide(pos_share, columns),
        ]
        + [wide(size) for size in (head_columns, head_columns, units, columns, columns) + (width,) * 6],
        (facts, seen, late_keep, turned_keep, late_came, mask_token, layouts),
        (SMEM,) + (VMEM,) * 6,
        scratch=[pltpu.VMEM((share, late_columns), wide_type), pltpu.VMEM((VECTOR_ROWS, LANES), wide_type)],
        final=True,
        cost=2.5,
    )
    return (
        grids, input_grad, qkv_weight_grad, query_bias_grad, value_bias_grad, out_weight_grad, out_bias_grad,
        first_gain_grad, first_shift_grad, second_gain_grad, second_shift_grad, up_weight_grad, up_bias_grad,
        down_weight_grad.T, down_bias_grad, proj_weight_grad, proj_bias_grad, mask_token_grad, pos_grad,
    )


def solution(mesh):
    return jax.shard_map(
        local,
        mesh=mesh,
        in_specs=(
            P("dp", None), P(), P(), P(), P(None, "mp"), P("mp"), P("mp"), P("mp", None), P(), P(), P(), P(), P(),
            P(None, "mp"), P("mp"), P("mp", None), P(), P(None, "mp"), P("mp"), P("mp"), P(None, "mp"),
            P("dp", None, "mp"),
        ),
        out_specs=(
            P("dp", None, "mp"), P(("dp", "mp"), None), P("dp", "mp"), P("mp"), P("mp"), P("mp", "dp"), P(), P(),
            P(), P(), P(), P("dp", "mp"), P("mp"), P("mp", "dp"), P(), P("dp", "mp"), P("mp"), P("mp"),
            P("dp", "mp"),
        ),
        check_vma=False,
    )
```

```python
import math

import jax
import jax.numpy as jnp
import numpy as np
from jax import lax
from jax.experimental import pallas as pl
from jax.experimental.pallas import tpu as pltpu
from jax.sharding import PartitionSpec as P

HEAD_DIM = 64
GRID = 256
VIS = 64
CHUNK = 512
LANES = 128

epsilon = 1e-06
low_type = jnp.bfloat16
wide_type = jnp.float32
scale_factor = HEAD_DIM ** (-0.5)

VMEM = pl.BlockSpec(memory_space=pltpu.VMEM)
SMEM = pl.BlockSpec(memory_space=pltpu.SMEM)
ANY = pl.BlockSpec(memory_space=pl.ANY)
PINNED_ROWS = 512


def grid_tables():
    grid_edge = math.isqrt(GRID)
    tables = []
    for side_cells in (10, 14):
        places = np.arange(side_cells)
        centers = ((2 * places + 1) * grid_edge - side_cells) / (2 * side_cells)
        lower = np.floor(centers).astype(np.int64)
        share = centers - lower
        lerp = np.zeros((side_cells, grid_edge))
        lerp[places, np.clip(lower, 0, grid_edge - 1)] += 1.0 - share
        lerp[places, np.clip(lower + 1, 0, grid_edge - 1)] += share
        table = np.zeros((GRID, GRID))
        table[: side_cells * side_cells] = np.kron(lerp, lerp)
        tables.append(table)
    return np.stack(tables).astype(np.float32)


def split_low(value):
    high = value.astype(low_type)
    return high, (value - high.astype(wide_type)).astype(low_type)


def dot(left, right):
    return lax.dot_general(left, right, (((1,), (0,)), ((), ())), preferred_element_type=wide_type)


def dot_right_t(left, right):
    return lax.dot_general(left, right, (((1,), (1,)), ((), ())), preferred_element_type=wide_type)


def dot_left_t(left, right):
    return lax.dot_general(left, right, (((0,), (0,)), ((), ())), preferred_element_type=wide_type)


def normalized(value):
    center = value - jnp.mean(value, axis=-1, keepdims=True)
    spread = lax.rsqrt(jnp.mean(center * center, axis=-1, keepdims=True) + epsilon)
    return center * spread, spread


def norm_back(grad, normed, spread, gain):
    scaled = grad * gain
    mean_one = jnp.mean(scaled, axis=-1, keepdims=True)
    mean_two = jnp.mean(scaled * normed, axis=-1, keepdims=True)
    return spread * (scaled - mean_one - normed * mean_two)


def row_sum(value):
    return jnp.sum(value, axis=0, keepdims=True)


def over_rows(total, size, body):
    size = min(size, total)
    if total <= 2 * size:
        for start in range(0, total, size):
            body(start, size)
        return

    def step(i, carry):
        body(pl.multiple_of(i * size, size), size)
        return carry

    lax.fori_loop(0, total // size, step, 0)


def size_of(shape, kind):
    return math.prod(shape) * jnp.dtype(kind).itemsize


RATE = 10**9
COST_SHARE = 1.0
BYTES = 0


class Order:
    def __init__(self, pinned):
        self.pinned = pinned
        self.last = None
        self.near = []
        self.far = []
        self.share = COST_SHARE

    def keep(self, value):
        if self.pinned:
            self.near.append((value, pltpu.VMEM))
        return value

    def leave(self, *values):
        self.far += values

    def placed(self, value):
        for near, space in self.near:
            if value is near:
                return pltpu.with_memory_space_constraint(value, space)
        if any(value is far for far in self.far):
            return pltpu.with_memory_space_constraint(value, pltpu.HBM)
        return value

    def __call__(
        self, kernel, outs, args, specs=None, scratch=(), out_specs=None, final=False, stage=(), cost=1.0, after=()
    ):
        args = tuple(args)
        specs = [VMEM] * len(args) if specs is None else list(specs)
        out_specs = [VMEM] * len(outs) if out_specs is None else list(out_specs)
        count, results_count = len(args), len(outs)
        staged = list(stage) if self.pinned else []
        self.leave(*staged)
        needed = sum(size_of(ref.shape, ref.dtype) for ref in scratch)
        needed += sum(
            size_of(arg.shape, arg.dtype) for arg in args if not any(arg is near for near, _ in self.near)
        )
        shapes = []
        for (shape, kind), spec in zip(outs, out_specs):
            if self.pinned and not final:
                shapes.append((pltpu.SMEM if spec is SMEM else pltpu.VMEM)(shape, kind))
            else:
                shapes.append(jax.ShapeDtypeStruct(shape, kind))
                needed += size_of(shape, kind)
        tail = len(staged)
        args += tuple(staged)
        specs += [ANY] * tail
        unread = tuple(after) if self.last is None else (*after, self.last)
        skipped = len(unread)
        args += unread
        specs += [ANY] * skipped

        def body(*refs):
            own, sources, refs = refs[:count], refs[count : count + tail], refs[count + tail + skipped :]
            results, targets, refs = (
                refs[:results_count], refs[results_count : results_count + tail], refs[results_count + tail :]
            )
            copies = []
            if tail:
                *refs, sems = refs
                copies = [
                    pltpu.make_async_copy(source, target, sems.at[at])
                    for at, (source, target) in enumerate(zip(sources, targets))
                ]
            for copy in copies:
                copy.start()
            kernel(*own, *results, *refs)
            for copy in copies:
                copy.wait()

        results = pl.pallas_call(
            body,
            out_shape=tuple(shapes) + tuple(pltpu.VMEM(array.shape, array.dtype) for array in staged),
            in_specs=specs,
            out_specs=tuple(out_specs) + (VMEM,) * tail,
            scratch_shapes=list(scratch) + ([pltpu.SemaphoreType.DMA((tail,))] if tail else []),
            compiler_params=pltpu.CompilerParams(
                vmem_limit_bytes=min(needed + needed // 4 + 10 * 2**20, 60 * 2**20)
            ),
            cost_estimate=pl.CostEstimate(
                flops=int(cost * RATE * self.share), bytes_accessed=int(cost * BYTES), transcendentals=0
            ),
        )(*(self.placed(arg) for arg in args))
        if self.pinned and not final:
            for result, spec in zip(results, out_specs + [VMEM] * tail):
                self.near.append((result, pltpu.SMEM if spec is SMEM else pltpu.VMEM))
        if not final:
            self.last = results[0]
        if stage and not self.pinned:
            return (*results, *stage)
        return results


class Info:
    def __init__(self, count):
        self.count = count
        self.size = 2 + 5 * count

    def dp(self, ref):
        return ref[0]

    def mp(self, ref):
        return ref[1]

    def owner(self, ref, image):
        return ref[2 + image]

    def live(self, ref, image):
        return ref[2 + self.count + image]

    def source(self, ref, slot):
        return ref[2 + 2 * self.count + slot]

    def cells(self, ref, slot):
        return ref[2 + 3 * self.count + slot]

    def image(self, ref, owner):
        return ref[2 + 4 * self.count + owner]


def fill_info(count, where_ref, owner_ref, patches_ref, info_ref):
    me = where_ref[0]
    info_ref[0] = me
    info_ref[1] = where_ref[1]

    def one(at):
        own = me * count + at
        info_ref[2 + at] = owner_ref[own]
        info_ref[2 + 4 * count + owner_ref[own]] = at
        info_ref[2 + count + at] = patches_ref[own] // 4

        def find(i, found):
            return jnp.where(owner_ref[at * count + i] == me, at * count + i, found)

        source = lax.fori_loop(0, count, find, at * count, unroll=count <= 8)
        info_ref[2 + 2 * count + at] = source
        info_ref[2 + 3 * count + at] = patches_ref[source]

    over_slots(count, one)


def over_slots(count, one_slot):
    if count <= 8:
        for slot in range(count):
            one_slot(slot)
    else:
        lax.fori_loop(0, count, lambda slot, carry: (one_slot(slot), carry)[1], 0)


def side_of(size):
    return (size >= 196).astype(jnp.int32) + (size >= 256).astype(jnp.int32)


def block_at(rest, place, bit):
    low = rest & ((1 << place) - 1)
    return ((rest - low) << 1) + (bit << place) + low


class Exchange:
    def __init__(self, count, bits, block, moved=0, shared=0):
        self.count, self.bits, self.block, self.moved, self.shared = count, bits, block, moved, shared

    def blocks(self, step):
        return self.count >> (step + 1)

    def place(self, step):
        bit = self.bits[step]
        return bit - sum(done < bit for done in self.bits[:step])

    def moved_at(self, step):
        return self.blocks(step) * self.block

    def shared_at(self, step):
        return self.moved_at(step) + self.count // 2 * self.moved

    def rows(self, step):
        return self.shared_at(step) + self.shared

    def own_bit(self, step, info_ref):
        return (info_ref[0] >> self.bits[step]) & 1

    def targets(self, step, info_ref, keep_ref, sent_ref):
        own = self.own_bit(step, info_ref)
        place = self.place(step)
        for ref, which in ((sent_ref, 1 - own), (keep_ref, own)):
            yield ref, [block_at(block, place, which) for block in range(self.blocks(step))]

    def kernel(self, step, parts, info_ref, *refs):
        *from_refs, next_keep_ref, next_sent_ref = refs
        pairs = list(zip(parts, from_refs[::2], from_refs[1::2]))
        sources = 1 << (step - 1)
        rests = self.blocks(step - 1)
        for ref, indices in self.targets(step, info_ref, next_keep_ref, next_sent_ref):
            first, moved_at, shared_at = 0, self.moved_at(step), self.shared_at(step)
            for part, keep_ref, other_ref in pairs:
                for block, index in enumerate(indices if part.block else ()):
                    rows = pl.ds(pl.multiple_of(index * part.block, 16), part.block)
                    at = block * self.block + first
                    ref[at : at + part.block, :] = (
                        keep_ref[rows, :].astype(wide_type) + other_ref[rows, :].astype(wide_type)
                    ).astype(low_type)
                first += part.block
                for from_ref in (keep_ref, other_ref) if part.moved else ():
                    for source in range(sources):
                        for index in indices:
                            rows = part.moved_at(step - 1) + (source * rests + index) * part.moved
                            ref[moved_at : moved_at + part.moved, :] = from_ref[
                                pl.ds(pl.multiple_of(rows, 16), part.moved), :
                            ]
                            moved_at += part.moved
                if part.shared:
                    at = part.shared_at(step - 1)
                    rows = slice(at, at + part.shared)
                    ref[shared_at : shared_at + part.shared, :] = (
                        keep_ref[rows, :].astype(wide_type) + other_ref[rows, :].astype(wide_type)
                    ).astype(low_type)

    def arrived(self, keep_ref, other_ref):
        last = len(self.bits) - 1
        sources = 1 << last
        for half, ref in enumerate((keep_ref, other_ref)):
            for source in range(sources):
                relative = 0
                for step, bit in enumerate(self.bits):
                    relative |= (((source + half * sources) >> step) & 1) << bit
                yield relative, ref, self.moved_at(last) + source * self.moved

    def total(self, keep_ref, other_ref, start, size):
        rows = slice(start, start + size)
        return keep_ref[rows, :].astype(wide_type) + other_ref[rows, :].astype(wide_type)

    def shared_total(self, keep_ref, other_ref):
        return self.total(keep_ref, other_ref, self.shared_at(len(self.bits) - 1), self.shared)


def cotangent_kernel(
    info, exchange, where_ref, owner_ref, patches_ref, visible_ref, cot_ref, keep_ref, sent_ref, info_ref, seen_ref,
    turned_ref,
):
    count = info.count
    fill_info(count, where_ref, owner_ref, patches_ref, info_ref)

    def take(slot):
        seen_ref[pl.ds(slot, 1), :] = visible_ref[pl.ds(info.source(info_ref, slot), 1), :]

    over_slots(count, take)
    turned_ref[...] = seen_ref[...].astype(wide_type).T
    cells = lax.broadcasted_iota(jnp.int32, (VIS, GRID), 1).astype(wide_type)
    own = exchange.own_bit(0, info_ref)
    place = exchange.place(0)
    for slot in range(count):
        onehot = (turned_ref[:, slot : slot + 1] == cells).astype(wide_type).astype(low_type)
        rows = dot(onehot, cot_ref[slot]).astype(low_type)
        rest = (slot & ((1 << place) - 1)) | ((slot >> (place + 1)) << place)
        kept = ((slot >> place) & 1) == own

        @pl.when(kept)
        def _(rest=rest, rows=rows):
            keep_ref[rest * VIS : (rest + 1) * VIS, :] = rows

        @pl.when(jnp.logical_not(kept))
        def _(rest=rest, rows=rows):
            sent_ref[rest * VIS : (rest + 1) * VIS, :] = rows


def position_kernel(
    info, info_ref, visible_ref, cot_ref, turned_high_ref, turned_low_ref, table_high_ref, table_low_ref, pos_ref,
    grad_ref, mask_ref, layout_ref, sums_ref,
):
    cells = lax.broadcasted_iota(jnp.int32, (GRID, VIS), 0)
    cell_column = lax.broadcasted_iota(jnp.int32, (GRID, 1), 0)
    sums_ref[...] = jnp.zeros_like(sums_ref)
    mask_ref[...] = jnp.zeros_like(mask_ref)

    def one_slot(slot):
        size = info.cells(info_ref, slot)
        seen = visible_ref[pl.ds(slot, 1), :] == cells
        fill = (cell_column < size).astype(wide_type) - jnp.sum(
            seen.astype(wide_type), axis=1, keepdims=True
        )
        wide = cot_ref[slot].astype(wide_type)
        mask_ref[...] += row_sum(fill * wide)
        sums_ref[side_of(size)] += wide

    over_slots(info.count, one_slot)
    total = sums_ref[2]
    for side in range(2):
        high, low = split_low(sums_ref[side])
        total += (
            dot(turned_high_ref[side], high) + dot(turned_high_ref[side], low) + dot(turned_low_ref[side], high)
        )
    grad_ref[...] = total
    table = pos_ref[...]
    for side in range(2):
        layout_ref[side] = dot(table_high_ref[side], table) + dot(table_low_ref[side], table)
    layout_ref[2] = table.astype(wide_type)


def wide_row(ref):
    return ref[...].astype(wide_type).reshape(1, ref.shape[0])


def enter_kernel(
    rows_ref, gain_ref, shift_ref, weight_ref, query_ref, value_ref, act_ref, qkv_ref
):
    gain, shift = wide_row(gain_ref), wide_row(shift_ref)
    query, value = wide_row(query_ref), wide_row(value_ref)
    nothing = jnp.zeros((1, HEAD_DIM), wide_type)
    pieces = []
    for start in range(0, query.shape[1], HEAD_DIM):
        pieces += [query[:, start : start + HEAD_DIM], nothing, value[:, start : start + HEAD_DIM]]
    bias = jnp.concatenate(pieces, axis=1)

    def body(start, size):
        rows = pl.ds(start, size)
        normed, _ = normalized(rows_ref[rows, :].astype(wide_type))
        act = (normed * gain + shift).astype(low_type)
        act_ref[rows, :] = act
        qkv_ref[rows, :] = (dot_right_t(act, weight_ref[...]) + bias).astype(low_type)

    over_rows(rows_ref.shape[0], CHUNK, body)


BLOCK = 4 * VIS


def attention_kernel(info, heads, first, info_ref, qkv_ref, packed_ref, prob_ref, attended_ref):
    key_image = lax.broadcasted_iota(jnp.int32, (BLOCK, BLOCK), 0) // VIS
    key_slot = lax.broadcasted_iota(jnp.int32, (BLOCK, BLOCK), 0) % VIS
    own_image = key_image == lax.broadcasted_iota(jnp.int32, (BLOCK, BLOCK), 1) // VIS
    columns = heads * HEAD_DIM
    full = columns // LANES * LANES
    rest = BLOCK * (columns - full) // LANES

    def body(start, size):
        rows = pl.ds(start, size)
        from_rows = pl.ds(first + start, size)
        limit = jnp.zeros((size, size), jnp.int32)
        for image in range(size // VIS):
            limit = jnp.where(key_image == image, info.live(info_ref, (first + start) // VIS + image), limit)
        live = jnp.logical_and(own_image, key_slot < limit)
        for head in range(heads):
            base = head * 3 * HEAD_DIM
            queries = qkv_ref[from_rows, base : base + HEAD_DIM]
            key_rows = qkv_ref[from_rows, base + HEAD_DIM : base + 2 * HEAD_DIM]
            value_rows = qkv_ref[from_rows, base + 2 * HEAD_DIM : base + 3 * HEAD_DIM]
            scores = jnp.where(live, dot_right_t(key_rows, queries) * scale_factor, -1e30)
            raised = jnp.exp(scores - jnp.max(scores, axis=0, keepdims=True))
            probs = (raised / jnp.sum(raised, axis=0, keepdims=True)).astype(low_type)
            prob_ref[rows, head * BLOCK : (head + 1) * BLOCK] = probs
            attended_ref[rows, head * HEAD_DIM : (head + 1) * HEAD_DIM] = dot_left_t(
                probs, value_rows
            ).astype(low_type)
        at = start // BLOCK * (full // LANES * BLOCK + rest)
        for tile in range(full // LANES):
            packed_ref[pl.ds(at, BLOCK), :] = attended_ref[rows, tile * LANES : (tile + 1) * LANES]
            at += BLOCK
        pieces = [
            attended_ref[pl.ds(start + piece * rest, rest), full:].astype(wide_type)
            for piece in range(BLOCK // rest)
        ]
        packed_ref[pl.ds(at, rest), :] = jnp.concatenate(pieces, axis=1).astype(low_type)

    over_rows(prob_ref.shape[0], BLOCK, body)


def unpack(own, packed_refs, start, columns, out_ref):
    full = columns // LANES * LANES
    width = columns - full
    rest = BLOCK * width // LANES
    at = start // BLOCK * (full // LANES * BLOCK + rest)
    count = len(packed_refs)
    for tile in range(full // LANES):
        for relative, ref in enumerate(packed_refs):
            lane = (tile * count + (own ^ relative)) * LANES
            out_ref[:, pl.ds(pl.multiple_of(lane, LANES), LANES)] = ref[pl.ds(at, BLOCK), :]
        at += BLOCK
    lane = full * count
    for other in range(0, count, LANES // width):
        pieces = []
        for part in range(other, other + LANES // width):
            rows = None
            for relative, ref in enumerate(packed_refs):
                here = ref[pl.ds(at, rest), :].astype(wide_type)
                rows = here if rows is None else jnp.where((own ^ relative) == part, here, rows)
            pieces.append(
                jnp.concatenate(
                    [rows[:, piece * width : (piece + 1) * width] for piece in range(BLOCK // rest)], axis=0
                )
            )
        out_ref[:, lane : lane + LANES] = jnp.concatenate(pieces, axis=1).astype(low_type)
        lane += LANES


def weights_kernel(parts, info_ref, *refs):
    out_refs, proj_refs, (out_ref, proj_ref) = refs[:parts], refs[parts : 2 * parts], refs[2 * parts :]
    own = info_ref[1]
    columns = out_refs[0].shape[0]
    full = columns // LANES * LANES
    width = columns - full
    for relative, (out_part_ref, proj_part_ref) in enumerate(zip(out_refs, proj_refs)):
        part = own ^ relative
        for tile in range(full // LANES):
            at = pl.multiple_of((tile * parts + part) * LANES, LANES)
            out_ref[pl.ds(at, LANES), :] = out_part_ref[tile * LANES : (tile + 1) * LANES, :]
        at = pl.multiple_of(full * parts + part * width, 16)
        out_ref[pl.ds(at, width), :] = out_part_ref[full:, :]
        size = proj_part_ref.shape[1]
        proj_ref[:, pl.ds(pl.multiple_of(part * size, LANES), size)] = proj_part_ref[...]


def halves(upper, left_ref, weight_ref, keep_ref, sent_ref, product):
    half = keep_ref.shape[0]
    for out_ref, which in ((sent_ref, 1 - upper), (keep_ref, upper)):

        def body(start, size, out_ref=out_ref, which=which):
            rows = pl.ds(pl.multiple_of(which * half + start, size), size)
            out_ref[pl.ds(start, size), :] = product(left_ref[rows, :], weight_ref[...]).astype(
                out_ref.dtype
            )

        over_rows(half, CHUNK, body)


def both_halves(upper, half, body):
    for source, which in enumerate((upper, 1 - upper)):

        def one(start, size, source=source, which=which):
            body(source, pl.ds(pl.multiple_of(which * half + start, size), size), pl.ds(start, size), size)

        over_rows(half, 256, one)


def back_kernel(info, exchange, info_ref, back_ref, back_other_ref, enc_ref):
    for relative, ref, start in exchange.arrived(back_ref, back_other_ref):
        image = info.image(info_ref, info_ref[0] ^ relative)
        enc_ref[pl.ds(pl.multiple_of(image * VIS, VIS), VIS), :] = ref[start : start + VIS, :]


def add_kernel(left_ref, right_ref, out_ref):
    out_ref[...] = (left_ref[...].astype(wide_type) + right_ref[...].astype(wide_type)).astype(low_type)


def forward_kernel(
    parts, columns, info_ref, rows_ref, out_bias_ref, gain_ref, shift_ref, up_ref, up_bias_ref, weight_ref, *refs
):
    attended_refs = (refs[:parts], refs[parts : 2 * parts])
    hidden_ref, act_ref, acted_ref, slope_ref, all_ref = refs[2 * parts :]
    half = rows_ref.shape[0] // 2
    out_bias, gain, shift, up_bias = (
        wide_row(ref) for ref in (out_bias_ref, gain_ref, shift_ref, up_bias_ref)
    )

    def body(which, start, size):
        rows = pl.ds(which * half + start, size)
        unpack(info_ref[1], attended_refs[which], start, columns, all_ref)
        total = dot(all_ref[...], weight_ref[...])
        hidden = rows_ref[rows, :].astype(wide_type) + total + out_bias
        hidden_ref[rows, :] = hidden
        normed, _ = normalized(hidden)
        act = (normed * gain + shift).astype(low_type)
        act_ref[rows, :] = act
        up_pre = dot(act, up_ref[...]) + up_bias
        cdf = 0.5 + 0.5 * lax.erf(up_pre * math.sqrt(0.5))
        acted_ref[rows, :] = (up_pre * cdf).astype(low_type)
        slope_ref[rows, :] = cdf + up_pre * jnp.exp(-0.5 * up_pre * up_pre) * (
            1.0 / math.sqrt(2.0 * math.pi)
        )

    for which in range(2):
        over_rows(half, BLOCK, lambda start, size, which=which: body(which, start, size))


def forward_part_kernel(info_ref, acted_ref, down_ref, keep_ref, sent_ref):
    halves(info_ref[1] & 1, acted_ref, down_ref, keep_ref, sent_ref, dot)


def forward_grad_kernel(
    parts, own, info_ref, slope_ref, up_ref, down_ref, weight_ref, *refs
):
    enc_refs = refs[:parts]
    part_ref, up_low_ref, down_low_ref, bias_ref, all_ref = refs[parts:]
    upper = info_ref[1] & 1
    half = part_ref.shape[0]
    first = (upper if own else 1 - upper) * half
    bias_ref[...] = jnp.zeros_like(bias_ref)

    def body(start, size):
        from_rows = pl.ds(pl.multiple_of(first + start, size), size)
        rows = pl.ds(start, size)
        for relative, enc_ref in enumerate(enc_refs):
            columns = enc_ref.shape[1]
            lane = pl.multiple_of((info_ref[1] ^ relative) * columns, LANES)
            all_ref[:, pl.ds(lane, columns)] = enc_ref[from_rows, :]
        out_grad = dot_right_t(all_ref[...], weight_ref[...])
        down_low = out_grad.astype(low_type)
        down_low_ref[rows, :] = down_low
        up_low = dot_right_t(down_low, down_ref[...]) * slope_ref[from_rows, :]
        up_low_ref[rows, :] = up_low.astype(low_type)
        bias_ref[0:1, :] += row_sum(out_grad)
        bias_ref[1:2, :] += row_sum(up_low_ref[rows, :].astype(wide_type))
        part_ref[rows, :] = dot_right_t(up_low_ref[rows, :], up_ref[...]).astype(low_type)

    over_rows(half, BLOCK, body)


def put_blocks(exchange, info_ref, keep_ref, sent_ref, wide_ref, pad, first=0):
    share = wide_ref.shape[0] // exchange.count
    for ref, indices in exchange.targets(0, info_ref, keep_ref, sent_ref):
        for block, index in enumerate(indices):
            rows = pl.ds(pl.multiple_of(index * share, 8), share)
            for tile in range(wide_ref.shape[1] // LANES):
                at = block * exchange.block + first + tile * pad
                ref[at : at + share, :] = wide_ref[rows, tile * LANES : (tile + 1) * LANES].astype(low_type)


def halves_of(info_ref, refs):
    if len(refs) == 2:
        return refs[0][...], refs[1][...]
    half = refs[0].shape[0] // 2
    upper = info_ref[1] & 1
    return tuple(
        refs[0][pl.ds(pl.multiple_of(which * half, half), half), :] for which in (upper, 1 - upper)
    )


def early_grads_kernel(
    exchanges, pad, info_ref, low_ref, low_other_ref, acted_ref, act_ref, up_ref, up_other_ref, down_keep_ref,
    down_sent_ref, up_keep_ref, up_sent_ref, wide_ref,
):
    left, right = halves_of(info_ref, (low_ref, low_other_ref)), halves_of(info_ref, (acted_ref,))
    wide_ref[...] = dot_left_t(left[0], right[0]) + dot_left_t(left[1], right[1])
    put_blocks(exchanges[0], info_ref, down_keep_ref, down_sent_ref, wide_ref, pad)
    left, right = halves_of(info_ref, (act_ref,)), halves_of(info_ref, (up_ref, up_other_ref))
    wide_ref[...] = dot_left_t(left[0], right[0]) + dot_left_t(left[1], right[1])
    put_blocks(exchanges[1], info_ref, up_keep_ref, up_sent_ref, wide_ref, pad)


def attention_back_kernel(
    heads, info_ref, sum_ref, sum_other_ref, hidden_ref, low_ref, low_other_ref, gain_ref, weight_ref, qkv_ref,
    prob_ref, prob_last_ref, grads_ref, attn_low_ref, own_ref, bias_ref, grad_ref, probs_ref,
):
    gain = wide_row(gain_ref)
    bias_ref[...] = jnp.zeros_like(bias_ref)
    half = prob_ref.shape[0]
    probs_ref[:half, :] = prob_ref[...]
    probs_ref[half:, :] = prob_last_ref[...]

    def body(source, rows, part, size):
        normed, spread = normalized(hidden_ref[rows, :])
        grad = (sum_ref, sum_other_ref)[source][part, :].astype(wide_type)
        bias_ref[0:1, :] += row_sum(grad * normed)
        bias_ref[1:2, :] += row_sum(grad)
        down_low = (low_ref, low_other_ref)[source][part, :].astype(wide_type)
        hidden_grad = down_low + norm_back(grad, normed, spread, gain)
        grad_ref[rows, :] = hidden_grad
        bias_ref[2:3, :] += row_sum(hidden_grad)
        attn_low = hidden_grad.astype(low_type)
        attn_low_ref[rows, :] = attn_low
        attended_grad = dot_right_t(attn_low, weight_ref[...]).astype(low_type)
        for head in range(heads):
            base = head * 3 * HEAD_DIM
            queries = qkv_ref[rows, base : base + HEAD_DIM]
            key_rows = qkv_ref[rows, base + HEAD_DIM : base + 2 * HEAD_DIM]
            value_rows = qkv_ref[rows, base + 2 * HEAD_DIM : base + 3 * HEAD_DIM]
            probs = probs_ref[rows, head * BLOCK : (head + 1) * BLOCK]
            grad_rows = attended_grad[:, head * HEAD_DIM : (head + 1) * HEAD_DIM]
            value_low = dot(probs, grad_rows).astype(low_type)
            prob_grad = dot_right_t(value_rows, grad_rows)
            wide_probs = probs.astype(wide_type)
            weighted = wide_probs * prob_grad
            score_low = (
                weighted - wide_probs * jnp.sum(weighted, axis=0, keepdims=True)
            ).astype(low_type)
            query_low = (dot_left_t(score_low, key_rows) * scale_factor).astype(low_type)
            key_low = (dot(score_low, queries) * scale_factor).astype(low_type)
            grads_ref[rows, base : base + HEAD_DIM] = query_low
            grads_ref[rows, base + HEAD_DIM : base + 2 * HEAD_DIM] = key_low
            grads_ref[rows, base + 2 * HEAD_DIM : base + 3 * HEAD_DIM] = value_low

    both_halves(info_ref[1] & 1, sum_ref.shape[0], body)
    share = own_ref.shape[0]
    own_ref[...] = grad_ref[pl.ds(pl.multiple_of(info_ref[1] * share, share), share), :]


def views(ref, sizes):
    starts = [sum(sizes[:at]) for at in range(len(sizes))]
    return [ref.at[pl.ds(start, size), :] for start, size in zip(starts, sizes)]


def step_kernel(moves, sizes, info_ref, *refs):
    parted = [None if size is None else views(ref, size) for ref, size in zip(refs, sizes)]
    for exchange, step, sources, kept, (sent, place) in moves:
        pairs = []
        for _, keep, (came, at) in sources:
            pairs += [refs[keep], parted[came][at]]
        exchange.kernel(step, [part for part, _, _ in sources], info_ref, *pairs, refs[kept], parted[sent][place])


def late_grads_kernel(
    exchanges, pad, middle, info_ref, act_ref, grads_ref, attn_low_ref, first_ref, last_ref, keep_ref, sent_ref,
    turned_keep_ref, turned_sent_ref, bias_ref, wide_ref,
):
    columns = grads_ref.shape[1]
    half, first = first_ref.shape
    wide_ref[:, :first] = dot_left_t(attn_low_ref[:half, :], first_ref[...]) + dot_left_t(
        attn_low_ref[half:, :], last_ref[...]
    )
    wide_ref[:, first : first + columns] = dot_left_t(act_ref[...], grads_ref[...])
    put_blocks(exchanges[0], info_ref, keep_ref, sent_ref, wide_ref.at[:, pl.ds(0, middle)], pad)
    put_blocks(
        exchanges[1], info_ref, turned_keep_ref, turned_sent_ref,
        wide_ref.at[:, pl.ds(middle, wide_ref.shape[1] - middle)], pad,
    )
    bias_ref[...] = row_sum(grads_ref[...].astype(wide_type))


EXTRA = 16


def put_extra(ref, start, gain, shift):
    rows = []
    for value in (gain, shift):
        rows += list(split_low(value))
    rows.append(jnp.zeros((EXTRA - 4, gain.shape[1]), low_type))
    ref[start : start + EXTRA, :] = jnp.concatenate(rows, axis=0)


def get_extra(ref, start):
    rows = ref[start : start + EXTRA, :].astype(wide_type)
    return rows[0:1] + rows[1:2], rows[2:3] + rows[3:4]


def norm_kernel(rows_ref, normed_ref):
    def body(start, size):
        rows = pl.ds(start, size)
        normed_ref[rows, :] = normalized(rows_ref[rows, :].astype(wide_type))[0].astype(low_type)

    over_rows(rows_ref.shape[0], CHUNK, body)


def input_part_kernel(info_ref, normed_ref, grads_ref, weight_ref, keep_ref, sent_ref, part_ref, bias_ref):
    lower_bit = info_ref[1] & 1
    bias_ref[...] = jnp.zeros_like(bias_ref)

    def body(start, size):
        rows = pl.ds(start, size)
        grad = dot(grads_ref[rows, :], weight_ref[...])
        part_ref[rows, :] = grad
        bias_ref[0:1, :] += row_sum(grad * normed_ref[rows, :].astype(wide_type))
        bias_ref[1:2, :] += row_sum(grad)

    over_rows(normed_ref.shape[0], CHUNK, body)
    size = keep_ref.shape[0] - EXTRA
    share = size // (lax.axis_size("mp") // 2)
    for out_ref, which in ((sent_ref, 1 - lower_bit), (keep_ref, lower_bit)):
        for block in range(size // share):
            rows = pl.ds(pl.multiple_of((2 * block + which) * share, share), share)
            out_ref[block * share : (block + 1) * share, :] = part_ref[rows, :].astype(low_type)
        put_extra(out_ref, size, bias_ref[0:1, :], bias_ref[1:2, :])


def input_halve_kernel(bit, info_ref, keep_ref, other_ref, next_keep_ref, next_sent_ref, total_ref):
    upper = (info_ref[1] >> bit) & 1
    half = next_keep_ref.shape[0] - EXTRA
    size = 2 * half
    share = total_ref.shape[0] - size
    total_ref[:size, :] = keep_ref[:size, :].astype(wide_type) + other_ref[:size, :].astype(wide_type)
    own, other = get_extra(keep_ref, size), get_extra(other_ref, size)
    for out_ref, which in ((next_sent_ref, 1 - upper), (next_keep_ref, upper)):
        for block in range(half // share):
            rows = pl.ds(pl.multiple_of((2 * block + which) * share, share), share)
            out_ref[block * share : (block + 1) * share, :] = total_ref[rows, :].astype(low_type)
        put_extra(out_ref, half, own[0] + other[0], own[1] + other[1])


def input_grad_kernel(info_ref, rows_ref, keep_ref, other_ref, own_ref, gain_ref, out_ref):
    share = out_ref.shape[0]
    rows = pl.ds(pl.multiple_of(info_ref[1] * share, share), share)
    normed, spread = normalized(rows_ref[rows, :].astype(wide_type))
    grad = keep_ref[:share, :].astype(wide_type) + other_ref[:share, :].astype(wide_type)
    out_ref[...] = (own_ref[...] + norm_back(grad, normed, spread, wide_row(gain_ref))).astype(low_type)


VECTOR_ROWS = 48


def put_rows(values, rows_ref):
    row = 0
    for value in values:
        for tile in range(value.shape[1] // LANES):
            rows_ref[row : row + 1, :] = value[:, tile * LANES : (tile + 1) * LANES]
            row += 1


def take_rows(rows_ref, refs):
    row = 0
    for ref in refs:
        size = ref.shape[0]
        for tile in range(-(-size // LANES)):
            width = min(LANES, size - tile * LANES)
            ref[tile * LANES : tile * LANES + width] = rows_ref[row, :width]
            row += 1


def encoded_kernel(
    info_ref, hidden_ref, sum_ref, sum_other_ref, down_bias_ref, weight_ref, bias_ref, enc_ref, encoded_ref, wide_ref,
    low_ref,
):
    down_bias, bias = wide_row(down_bias_ref), wide_row(bias_ref)

    def body(source, rows, part, size):
        total = (sum_ref, sum_other_ref)[source][part, :].astype(wide_type)
        out_low = (hidden_ref[rows, :] + total + down_bias).astype(low_type)
        low_ref[rows, :] = out_low
        encoded_ref[rows, :] = (dot(out_low, weight_ref[...]) + bias).astype(low_type)

    both_halves(info_ref[1] & 1, sum_ref.shape[0], body)
    wide_ref[...] = dot_left_t(low_ref[...], enc_ref[...])


def last_kernel(
    info, exchange, heads, pad, info_ref, encoded_ref, wide_ref, enc_ref, pos_ref, mask_ref, grads_ref, grads_other_ref,
    second_ref, qkv_ref, first_ref, first_other_ref, keep_ref, sent_ref, rows_ref,
):
    put_blocks(exchange, info_ref, keep_ref, sent_ref, wide_ref, 0)
    put_blocks(exchange, info_ref, keep_ref, sent_ref, pos_ref, 0, pad)
    for ref, indices in exchange.targets(0, info_ref, keep_ref, sent_ref):
        at = exchange.moved_at(0)
        for index in indices:
            image = info.image(info_ref, index)
            ref[at : at + VIS, :] = encoded_ref[pl.ds(pl.multiple_of(image * VIS, VIS), VIS), :]
            at += VIS
    qkv, early = qkv_ref[...], grads_ref[...] + grads_other_ref[...]
    empty = jnp.zeros((1, 2 * LANES - heads * HEAD_DIM), wide_type)
    spread = []
    for part in (0, 2):
        spread += [
            qkv[:, (3 * head + part) * HEAD_DIM : (3 * head + part + 1) * HEAD_DIM] for head in range(heads)
        ] + [empty]
    own = get_extra(first_ref, first_ref.shape[0] - EXTRA)
    other = get_extra(first_other_ref, first_ref.shape[0] - EXTRA)
    put_rows(
        (
            jnp.concatenate(spread, axis=1), early[1:2], row_sum(enc_ref[...].astype(wide_type)), mask_ref[...],
            own[0] + other[0], own[1] + other[1], second_ref[0:1, :], second_ref[1:2, :], second_ref[2:3, :],
            early[0:1],
        ),
        rows_ref,
    )
    for ref in (keep_ref, sent_ref):
        ref[exchange.shared_at(0) :, :] = rows_ref[...].astype(low_type)


def late_out_kernel(
    info, exchange, turned_exchange, pad, middle, sizes, info_ref, seen_ref, keep_ref, turned_ref, came_ref, mask_ref,
    layout_ref, grids_ref, out_ref, qkv_ref, proj_ref, pos_ref, *refs
):
    *vector_refs, wide_ref, rows_ref = refs
    other_ref, turned_other_ref = views(came_ref, sizes)
    cells = lax.broadcasted_iota(jnp.int32, (GRID, VIS), 0)
    cell_column = lax.broadcasted_iota(jnp.int32, (GRID, 1), 0)
    mask_row = wide_row(mask_ref)
    for relative, ref, start in exchange.arrived(keep_ref, other_ref):
        slot = info_ref[0] ^ relative
        seen = seen_ref[pl.ds(slot, 1), :] == cells
        size = info.cells(info_ref, slot)
        fill = (cell_column < size).astype(wide_type) - jnp.sum(
            seen.astype(wide_type), axis=1, keepdims=True
        )
        placed = dot(seen.astype(low_type), ref[start : start + VIS, :])
        grids_ref[slot] = (placed + fill * mask_row + layout_ref[side_of(size)]).astype(low_type)
    share = proj_ref.shape[0]
    tiles = wide_ref.shape[1] // LANES
    for tile in range(tiles):
        here = (exchange, keep_ref, other_ref, tile) if tile < middle else (
            turned_exchange, turned_ref, turned_other_ref, tile - middle
        )
        wide_ref[:, tile * LANES : (tile + 1) * LANES] = here[0].total(here[1], here[2], here[3] * pad, share)
    columns = out_ref.shape[0]
    wide_out = -(-columns // LANES) * LANES
    out_ref[...] = wide_ref[:, :wide_out].T[:columns]
    qkv_ref[...] = wide_ref[:, columns:]
    proj_ref[...] = exchange.total(keep_ref, other_ref, middle * pad, share)
    pos_ref[...] = exchange.total(keep_ref, other_ref, (middle + 1) * pad, pos_ref.shape[0])
    rows_ref[...] = exchange.shared_total(keep_ref, other_ref)
    take_rows(rows_ref, vector_refs)


def early_out_kernel(exchanges, pad, *refs):
    for exchange, keep_ref, other_ref, out_ref in zip(exchanges, refs[:2], refs[2:4], refs[4:]):
        for tile in range(out_ref.shape[1] // LANES):
            out_ref[:, tile * LANES : (tile + 1) * LANES] = exchange.total(
                keep_ref, other_ref, tile * pad, out_ref.shape[0]
            )


def swap(value, axis, bit):
    count = lax.axis_size(axis)
    return lax.ppermute(value, axis, [(i, i ^ bit) for i in range(count)])


def local(
    patch_rows, patches, visible, owner, qkv_weight, query_bias, value_bias, out_weight, out_bias, first_gain,
    first_shift, second_gain, second_shift, up_weight, up_bias, down_weight, down_bias, proj_weight, proj_bias,
    mask_token, decoder_pos, grid_cotangent,
):
    count = lax.axis_size("dp")
    parts = lax.axis_size("mp")
    where = jnp.stack([lax.axis_index("dp"), lax.axis_index("mp")]).astype(jnp.int32)
    rows, width = patch_rows.shape
    images = rows // VIS
    heads = qkv_weight.shape[1] // (3 * HEAD_DIM)
    head_columns = heads * HEAD_DIM
    qkv_columns = qkv_weight.shape[1]
    units = up_weight.shape[1]
    columns = proj_weight.shape[1]
    share = width // count
    pos_share = GRID // count
    half = rows // 2
    own_rows = rows // parts
    pads = (-(-share // 16) * 16, -(-pos_share // 16) * 16)
    run = Order(rows <= PINNED_ROWS)

    tables = grid_tables()
    table_high = tables.astype(low_type)
    table_low = (tables - table_high.astype(np.float32)).astype(low_type)
    turned_high = jnp.asarray(np.ascontiguousarray(table_high.transpose(0, 2, 1)))
    turned_low = jnp.asarray(np.ascontiguousarray(table_low.transpose(0, 2, 1)))
    table_high, table_low = jnp.asarray(table_high), jnp.asarray(table_low)
    qkv_weight_t = qkv_weight.T
    run.leave(owner, visible, patches, grid_cotangent, turned_high, turned_low, table_high, table_low, decoder_pos)
    info = Info(count)
    bits = tuple(range(count.bit_length() - 1))
    late_columns = qkv_columns + head_columns
    turned = (1, 0) + bits[2:]
    back_exchange = Exchange(count, bits, 0, moved=VIS)
    far = (0, 2, 1) + bits[3:]
    up_exchange = Exchange(count, far, units // LANES * pads[0])
    down_exchange = Exchange(count, turned, units // LANES * pads[0])
    tiles = late_columns // LANES
    middle = 3 * tiles // 6
    late_exchange = Exchange(count, bits, middle * pads[0])
    turned_exchange = Exchange(count, turned, (tiles - middle) * pads[0])
    last_exchange = Exchange(count, bits, sum(pads), moved=VIS, shared=VECTOR_ROWS)
    joint_exchange = Exchange(
        count, bits, late_exchange.block + last_exchange.block, moved=VIS, shared=VECTOR_ROWS
    )

    def low(*shape):
        return (shape, low_type)

    def wide(*shape):
        return (shape, wide_type)

    def moved(value, axis, bit):
        return run.keep(swap(value, axis, bit))

    def model_steps(keep, received):
        (total,) = run(add_kernel, [low(half, width)], (keep, received), cost=0.6)
        bit = 2
        while bit < parts:
            received = moved(total, "mp", bit)
            yield
            (total,) = run(add_kernel, [low(half, width)], (total, received), cost=0.6)
            bit *= 2
        other = moved(total, "mp", 1)
        yield
        return total, other

    def model_gather(value):
        values = {0: value}
        bit = parts // 2
        while bit:
            values.update({other | bit: moved(values[other], "mp", bit) for other in tuple(values)})
            bit //= 2
        return tuple(values[at] for at in range(parts))

    def data_step(step, exchange, pairs):
        keep, sent = run(
            lambda *refs: exchange.kernel(step, [part for part, _, _ in pairs], *refs),
            [low(exchange.rows(step), LANES)] * 2,
            (facts,) + tuple(array for _, *arrays in pairs for array in arrays),
            (SMEM,) + (VMEM,) * (2 * len(pairs)),
            cost=1.2,
        )
        return keep, moved(sent, "dp", 2 ** exchange.bits[step])

    def data_steps(exchange, keep, sent):
        received = moved(sent, "dp", 2 ** exchange.bits[0])
        yield keep, received
        for step in range(1, len(exchange.bits)):
            keep, received = data_step(step, exchange, [(exchange, keep, received)])
            yield keep, received

    def steps(kept, arrays, moves, sends, cost=1.0):
        first = len(kept) + len(arrays)
        sizes = [None] * len(kept) + [size for _, size in arrays] + [None] * len(moves)
        sizes += [size for _, size in sends]
        placed = [
            (exchange, step, sources, first + at, (first + len(moves) + to[0], to[1]))
            for at, (exchange, step, sources, to) in enumerate(moves)
        ]
        results = run(
            lambda *refs: step_kernel(placed, sizes, *refs),
            [low(exchange.rows(step), LANES) for exchange, step, _, _ in moves]
            + [low(sum(size), LANES) for _, size in sends],
            (facts, *kept) + tuple(array for array, _ in arrays),
            (SMEM,) + (VMEM,) * first,
            cost=cost,
        )
        return results[: len(moves)], [
            moved(sent, "dp", 2**bit) for sent, (bit, _) in zip(results[len(moves) :], sends)
        ]

    def finish_pair(steps):
        *_, last = steps
        return last

    def finish(steps):
        while True:
            try:
                next(steps)
            except StopIteration as stop:
                return stop.value

    out_all = model_gather(out_weight)
    proj_all = model_gather(proj_weight)
    (
        back_keep, back_sent, facts, seen, patch_rows, qkv_weight_t, first_gain, first_shift, query_bias, value_bias,
    ) = run(
        lambda *refs: cotangent_kernel(info, back_exchange, *refs),
        [
            low(back_exchange.rows(0), columns), low(back_exchange.rows(0), columns), ((info.size,), jnp.int32),
            ((count, VIS), jnp.int32),
        ],
        (where, owner, patches, visible, grid_cotangent),
        (SMEM, SMEM, SMEM, VMEM, VMEM),
        out_specs=(VMEM, VMEM, SMEM, VMEM),
        scratch=[pltpu.VMEM((VIS, count), wide_type)],
        stage=(patch_rows, qkv_weight_t, first_gain, first_shift, query_bias, value_bias),
        cost=3.0,
    )
    back_steps = data_steps(back_exchange, back_keep, back_sent)
    next(back_steps)
    act_one, qkv = run(
        enter_kernel,
        [low(rows, width), low(rows, qkv_columns)],
        (patch_rows, first_gain, first_shift, qkv_weight_t, query_bias, value_bias),
        cost=1.2,
        after=(out_all[1], proj_all[1]),
    )
    next(back_steps)
    packed_rows = half * head_columns // LANES
    packed, first_probs, first_attended, out_bias, second_gain, second_shift, up_weight, up_bias = run(
        lambda *refs: attention_kernel(info, heads, 0, *refs),
        [low(packed_rows, LANES), low(half, heads * BLOCK), low(half, head_columns)],
        (facts, qkv),
        (SMEM, VMEM),
        stage=(out_bias, second_gain, second_shift, up_weight, up_bias),
        cost=2.8,
    )
    first_all = model_gather(packed)
    back_own, back_other = finish_pair(back_steps)
    (
        packed, last_probs, last_attended, down_weight, down_bias, proj_bias, out_near, proj_near, out_core, proj_core
    ) = run(
        lambda *refs: attention_kernel(info, heads, half, *refs),
        [low(packed_rows, LANES), low(half, heads * BLOCK), low(half, head_columns)],
        (facts, qkv),
        (SMEM, VMEM),
        stage=(down_weight, down_bias, proj_bias, out_weight, proj_weight, out_all[1], proj_all[1]),
        cost=2.5,
        after=(out_all[parts // 2], proj_all[parts // 2]),
    )
    last_all = model_gather(packed)
    out_whole, proj_whole = run(
        lambda *refs: weights_kernel(parts, *refs),
        [low(parts * head_columns, width), low(width, parts * columns)],
        (facts, out_near, out_core) + out_all[2:] + (proj_near, proj_core) + proj_all[2:],
        (SMEM,) + (VMEM,) * (2 * parts),
        cost=0.0,
    )
    (enc_grad,) = run(
        lambda *refs: back_kernel(info, back_exchange, *refs),
        [low(rows, columns)],
        (facts, back_own, back_other),
        (SMEM, VMEM, VMEM),
        cost=0.4,
    )
    enc_all = model_gather(enc_grad)
    hidden, act_two, acted, slope = run(
        lambda *refs: forward_kernel(parts, head_columns, *refs),
        [wide(rows, width), low(rows, width), low(rows, units), wide(rows, units)],
        (facts, patch_rows, out_bias, second_gain, second_shift, up_weight, up_bias, out_whole)
        + first_all
        + last_all,
        (SMEM,) + (VMEM,) * (7 + 2 * parts),
        scratch=[pltpu.VMEM((BLOCK, parts * head_columns), low_type)],
        cost=2.6,
    )

    def forward_grad(own):
        return run(
            lambda *refs: forward_grad_kernel(parts, own, *refs),
            [low(half, width), low(half, units), low(half, width), wide(2, width)],
            (facts, slope, up_weight, down_weight, proj_whole) + enc_all,
            (SMEM,) + (VMEM,) * (4 + parts),
            scratch=[pltpu.VMEM((BLOCK, parts * columns), low_type)],
            cost=1.2,
        )

    sent, up_low_other, down_low_other, bias_grads_other = forward_grad(False)
    second_other = moved(sent, "mp", 1)
    keep, up_low, down_low, bias_grads = forward_grad(True)
    second_steps = model_steps(keep, second_other)
    next(second_steps)
    down_keep, down_sent, up_keep, up_sent = run(
        lambda *refs: early_grads_kernel((down_exchange, up_exchange), pads[0], *refs),
        [low(down_exchange.rows(0), LANES)] * 2 + [low(up_exchange.rows(0), LANES)] * 2,
        (facts, down_low, down_low_other, acted, act_two, up_low, up_low_other),
        (SMEM,) + (VMEM,) * 6,
        scratch=[pltpu.VMEM((width, units), wide_type)],
        cost=2.2,
    )
    down_pair = (down_keep, moved(down_sent, "dp", 2 ** turned[0]))
    up_pair = (up_keep, moved(up_sent, "dp", 2 ** bits[0]))
    keep, sent = run(
        forward_part_kernel,
        [low(half, width), low(half, width)],
        (facts, acted, down_weight),
        (SMEM, VMEM, VMEM),
        cost=0.7,
    )
    out_steps = model_steps(keep, moved(sent, "mp", 1))

    pos_grad_own, mask_grad, layouts = run(
        lambda *refs: position_kernel(info, *refs),
        [wide(GRID, columns), wide(1, columns), wide(3, GRID, columns)],
        (facts, seen, grid_cotangent, turned_high, turned_low, table_high, table_low, decoder_pos),
        (SMEM,) + (VMEM,) * 7,
        scratch=[pltpu.VMEM((3, GRID, columns), wide_type)],
        cost=20.0,
    )
    next(out_steps)
    next(second_steps)
    second_sum, second_other = finish(second_steps)
    (normed_low,) = run(norm_kernel, [low(rows, width)], (patch_rows,), cost=40.0)
    run.share = 3.0
    grads, attn_low, own_grad, second_grads = run(
        lambda *refs: attention_back_kernel(heads, *refs),
        [low(rows, qkv_columns), low(rows, width), wide(own_rows, width), wide(3, width)],
        (
            facts, second_sum, second_other, hidden, down_low, down_low_other, second_gain, out_near, qkv,
            first_probs, last_probs,
        ),
        (SMEM,) + (VMEM,) * 10,
        scratch=[pltpu.VMEM((rows, width), wide_type), pltpu.VMEM((rows, heads * BLOCK), low_type)],
        cost=5.5,
    )
    in_keep, in_sent = run(
        input_part_kernel,
        [low(half + EXTRA, width)] * 2,
        (facts, normed_low, grads, qkv_weight_t),
        (SMEM,) + (VMEM,) * 3,
        scratch=[pltpu.VMEM((rows, width), wide_type), pltpu.VMEM((2, width), wide_type)],
        cost=2.0,
    )
    in_other = moved(in_sent, "mp", 1)
    in_other = moved(in_sent, "mp", 1)
    late_keep, late_sent, turned_keep, turned_sent, qkv_bias_grad = run(
        lambda *refs: late_grads_kernel((late_exchange, turned_exchange), pads[0], middle * LANES, *refs),
        [low(late_exchange.rows(0), LANES)] * 2
        + [low(turned_exchange.rows(0), LANES)] * 2
        + [wide(1, qkv_columns)],
        (facts, act_one, grads, attn_low, first_attended, last_attended),
        (SMEM,) + (VMEM,) * 5,
        scratch=[pltpu.VMEM((width, late_columns), wide_type)],
        cost=40.0,
    )
    turned_came = moved(turned_sent, "dp", 2 ** turned[0])
    late_came = moved(late_sent, "dp", 2 ** bits[0])
    bit = 1
    size = half
    while 2**bit < parts:
        in_keep, in_sent = run(
            lambda *refs, bit=bit: input_halve_kernel(bit, *refs),
            [low(size // 2 + EXTRA, width)] * 2,
            (facts, in_keep, in_other),
            (SMEM, VMEM, VMEM),
            scratch=[pltpu.VMEM((size + own_rows, width), wide_type)],
            cost=1.1,
            after=(up_pair[1], down_pair[1]),
        )
        in_other = moved(in_sent, "mp", 2**bit)
        size //= 2
        bit += 1
    next(out_steps)
    early_sizes = [[exchange.rows(1)] for exchange in (up_exchange, down_exchange)]
    (up_keep,), (up_came,) = steps(
        (up_pair[0],),
        ((up_pair[1], [up_exchange.rows(0)]),),
        [(up_exchange, 1, [(up_exchange, 0, (1, 0))], (0, 0))],
        [(far[1], early_sizes[0])],
        cost=40.0,
    )
    out_sum, out_other = finish(out_steps)
    encoded, proj_grad = run(
        encoded_kernel,
        [low(rows, columns), wide(width, columns)],
        (facts, hidden, out_sum, out_other, down_bias, proj_near, proj_bias, enc_grad),
        (SMEM,) + (VMEM,) * 7,
        scratch=[pltpu.VMEM((rows, width), low_type)],
        cost=1.0,
    )
    last_keep, last_sent = run(
        lambda *refs: last_kernel(info, last_exchange, heads, pads[0], *refs),
        [low(last_exchange.rows(0), LANES)] * 2,
        (
            facts, encoded, proj_grad, enc_grad, pos_grad_own, mask_grad, bias_grads, bias_grads_other, second_grads,
            qkv_bias_grad, in_keep, in_other,
        ),
        (SMEM,) + (VMEM,) * 11,
        scratch=[pltpu.VMEM((VECTOR_ROWS, LANES), wide_type)],
        cost=0.6,
    )
    last_came = moved(last_sent, "dp", 2 ** bits[0])
    (down_keep,), (down_came,) = steps(
        (down_pair[0],),
        ((down_pair[1], [down_exchange.rows(0)]),),
        [(down_exchange, 1, [(down_exchange, 0, (1, 0))], (0, 0))],
        [(turned[1], early_sizes[1])],
    )
    (input_grad,) = run(
        input_grad_kernel,
        [low(own_rows, width)],
        (facts, patch_rows, in_keep, in_other, own_grad, first_gain),
        (SMEM,) + (VMEM,) * 5,
        final=True,
        cost=0.8,
    )

    early = (up_exchange, down_exchange)
    late = (joint_exchange, turned_exchange)
    joint_sizes = [[exchange.rows(1)] for exchange in late]
    (late_keep, turned_keep), late_came = steps(
        (late_keep, last_keep, turned_keep),
        (
            (late_came, [late_exchange.rows(0)]), (last_came, [last_exchange.rows(0)]),
            (turned_came, [turned_exchange.rows(0)]),
        ),
        [
            (joint_exchange, 1, [(late_exchange, 0, (3, 0)), (last_exchange, 1, (4, 0))], (0, 0)),
            (turned_exchange, 1, [(turned_exchange, 2, (5, 0))], (1, 0)),
        ],
        [(bits[1], joint_sizes[0]), (turned[1], joint_sizes[1])],
    )
    (down_keep,), (down_came,) = steps(
        (down_keep,),
        ((down_came, early_sizes[1]),),
        [(down_exchange, 2, [(down_exchange, 0, (1, 0))], (0, 0))],
        [(turned[2], [down_exchange.rows(2)])],
    )
    (up_keep,), (up_came,) = steps(
        (up_keep,),
        ((up_came, early_sizes[0]),),
        [(up_exchange, 2, [(up_exchange, 0, (1, 0))], (0, 0))],
        [(far[2], [up_exchange.rows(2)])],
    )
    early_came = (up_came, down_came)
    early_sizes = [[exchange.rows(2)] for exchange in early]
    last_sizes = [exchange.rows(2) for exchange in late]
    (late_keep, turned_keep), (late_came,) = steps(
        (late_keep, turned_keep),
        ((late_came[0], joint_sizes[0]), (late_came[1], joint_sizes[1])),
        [
            (joint_exchange, 2, [(joint_exchange, 0, (2, 0))], (0, 0)),
            (turned_exchange, 2, [(turned_exchange, 1, (3, 0))], (0, 1)),
        ],
        [(2, last_sizes)],
    )
    for step in range(3, len(bits)):
        old_sizes, early_sizes = early_sizes, [[exchange.rows(step)] for exchange in early]
        (up_keep, down_keep), early_came = steps(
            (up_keep, down_keep),
            ((early_came[0], old_sizes[0]), (early_came[1], old_sizes[1])),
            [(exchange, step, [(exchange, at, (2 + at, 0))], (at, 0)) for at, exchange in enumerate(early)],
            [(step, early_sizes[0]), (step, early_sizes[1])],
        )
        old_sizes, last_sizes = last_sizes, [exchange.rows(step) for exchange in late]
        (late_keep, turned_keep), (late_came,) = steps(
            (late_keep, turned_keep),
            ((late_came, old_sizes),),
            [(exchange, step, [(exchange, at, (2, at))], (0, at)) for at, exchange in enumerate(late)],
            [(step, last_sizes)],
        )
    up_weight_grad, down_weight_grad = run(
        lambda *refs: early_out_kernel(early, pads[0], *refs),
        [wide(share, units)] * 2,
        (up_keep, down_keep, *early_came),
        final=True,
        cost=1.0,
    )
    (
        grids, out_weight_grad, qkv_weight_grad, proj_weight_grad, pos_grad, query_bias_grad, value_bias_grad,
        up_bias_grad, proj_bias_grad, mask_token_grad, first_gain_grad, first_shift_grad, second_gain_grad,
        second_shift_grad, out_bias_grad, down_bias_grad,
    ) = run(
        lambda *refs: late_out_kernel(info, joint_exchange, turned_exchange, pads[0], middle, last_sizes, *refs),
        [
            low(count, GRID, columns), wide(head_columns, share), wide(share, qkv_columns), wide(share, columns),
            wide(pos_share, columns),
        ]
        + [wide(size) for size in (head_columns, head_columns, units, columns, columns) + (width,) * 6],
        (facts, seen, late_keep, turned_keep, late_came, mask_token, layouts),
        (SMEM,) + (VMEM,) * 6,
        scratch=[pltpu.VMEM((share, late_columns), wide_type), pltpu.VMEM((VECTOR_ROWS, LANES), wide_type)],
        final=True,
        cost=2.5,
    )
    return (
        grids, input_grad, qkv_weight_grad, query_bias_grad, value_bias_grad, out_weight_grad, out_bias_grad,
        first_gain_grad, first_shift_grad, second_gain_grad, second_shift_grad, up_weight_grad, up_bias_grad,
        down_weight_grad.T, down_bias_grad, proj_weight_grad, proj_bias_grad, mask_token_grad, pos_grad,
    )


def solution(mesh):
    return jax.shard_map(
        local,
        mesh=mesh,
        in_specs=(
            P("dp", None), P(), P(), P(), P(None, "mp"), P("mp"), P("mp"), P("mp", None), P(), P(), P(), P(), P(),
            P(None, "mp"), P("mp"), P("mp", None), P(), P(None, "mp"), P("mp"), P("mp"), P(None, "mp"),
            P("dp", None, "mp"),
        ),
        out_specs=(
            P("dp", None, "mp"), P(("dp", "mp"), None), P("dp", "mp"), P("mp"), P("mp"), P("mp", "dp"), P(), P(),
            P(), P(), P(), P("dp", "mp"), P("mp"), P("mp", "dp"), P(), P("dp", "mp"), P("mp"), P("mp"),
            P("dp", "mp"),
        ),
        check_vma=False,
    )
```

```python
import math

import jax
import jax.numpy as jnp
import numpy as np
from jax import lax
from jax.experimental import pallas as pl
from jax.experimental.pallas import tpu as pltpu
from jax.sharding import PartitionSpec as P

HEAD_DIM = 64
GRID = 256
VIS = 64
CHUNK = 512
LANES = 128

epsilon = 1e-06
low_type = jnp.bfloat16
wide_type = jnp.float32
scale_factor = HEAD_DIM ** (-0.5)

VMEM = pl.BlockSpec(memory_space=pltpu.VMEM)
SMEM = pl.BlockSpec(memory_space=pltpu.SMEM)
ANY = pl.BlockSpec(memory_space=pl.ANY)
PINNED_ROWS = 512


def grid_tables():
    grid_edge = math.isqrt(GRID)
    tables = []
    for side_cells in (10, 14):
        places = np.arange(side_cells)
        centers = ((2 * places + 1) * grid_edge - side_cells) / (2 * side_cells)
        lower = np.floor(centers).astype(np.int64)
        share = centers - lower
        lerp = np.zeros((side_cells, grid_edge))
        lerp[places, np.clip(lower, 0, grid_edge - 1)] += 1.0 - share
        lerp[places, np.clip(lower + 1, 0, grid_edge - 1)] += share
        table = np.zeros((GRID, GRID))
        table[: side_cells * side_cells] = np.kron(lerp, lerp)
        tables.append(table)
    return np.stack(tables).astype(np.float32)


def split_low(value):
    high = value.astype(low_type)
    return high, (value - high.astype(wide_type)).astype(low_type)


def dot(left, right):
    return lax.dot_general(left, right, (((1,), (0,)), ((), ())), preferred_element_type=wide_type)


def dot_right_t(left, right):
    return lax.dot_general(left, right, (((1,), (1,)), ((), ())), preferred_element_type=wide_type)


def dot_left_t(left, right):
    return lax.dot_general(left, right, (((0,), (0,)), ((), ())), preferred_element_type=wide_type)


def normalized(value):
    center = value - jnp.mean(value, axis=-1, keepdims=True)
    spread = lax.rsqrt(jnp.mean(center * center, axis=-1, keepdims=True) + epsilon)
    return center * spread, spread


def norm_back(grad, normed, spread, gain):
    scaled = grad * gain
    mean_one = jnp.mean(scaled, axis=-1, keepdims=True)
    mean_two = jnp.mean(scaled * normed, axis=-1, keepdims=True)
    return spread * (scaled - mean_one - normed * mean_two)


def row_sum(value):
    return jnp.sum(value, axis=0, keepdims=True)


def over_rows(total, size, body):
    size = min(size, total)
    if total <= 2 * size:
        for start in range(0, total, size):
            body(start, size)
        return

    def step(i, carry):
        body(pl.multiple_of(i * size, size), size)
        return carry

    lax.fori_loop(0, total // size, step, 0)


def size_of(shape, kind):
    return math.prod(shape) * jnp.dtype(kind).itemsize


RATE = 10**9
COST_SHARE = 1.0
COVER = 40.0
BYTES = 0


class Order:
    def __init__(self, pinned):
        self.pinned = pinned
        self.last = None
        self.near = []
        self.far = []
        self.share = COST_SHARE

    def keep(self, value):
        if self.pinned:
            self.near.append((value, pltpu.VMEM))
        return value

    def leave(self, *values):
        self.far += values

    def placed(self, value):
        for near, space in self.near:
            if value is near:
                return pltpu.with_memory_space_constraint(value, space)
        if any(value is far for far in self.far):
            return pltpu.with_memory_space_constraint(value, pltpu.HBM)
        return value

    def __call__(
        self, kernel, outs, args, specs=None, scratch=(), out_specs=None, final=False, stage=(), cost=1.0, after=()
    ):
        args = tuple(args)
        specs = [VMEM] * len(args) if specs is None else list(specs)
        out_specs = [VMEM] * len(outs) if out_specs is None else list(out_specs)
        count, results_count = len(args), len(outs)
        staged = list(stage) if self.pinned else []
        self.leave(*staged)
        needed = sum(size_of(ref.shape, ref.dtype) for ref in scratch)
        needed += sum(
            size_of(arg.shape, arg.dtype) for arg in args if not any(arg is near for near, _ in self.near)
        )
        shapes = []
        for (shape, kind), spec in zip(outs, out_specs):
            if self.pinned and not final:
                shapes.append((pltpu.SMEM if spec is SMEM else pltpu.VMEM)(shape, kind))
            else:
                shapes.append(jax.ShapeDtypeStruct(shape, kind))
                needed += size_of(shape, kind)
        tail = len(staged)
        args += tuple(staged)
        specs += [ANY] * tail
        unread = tuple(after) if self.last is None else (*after, self.last)
        skipped = len(unread)
        args += unread
        specs += [ANY] * skipped

        def body(*refs):
            own, sources, refs = refs[:count], refs[count : count + tail], refs[count + tail + skipped :]
            results, targets, refs = (
                refs[:results_count], refs[results_count : results_count + tail], refs[results_count + tail :]
            )
            copies = []
            if tail:
                *refs, sems = refs
                copies = [
                    pltpu.make_async_copy(source, target, sems.at[at])
                    for at, (source, target) in enumerate(zip(sources, targets))
                ]
            for copy in copies:
                copy.start()
            kernel(*own, *results, *refs)
            for copy in copies:
                copy.wait()

        results = pl.pallas_call(
            body,
            out_shape=tuple(shapes) + tuple(pltpu.VMEM(array.shape, array.dtype) for array in staged),
            in_specs=specs,
            out_specs=tuple(out_specs) + (VMEM,) * tail,
            scratch_shapes=list(scratch) + ([pltpu.SemaphoreType.DMA((tail,))] if tail else []),
            compiler_params=pltpu.CompilerParams(
                vmem_limit_bytes=min(needed + needed // 4 + 10 * 2**20, 60 * 2**20)
            ),
            cost_estimate=pl.CostEstimate(
                flops=int(cost * RATE * self.share), bytes_accessed=int(cost * BYTES), transcendentals=0
            ),
        )(*(self.placed(arg) for arg in args))
        if self.pinned and not final:
            for result, spec in zip(results, out_specs + [VMEM] * tail):
                self.near.append((result, pltpu.SMEM if spec is SMEM else pltpu.VMEM))
        if not final:
            self.last = results[0]
        if stage and not self.pinned:
            return (*results, *stage)
        return results


class Info:
    def __init__(self, count):
        self.count = count
        self.size = 2 + 5 * count

    def dp(self, ref):
        return ref[0]

    def mp(self, ref):
        return ref[1]

    def owner(self, ref, image):
        return ref[2 + image]

    def live(self, ref, image):
        return ref[2 + self.count + image]

    def source(self, ref, slot):
        return ref[2 + 2 * self.count + slot]

    def cells(self, ref, slot):
        return ref[2 + 3 * self.count + slot]

    def image(self, ref, owner):
        return ref[2 + 4 * self.count + owner]


def fill_info(count, where_ref, owner_ref, patches_ref, info_ref):
    me = where_ref[0]
    info_ref[0] = me
    info_ref[1] = where_ref[1]

    def one(at):
        own = me * count + at
        info_ref[2 + at] = owner_ref[own]
        info_ref[2 + 4 * count + owner_ref[own]] = at
        info_ref[2 + count + at] = patches_ref[own] // 4

        def find(i, found):
            return jnp.where(owner_ref[at * count + i] == me, at * count + i, found)

        source = lax.fori_loop(0, count, find, at * count, unroll=count <= 8)
        info_ref[2 + 2 * count + at] = source
        info_ref[2 + 3 * count + at] = patches_ref[source]

    over_slots(count, one)


def over_slots(count, one_slot):
    if count <= 8:
        for slot in range(count):
            one_slot(slot)
    else:
        lax.fori_loop(0, count, lambda slot, carry: (one_slot(slot), carry)[1], 0)


def side_of(size):
    return (size >= 196).astype(jnp.int32) + (size >= 256).astype(jnp.int32)


def block_at(rest, place, bit):
    low = rest & ((1 << place) - 1)
    return ((rest - low) << 1) + (bit << place) + low


class Exchange:
    def __init__(self, count, bits, block, moved=0, shared=0):
        self.count, self.bits, self.block, self.moved, self.shared = count, bits, block, moved, shared

    def blocks(self, step):
        return self.count >> (step + 1)

    def place(self, step):
        bit = self.bits[step]
        return bit - sum(done < bit for done in self.bits[:step])

    def moved_at(self, step):
        return self.blocks(step) * self.block

    def shared_at(self, step):
        return self.moved_at(step) + self.count // 2 * self.moved

    def rows(self, step):
        return self.shared_at(step) + self.shared

    def own_bit(self, step, info_ref):
        return (info_ref[0] >> self.bits[step]) & 1

    def targets(self, step, info_ref, keep_ref, sent_ref):
        own = self.own_bit(step, info_ref)
        place = self.place(step)
        for ref, which in ((sent_ref, 1 - own), (keep_ref, own)):
            yield ref, [block_at(block, place, which) for block in range(self.blocks(step))]

    def kernel(self, step, parts, info_ref, *refs):
        *from_refs, next_keep_ref, next_sent_ref = refs
        pairs = list(zip(parts, from_refs[::2], from_refs[1::2]))
        sources = 1 << (step - 1)
        rests = self.blocks(step - 1)
        for ref, indices in self.targets(step, info_ref, next_keep_ref, next_sent_ref):
            first, moved_at, shared_at = 0, self.moved_at(step), self.shared_at(step)
            for part, keep_ref, other_ref in pairs:
                for block, index in enumerate(indices if part.block else ()):
                    rows = pl.ds(pl.multiple_of(index * part.block, 16), part.block)
                    at = block * self.block + first
                    ref[at : at + part.block, :] = (
                        keep_ref[rows, :].astype(wide_type) + other_ref[rows, :].astype(wide_type)
                    ).astype(low_type)
                first += part.block
                for from_ref in (keep_ref, other_ref) if part.moved else ():
                    for source in range(sources):
                        for index in indices:
                            rows = part.moved_at(step - 1) + (source * rests + index) * part.moved
                            ref[moved_at : moved_at + part.moved, :] = from_ref[
                                pl.ds(pl.multiple_of(rows, 16), part.moved), :
                            ]
                            moved_at += part.moved
                if part.shared:
                    at = part.shared_at(step - 1)
                    rows = slice(at, at + part.shared)
                    ref[shared_at : shared_at + part.shared, :] = (
                        keep_ref[rows, :].astype(wide_type) + other_ref[rows, :].astype(wide_type)
                    ).astype(low_type)

    def arrived(self, keep_ref, other_ref):
        last = len(self.bits) - 1
        sources = 1 << last
        for half, ref in enumerate((keep_ref, other_ref)):
            for source in range(sources):
                relative = 0
                for step, bit in enumerate(self.bits):
                    relative |= (((source + half * sources) >> step) & 1) << bit
                yield relative, ref, self.moved_at(last) + source * self.moved

    def total(self, keep_ref, other_ref, start, size):
        rows = slice(start, start + size)
        return keep_ref[rows, :].astype(wide_type) + other_ref[rows, :].astype(wide_type)

    def shared_total(self, keep_ref, other_ref):
        return self.total(keep_ref, other_ref, self.shared_at(len(self.bits) - 1), self.shared)


def cotangent_kernel(
    info, exchange, where_ref, owner_ref, patches_ref, visible_ref, cot_ref, keep_ref, sent_ref, info_ref, seen_ref,
    turned_ref,
):
    count = info.count
    fill_info(count, where_ref, owner_ref, patches_ref, info_ref)

    def take(slot):
        seen_ref[pl.ds(slot, 1), :] = visible_ref[pl.ds(info.source(info_ref, slot), 1), :]

    over_slots(count, take)
    turned_ref[...] = seen_ref[...].astype(wide_type).T
    cells = lax.broadcasted_iota(jnp.int32, (VIS, GRID), 1).astype(wide_type)
    own = exchange.own_bit(0, info_ref)
    place = exchange.place(0)
    for slot in range(count):
        onehot = (turned_ref[:, slot : slot + 1] == cells).astype(wide_type).astype(low_type)
        rows = dot(onehot, cot_ref[slot]).astype(low_type)
        rest = (slot & ((1 << place) - 1)) | ((slot >> (place + 1)) << place)
        kept = ((slot >> place) & 1) == own

        @pl.when(kept)
        def _(rest=rest, rows=rows):
            keep_ref[rest * VIS : (rest + 1) * VIS, :] = rows

        @pl.when(jnp.logical_not(kept))
        def _(rest=rest, rows=rows):
            sent_ref[rest * VIS : (rest + 1) * VIS, :] = rows


def position_kernel(
    info, info_ref, visible_ref, cot_ref, turned_high_ref, turned_low_ref, table_high_ref, table_low_ref, pos_ref,
    grad_ref, mask_ref, layout_ref, sums_ref,
):
    cells = lax.broadcasted_iota(jnp.int32, (GRID, VIS), 0)
    cell_column = lax.broadcasted_iota(jnp.int32, (GRID, 1), 0)
    sums_ref[...] = jnp.zeros_like(sums_ref)
    mask_ref[...] = jnp.zeros_like(mask_ref)

    def one_slot(slot):
        size = info.cells(info_ref, slot)
        seen = visible_ref[pl.ds(slot, 1), :] == cells
        fill = (cell_column < size).astype(wide_type) - jnp.sum(
            seen.astype(wide_type), axis=1, keepdims=True
        )
        wide = cot_ref[slot].astype(wide_type)
        mask_ref[...] += row_sum(fill * wide)
        sums_ref[side_of(size)] += wide

    over_slots(info.count, one_slot)
    total = sums_ref[2]
    for side in range(2):
        high, low = split_low(sums_ref[side])
        total += (
            dot(turned_high_ref[side], high) + dot(turned_high_ref[side], low) + dot(turned_low_ref[side], high)
        )
    grad_ref[...] = total
    table = pos_ref[...]
    for side in range(2):
        layout_ref[side] = dot(table_high_ref[side], table) + dot(table_low_ref[side], table)
    layout_ref[2] = table.astype(wide_type)


def wide_row(ref):
    return ref[...].astype(wide_type).reshape(1, ref.shape[0])


def enter_kernel(
    rows_ref, gain_ref, shift_ref, weight_ref, query_ref, value_ref, act_ref, qkv_ref
):
    gain, shift = wide_row(gain_ref), wide_row(shift_ref)
    query, value = wide_row(query_ref), wide_row(value_ref)
    nothing = jnp.zeros((1, HEAD_DIM), wide_type)
    pieces = []
    for start in range(0, query.shape[1], HEAD_DIM):
        pieces += [query[:, start : start + HEAD_DIM], nothing, value[:, start : start + HEAD_DIM]]
    bias = jnp.concatenate(pieces, axis=1)

    def body(start, size):
        rows = pl.ds(start, size)
        normed, _ = normalized(rows_ref[rows, :].astype(wide_type))
        act = (normed * gain + shift).astype(low_type)
        act_ref[rows, :] = act
        qkv_ref[rows, :] = (dot_right_t(act, weight_ref[...]) + bias).astype(low_type)

    over_rows(rows_ref.shape[0], CHUNK, body)


BLOCK = 4 * VIS


def attention_kernel(info, heads, first, info_ref, qkv_ref, packed_ref, prob_ref, attended_ref):
    key_image = lax.broadcasted_iota(jnp.int32, (BLOCK, BLOCK), 0) // VIS
    key_slot = lax.broadcasted_iota(jnp.int32, (BLOCK, BLOCK), 0) % VIS
    own_image = key_image == lax.broadcasted_iota(jnp.int32, (BLOCK, BLOCK), 1) // VIS
    columns = heads * HEAD_DIM
    full = columns // LANES * LANES
    rest = BLOCK * (columns - full) // LANES

    def body(start, size):
        rows = pl.ds(start, size)
        from_rows = pl.ds(first + start, size)
        limit = jnp.zeros((size, size), jnp.int32)
        for image in range(size // VIS):
            limit = jnp.where(key_image == image, info.live(info_ref, (first + start) // VIS + image), limit)
        live = jnp.logical_and(own_image, key_slot < limit)
        for head in range(heads):
            base = head * 3 * HEAD_DIM
            queries = qkv_ref[from_rows, base : base + HEAD_DIM]
            key_rows = qkv_ref[from_rows, base + HEAD_DIM : base + 2 * HEAD_DIM]
            value_rows = qkv_ref[from_rows, base + 2 * HEAD_DIM : base + 3 * HEAD_DIM]
            scores = jnp.where(live, dot_right_t(key_rows, queries) * scale_factor, -1e30)
            raised = jnp.exp(scores - jnp.max(scores, axis=0, keepdims=True))
            probs = (raised / jnp.sum(raised, axis=0, keepdims=True)).astype(low_type)
            prob_ref[rows, head * BLOCK : (head + 1) * BLOCK] = probs
            attended_ref[rows, head * HEAD_DIM : (head + 1) * HEAD_DIM] = dot_left_t(
                probs, value_rows
            ).astype(low_type)
        at = start // BLOCK * (full // LANES * BLOCK + rest)
        for tile in range(full // LANES):
            packed_ref[pl.ds(at, BLOCK), :] = attended_ref[rows, tile * LANES : (tile + 1) * LANES]
            at += BLOCK
        pieces = [
            attended_ref[pl.ds(start + piece * rest, rest), full:].astype(wide_type)
            for piece in range(BLOCK // rest)
        ]
        packed_ref[pl.ds(at, rest), :] = jnp.concatenate(pieces, axis=1).astype(low_type)

    over_rows(prob_ref.shape[0], BLOCK, body)


def unpack(own, packed_refs, start, columns, out_ref):
    full = columns // LANES * LANES
    width = columns - full
    rest = BLOCK * width // LANES
    at = start // BLOCK * (full // LANES * BLOCK + rest)
    count = len(packed_refs)
    for tile in range(full // LANES):
        for relative, ref in enumerate(packed_refs):
            lane = (tile * count + (own ^ relative)) * LANES
            out_ref[:, pl.ds(pl.multiple_of(lane, LANES), LANES)] = ref[pl.ds(at, BLOCK), :]
        at += BLOCK
    lane = full * count
    for other in range(0, count, LANES // width):
        pieces = []
        for part in range(other, other + LANES // width):
            rows = None
            for relative, ref in enumerate(packed_refs):
                here = ref[pl.ds(at, rest), :].astype(wide_type)
                rows = here if rows is None else jnp.where((own ^ relative) == part, here, rows)
            pieces.append(
                jnp.concatenate(
                    [rows[:, piece * width : (piece + 1) * width] for piece in range(BLOCK // rest)], axis=0
                )
            )
        out_ref[:, lane : lane + LANES] = jnp.concatenate(pieces, axis=1).astype(low_type)
        lane += LANES


def weights_kernel(parts, info_ref, *refs):
    out_refs, proj_refs, (out_ref, proj_ref) = refs[:parts], refs[parts : 2 * parts], refs[2 * parts :]
    own = info_ref[1]
    columns = out_refs[0].shape[0]
    full = columns // LANES * LANES
    width = columns - full
    for relative, (out_part_ref, proj_part_ref) in enumerate(zip(out_refs, proj_refs)):
        part = own ^ relative
        for tile in range(full // LANES):
            at = pl.multiple_of((tile * parts + part) * LANES, LANES)
            out_ref[pl.ds(at, LANES), :] = out_part_ref[tile * LANES : (tile + 1) * LANES, :]
        at = pl.multiple_of(full * parts + part * width, 16)
        out_ref[pl.ds(at, width), :] = out_part_ref[full:, :]
        size = proj_part_ref.shape[1]
        proj_ref[:, pl.ds(pl.multiple_of(part * size, LANES), size)] = proj_part_ref[...]


def halves(upper, left_ref, weight_ref, keep_ref, sent_ref, product):
    half = keep_ref.shape[0]
    for out_ref, which in ((sent_ref, 1 - upper), (keep_ref, upper)):

        def body(start, size, out_ref=out_ref, which=which):
            rows = pl.ds(pl.multiple_of(which * half + start, size), size)
            out_ref[pl.ds(start, size), :] = product(left_ref[rows, :], weight_ref[...]).astype(
                out_ref.dtype
            )

        over_rows(half, CHUNK, body)


def both_halves(upper, half, body):
    for source, which in enumerate((upper, 1 - upper)):

        def one(start, size, source=source, which=which):
            body(source, pl.ds(pl.multiple_of(which * half + start, size), size), pl.ds(start, size), size)

        over_rows(half, 256, one)


def back_kernel(info, exchange, info_ref, back_ref, back_other_ref, enc_ref):
    for relative, ref, start in exchange.arrived(back_ref, back_other_ref):
        image = info.image(info_ref, info_ref[0] ^ relative)
        enc_ref[pl.ds(pl.multiple_of(image * VIS, VIS), VIS), :] = ref[start : start + VIS, :]


def add_kernel(left_ref, right_ref, out_ref):
    out_ref[...] = (left_ref[...].astype(wide_type) + right_ref[...].astype(wide_type)).astype(low_type)


def forward_kernel(
    parts, columns, info_ref, rows_ref, out_bias_ref, gain_ref, shift_ref, up_ref, up_bias_ref, weight_ref, *refs
):
    attended_refs = (refs[:parts], refs[parts : 2 * parts])
    hidden_ref, act_ref, acted_ref, slope_ref, all_ref = refs[2 * parts :]
    half = rows_ref.shape[0] // 2
    out_bias, gain, shift, up_bias = (
        wide_row(ref) for ref in (out_bias_ref, gain_ref, shift_ref, up_bias_ref)
    )

    def body(which, start, size):
        rows = pl.ds(which * half + start, size)
        unpack(info_ref[1], attended_refs[which], start, columns, all_ref)
        total = dot(all_ref[...], weight_ref[...])
        hidden = rows_ref[rows, :].astype(wide_type) + total + out_bias
        hidden_ref[rows, :] = hidden
        normed, _ = normalized(hidden)
        act = (normed * gain + shift).astype(low_type)
        act_ref[rows, :] = act
        up_pre = dot(act, up_ref[...]) + up_bias
        cdf = 0.5 + 0.5 * lax.erf(up_pre * math.sqrt(0.5))
        acted_ref[rows, :] = (up_pre * cdf).astype(low_type)
        slope_ref[rows, :] = cdf + up_pre * jnp.exp(-0.5 * up_pre * up_pre) * (
            1.0 / math.sqrt(2.0 * math.pi)
        )

    for which in range(2):
        over_rows(half, BLOCK, lambda start, size, which=which: body(which, start, size))


def forward_part_kernel(info_ref, acted_ref, down_ref, keep_ref, sent_ref):
    halves(info_ref[1] & 1, acted_ref, down_ref, keep_ref, sent_ref, dot)


def forward_grad_kernel(
    parts, own, info_ref, slope_ref, up_ref, down_ref, weight_ref, *refs
):
    enc_refs = refs[:parts]
    part_ref, up_low_ref, down_low_ref, bias_ref, all_ref = refs[parts:]
    upper = info_ref[1] & 1
    half = part_ref.shape[0]
    first = (upper if own else 1 - upper) * half
    bias_ref[...] = jnp.zeros_like(bias_ref)

    def body(start, size):
        from_rows = pl.ds(pl.multiple_of(first + start, size), size)
        rows = pl.ds(start, size)
        for relative, enc_ref in enumerate(enc_refs):
            columns = enc_ref.shape[1]
            lane = pl.multiple_of((info_ref[1] ^ relative) * columns, LANES)
            all_ref[:, pl.ds(lane, columns)] = enc_ref[from_rows, :]
        out_grad = dot_right_t(all_ref[...], weight_ref[...])
        down_low = out_grad.astype(low_type)
        down_low_ref[rows, :] = down_low
        up_low = dot_right_t(down_low, down_ref[...]) * slope_ref[from_rows, :]
        up_low_ref[rows, :] = up_low.astype(low_type)
        bias_ref[0:1, :] += row_sum(out_grad)
        bias_ref[1:2, :] += row_sum(up_low_ref[rows, :].astype(wide_type))
        part_ref[rows, :] = dot_right_t(up_low_ref[rows, :], up_ref[...]).astype(low_type)

    over_rows(half, BLOCK, body)


def put_blocks(exchange, info_ref, keep_ref, sent_ref, wide_ref, pad, first=0):
    share = wide_ref.shape[0] // exchange.count
    for ref, indices in exchange.targets(0, info_ref, keep_ref, sent_ref):
        for block, index in enumerate(indices):
            rows = pl.ds(pl.multiple_of(index * share, 8), share)
            for tile in range(wide_ref.shape[1] // LANES):
                at = block * exchange.block + first + tile * pad
                ref[at : at + share, :] = wide_ref[rows, tile * LANES : (tile + 1) * LANES].astype(low_type)


def halves_of(info_ref, refs):
    if len(refs) == 2:
        return refs[0][...], refs[1][...]
    half = refs[0].shape[0] // 2
    upper = info_ref[1] & 1
    return tuple(
        refs[0][pl.ds(pl.multiple_of(which * half, half), half), :] for which in (upper, 1 - upper)
    )


def early_grads_kernel(
    exchanges, pad, info_ref, low_ref, low_other_ref, acted_ref, act_ref, up_ref, up_other_ref, down_keep_ref,
    down_sent_ref, up_keep_ref, up_sent_ref, wide_ref,
):
    left, right = halves_of(info_ref, (low_ref, low_other_ref)), halves_of(info_ref, (acted_ref,))
    wide_ref[...] = dot_left_t(left[0], right[0]) + dot_left_t(left[1], right[1])
    put_blocks(exchanges[0], info_ref, down_keep_ref, down_sent_ref, wide_ref, pad)
    left, right = halves_of(info_ref, (act_ref,)), halves_of(info_ref, (up_ref, up_other_ref))
    wide_ref[...] = dot_left_t(left[0], right[0]) + dot_left_t(left[1], right[1])
    put_blocks(exchanges[1], info_ref, up_keep_ref, up_sent_ref, wide_ref, pad)


def attention_back_kernel(
    heads, own, info_ref, sum_ref, hidden_ref, low_ref, gain_ref, weight_ref, qkv_ref, prob_ref, prob_last_ref,
    grads_ref, attn_low_ref, grad_ref, bias_ref, probs_ref,
):
    gain = wide_row(gain_ref)
    bias_ref[...] = jnp.zeros_like(bias_ref)
    half = sum_ref.shape[0]
    upper = info_ref[1] & 1
    which = upper if own else 1 - upper

    @pl.when(which == 0)
    def _():
        probs_ref[...] = prob_ref[...]

    @pl.when(which == 1)
    def _():
        probs_ref[...] = prob_last_ref[...]

    def body(start, size):
        part = pl.ds(start, size)
        rows = pl.ds(pl.multiple_of(which * half + start, size), size)
        normed, spread = normalized(hidden_ref[rows, :])
        grad = sum_ref[part, :].astype(wide_type)
        bias_ref[0:1, :] += row_sum(grad * normed)
        bias_ref[1:2, :] += row_sum(grad)
        hidden_grad = low_ref[part, :].astype(wide_type) + norm_back(grad, normed, spread, gain)
        grad_ref[part, :] = hidden_grad
        bias_ref[2:3, :] += row_sum(hidden_grad)
        attn_low = hidden_grad.astype(low_type)
        attn_low_ref[part, :] = attn_low
        attended_grad = dot_right_t(attn_low, weight_ref[...]).astype(low_type)
        for head in range(heads):
            base = head * 3 * HEAD_DIM
            queries = qkv_ref[rows, base : base + HEAD_DIM]
            key_rows = qkv_ref[rows, base + HEAD_DIM : base + 2 * HEAD_DIM]
            value_rows = qkv_ref[rows, base + 2 * HEAD_DIM : base + 3 * HEAD_DIM]
            probs = probs_ref[part, head * BLOCK : (head + 1) * BLOCK]
            grad_rows = attended_grad[:, head * HEAD_DIM : (head + 1) * HEAD_DIM]
            value_low = dot(probs, grad_rows).astype(low_type)
            prob_grad = dot_right_t(value_rows, grad_rows)
            wide_probs = probs.astype(wide_type)
            weighted = wide_probs * prob_grad
            score_low = (
                weighted - wide_probs * jnp.sum(weighted, axis=0, keepdims=True)
            ).astype(low_type)
            query_low = (dot_left_t(score_low, key_rows) * scale_factor).astype(low_type)
            key_low = (dot(score_low, queries) * scale_factor).astype(low_type)
            grads_ref[part, base : base + HEAD_DIM] = query_low
            grads_ref[part, base + HEAD_DIM : base + 2 * HEAD_DIM] = key_low
            grads_ref[part, base + 2 * HEAD_DIM : base + 3 * HEAD_DIM] = value_low

    over_rows(half, BLOCK, body)


def views(ref, sizes):
    starts = [sum(sizes[:at]) for at in range(len(sizes))]
    return [ref.at[pl.ds(start, size), :] for start, size in zip(starts, sizes)]


def step_kernel(moves, sizes, info_ref, *refs):
    parted = [None if size is None else views(ref, size) for ref, size in zip(refs, sizes)]
    for exchange, step, sources, kept, (sent, place) in moves:
        pairs = []
        for _, keep, (came, at) in sources:
            pairs += [refs[keep], parted[came][at]]
        exchange.kernel(step, [part for part, _, _ in sources], info_ref, *pairs, refs[kept], parted[sent][place])


def late_grads_kernel(
    exchanges, pad, middle, info_ref, act_ref, grads_ref, grads_other_ref, low_ref, low_other_ref, first_ref, last_ref,
    keep_ref, sent_ref, turned_keep_ref, turned_sent_ref, bias_ref, wide_ref,
):
    columns = grads_ref.shape[1]
    first = first_ref.shape[1]
    lower = (info_ref[1] & 1) == 0
    attended = (first_ref[...].astype(wide_type), last_ref[...].astype(wide_type))
    attended_own = jnp.where(lower, attended[0], attended[1]).astype(low_type)
    attended_other = jnp.where(lower, attended[1], attended[0]).astype(low_type)
    act_own, act_other = halves_of(info_ref, (act_ref,))
    wide_ref[:, :first] = dot_left_t(low_ref[...], attended_own) + dot_left_t(
        low_other_ref[...], attended_other
    )
    wide_ref[:, first : first + columns] = dot_left_t(act_own, grads_ref[...]) + dot_left_t(
        act_other, grads_other_ref[...]
    )
    put_blocks(exchanges[0], info_ref, keep_ref, sent_ref, wide_ref.at[:, pl.ds(0, middle)], pad)
    put_blocks(
        exchanges[1], info_ref, turned_keep_ref, turned_sent_ref,
        wide_ref.at[:, pl.ds(middle, wide_ref.shape[1] - middle)], pad,
    )
    bias_ref[...] = row_sum(grads_ref[...].astype(wide_type)) + row_sum(grads_other_ref[...].astype(wide_type))


EXTRA = 16


def put_extra(ref, start, gain, shift):
    rows = []
    for value in (gain, shift):
        rows += list(split_low(value))
    rows.append(jnp.zeros((EXTRA - 4, gain.shape[1]), low_type))
    ref[start : start + EXTRA, :] = jnp.concatenate(rows, axis=0)


def get_extra(ref, start):
    rows = ref[start : start + EXTRA, :].astype(wide_type)
    return rows[0:1] + rows[1:2], rows[2:3] + rows[3:4]


def norm_kernel(rows_ref, normed_ref):
    def body(start, size):
        rows = pl.ds(start, size)
        normed_ref[rows, :] = normalized(rows_ref[rows, :].astype(wide_type))[0].astype(low_type)

    over_rows(rows_ref.shape[0], CHUNK, body)


def input_part_kernel(
    info_ref, normed_ref, grads_ref, grads_other_ref, weight_ref, keep_ref, sent_ref, part_ref, bias_ref
):
    lower_bit = info_ref[1] & 1
    bias_ref[...] = jnp.zeros_like(bias_ref)

    def body(source, rows, part, size):
        grad = dot((grads_ref, grads_other_ref)[source][part, :], weight_ref[...])
        part_ref[rows, :] = grad
        bias_ref[0:1, :] += row_sum(grad * normed_ref[rows, :].astype(wide_type))
        bias_ref[1:2, :] += row_sum(grad)

    both_halves(lower_bit, grads_ref.shape[0], body)
    size = keep_ref.shape[0] - EXTRA
    share = size // (lax.axis_size("mp") // 2)
    for out_ref, which in ((sent_ref, 1 - lower_bit), (keep_ref, lower_bit)):
        for block in range(size // share):
            rows = pl.ds(pl.multiple_of((2 * block + which) * share, share), share)
            out_ref[block * share : (block + 1) * share, :] = part_ref[rows, :].astype(low_type)
        put_extra(out_ref, size, bias_ref[0:1, :], bias_ref[1:2, :])


def input_halve_kernel(bit, info_ref, keep_ref, other_ref, next_keep_ref, next_sent_ref, total_ref):
    upper = (info_ref[1] >> bit) & 1
    half = next_keep_ref.shape[0] - EXTRA
    size = 2 * half
    share = total_ref.shape[0] - size
    total_ref[:size, :] = keep_ref[:size, :].astype(wide_type) + other_ref[:size, :].astype(wide_type)
    own, other = get_extra(keep_ref, size), get_extra(other_ref, size)
    for out_ref, which in ((next_sent_ref, 1 - upper), (next_keep_ref, upper)):
        for block in range(half // share):
            rows = pl.ds(pl.multiple_of((2 * block + which) * share, share), share)
            out_ref[block * share : (block + 1) * share, :] = total_ref[rows, :].astype(low_type)
        put_extra(out_ref, half, own[0] + other[0], own[1] + other[1])


def input_grad_kernel(info_ref, rows_ref, keep_ref, other_ref, grad_ref, grad_other_ref, gain_ref, out_ref):
    share = out_ref.shape[0]
    half = grad_ref.shape[0]
    start = info_ref[1] * share
    rows = pl.ds(pl.multiple_of(start, share), share)
    part = pl.ds(pl.multiple_of(start % half, share), share)
    own = start // half == (info_ref[1] & 1)
    normed, spread = normalized(rows_ref[rows, :].astype(wide_type))
    grad = keep_ref[:share, :].astype(wide_type) + other_ref[:share, :].astype(wide_type)
    hidden_grad = jnp.where(own, grad_ref[part, :], grad_other_ref[part, :])
    out_ref[...] = (hidden_grad + norm_back(grad, normed, spread, wide_row(gain_ref))).astype(low_type)


VECTOR_ROWS = 48


def put_rows(values, rows_ref):
    row = 0
    for value in values:
        for tile in range(value.shape[1] // LANES):
            rows_ref[row : row + 1, :] = value[:, tile * LANES : (tile + 1) * LANES]
            row += 1


def take_rows(rows_ref, refs):
    row = 0
    for ref in refs:
        size = ref.shape[0]
        for tile in range(-(-size // LANES)):
            width = min(LANES, size - tile * LANES)
            ref[tile * LANES : tile * LANES + width] = rows_ref[row, :width]
            row += 1


def encoded_kernel(
    info_ref, hidden_ref, sum_ref, sum_other_ref, down_bias_ref, weight_ref, bias_ref, enc_ref, encoded_ref, wide_ref,
    low_ref,
):
    down_bias, bias = wide_row(down_bias_ref), wide_row(bias_ref)

    def body(source, rows, part, size):
        total = (sum_ref, sum_other_ref)[source][part, :].astype(wide_type)
        out_low = (hidden_ref[rows, :] + total + down_bias).astype(low_type)
        low_ref[rows, :] = out_low
        encoded_ref[rows, :] = (dot(out_low, weight_ref[...]) + bias).astype(low_type)

    both_halves(info_ref[1] & 1, sum_ref.shape[0], body)
    wide_ref[...] = dot_left_t(low_ref[...], enc_ref[...])


def last_kernel(
    info, exchange, heads, pad, info_ref, encoded_ref, wide_ref, enc_ref, pos_ref, mask_ref, grads_ref, grads_other_ref,
    second_ref, second_other_ref, qkv_ref, first_ref, first_other_ref, keep_ref, sent_ref, rows_ref,
):
    put_blocks(exchange, info_ref, keep_ref, sent_ref, wide_ref, 0)
    put_blocks(exchange, info_ref, keep_ref, sent_ref, pos_ref, 0, pad)
    for ref, indices in exchange.targets(0, info_ref, keep_ref, sent_ref):
        at = exchange.moved_at(0)
        for index in indices:
            image = info.image(info_ref, index)
            ref[at : at + VIS, :] = encoded_ref[pl.ds(pl.multiple_of(image * VIS, VIS), VIS), :]
            at += VIS
    qkv, early = qkv_ref[...], grads_ref[...] + grads_other_ref[...]
    second = second_ref[...] + second_other_ref[...]
    empty = jnp.zeros((1, 2 * LANES - heads * HEAD_DIM), wide_type)
    spread = []
    for part in (0, 2):
        spread += [
            qkv[:, (3 * head + part) * HEAD_DIM : (3 * head + part + 1) * HEAD_DIM] for head in range(heads)
        ] + [empty]
    own = get_extra(first_ref, first_ref.shape[0] - EXTRA)
    other = get_extra(first_other_ref, first_ref.shape[0] - EXTRA)
    put_rows(
        (
            jnp.concatenate(spread, axis=1), early[1:2], row_sum(enc_ref[...].astype(wide_type)), mask_ref[...],
            own[0] + other[0], own[1] + other[1], second[0:1], second[1:2], second[2:3],
            early[0:1],
        ),
        rows_ref,
    )
    for ref in (keep_ref, sent_ref):
        ref[exchange.shared_at(0) :, :] = rows_ref[...].astype(low_type)


def late_out_kernel(
    info, exchange, turned_exchange, pad, middle, sizes, info_ref, seen_ref, keep_ref, turned_ref, came_ref, mask_ref,
    layout_ref, grids_ref, out_ref, qkv_ref, proj_ref, pos_ref, *refs
):
    *vector_refs, wide_ref, rows_ref = refs
    other_ref, turned_other_ref = views(came_ref, sizes)
    cells = lax.broadcasted_iota(jnp.int32, (GRID, VIS), 0)
    cell_column = lax.broadcasted_iota(jnp.int32, (GRID, 1), 0)
    mask_row = wide_row(mask_ref)
    for relative, ref, start in exchange.arrived(keep_ref, other_ref):
        slot = info_ref[0] ^ relative
        seen = seen_ref[pl.ds(slot, 1), :] == cells
        size = info.cells(info_ref, slot)
        fill = (cell_column < size).astype(wide_type) - jnp.sum(
            seen.astype(wide_type), axis=1, keepdims=True
        )
        placed = dot(seen.astype(low_type), ref[start : start + VIS, :])
        grids_ref[slot] = (placed + fill * mask_row + layout_ref[side_of(size)]).astype(low_type)
    share = proj_ref.shape[0]
    tiles = wide_ref.shape[1] // LANES
    for tile in range(tiles):
        here = (exchange, keep_ref, other_ref, tile) if tile < middle else (
            turned_exchange, turned_ref, turned_other_ref, tile - middle
        )
        wide_ref[:, tile * LANES : (tile + 1) * LANES] = here[0].total(here[1], here[2], here[3] * pad, share)
    columns = out_ref.shape[0]
    wide_out = -(-columns // LANES) * LANES
    out_ref[...] = wide_ref[:, :wide_out].T[:columns]
    qkv_ref[...] = wide_ref[:, columns:]
    proj_ref[...] = exchange.total(keep_ref, other_ref, middle * pad, share)
    pos_ref[...] = exchange.total(keep_ref, other_ref, (middle + 1) * pad, pos_ref.shape[0])
    rows_ref[...] = exchange.shared_total(keep_ref, other_ref)
    take_rows(rows_ref, vector_refs)


def early_out_kernel(exchanges, pad, *refs):
    for exchange, keep_ref, other_ref, out_ref in zip(exchanges, refs[:2], refs[2:4], refs[4:]):
        for tile in range(out_ref.shape[1] // LANES):
            out_ref[:, tile * LANES : (tile + 1) * LANES] = exchange.total(
                keep_ref, other_ref, tile * pad, out_ref.shape[0]
            )


def swap(value, axis, bit):
    count = lax.axis_size(axis)
    return lax.ppermute(value, axis, [(i, i ^ bit) for i in range(count)])


def local(
    patch_rows, patches, visible, owner, qkv_weight, query_bias, value_bias, out_weight, out_bias, first_gain,
    first_shift, second_gain, second_shift, up_weight, up_bias, down_weight, down_bias, proj_weight, proj_bias,
    mask_token, decoder_pos, grid_cotangent,
):
    count = lax.axis_size("dp")
    parts = lax.axis_size("mp")
    where = jnp.stack([lax.axis_index("dp"), lax.axis_index("mp")]).astype(jnp.int32)
    rows, width = patch_rows.shape
    images = rows // VIS
    heads = qkv_weight.shape[1] // (3 * HEAD_DIM)
    head_columns = heads * HEAD_DIM
    qkv_columns = qkv_weight.shape[1]
    units = up_weight.shape[1]
    columns = proj_weight.shape[1]
    share = width // count
    pos_share = GRID // count
    half = rows // 2
    own_rows = rows // parts
    pads = (-(-share // 16) * 16, -(-pos_share // 16) * 16)
    run = Order(rows <= PINNED_ROWS)

    tables = grid_tables()
    table_high = tables.astype(low_type)
    table_low = (tables - table_high.astype(np.float32)).astype(low_type)
    turned_high = jnp.asarray(np.ascontiguousarray(table_high.transpose(0, 2, 1)))
    turned_low = jnp.asarray(np.ascontiguousarray(table_low.transpose(0, 2, 1)))
    table_high, table_low = jnp.asarray(table_high), jnp.asarray(table_low)
    qkv_weight_t = qkv_weight.T
    run.leave(owner, visible, patches, grid_cotangent, turned_high, turned_low, table_high, table_low, decoder_pos)
    info = Info(count)
    bits = tuple(range(count.bit_length() - 1))
    late_columns = qkv_columns + head_columns
    turned = (1, 0) + bits[2:]
    back_exchange = Exchange(count, bits, 0, moved=VIS)
    far = bits
    up_exchange = Exchange(count, far, units // LANES * pads[0])
    down_exchange = Exchange(count, turned, units // LANES * pads[0])
    tiles = late_columns // LANES
    middle = 3 * tiles // 6
    late_exchange = Exchange(count, bits, middle * pads[0])
    turned_exchange = Exchange(count, turned, (tiles - middle) * pads[0])
    last_exchange = Exchange(count, bits, sum(pads), moved=VIS, shared=VECTOR_ROWS)
    joint_exchange = Exchange(
        count, bits, late_exchange.block + last_exchange.block, moved=VIS, shared=VECTOR_ROWS
    )

    def low(*shape):
        return (shape, low_type)

    def wide(*shape):
        return (shape, wide_type)

    def moved(value, axis, bit):
        return run.keep(swap(value, axis, bit))

    def model_steps(keep, received):
        (total,) = run(add_kernel, [low(half, width)], (keep, received), cost=0.6)
        bit = 2
        while bit < parts:
            received = moved(total, "mp", bit)
            yield
            (total,) = run(add_kernel, [low(half, width)], (total, received), cost=0.6)
            bit *= 2
        other = moved(total, "mp", 1)
        yield
        return total, other

    def model_gather(value):
        values = {0: value}
        bit = parts // 2
        while bit:
            values.update({other | bit: moved(values[other], "mp", bit) for other in tuple(values)})
            bit //= 2
        return tuple(values[at] for at in range(parts))

    def data_step(step, exchange, pairs):
        keep, sent = run(
            lambda *refs: exchange.kernel(step, [part for part, _, _ in pairs], *refs),
            [low(exchange.rows(step), LANES)] * 2,
            (facts,) + tuple(array for _, *arrays in pairs for array in arrays),
            (SMEM,) + (VMEM,) * (2 * len(pairs)),
            cost=1.2,
        )
        return keep, moved(sent, "dp", 2 ** exchange.bits[step])

    def data_steps(exchange, keep, sent):
        received = moved(sent, "dp", 2 ** exchange.bits[0])
        yield keep, received
        for step in range(1, len(exchange.bits)):
            keep, received = data_step(step, exchange, [(exchange, keep, received)])
            yield keep, received

    def steps(kept, arrays, moves, sends, cost=1.0):
        first = len(kept) + len(arrays)
        sizes = [None] * len(kept) + [size for _, size in arrays] + [None] * len(moves)
        sizes += [size for _, size in sends]
        placed = [
            (exchange, step, sources, first + at, (first + len(moves) + to[0], to[1]))
            for at, (exchange, step, sources, to) in enumerate(moves)
        ]
        results = run(
            lambda *refs: step_kernel(placed, sizes, *refs),
            [low(exchange.rows(step), LANES) for exchange, step, _, _ in moves]
            + [low(sum(size), LANES) for _, size in sends],
            (facts, *kept) + tuple(array for array, _ in arrays),
            (SMEM,) + (VMEM,) * first,
            cost=cost,
        )
        return results[: len(moves)], [
            moved(sent, "dp", 2**bit) for sent, (bit, _) in zip(results[len(moves) :], sends)
        ]

    def finish_pair(steps):
        *_, last = steps
        return last

    def finish(steps):
        while True:
            try:
                next(steps)
            except StopIteration as stop:
                return stop.value

    out_all = model_gather(out_weight)
    proj_all = model_gather(proj_weight)
    (
        back_keep, back_sent, facts, seen, patch_rows, qkv_weight_t, first_gain, first_shift, query_bias, value_bias,
    ) = run(
        lambda *refs: cotangent_kernel(info, back_exchange, *refs),
        [
            low(back_exchange.rows(0), columns), low(back_exchange.rows(0), columns), ((info.size,), jnp.int32),
            ((count, VIS), jnp.int32),
        ],
        (where, owner, patches, visible, grid_cotangent),
        (SMEM, SMEM, SMEM, VMEM, VMEM),
        out_specs=(VMEM, VMEM, SMEM, VMEM),
        scratch=[pltpu.VMEM((VIS, count), wide_type)],
        stage=(patch_rows, qkv_weight_t, first_gain, first_shift, query_bias, value_bias),
        cost=3.0,
    )
    back_steps = data_steps(back_exchange, back_keep, back_sent)
    next(back_steps)
    act_one, qkv = run(
        enter_kernel,
        [low(rows, width), low(rows, qkv_columns)],
        (patch_rows, first_gain, first_shift, qkv_weight_t, query_bias, value_bias),
        cost=1.2,
        after=(out_all[1], proj_all[1]),
    )
    next(back_steps)
    packed_rows = half * head_columns // LANES
    packed, first_probs, first_attended, out_bias, second_gain, second_shift, up_weight, up_bias = run(
        lambda *refs: attention_kernel(info, heads, 0, *refs),
        [low(packed_rows, LANES), low(half, heads * BLOCK), low(half, head_columns)],
        (facts, qkv),
        (SMEM, VMEM),
        stage=(out_bias, second_gain, second_shift, up_weight, up_bias),
        cost=2.8,
    )
    first_all = model_gather(packed)
    back_own, back_other = finish_pair(back_steps)
    (
        packed, last_probs, last_attended, down_weight, down_bias, proj_bias, out_near, proj_near, out_core, proj_core
    ) = run(
        lambda *refs: attention_kernel(info, heads, half, *refs),
        [low(packed_rows, LANES), low(half, heads * BLOCK), low(half, head_columns)],
        (facts, qkv),
        (SMEM, VMEM),
        stage=(down_weight, down_bias, proj_bias, out_weight, proj_weight, out_all[1], proj_all[1]),
        cost=2.5,
        after=(out_all[parts // 2], proj_all[parts // 2]),
    )
    last_all = model_gather(packed)
    out_whole, proj_whole = run(
        lambda *refs: weights_kernel(parts, *refs),
        [low(parts * head_columns, width), low(width, parts * columns)],
        (facts, out_near, out_core) + out_all[2:] + (proj_near, proj_core) + proj_all[2:],
        (SMEM,) + (VMEM,) * (2 * parts),
        cost=0.0,
    )
    (enc_grad,) = run(
        lambda *refs: back_kernel(info, back_exchange, *refs),
        [low(rows, columns)],
        (facts, back_own, back_other),
        (SMEM, VMEM, VMEM),
        cost=0.4,
    )
    enc_all = model_gather(enc_grad)
    hidden, act_two, acted, slope = run(
        lambda *refs: forward_kernel(parts, head_columns, *refs),
        [wide(rows, width), low(rows, width), low(rows, units), wide(rows, units)],
        (facts, patch_rows, out_bias, second_gain, second_shift, up_weight, up_bias, out_whole)
        + first_all
        + last_all,
        (SMEM,) + (VMEM,) * (7 + 2 * parts),
        scratch=[pltpu.VMEM((BLOCK, parts * head_columns), low_type)],
        cost=2.6,
    )

    def forward_grad(own):
        return run(
            lambda *refs: forward_grad_kernel(parts, own, *refs),
            [low(half, width), low(half, units), low(half, width), wide(2, width)],
            (facts, slope, up_weight, down_weight, proj_whole) + enc_all,
            (SMEM,) + (VMEM,) * (4 + parts),
            scratch=[pltpu.VMEM((BLOCK, parts * columns), low_type)],
            cost=1.2,
        )

    sent, up_low_other, down_low_other, bias_grads_other = forward_grad(False)
    second_other = moved(sent, "mp", 1)
    keep, up_low, down_low, bias_grads = forward_grad(True)
    second_steps = model_steps(keep, second_other)
    next(second_steps)
    down_keep, down_sent, up_keep, up_sent = run(
        lambda *refs: early_grads_kernel((down_exchange, up_exchange), pads[0], *refs),
        [low(down_exchange.rows(0), LANES)] * 2 + [low(up_exchange.rows(0), LANES)] * 2,
        (facts, down_low, down_low_other, acted, act_two, up_low, up_low_other),
        (SMEM,) + (VMEM,) * 6,
        scratch=[pltpu.VMEM((width, units), wide_type)],
        cost=2.2,
    )
    down_pair = (down_keep, moved(down_sent, "dp", 2 ** turned[0]))
    up_pair = (up_keep, moved(up_sent, "dp", 2 ** bits[0]))
    keep, sent = run(
        forward_part_kernel,
        [low(half, width), low(half, width)],
        (facts, acted, down_weight),
        (SMEM, VMEM, VMEM),
        cost=0.7,
    )
    out_steps = model_steps(keep, moved(sent, "mp", 1))

    pos_grad_own, mask_grad, layouts = run(
        lambda *refs: position_kernel(info, *refs),
        [wide(GRID, columns), wide(1, columns), wide(3, GRID, columns)],
        (facts, seen, grid_cotangent, turned_high, turned_low, table_high, table_low, decoder_pos),
        (SMEM,) + (VMEM,) * 7,
        scratch=[pltpu.VMEM((3, GRID, columns), wide_type)],
        cost=20.0,
    )
    next(out_steps)
    (normed_low,) = run(norm_kernel, [low(rows, width)], (patch_rows,), cost=0.6)
    next(second_steps)
    second_sum, second_other = finish(second_steps)

    def attention_back(own, total, down_part, cost):
        return run(
            lambda *refs: attention_back_kernel(heads, own, *refs),
            [low(half, qkv_columns), low(half, width), wide(half, width), wide(3, width)],
            (facts, total, hidden, down_part, second_gain, out_near, qkv, first_probs, last_probs),
            (SMEM,) + (VMEM,) * 8,
            scratch=[pltpu.VMEM((half, heads * BLOCK), low_type)],
            cost=cost,
        )

    grads, attn_low, hidden_grad, second_grads = attention_back(True, second_sum, down_low, COVER)
    run.share = 2.0
    grads_other, attn_low_other, hidden_grad_other, second_grads_other = attention_back(
        False, second_other, down_low_other, 2.0
    )
    in_keep, in_sent = run(
        input_part_kernel,
        [low(half + EXTRA, width)] * 2,
        (facts, normed_low, grads, grads_other, qkv_weight_t),
        (SMEM,) + (VMEM,) * 4,
        scratch=[pltpu.VMEM((rows, width), wide_type), pltpu.VMEM((2, width), wide_type)],
        cost=2.0,
    )
    in_other = moved(in_sent, "mp", 1)
    in_other = moved(in_sent, "mp", 1)
    late_keep, late_sent, turned_keep, turned_sent, qkv_bias_grad = run(
        lambda *refs: late_grads_kernel((late_exchange, turned_exchange), pads[0], middle * LANES, *refs),
        [low(late_exchange.rows(0), LANES)] * 2
        + [low(turned_exchange.rows(0), LANES)] * 2
        + [wide(1, qkv_columns)],
        (facts, act_one, grads, grads_other, attn_low, attn_low_other, first_attended, last_attended),
        (SMEM,) + (VMEM,) * 7,
        scratch=[pltpu.VMEM((width, late_columns), wide_type)],
        cost=40.0,
    )
    turned_came = moved(turned_sent, "dp", 2 ** turned[0])
    late_came = moved(late_sent, "dp", 2 ** bits[0])
    bit = 1
    size = half
    while 2**bit < parts:
        in_keep, in_sent = run(
            lambda *refs, bit=bit: input_halve_kernel(bit, *refs),
            [low(size // 2 + EXTRA, width)] * 2,
            (facts, in_keep, in_other),
            (SMEM, VMEM, VMEM),
            scratch=[pltpu.VMEM((size + own_rows, width), wide_type)],
            cost=1.1,
            after=(up_pair[1], down_pair[1]),
        )
        in_other = moved(in_sent, "mp", 2**bit)
        size //= 2
        bit += 1
    next(out_steps)
    early_sizes = [[exchange.rows(1)] for exchange in (up_exchange, down_exchange)]
    (up_keep,), (up_came,) = steps(
        (up_pair[0],),
        ((up_pair[1], [up_exchange.rows(0)]),),
        [(up_exchange, 1, [(up_exchange, 0, (1, 0))], (0, 0))],
        [(far[1], early_sizes[0])],
        cost=40.0,
    )
    out_sum, out_other = finish(out_steps)
    encoded, proj_grad = run(
        encoded_kernel,
        [low(rows, columns), wide(width, columns)],
        (facts, hidden, out_sum, out_other, down_bias, proj_near, proj_bias, enc_grad),
        (SMEM,) + (VMEM,) * 7,
        scratch=[pltpu.VMEM((rows, width), low_type)],
        cost=1.0,
    )
    last_keep, last_sent = run(
        lambda *refs: last_kernel(info, last_exchange, heads, pads[0], *refs),
        [low(last_exchange.rows(0), LANES)] * 2,
        (
            facts, encoded, proj_grad, enc_grad, pos_grad_own, mask_grad, bias_grads, bias_grads_other, second_grads,
            second_grads_other, qkv_bias_grad, in_keep, in_other,
        ),
        (SMEM,) + (VMEM,) * 12,
        scratch=[pltpu.VMEM((VECTOR_ROWS, LANES), wide_type)],
        cost=0.6,
    )
    last_came = moved(last_sent, "dp", 2 ** bits[0])
    (down_keep,), (down_came,) = steps(
        (down_pair[0],),
        ((down_pair[1], [down_exchange.rows(0)]),),
        [(down_exchange, 1, [(down_exchange, 0, (1, 0))], (0, 0))],
        [(turned[1], early_sizes[1])],
    )
    (input_grad,) = run(
        input_grad_kernel,
        [low(own_rows, width)],
        (facts, patch_rows, in_keep, in_other, hidden_grad, hidden_grad_other, first_gain),
        (SMEM,) + (VMEM,) * 6,
        final=True,
        cost=0.8,
    )

    early = (up_exchange, down_exchange)
    late = (joint_exchange, turned_exchange)
    joint_sizes = [[exchange.rows(1)] for exchange in late]
    (late_keep, turned_keep), late_came = steps(
        (late_keep, last_keep, turned_keep),
        (
            (late_came, [late_exchange.rows(0)]), (last_came, [last_exchange.rows(0)]),
            (turned_came, [turned_exchange.rows(0)]),
        ),
        [
            (joint_exchange, 1, [(late_exchange, 0, (3, 0)), (last_exchange, 1, (4, 0))], (0, 0)),
            (turned_exchange, 1, [(turned_exchange, 2, (5, 0))], (1, 0)),
        ],
        [(bits[1], joint_sizes[0]), (turned[1], joint_sizes[1])],
    )
    (up_keep,), (up_came,) = steps(
        (up_keep,),
        ((up_came, early_sizes[0]),),
        [(up_exchange, 2, [(up_exchange, 0, (1, 0))], (0, 0))],
        [(far[2], [up_exchange.rows(2)])],
    )
    (down_keep,), (down_came,) = steps(
        (down_keep,),
        ((down_came, early_sizes[1]),),
        [(down_exchange, 2, [(down_exchange, 0, (1, 0))], (0, 0))],
        [(turned[2], [down_exchange.rows(2)])],
    )
    early_came = (up_came, down_came)
    early_sizes = [[exchange.rows(2)] for exchange in early]
    last_sizes = [exchange.rows(2) for exchange in late]
    (late_keep, turned_keep), (late_came,) = steps(
        (late_keep, turned_keep),
        ((late_came[0], joint_sizes[0]), (late_came[1], joint_sizes[1])),
        [
            (joint_exchange, 2, [(joint_exchange, 0, (2, 0))], (0, 0)),
            (turned_exchange, 2, [(turned_exchange, 1, (3, 0))], (0, 1)),
        ],
        [(2, last_sizes)],
    )
    for step in range(3, len(bits)):
        old_sizes, early_sizes = early_sizes, [[exchange.rows(step)] for exchange in early]
        (up_keep, down_keep), early_came = steps(
            (up_keep, down_keep),
            ((early_came[0], old_sizes[0]), (early_came[1], old_sizes[1])),
            [(exchange, step, [(exchange, at, (2 + at, 0))], (at, 0)) for at, exchange in enumerate(early)],
            [(step, early_sizes[0]), (step, early_sizes[1])],
        )
        old_sizes, last_sizes = last_sizes, [exchange.rows(step) for exchange in late]
        (late_keep, turned_keep), (late_came,) = steps(
            (late_keep, turned_keep),
            ((late_came, old_sizes),),
            [(exchange, step, [(exchange, at, (2, at))], (0, at)) for at, exchange in enumerate(late)],
            [(step, last_sizes)],
        )
    up_weight_grad, down_weight_grad = run(
        lambda *refs: early_out_kernel(early, pads[0], *refs),
        [wide(share, units)] * 2,
        (up_keep, down_keep, *early_came),
        final=True,
        cost=1.0,
    )
    (
        grids, out_weight_grad, qkv_weight_grad, proj_weight_grad, pos_grad, query_bias_grad, value_bias_grad,
        up_bias_grad, proj_bias_grad, mask_token_grad, first_gain_grad, first_shift_grad, second_gain_grad,
        second_shift_grad, out_bias_grad, down_bias_grad,
    ) = run(
        lambda *refs: late_out_kernel(info, joint_exchange, turned_exchange, pads[0], middle, last_sizes, *refs),
        [
            low(count, GRID, columns), wide(head_columns, share), wide(share, qkv_columns), wide(share, columns),
            wide(pos_share, columns),
        ]
        + [wide(size) for size in (head_columns, head_columns, units, columns, columns) + (width,) * 6],
        (facts, seen, late_keep, turned_keep, late_came, mask_token, layouts),
        (SMEM,) + (VMEM,) * 6,
        scratch=[pltpu.VMEM((share, late_columns), wide_type), pltpu.VMEM((VECTOR_ROWS, LANES), wide_type)],
        final=True,
        cost=2.5,
    )
    return (
        grids, input_grad, qkv_weight_grad, query_bias_grad, value_bias_grad, out_weight_grad, out_bias_grad,
        first_gain_grad, first_shift_grad, second_gain_grad, second_shift_grad, up_weight_grad, up_bias_grad,
        down_weight_grad.T, down_bias_grad, proj_weight_grad, proj_bias_grad, mask_token_grad, pos_grad,
    )


def solution(mesh):
    return jax.shard_map(
        local,
        mesh=mesh,
        in_specs=(
            P("dp", None), P(), P(), P(), P(None, "mp"), P("mp"), P("mp"), P("mp", None), P(), P(), P(), P(), P(),
            P(None, "mp"), P("mp"), P("mp", None), P(), P(None, "mp"), P("mp"), P("mp"), P(None, "mp"),
            P("dp", None, "mp"),
        ),
        out_specs=(
            P("dp", None, "mp"), P(("dp", "mp"), None), P("dp", "mp"), P("mp"), P("mp"), P("mp", "dp"), P(), P(),
            P(), P(), P(), P("dp", "mp"), P("mp"), P("mp", "dp"), P(), P("dp", "mp"), P("mp"), P("mp"),
            P("dp", "mp"),
        ),
        check_vma=False,
    )
```

```python
import math

import jax
import jax.numpy as jnp
import numpy as np
from jax import lax
from jax.experimental import pallas as pl
from jax.experimental.pallas import tpu as pltpu
from jax.sharding import PartitionSpec as P

HEAD_DIM = 64
GRID = 256
VIS = 64
CHUNK = 512
LANES = 128

epsilon = 1e-06
low_type = jnp.bfloat16
wide_type = jnp.float32
scale_factor = HEAD_DIM ** (-0.5)

VMEM = pl.BlockSpec(memory_space=pltpu.VMEM)
SMEM = pl.BlockSpec(memory_space=pltpu.SMEM)
ANY = pl.BlockSpec(memory_space=pl.ANY)
PINNED_ROWS = 512


def grid_tables():
    grid_edge = math.isqrt(GRID)
    tables = []
    for side_cells in (10, 14):
        places = np.arange(side_cells)
        centers = ((2 * places + 1) * grid_edge - side_cells) / (2 * side_cells)
        lower = np.floor(centers).astype(np.int64)
        share = centers - lower
        lerp = np.zeros((side_cells, grid_edge))
        lerp[places, np.clip(lower, 0, grid_edge - 1)] += 1.0 - share
        lerp[places, np.clip(lower + 1, 0, grid_edge - 1)] += share
        table = np.zeros((GRID, GRID))
        table[: side_cells * side_cells] = np.kron(lerp, lerp)
        tables.append(table)
    return np.stack(tables).astype(np.float32)


def split_low(value):
    high = value.astype(low_type)
    return high, (value - high.astype(wide_type)).astype(low_type)


def dot(left, right):
    return lax.dot_general(left, right, (((1,), (0,)), ((), ())), preferred_element_type=wide_type)


def dot_right_t(left, right):
    return lax.dot_general(left, right, (((1,), (1,)), ((), ())), preferred_element_type=wide_type)


def dot_left_t(left, right):
    return lax.dot_general(left, right, (((0,), (0,)), ((), ())), preferred_element_type=wide_type)


def normalized(value):
    center = value - jnp.mean(value, axis=-1, keepdims=True)
    spread = lax.rsqrt(jnp.mean(center * center, axis=-1, keepdims=True) + epsilon)
    return center * spread, spread


def norm_back(grad, normed, spread, gain):
    scaled = grad * gain
    mean_one = jnp.mean(scaled, axis=-1, keepdims=True)
    mean_two = jnp.mean(scaled * normed, axis=-1, keepdims=True)
    return spread * (scaled - mean_one - normed * mean_two)


def row_sum(value):
    return jnp.sum(value, axis=0, keepdims=True)


def over_rows(total, size, body):
    size = min(size, total)
    if total <= 2 * size:
        for start in range(0, total, size):
            body(start, size)
        return

    def step(i, carry):
        body(pl.multiple_of(i * size, size), size)
        return carry

    lax.fori_loop(0, total // size, step, 0)


def size_of(shape, kind):
    return math.prod(shape) * jnp.dtype(kind).itemsize


RATE = 10**9
COST_SHARE = 1.0
COVER = 40.0
BYTES = 0


class Order:
    def __init__(self, pinned):
        self.pinned = pinned
        self.last = None
        self.near = []
        self.far = []
        self.share = COST_SHARE

    def keep(self, value):
        if self.pinned:
            self.near.append((value, pltpu.VMEM))
        return value

    def leave(self, *values):
        self.far += values

    def placed(self, value):
        for near, space in self.near:
            if value is near:
                return pltpu.with_memory_space_constraint(value, space)
        if any(value is far for far in self.far):
            return pltpu.with_memory_space_constraint(value, pltpu.HBM)
        return value

    def __call__(
        self, kernel, outs, args, specs=None, scratch=(), out_specs=None, final=False, stage=(), cost=1.0, after=()
    ):
        args = tuple(args)
        specs = [VMEM] * len(args) if specs is None else list(specs)
        out_specs = [VMEM] * len(outs) if out_specs is None else list(out_specs)
        count, results_count = len(args), len(outs)
        staged = list(stage) if self.pinned else []
        self.leave(*staged)
        needed = sum(size_of(ref.shape, ref.dtype) for ref in scratch)
        needed += sum(
            size_of(arg.shape, arg.dtype) for arg in args if not any(arg is near for near, _ in self.near)
        )
        shapes = []
        for (shape, kind), spec in zip(outs, out_specs):
            if self.pinned and not final:
                shapes.append((pltpu.SMEM if spec is SMEM else pltpu.VMEM)(shape, kind))
            else:
                shapes.append(jax.ShapeDtypeStruct(shape, kind))
                needed += size_of(shape, kind)
        tail = len(staged)
        args += tuple(staged)
        specs += [ANY] * tail
        unread = tuple(after) if self.last is None else (*after, self.last)
        skipped = len(unread)
        args += unread
        specs += [ANY] * skipped

        def body(*refs):
            own, sources, refs = refs[:count], refs[count : count + tail], refs[count + tail + skipped :]
            results, targets, refs = (
                refs[:results_count], refs[results_count : results_count + tail], refs[results_count + tail :]
            )
            copies = []
            if tail:
                *refs, sems = refs
                copies = [
                    pltpu.make_async_copy(source, target, sems.at[at])
                    for at, (source, target) in enumerate(zip(sources, targets))
                ]
            for copy in copies:
                copy.start()
            kernel(*own, *results, *refs)
            for copy in copies:
                copy.wait()

        results = pl.pallas_call(
            body,
            out_shape=tuple(shapes) + tuple(pltpu.VMEM(array.shape, array.dtype) for array in staged),
            in_specs=specs,
            out_specs=tuple(out_specs) + (VMEM,) * tail,
            scratch_shapes=list(scratch) + ([pltpu.SemaphoreType.DMA((tail,))] if tail else []),
            compiler_params=pltpu.CompilerParams(
                vmem_limit_bytes=min(needed + needed // 4 + 10 * 2**20, 60 * 2**20)
            ),
            cost_estimate=pl.CostEstimate(
                flops=int(cost * RATE * self.share), bytes_accessed=int(cost * BYTES), transcendentals=0
            ),
        )(*(self.placed(arg) for arg in args))
        if self.pinned and not final:
            for result, spec in zip(results, out_specs + [VMEM] * tail):
                self.near.append((result, pltpu.SMEM if spec is SMEM else pltpu.VMEM))
        if not final:
            self.last = results[0]
        if stage and not self.pinned:
            return (*results, *stage)
        return results


class Info:
    def __init__(self, count):
        self.count = count
        self.size = 2 + 5 * count

    def dp(self, ref):
        return ref[0]

    def mp(self, ref):
        return ref[1]

    def owner(self, ref, image):
        return ref[2 + image]

    def live(self, ref, image):
        return ref[2 + self.count + image]

    def source(self, ref, slot):
        return ref[2 + 2 * self.count + slot]

    def cells(self, ref, slot):
        return ref[2 + 3 * self.count + slot]

    def image(self, ref, owner):
        return ref[2 + 4 * self.count + owner]


def fill_info(count, where_ref, owner_ref, patches_ref, info_ref):
    me = where_ref[0]
    info_ref[0] = me
    info_ref[1] = where_ref[1]

    def one(at):
        own = me * count + at
        info_ref[2 + at] = owner_ref[own]
        info_ref[2 + 4 * count + owner_ref[own]] = at
        info_ref[2 + count + at] = patches_ref[own] // 4

        def find(i, found):
            return jnp.where(owner_ref[at * count + i] == me, at * count + i, found)

        source = lax.fori_loop(0, count, find, at * count, unroll=count <= 8)
        info_ref[2 + 2 * count + at] = source
        info_ref[2 + 3 * count + at] = patches_ref[source]

    over_slots(count, one)


def over_slots(count, one_slot):
    if count <= 8:
        for slot in range(count):
            one_slot(slot)
    else:
        lax.fori_loop(0, count, lambda slot, carry: (one_slot(slot), carry)[1], 0)


def side_of(size):
    return (size >= 196).astype(jnp.int32) + (size >= 256).astype(jnp.int32)


def block_at(rest, place, bit):
    low = rest & ((1 << place) - 1)
    return ((rest - low) << 1) + (bit << place) + low


class Exchange:
    def __init__(self, count, bits, block, moved=0, shared=0):
        self.count, self.bits, self.block, self.moved, self.shared = count, bits, block, moved, shared

    def blocks(self, step):
        return self.count >> (step + 1)

    def place(self, step):
        bit = self.bits[step]
        return bit - sum(done < bit for done in self.bits[:step])

    def moved_at(self, step):
        return self.blocks(step) * self.block

    def shared_at(self, step):
        return self.moved_at(step) + self.count // 2 * self.moved

    def rows(self, step):
        return self.shared_at(step) + self.shared

    def own_bit(self, step, info_ref):
        return (info_ref[0] >> self.bits[step]) & 1

    def targets(self, step, info_ref, keep_ref, sent_ref):
        own = self.own_bit(step, info_ref)
        place = self.place(step)
        for ref, which in ((sent_ref, 1 - own), (keep_ref, own)):
            yield ref, [block_at(block, place, which) for block in range(self.blocks(step))]

    def kernel(self, step, parts, info_ref, *refs):
        *from_refs, next_keep_ref, next_sent_ref = refs
        pairs = list(zip(parts, from_refs[::2], from_refs[1::2]))
        sources = 1 << (step - 1)
        rests = self.blocks(step - 1)
        for ref, indices in self.targets(step, info_ref, next_keep_ref, next_sent_ref):
            first, moved_at, shared_at = 0, self.moved_at(step), self.shared_at(step)
            for part, keep_ref, other_ref in pairs:
                for block, index in enumerate(indices if part.block else ()):
                    rows = pl.ds(pl.multiple_of(index * part.block, 16), part.block)
                    at = block * self.block + first
                    ref[at : at + part.block, :] = (
                        keep_ref[rows, :].astype(wide_type) + other_ref[rows, :].astype(wide_type)
                    ).astype(low_type)
                first += part.block
                for from_ref in (keep_ref, other_ref) if part.moved else ():
                    for source in range(sources):
                        for index in indices:
                            rows = part.moved_at(step - 1) + (source * rests + index) * part.moved
                            ref[moved_at : moved_at + part.moved, :] = from_ref[
                                pl.ds(pl.multiple_of(rows, 16), part.moved), :
                            ]
                            moved_at += part.moved
                if part.shared:
                    at = part.shared_at(step - 1)
                    rows = slice(at, at + part.shared)
                    ref[shared_at : shared_at + part.shared, :] = (
                        keep_ref[rows, :].astype(wide_type) + other_ref[rows, :].astype(wide_type)
                    ).astype(low_type)

    def arrived(self, keep_ref, other_ref):
        last = len(self.bits) - 1
        sources = 1 << last
        for half, ref in enumerate((keep_ref, other_ref)):
            for source in range(sources):
                relative = 0
                for step, bit in enumerate(self.bits):
                    relative |= (((source + half * sources) >> step) & 1) << bit
                yield relative, ref, self.moved_at(last) + source * self.moved

    def total(self, keep_ref, other_ref, start, size):
        rows = slice(start, start + size)
        return keep_ref[rows, :].astype(wide_type) + other_ref[rows, :].astype(wide_type)

    def shared_total(self, keep_ref, other_ref):
        return self.total(keep_ref, other_ref, self.shared_at(len(self.bits) - 1), self.shared)


def cotangent_kernel(
    info, exchange, where_ref, owner_ref, patches_ref, visible_ref, cot_ref, keep_ref, sent_ref, info_ref, seen_ref,
    turned_ref,
):
    count = info.count
    fill_info(count, where_ref, owner_ref, patches_ref, info_ref)

    def take(slot):
        seen_ref[pl.ds(slot, 1), :] = visible_ref[pl.ds(info.source(info_ref, slot), 1), :]

    over_slots(count, take)
    turned_ref[...] = seen_ref[...].astype(wide_type).T
    cells = lax.broadcasted_iota(jnp.int32, (VIS, GRID), 1).astype(wide_type)
    own = exchange.own_bit(0, info_ref)
    place = exchange.place(0)
    for slot in range(count):
        onehot = (turned_ref[:, slot : slot + 1] == cells).astype(wide_type).astype(low_type)
        rows = dot(onehot, cot_ref[slot]).astype(low_type)
        rest = (slot & ((1 << place) - 1)) | ((slot >> (place + 1)) << place)
        kept = ((slot >> place) & 1) == own

        @pl.when(kept)
        def _(rest=rest, rows=rows):
            keep_ref[rest * VIS : (rest + 1) * VIS, :] = rows

        @pl.when(jnp.logical_not(kept))
        def _(rest=rest, rows=rows):
            sent_ref[rest * VIS : (rest + 1) * VIS, :] = rows


def position_kernel(
    info, info_ref, visible_ref, cot_ref, turned_high_ref, turned_low_ref, table_high_ref, table_low_ref, pos_ref,
    grad_ref, mask_ref, layout_ref, sums_ref,
):
    cells = lax.broadcasted_iota(jnp.int32, (GRID, VIS), 0)
    cell_column = lax.broadcasted_iota(jnp.int32, (GRID, 1), 0)
    sums_ref[...] = jnp.zeros_like(sums_ref)
    mask_ref[...] = jnp.zeros_like(mask_ref)

    def one_slot(slot):
        size = info.cells(info_ref, slot)
        seen = visible_ref[pl.ds(slot, 1), :] == cells
        fill = (cell_column < size).astype(wide_type) - jnp.sum(
            seen.astype(wide_type), axis=1, keepdims=True
        )
        wide = cot_ref[slot].astype(wide_type)
        mask_ref[...] += row_sum(fill * wide)
        sums_ref[side_of(size)] += wide

    over_slots(info.count, one_slot)
    total = sums_ref[2]
    for side in range(2):
        high, low = split_low(sums_ref[side])
        total += (
            dot(turned_high_ref[side], high) + dot(turned_high_ref[side], low) + dot(turned_low_ref[side], high)
        )
    grad_ref[...] = total
    table = pos_ref[...]
    for side in range(2):
        layout_ref[side] = dot(table_high_ref[side], table) + dot(table_low_ref[side], table)
    layout_ref[2] = table.astype(wide_type)


def wide_row(ref):
    return ref[...].astype(wide_type).reshape(1, ref.shape[0])


def enter_kernel(
    rows_ref, gain_ref, shift_ref, weight_ref, query_ref, value_ref, act_ref, qkv_ref
):
    gain, shift = wide_row(gain_ref), wide_row(shift_ref)
    query, value = wide_row(query_ref), wide_row(value_ref)
    nothing = jnp.zeros((1, HEAD_DIM), wide_type)
    pieces = []
    for start in range(0, query.shape[1], HEAD_DIM):
        pieces += [query[:, start : start + HEAD_DIM], nothing, value[:, start : start + HEAD_DIM]]
    bias = jnp.concatenate(pieces, axis=1)

    def body(start, size):
        rows = pl.ds(start, size)
        normed, _ = normalized(rows_ref[rows, :].astype(wide_type))
        act = (normed * gain + shift).astype(low_type)
        act_ref[rows, :] = act
        qkv_ref[rows, :] = (dot_right_t(act, weight_ref[...]) + bias).astype(low_type)

    over_rows(rows_ref.shape[0], CHUNK, body)


BLOCK = 4 * VIS


def attention_kernel(info, heads, first, info_ref, qkv_ref, packed_ref, prob_ref, attended_ref):
    key_image = lax.broadcasted_iota(jnp.int32, (BLOCK, BLOCK), 0) // VIS
    key_slot = lax.broadcasted_iota(jnp.int32, (BLOCK, BLOCK), 0) % VIS
    own_image = key_image == lax.broadcasted_iota(jnp.int32, (BLOCK, BLOCK), 1) // VIS
    columns = heads * HEAD_DIM
    full = columns // LANES * LANES
    rest = BLOCK * (columns - full) // LANES

    def body(start, size):
        rows = pl.ds(start, size)
        from_rows = pl.ds(first + start, size)
        limit = jnp.zeros((size, size), jnp.int32)
        for image in range(size // VIS):
            limit = jnp.where(key_image == image, info.live(info_ref, (first + start) // VIS + image), limit)
        live = jnp.logical_and(own_image, key_slot < limit)
        for head in range(heads):
            base = head * 3 * HEAD_DIM
            queries = qkv_ref[from_rows, base : base + HEAD_DIM]
            key_rows = qkv_ref[from_rows, base + HEAD_DIM : base + 2 * HEAD_DIM]
            value_rows = qkv_ref[from_rows, base + 2 * HEAD_DIM : base + 3 * HEAD_DIM]
            scores = jnp.where(live, dot_right_t(key_rows, queries) * scale_factor, -1e30)
            raised = jnp.exp(scores - jnp.max(scores, axis=0, keepdims=True))
            probs = (raised / jnp.sum(raised, axis=0, keepdims=True)).astype(low_type)
            prob_ref[rows, head * BLOCK : (head + 1) * BLOCK] = probs
            attended_ref[rows, head * HEAD_DIM : (head + 1) * HEAD_DIM] = dot_left_t(
                probs, value_rows
            ).astype(low_type)
        at = start // BLOCK * (full // LANES * BLOCK + rest)
        for tile in range(full // LANES):
            packed_ref[pl.ds(at, BLOCK), :] = attended_ref[rows, tile * LANES : (tile + 1) * LANES]
            at += BLOCK
        pieces = [
            attended_ref[pl.ds(start + piece * rest, rest), full:].astype(wide_type)
            for piece in range(BLOCK // rest)
        ]
        packed_ref[pl.ds(at, rest), :] = jnp.concatenate(pieces, axis=1).astype(low_type)

    over_rows(prob_ref.shape[0], BLOCK, body)


def unpack(own, packed_refs, start, columns, out_ref):
    full = columns // LANES * LANES
    width = columns - full
    rest = BLOCK * width // LANES
    at = start // BLOCK * (full // LANES * BLOCK + rest)
    count = len(packed_refs)
    for tile in range(full // LANES):
        for relative, ref in enumerate(packed_refs):
            lane = (tile * count + (own ^ relative)) * LANES
            out_ref[:, pl.ds(pl.multiple_of(lane, LANES), LANES)] = ref[pl.ds(at, BLOCK), :]
        at += BLOCK
    lane = full * count
    for other in range(0, count, LANES // width):
        pieces = []
        for part in range(other, other + LANES // width):
            rows = None
            for relative, ref in enumerate(packed_refs):
                here = ref[pl.ds(at, rest), :].astype(wide_type)
                rows = here if rows is None else jnp.where((own ^ relative) == part, here, rows)
            pieces.append(
                jnp.concatenate(
                    [rows[:, piece * width : (piece + 1) * width] for piece in range(BLOCK // rest)], axis=0
                )
            )
        out_ref[:, lane : lane + LANES] = jnp.concatenate(pieces, axis=1).astype(low_type)
        lane += LANES


def weights_kernel(parts, info_ref, *refs):
    out_refs, proj_refs, (out_ref, proj_ref) = refs[:parts], refs[parts : 2 * parts], refs[2 * parts :]
    own = info_ref[1]
    columns = out_refs[0].shape[0]
    full = columns // LANES * LANES
    width = columns - full
    for relative, (out_part_ref, proj_part_ref) in enumerate(zip(out_refs, proj_refs)):
        part = own ^ relative
        for tile in range(full // LANES):
            at = pl.multiple_of((tile * parts + part) * LANES, LANES)
            out_ref[pl.ds(at, LANES), :] = out_part_ref[tile * LANES : (tile + 1) * LANES, :]
        at = pl.multiple_of(full * parts + part * width, 16)
        out_ref[pl.ds(at, width), :] = out_part_ref[full:, :]
        size = proj_part_ref.shape[1]
        proj_ref[:, pl.ds(pl.multiple_of(part * size, LANES), size)] = proj_part_ref[...]


def halves(upper, left_ref, weight_ref, keep_ref, sent_ref, product):
    half = keep_ref.shape[0]
    for out_ref, which in ((sent_ref, 1 - upper), (keep_ref, upper)):

        def body(start, size, out_ref=out_ref, which=which):
            rows = pl.ds(pl.multiple_of(which * half + start, size), size)
            out_ref[pl.ds(start, size), :] = product(left_ref[rows, :], weight_ref[...]).astype(
                out_ref.dtype
            )

        over_rows(half, CHUNK, body)


def both_halves(upper, half, body):
    for source, which in enumerate((upper, 1 - upper)):

        def one(start, size, source=source, which=which):
            body(source, pl.ds(pl.multiple_of(which * half + start, size), size), pl.ds(start, size), size)

        over_rows(half, 256, one)


def back_kernel(info, exchange, info_ref, back_ref, back_other_ref, enc_ref):
    for relative, ref, start in exchange.arrived(back_ref, back_other_ref):
        image = info.image(info_ref, info_ref[0] ^ relative)
        enc_ref[pl.ds(pl.multiple_of(image * VIS, VIS), VIS), :] = ref[start : start + VIS, :]


def add_kernel(left_ref, right_ref, out_ref):
    out_ref[...] = (left_ref[...].astype(wide_type) + right_ref[...].astype(wide_type)).astype(low_type)


def forward_kernel(
    parts, columns, info_ref, rows_ref, out_bias_ref, gain_ref, shift_ref, up_ref, up_bias_ref, weight_ref, *refs
):
    attended_refs = (refs[:parts], refs[parts : 2 * parts])
    hidden_ref, act_ref, acted_ref, slope_ref, all_ref = refs[2 * parts :]
    half = rows_ref.shape[0] // 2
    out_bias, gain, shift, up_bias = (
        wide_row(ref) for ref in (out_bias_ref, gain_ref, shift_ref, up_bias_ref)
    )

    def body(which, start, size):
        rows = pl.ds(which * half + start, size)
        unpack(info_ref[1], attended_refs[which], start, columns, all_ref)
        total = dot(all_ref[...], weight_ref[...])
        hidden = rows_ref[rows, :].astype(wide_type) + total + out_bias
        hidden_ref[rows, :] = hidden
        normed, _ = normalized(hidden)
        act = (normed * gain + shift).astype(low_type)
        act_ref[rows, :] = act
        up_pre = dot(act, up_ref[...]) + up_bias
        cdf = 0.5 + 0.5 * lax.erf(up_pre * math.sqrt(0.5))
        acted_ref[rows, :] = (up_pre * cdf).astype(low_type)
        slope_ref[rows, :] = cdf + up_pre * jnp.exp(-0.5 * up_pre * up_pre) * (
            1.0 / math.sqrt(2.0 * math.pi)
        )

    for which in range(2):
        over_rows(half, BLOCK, lambda start, size, which=which: body(which, start, size))


def forward_part_kernel(info_ref, acted_ref, down_ref, keep_ref, sent_ref):
    halves(info_ref[1] & 1, acted_ref, down_ref, keep_ref, sent_ref, dot)


def forward_grad_kernel(
    parts, own, info_ref, slope_ref, up_ref, down_ref, weight_ref, *refs
):
    enc_refs = refs[:parts]
    part_ref, up_low_ref, down_low_ref, bias_ref, all_ref = refs[parts:]
    upper = info_ref[1] & 1
    half = part_ref.shape[0]
    first = (upper if own else 1 - upper) * half
    bias_ref[...] = jnp.zeros_like(bias_ref)

    def body(start, size):
        from_rows = pl.ds(pl.multiple_of(first + start, size), size)
        rows = pl.ds(start, size)
        for relative, enc_ref in enumerate(enc_refs):
            columns = enc_ref.shape[1]
            lane = pl.multiple_of((info_ref[1] ^ relative) * columns, LANES)
            all_ref[:, pl.ds(lane, columns)] = enc_ref[from_rows, :]
        out_grad = dot_right_t(all_ref[...], weight_ref[...])
        down_low = out_grad.astype(low_type)
        down_low_ref[rows, :] = down_low
        up_low = dot_right_t(down_low, down_ref[...]) * slope_ref[from_rows, :]
        up_low_ref[rows, :] = up_low.astype(low_type)
        bias_ref[0:1, :] += row_sum(out_grad)
        bias_ref[1:2, :] += row_sum(up_low_ref[rows, :].astype(wide_type))
        part_ref[rows, :] = dot_right_t(up_low_ref[rows, :], up_ref[...]).astype(low_type)

    over_rows(half, BLOCK, body)


def put_blocks(exchange, info_ref, keep_ref, sent_ref, wide_ref, pad, first=0):
    share = wide_ref.shape[0] // exchange.count
    for ref, indices in exchange.targets(0, info_ref, keep_ref, sent_ref):
        for block, index in enumerate(indices):
            rows = pl.ds(pl.multiple_of(index * share, 8), share)
            for tile in range(wide_ref.shape[1] // LANES):
                at = block * exchange.block + first + tile * pad
                ref[at : at + share, :] = wide_ref[rows, tile * LANES : (tile + 1) * LANES].astype(low_type)


def halves_of(info_ref, refs):
    if len(refs) == 2:
        return refs[0][...], refs[1][...]
    half = refs[0].shape[0] // 2
    upper = info_ref[1] & 1
    return tuple(
        refs[0][pl.ds(pl.multiple_of(which * half, half), half), :] for which in (upper, 1 - upper)
    )


def early_grads_kernel(
    exchanges, pad, info_ref, low_ref, low_other_ref, acted_ref, act_ref, up_ref, up_other_ref, down_keep_ref,
    down_sent_ref, up_keep_ref, up_sent_ref, wide_ref,
):
    left, right = halves_of(info_ref, (low_ref, low_other_ref)), halves_of(info_ref, (acted_ref,))
    wide_ref[...] = dot_left_t(left[0], right[0]) + dot_left_t(left[1], right[1])
    put_blocks(exchanges[0], info_ref, down_keep_ref, down_sent_ref, wide_ref, pad)
    left, right = halves_of(info_ref, (act_ref,)), halves_of(info_ref, (up_ref, up_other_ref))
    wide_ref[...] = dot_left_t(left[0], right[0]) + dot_left_t(left[1], right[1])
    put_blocks(exchanges[1], info_ref, up_keep_ref, up_sent_ref, wide_ref, pad)


def attention_back_kernel(
    heads, own, info_ref, sum_ref, hidden_ref, low_ref, gain_ref, weight_ref, qkv_ref, prob_ref, prob_last_ref,
    grads_ref, attn_low_ref, grad_ref, bias_ref, probs_ref,
):
    gain = wide_row(gain_ref)
    bias_ref[...] = jnp.zeros_like(bias_ref)
    half = sum_ref.shape[0]
    upper = info_ref[1] & 1
    which = upper if own else 1 - upper

    @pl.when(which == 0)
    def _():
        probs_ref[...] = prob_ref[...]

    @pl.when(which == 1)
    def _():
        probs_ref[...] = prob_last_ref[...]

    def body(start, size):
        part = pl.ds(start, size)
        rows = pl.ds(pl.multiple_of(which * half + start, size), size)
        normed, spread = normalized(hidden_ref[rows, :])
        grad = sum_ref[part, :].astype(wide_type)
        bias_ref[0:1, :] += row_sum(grad * normed)
        bias_ref[1:2, :] += row_sum(grad)
        hidden_grad = low_ref[part, :].astype(wide_type) + norm_back(grad, normed, spread, gain)
        grad_ref[part, :] = hidden_grad
        bias_ref[2:3, :] += row_sum(hidden_grad)
        attn_low = hidden_grad.astype(low_type)
        attn_low_ref[part, :] = attn_low
        attended_grad = dot_right_t(attn_low, weight_ref[...]).astype(low_type)
        for head in range(heads):
            base = head * 3 * HEAD_DIM
            queries = qkv_ref[rows, base : base + HEAD_DIM]
            key_rows = qkv_ref[rows, base + HEAD_DIM : base + 2 * HEAD_DIM]
            value_rows = qkv_ref[rows, base + 2 * HEAD_DIM : base + 3 * HEAD_DIM]
            probs = probs_ref[part, head * BLOCK : (head + 1) * BLOCK]
            grad_rows = attended_grad[:, head * HEAD_DIM : (head + 1) * HEAD_DIM]
            value_low = dot(probs, grad_rows).astype(low_type)
            prob_grad = dot_right_t(value_rows, grad_rows)
            wide_probs = probs.astype(wide_type)
            weighted = wide_probs * prob_grad
            score_low = (
                weighted - wide_probs * jnp.sum(weighted, axis=0, keepdims=True)
            ).astype(low_type)
            query_low = (dot_left_t(score_low, key_rows) * scale_factor).astype(low_type)
            key_low = (dot(score_low, queries) * scale_factor).astype(low_type)
            grads_ref[part, base : base + HEAD_DIM] = query_low
            grads_ref[part, base + HEAD_DIM : base + 2 * HEAD_DIM] = key_low
            grads_ref[part, base + 2 * HEAD_DIM : base + 3 * HEAD_DIM] = value_low

    over_rows(half, BLOCK, body)


def views(ref, sizes):
    starts = [sum(sizes[:at]) for at in range(len(sizes))]
    return [ref.at[pl.ds(start, size), :] for start, size in zip(starts, sizes)]


def step_kernel(moves, sizes, info_ref, *refs):
    parted = [None if size is None else views(ref, size) for ref, size in zip(refs, sizes)]
    for exchange, step, sources, kept, (sent, place) in moves:
        pairs = []
        for _, keep, (came, at) in sources:
            pairs += [refs[keep], parted[came][at]]
        exchange.kernel(step, [part for part, _, _ in sources], info_ref, *pairs, refs[kept], parted[sent][place])


def late_grads_kernel(
    exchanges, pad, middle, info_ref, act_ref, grads_ref, grads_other_ref, low_ref, low_other_ref, first_ref, last_ref,
    keep_ref, sent_ref, turned_keep_ref, turned_sent_ref, bias_ref, wide_ref,
):
    columns = grads_ref.shape[1]
    first = first_ref.shape[1]
    lower = (info_ref[1] & 1) == 0
    attended = (first_ref[...].astype(wide_type), last_ref[...].astype(wide_type))
    attended_own = jnp.where(lower, attended[0], attended[1]).astype(low_type)
    attended_other = jnp.where(lower, attended[1], attended[0]).astype(low_type)
    act_own, act_other = halves_of(info_ref, (act_ref,))
    wide_ref[:, :first] = dot_left_t(low_ref[...], attended_own) + dot_left_t(
        low_other_ref[...], attended_other
    )
    wide_ref[:, first : first + columns] = dot_left_t(act_own, grads_ref[...]) + dot_left_t(
        act_other, grads_other_ref[...]
    )
    put_blocks(exchanges[0], info_ref, keep_ref, sent_ref, wide_ref.at[:, pl.ds(0, middle)], pad)
    put_blocks(
        exchanges[1], info_ref, turned_keep_ref, turned_sent_ref,
        wide_ref.at[:, pl.ds(middle, wide_ref.shape[1] - middle)], pad,
    )
    bias_ref[...] = row_sum(grads_ref[...].astype(wide_type)) + row_sum(grads_other_ref[...].astype(wide_type))


EXTRA = 16


def put_extra(ref, start, gain, shift):
    rows = []
    for value in (gain, shift):
        rows += list(split_low(value))
    rows.append(jnp.zeros((EXTRA - 4, gain.shape[1]), low_type))
    ref[start : start + EXTRA, :] = jnp.concatenate(rows, axis=0)


def get_extra(ref, start):
    rows = ref[start : start + EXTRA, :].astype(wide_type)
    return rows[0:1] + rows[1:2], rows[2:3] + rows[3:4]


def norm_kernel(rows_ref, normed_ref):
    def body(start, size):
        rows = pl.ds(start, size)
        normed_ref[rows, :] = normalized(rows_ref[rows, :].astype(wide_type))[0].astype(low_type)

    over_rows(rows_ref.shape[0], CHUNK, body)


def input_part_kernel(
    info_ref, normed_ref, grads_ref, grads_other_ref, weight_ref, keep_ref, sent_ref, part_ref, bias_ref
):
    lower_bit = info_ref[1] & 1
    bias_ref[...] = jnp.zeros_like(bias_ref)

    def body(source, rows, part, size):
        grad = dot((grads_ref, grads_other_ref)[source][part, :], weight_ref[...])
        part_ref[rows, :] = grad
        bias_ref[0:1, :] += row_sum(grad * normed_ref[rows, :].astype(wide_type))
        bias_ref[1:2, :] += row_sum(grad)

    both_halves(lower_bit, grads_ref.shape[0], body)
    size = keep_ref.shape[0] - EXTRA
    share = size // (lax.axis_size("mp") // 2)
    for out_ref, which in ((sent_ref, 1 - lower_bit), (keep_ref, lower_bit)):
        for block in range(size // share):
            rows = pl.ds(pl.multiple_of((2 * block + which) * share, share), share)
            out_ref[block * share : (block + 1) * share, :] = part_ref[rows, :].astype(low_type)
        put_extra(out_ref, size, bias_ref[0:1, :], bias_ref[1:2, :])


def input_halve_kernel(bit, info_ref, keep_ref, other_ref, next_keep_ref, next_sent_ref, total_ref):
    upper = (info_ref[1] >> bit) & 1
    half = next_keep_ref.shape[0] - EXTRA
    size = 2 * half
    share = total_ref.shape[0] - size
    total_ref[:size, :] = keep_ref[:size, :].astype(wide_type) + other_ref[:size, :].astype(wide_type)
    own, other = get_extra(keep_ref, size), get_extra(other_ref, size)
    for out_ref, which in ((next_sent_ref, 1 - upper), (next_keep_ref, upper)):
        for block in range(half // share):
            rows = pl.ds(pl.multiple_of((2 * block + which) * share, share), share)
            out_ref[block * share : (block + 1) * share, :] = total_ref[rows, :].astype(low_type)
        put_extra(out_ref, half, own[0] + other[0], own[1] + other[1])


def input_grad_kernel(info_ref, rows_ref, keep_ref, other_ref, grad_ref, grad_other_ref, gain_ref, out_ref):
    share = out_ref.shape[0]
    half = grad_ref.shape[0]
    start = info_ref[1] * share
    rows = pl.ds(pl.multiple_of(start, share), share)
    part = pl.ds(pl.multiple_of(start % half, share), share)
    own = start // half == (info_ref[1] & 1)
    normed, spread = normalized(rows_ref[rows, :].astype(wide_type))
    grad = keep_ref[:share, :].astype(wide_type) + other_ref[:share, :].astype(wide_type)
    hidden_grad = jnp.where(own, grad_ref[part, :], grad_other_ref[part, :])
    out_ref[...] = (hidden_grad + norm_back(grad, normed, spread, wide_row(gain_ref))).astype(low_type)


VECTOR_ROWS = 48


def put_rows(values, rows_ref):
    row = 0
    for value in values:
        for tile in range(value.shape[1] // LANES):
            rows_ref[row : row + 1, :] = value[:, tile * LANES : (tile + 1) * LANES]
            row += 1


def take_rows(rows_ref, refs):
    row = 0
    for ref in refs:
        size = ref.shape[0]
        for tile in range(-(-size // LANES)):
            width = min(LANES, size - tile * LANES)
            ref[tile * LANES : tile * LANES + width] = rows_ref[row, :width]
            row += 1


def encoded_kernel(
    info_ref, hidden_ref, sum_ref, sum_other_ref, down_bias_ref, weight_ref, bias_ref, enc_ref, encoded_ref, wide_ref,
    low_ref,
):
    down_bias, bias = wide_row(down_bias_ref), wide_row(bias_ref)

    def body(source, rows, part, size):
        total = (sum_ref, sum_other_ref)[source][part, :].astype(wide_type)
        out_low = (hidden_ref[rows, :] + total + down_bias).astype(low_type)
        low_ref[rows, :] = out_low
        encoded_ref[rows, :] = (dot(out_low, weight_ref[...]) + bias).astype(low_type)

    both_halves(info_ref[1] & 1, sum_ref.shape[0], body)
    wide_ref[...] = dot_left_t(low_ref[...], enc_ref[...])


def last_kernel(
    info, exchange, heads, pad, info_ref, encoded_ref, wide_ref, enc_ref, pos_ref, mask_ref, grads_ref, grads_other_ref,
    second_ref, second_other_ref, qkv_ref, first_ref, first_other_ref, keep_ref, sent_ref, rows_ref,
):
    put_blocks(exchange, info_ref, keep_ref, sent_ref, wide_ref, 0)
    put_blocks(exchange, info_ref, keep_ref, sent_ref, pos_ref, 0, pad)
    for ref, indices in exchange.targets(0, info_ref, keep_ref, sent_ref):
        at = exchange.moved_at(0)
        for index in indices:
            image = info.image(info_ref, index)
            ref[at : at + VIS, :] = encoded_ref[pl.ds(pl.multiple_of(image * VIS, VIS), VIS), :]
            at += VIS
    qkv, early = qkv_ref[...], grads_ref[...] + grads_other_ref[...]
    second = second_ref[...] + second_other_ref[...]
    empty = jnp.zeros((1, 2 * LANES - heads * HEAD_DIM), wide_type)
    spread = []
    for part in (0, 2):
        spread += [
            qkv[:, (3 * head + part) * HEAD_DIM : (3 * head + part + 1) * HEAD_DIM] for head in range(heads)
        ] + [empty]
    own = get_extra(first_ref, first_ref.shape[0] - EXTRA)
    other = get_extra(first_other_ref, first_ref.shape[0] - EXTRA)
    put_rows(
        (
            jnp.concatenate(spread, axis=1), early[1:2], row_sum(enc_ref[...].astype(wide_type)), mask_ref[...],
            own[0] + other[0], own[1] + other[1], second[0:1], second[1:2], second[2:3],
            early[0:1],
        ),
        rows_ref,
    )
    for ref in (keep_ref, sent_ref):
        ref[exchange.shared_at(0) :, :] = rows_ref[...].astype(low_type)


def base_kernel(info, info_ref, seen_ref, mask_ref, layout_ref, base_ref):
    cells = lax.broadcasted_iota(jnp.int32, (GRID, VIS), 0)
    cell_column = lax.broadcasted_iota(jnp.int32, (GRID, 1), 0)
    mask_row = wide_row(mask_ref)

    def one_slot(slot):
        size = info.cells(info_ref, slot)
        seen = (seen_ref[pl.ds(slot, 1), :] == cells).astype(wide_type)
        fill = (cell_column < size).astype(wide_type) - jnp.sum(seen, axis=1, keepdims=True)
        base_ref[slot] = fill * mask_row + layout_ref[side_of(size)]

    over_slots(info.count, one_slot)


def late_out_kernel(
    info, exchange, turned_exchange, pad, middle, sizes, info_ref, seen_ref, keep_ref, turned_ref, came_ref, base_ref,
    grids_ref, out_ref, qkv_ref, proj_ref, pos_ref, *refs
):
    *vector_refs, wide_ref, rows_ref = refs
    other_ref, turned_other_ref = views(came_ref, sizes)
    cells = lax.broadcasted_iota(jnp.int32, (GRID, VIS), 0)
    for relative, ref, start in exchange.arrived(keep_ref, other_ref):
        slot = info_ref[0] ^ relative
        seen = seen_ref[pl.ds(slot, 1), :] == cells
        placed = dot(seen.astype(low_type), ref[start : start + VIS, :])
        grids_ref[slot] = (placed + base_ref[slot]).astype(low_type)
    share = proj_ref.shape[0]
    tiles = wide_ref.shape[1] // LANES
    for tile in range(tiles):
        here = (exchange, keep_ref, other_ref, tile) if tile < middle else (
            turned_exchange, turned_ref, turned_other_ref, tile - middle
        )
        wide_ref[:, tile * LANES : (tile + 1) * LANES] = here[0].total(here[1], here[2], here[3] * pad, share)
    columns = out_ref.shape[0]
    wide_out = -(-columns // LANES) * LANES
    out_ref[...] = wide_ref[:, :wide_out].T[:columns]
    qkv_ref[...] = wide_ref[:, columns:]
    proj_ref[...] = exchange.total(keep_ref, other_ref, middle * pad, share)
    pos_ref[...] = exchange.total(keep_ref, other_ref, (middle + 1) * pad, pos_ref.shape[0])
    rows_ref[...] = exchange.shared_total(keep_ref, other_ref)
    take_rows(rows_ref, vector_refs)


def early_out_kernel(exchanges, pad, *refs):
    for exchange, keep_ref, other_ref, out_ref in zip(exchanges, refs[:2], refs[2:4], refs[4:]):
        for tile in range(out_ref.shape[1] // LANES):
            out_ref[:, tile * LANES : (tile + 1) * LANES] = exchange.total(
                keep_ref, other_ref, tile * pad, out_ref.shape[0]
            )


def swap(value, axis, bit):
    count = lax.axis_size(axis)
    return lax.ppermute(value, axis, [(i, i ^ bit) for i in range(count)])


def local(
    patch_rows, patches, visible, owner, qkv_weight, query_bias, value_bias, out_weight, out_bias, first_gain,
    first_shift, second_gain, second_shift, up_weight, up_bias, down_weight, down_bias, proj_weight, proj_bias,
    mask_token, decoder_pos, grid_cotangent,
):
    count = lax.axis_size("dp")
    parts = lax.axis_size("mp")
    where = jnp.stack([lax.axis_index("dp"), lax.axis_index("mp")]).astype(jnp.int32)
    rows, width = patch_rows.shape
    images = rows // VIS
    heads = qkv_weight.shape[1] // (3 * HEAD_DIM)
    head_columns = heads * HEAD_DIM
    qkv_columns = qkv_weight.shape[1]
    units = up_weight.shape[1]
    columns = proj_weight.shape[1]
    share = width // count
    pos_share = GRID // count
    half = rows // 2
    own_rows = rows // parts
    pads = (-(-share // 16) * 16, -(-pos_share // 16) * 16)
    run = Order(rows <= PINNED_ROWS)

    tables = grid_tables()
    table_high = tables.astype(low_type)
    table_low = (tables - table_high.astype(np.float32)).astype(low_type)
    turned_high = jnp.asarray(np.ascontiguousarray(table_high.transpose(0, 2, 1)))
    turned_low = jnp.asarray(np.ascontiguousarray(table_low.transpose(0, 2, 1)))
    table_high, table_low = jnp.asarray(table_high), jnp.asarray(table_low)
    qkv_weight_t = qkv_weight.T
    run.leave(owner, visible, patches, grid_cotangent, turned_high, turned_low, table_high, table_low, decoder_pos)
    info = Info(count)
    bits = tuple(range(count.bit_length() - 1))
    late_columns = qkv_columns + head_columns
    turned = (1, 0) + bits[2:]
    back_exchange = Exchange(count, bits, 0, moved=VIS)
    far = bits
    up_exchange = Exchange(count, far, units // LANES * pads[0])
    down_exchange = Exchange(count, turned, units // LANES * pads[0])
    tiles = late_columns // LANES
    middle = 3 * tiles // 6
    late_exchange = Exchange(count, bits, middle * pads[0])
    turned_exchange = Exchange(count, turned, (tiles - middle) * pads[0])
    last_exchange = Exchange(count, bits, sum(pads), moved=VIS, shared=VECTOR_ROWS)
    joint_exchange = Exchange(
        count, bits, late_exchange.block + last_exchange.block, moved=VIS, shared=VECTOR_ROWS
    )

    def low(*shape):
        return (shape, low_type)

    def wide(*shape):
        return (shape, wide_type)

    def moved(value, axis, bit):
        return run.keep(swap(value, axis, bit))

    def model_steps(keep, received):
        (total,) = run(add_kernel, [low(half, width)], (keep, received), cost=0.6)
        bit = 2
        while bit < parts:
            received = moved(total, "mp", bit)
            yield
            (total,) = run(add_kernel, [low(half, width)], (total, received), cost=0.6)
            bit *= 2
        other = moved(total, "mp", 1)
        yield
        return total, other

    def model_gather(value):
        values = {0: value}
        bit = parts // 2
        while bit:
            values.update({other | bit: moved(values[other], "mp", bit) for other in tuple(values)})
            bit //= 2
        return tuple(values[at] for at in range(parts))

    def data_step(step, exchange, pairs):
        keep, sent = run(
            lambda *refs: exchange.kernel(step, [part for part, _, _ in pairs], *refs),
            [low(exchange.rows(step), LANES)] * 2,
            (facts,) + tuple(array for _, *arrays in pairs for array in arrays),
            (SMEM,) + (VMEM,) * (2 * len(pairs)),
            cost=1.2,
        )
        return keep, moved(sent, "dp", 2 ** exchange.bits[step])

    def data_steps(exchange, keep, sent):
        received = moved(sent, "dp", 2 ** exchange.bits[0])
        yield keep, received
        for step in range(1, len(exchange.bits)):
            keep, received = data_step(step, exchange, [(exchange, keep, received)])
            yield keep, received

    def steps(kept, arrays, moves, sends, cost=1.0):
        first = len(kept) + len(arrays)
        sizes = [None] * len(kept) + [size for _, size in arrays] + [None] * len(moves)
        sizes += [size for _, size in sends]
        placed = [
            (exchange, step, sources, first + at, (first + len(moves) + to[0], to[1]))
            for at, (exchange, step, sources, to) in enumerate(moves)
        ]
        results = run(
            lambda *refs: step_kernel(placed, sizes, *refs),
            [low(exchange.rows(step), LANES) for exchange, step, _, _ in moves]
            + [low(sum(size), LANES) for _, size in sends],
            (facts, *kept) + tuple(array for array, _ in arrays),
            (SMEM,) + (VMEM,) * first,
            cost=cost,
        )
        return results[: len(moves)], [
            moved(sent, "dp", 2**bit) for sent, (bit, _) in zip(results[len(moves) :], sends)
        ]

    def finish_pair(steps):
        *_, last = steps
        return last

    def finish(steps):
        while True:
            try:
                next(steps)
            except StopIteration as stop:
                return stop.value

    out_all = model_gather(out_weight)
    proj_all = model_gather(proj_weight)
    (
        back_keep, back_sent, facts, seen, patch_rows, qkv_weight_t, first_gain, first_shift, query_bias, value_bias,
    ) = run(
        lambda *refs: cotangent_kernel(info, back_exchange, *refs),
        [
            low(back_exchange.rows(0), columns), low(back_exchange.rows(0), columns), ((info.size,), jnp.int32),
            ((count, VIS), jnp.int32),
        ],
        (where, owner, patches, visible, grid_cotangent),
        (SMEM, SMEM, SMEM, VMEM, VMEM),
        out_specs=(VMEM, VMEM, SMEM, VMEM),
        scratch=[pltpu.VMEM((VIS, count), wide_type)],
        stage=(patch_rows, qkv_weight_t, first_gain, first_shift, query_bias, value_bias),
        cost=3.0,
    )
    back_steps = data_steps(back_exchange, back_keep, back_sent)
    next(back_steps)
    act_one, qkv = run(
        enter_kernel,
        [low(rows, width), low(rows, qkv_columns)],
        (patch_rows, first_gain, first_shift, qkv_weight_t, query_bias, value_bias),
        cost=1.2,
        after=(out_all[1], proj_all[1]),
    )
    next(back_steps)
    packed_rows = half * head_columns // LANES
    packed, first_probs, first_attended, out_bias, second_gain, second_shift, up_weight, up_bias = run(
        lambda *refs: attention_kernel(info, heads, 0, *refs),
        [low(packed_rows, LANES), low(half, heads * BLOCK), low(half, head_columns)],
        (facts, qkv),
        (SMEM, VMEM),
        stage=(out_bias, second_gain, second_shift, up_weight, up_bias),
        cost=2.8,
    )
    first_all = model_gather(packed)
    back_own, back_other = finish_pair(back_steps)
    (
        packed, last_probs, last_attended, down_weight, down_bias, proj_bias, out_near, proj_near, out_core, proj_core
    ) = run(
        lambda *refs: attention_kernel(info, heads, half, *refs),
        [low(packed_rows, LANES), low(half, heads * BLOCK), low(half, head_columns)],
        (facts, qkv),
        (SMEM, VMEM),
        stage=(down_weight, down_bias, proj_bias, out_weight, proj_weight, out_all[1], proj_all[1]),
        cost=2.5,
        after=(out_all[parts // 2], proj_all[parts // 2]),
    )
    last_all = model_gather(packed)
    out_whole, proj_whole = run(
        lambda *refs: weights_kernel(parts, *refs),
        [low(parts * head_columns, width), low(width, parts * columns)],
        (facts, out_near, out_core) + out_all[2:] + (proj_near, proj_core) + proj_all[2:],
        (SMEM,) + (VMEM,) * (2 * parts),
        cost=0.0,
    )
    (enc_grad,) = run(
        lambda *refs: back_kernel(info, back_exchange, *refs),
        [low(rows, columns)],
        (facts, back_own, back_other),
        (SMEM, VMEM, VMEM),
        cost=0.4,
    )
    enc_all = model_gather(enc_grad)
    hidden, act_two, acted, slope = run(
        lambda *refs: forward_kernel(parts, head_columns, *refs),
        [wide(rows, width), low(rows, width), low(rows, units), wide(rows, units)],
        (facts, patch_rows, out_bias, second_gain, second_shift, up_weight, up_bias, out_whole)
        + first_all
        + last_all,
        (SMEM,) + (VMEM,) * (7 + 2 * parts),
        scratch=[pltpu.VMEM((BLOCK, parts * head_columns), low_type)],
        cost=2.6,
    )

    def forward_grad(own):
        return run(
            lambda *refs: forward_grad_kernel(parts, own, *refs),
            [low(half, width), low(half, units), low(half, width), wide(2, width)],
            (facts, slope, up_weight, down_weight, proj_whole) + enc_all,
            (SMEM,) + (VMEM,) * (4 + parts),
            scratch=[pltpu.VMEM((BLOCK, parts * columns), low_type)],
            cost=1.2,
        )

    sent, up_low_other, down_low_other, bias_grads_other = forward_grad(False)
    second_other = moved(sent, "mp", 1)
    keep, up_low, down_low, bias_grads = forward_grad(True)
    second_steps = model_steps(keep, second_other)
    next(second_steps)
    down_keep, down_sent, up_keep, up_sent = run(
        lambda *refs: early_grads_kernel((down_exchange, up_exchange), pads[0], *refs),
        [low(down_exchange.rows(0), LANES)] * 2 + [low(up_exchange.rows(0), LANES)] * 2,
        (facts, down_low, down_low_other, acted, act_two, up_low, up_low_other),
        (SMEM,) + (VMEM,) * 6,
        scratch=[pltpu.VMEM((width, units), wide_type)],
        cost=2.2,
    )
    down_pair = (down_keep, moved(down_sent, "dp", 2 ** turned[0]))
    up_pair = (up_keep, moved(up_sent, "dp", 2 ** bits[0]))
    keep, sent = run(
        forward_part_kernel,
        [low(half, width), low(half, width)],
        (facts, acted, down_weight),
        (SMEM, VMEM, VMEM),
        cost=0.7,
    )
    out_steps = model_steps(keep, moved(sent, "mp", 1))

    pos_grad_own, mask_grad, layouts = run(
        lambda *refs: position_kernel(info, *refs),
        [wide(GRID, columns), wide(1, columns), wide(3, GRID, columns)],
        (facts, seen, grid_cotangent, turned_high, turned_low, table_high, table_low, decoder_pos),
        (SMEM,) + (VMEM,) * 7,
        scratch=[pltpu.VMEM((3, GRID, columns), wide_type)],
        cost=20.0,
    )
    next(out_steps)
    (normed_low,) = run(norm_kernel, [low(rows, width)], (patch_rows,), cost=0.6)
    next(second_steps)
    second_sum, second_other = finish(second_steps)

    def attention_back(own, total, down_part, cost):
        return run(
            lambda *refs: attention_back_kernel(heads, own, *refs),
            [low(half, qkv_columns), low(half, width), wide(half, width), wide(3, width)],
            (facts, total, hidden, down_part, second_gain, out_near, qkv, first_probs, last_probs),
            (SMEM,) + (VMEM,) * 8,
            scratch=[pltpu.VMEM((half, heads * BLOCK), low_type)],
            cost=cost,
        )

    grads, attn_low, hidden_grad, second_grads = attention_back(True, second_sum, down_low, COVER)
    run.share = 2.0
    grads_other, attn_low_other, hidden_grad_other, second_grads_other = attention_back(
        False, second_other, down_low_other, 2.0
    )
    in_keep, in_sent = run(
        input_part_kernel,
        [low(half + EXTRA, width)] * 2,
        (facts, normed_low, grads, grads_other, qkv_weight_t),
        (SMEM,) + (VMEM,) * 4,
        scratch=[pltpu.VMEM((rows, width), wide_type), pltpu.VMEM((2, width), wide_type)],
        cost=2.0,
    )
    in_other = moved(in_sent, "mp", 1)
    in_other = moved(in_sent, "mp", 1)
    late_keep, late_sent, turned_keep, turned_sent, qkv_bias_grad = run(
        lambda *refs: late_grads_kernel((late_exchange, turned_exchange), pads[0], middle * LANES, *refs),
        [low(late_exchange.rows(0), LANES)] * 2
        + [low(turned_exchange.rows(0), LANES)] * 2
        + [wide(1, qkv_columns)],
        (facts, act_one, grads, grads_other, attn_low, attn_low_other, first_attended, last_attended),
        (SMEM,) + (VMEM,) * 7,
        scratch=[pltpu.VMEM((width, late_columns), wide_type)],
        cost=40.0,
    )
    turned_came = moved(turned_sent, "dp", 2 ** turned[0])
    late_came = moved(late_sent, "dp", 2 ** bits[0])
    bit = 1
    size = half
    while 2**bit < parts:
        in_keep, in_sent = run(
            lambda *refs, bit=bit: input_halve_kernel(bit, *refs),
            [low(size // 2 + EXTRA, width)] * 2,
            (facts, in_keep, in_other),
            (SMEM, VMEM, VMEM),
            scratch=[pltpu.VMEM((size + own_rows, width), wide_type)],
            cost=1.1,
            after=(up_pair[1], down_pair[1]),
        )
        in_other = moved(in_sent, "mp", 2**bit)
        size //= 2
        bit += 1
    next(out_steps)
    early_sizes = [[exchange.rows(1)] for exchange in (up_exchange, down_exchange)]
    (up_keep,), (up_came,) = steps(
        (up_pair[0],),
        ((up_pair[1], [up_exchange.rows(0)]),),
        [(up_exchange, 1, [(up_exchange, 0, (1, 0))], (0, 0))],
        [(far[1], early_sizes[0])],
        cost=40.0,
    )
    out_sum, out_other = finish(out_steps)
    encoded, proj_grad = run(
        encoded_kernel,
        [low(rows, columns), wide(width, columns)],
        (facts, hidden, out_sum, out_other, down_bias, proj_near, proj_bias, enc_grad),
        (SMEM,) + (VMEM,) * 7,
        scratch=[pltpu.VMEM((rows, width), low_type)],
        cost=1.0,
    )
    last_keep, last_sent = run(
        lambda *refs: last_kernel(info, last_exchange, heads, pads[0], *refs),
        [low(last_exchange.rows(0), LANES)] * 2,
        (
            facts, encoded, proj_grad, enc_grad, pos_grad_own, mask_grad, bias_grads, bias_grads_other, second_grads,
            second_grads_other, qkv_bias_grad, in_keep, in_other,
        ),
        (SMEM,) + (VMEM,) * 12,
        scratch=[pltpu.VMEM((VECTOR_ROWS, LANES), wide_type)],
        cost=0.6,
    )
    last_came = moved(last_sent, "dp", 2 ** bits[0])
    (down_keep,), (down_came,) = steps(
        (down_pair[0],),
        ((down_pair[1], [down_exchange.rows(0)]),),
        [(down_exchange, 1, [(down_exchange, 0, (1, 0))], (0, 0))],
        [(turned[1], early_sizes[1])],
    )
    (input_grad,) = run(
        input_grad_kernel,
        [low(own_rows, width)],
        (facts, patch_rows, in_keep, in_other, hidden_grad, hidden_grad_other, first_gain),
        (SMEM,) + (VMEM,) * 6,
        final=True,
        cost=0.8,
    )

    early = (up_exchange, down_exchange)
    late = (joint_exchange, turned_exchange)
    (base,) = run(
        lambda *refs: base_kernel(info, *refs),
        [wide(count, GRID, columns)],
        (facts, seen, mask_token, layouts),
        (SMEM,) + (VMEM,) * 3,
        cost=0.8,
    )
    joint_sizes = [[exchange.rows(1)] for exchange in late]
    (late_keep, turned_keep), late_came = steps(
        (late_keep, last_keep, turned_keep),
        (
            (late_came, [late_exchange.rows(0)]), (last_came, [last_exchange.rows(0)]),
            (turned_came, [turned_exchange.rows(0)]),
        ),
        [
            (joint_exchange, 1, [(late_exchange, 0, (3, 0)), (last_exchange, 1, (4, 0))], (0, 0)),
            (turned_exchange, 1, [(turned_exchange, 2, (5, 0))], (1, 0)),
        ],
        [(bits[1], joint_sizes[0]), (turned[1], joint_sizes[1])],
    )
    (up_keep,), (up_came,) = steps(
        (up_keep,),
        ((up_came, early_sizes[0]),),
        [(up_exchange, 2, [(up_exchange, 0, (1, 0))], (0, 0))],
        [(far[2], [up_exchange.rows(2)])],
    )
    (down_keep,), (down_came,) = steps(
        (down_keep,),
        ((down_came, early_sizes[1]),),
        [(down_exchange, 2, [(down_exchange, 0, (1, 0))], (0, 0))],
        [(turned[2], [down_exchange.rows(2)])],
    )
    early_came = (up_came, down_came)
    early_sizes = [[exchange.rows(2)] for exchange in early]
    last_sizes = [exchange.rows(2) for exchange in late]
    (late_keep, turned_keep), (late_came,) = steps(
        (late_keep, turned_keep),
        ((late_came[0], joint_sizes[0]), (late_came[1], joint_sizes[1])),
        [
            (joint_exchange, 2, [(joint_exchange, 0, (2, 0))], (0, 0)),
            (turned_exchange, 2, [(turned_exchange, 1, (3, 0))], (0, 1)),
        ],
        [(2, last_sizes)],
    )
    for step in range(3, len(bits)):
        old_sizes, early_sizes = early_sizes, [[exchange.rows(step)] for exchange in early]
        (up_keep, down_keep), early_came = steps(
            (up_keep, down_keep),
            ((early_came[0], old_sizes[0]), (early_came[1], old_sizes[1])),
            [(exchange, step, [(exchange, at, (2 + at, 0))], (at, 0)) for at, exchange in enumerate(early)],
            [(step, early_sizes[0]), (step, early_sizes[1])],
        )
        old_sizes, last_sizes = last_sizes, [exchange.rows(step) for exchange in late]
        (late_keep, turned_keep), (late_came,) = steps(
            (late_keep, turned_keep),
            ((late_came, old_sizes),),
            [(exchange, step, [(exchange, at, (2, at))], (0, at)) for at, exchange in enumerate(late)],
            [(step, last_sizes)],
        )
    up_weight_grad, down_weight_grad = run(
        lambda *refs: early_out_kernel(early, pads[0], *refs),
        [wide(share, units)] * 2,
        (up_keep, down_keep, *early_came),
        final=True,
        cost=1.0,
    )
    (
        grids, out_weight_grad, qkv_weight_grad, proj_weight_grad, pos_grad, query_bias_grad, value_bias_grad,
        up_bias_grad, proj_bias_grad, mask_token_grad, first_gain_grad, first_shift_grad, second_gain_grad,
        second_shift_grad, out_bias_grad, down_bias_grad,
    ) = run(
        lambda *refs: late_out_kernel(info, joint_exchange, turned_exchange, pads[0], middle, last_sizes, *refs),
        [
            low(count, GRID, columns), wide(head_columns, share), wide(share, qkv_columns), wide(share, columns),
            wide(pos_share, columns),
        ]
        + [wide(size) for size in (head_columns, head_columns, units, columns, columns) + (width,) * 6],
        (facts, seen, late_keep, turned_keep, late_came, base),
        (SMEM,) + (VMEM,) * 5,
        scratch=[pltpu.VMEM((share, late_columns), wide_type), pltpu.VMEM((VECTOR_ROWS, LANES), wide_type)],
        final=True,
        cost=2.5,
    )
    return (
        grids, input_grad, qkv_weight_grad, query_bias_grad, value_bias_grad, out_weight_grad, out_bias_grad,
        first_gain_grad, first_shift_grad, second_gain_grad, second_shift_grad, up_weight_grad, up_bias_grad,
        down_weight_grad.T, down_bias_grad, proj_weight_grad, proj_bias_grad, mask_token_grad, pos_grad,
    )


def solution(mesh):
    return jax.shard_map(
        local,
        mesh=mesh,
        in_specs=(
            P("dp", None), P(), P(), P(), P(None, "mp"), P("mp"), P("mp"), P("mp", None), P(), P(), P(), P(), P(),
            P(None, "mp"), P("mp"), P("mp", None), P(), P(None, "mp"), P("mp"), P("mp"), P(None, "mp"),
            P("dp", None, "mp"),
        ),
        out_specs=(
            P("dp", None, "mp"), P(("dp", "mp"), None), P("dp", "mp"), P("mp"), P("mp"), P("mp", "dp"), P(), P(),
            P(), P(), P(), P("dp", "mp"), P("mp"), P("mp", "dp"), P(), P("dp", "mp"), P("mp"), P("mp"),
            P("dp", "mp"),
        ),
        check_vma=False,
    )
```

```python
import math

import jax
import jax.numpy as jnp
import numpy as np
from jax import lax
from jax.experimental import pallas as pl
from jax.experimental.pallas import tpu as pltpu
from jax.sharding import PartitionSpec as P

HEAD_DIM = 64
GRID = 256
VIS = 64
CHUNK = 512
LANES = 128

epsilon = 1e-06
low_type = jnp.bfloat16
wide_type = jnp.float32
scale_factor = HEAD_DIM ** (-0.5)

VMEM = pl.BlockSpec(memory_space=pltpu.VMEM)
SMEM = pl.BlockSpec(memory_space=pltpu.SMEM)
ANY = pl.BlockSpec(memory_space=pl.ANY)
PINNED_ROWS = 512


def grid_tables():
    grid_edge = math.isqrt(GRID)
    tables = []
    for side_cells in (10, 14):
        places = np.arange(side_cells)
        centers = ((2 * places + 1) * grid_edge - side_cells) / (2 * side_cells)
        lower = np.floor(centers).astype(np.int64)
        share = centers - lower
        lerp = np.zeros((side_cells, grid_edge))
        lerp[places, np.clip(lower, 0, grid_edge - 1)] += 1.0 - share
        lerp[places, np.clip(lower + 1, 0, grid_edge - 1)] += share
        table = np.zeros((GRID, GRID))
        table[: side_cells * side_cells] = np.kron(lerp, lerp)
        tables.append(table)
    return np.stack(tables).astype(np.float32)


def split_low(value):
    high = value.astype(low_type)
    return high, (value - high.astype(wide_type)).astype(low_type)


def dot(left, right):
    return lax.dot_general(left, right, (((1,), (0,)), ((), ())), preferred_element_type=wide_type)


def dot_right_t(left, right):
    return lax.dot_general(left, right, (((1,), (1,)), ((), ())), preferred_element_type=wide_type)


def dot_left_t(left, right):
    return lax.dot_general(left, right, (((0,), (0,)), ((), ())), preferred_element_type=wide_type)


def normalized(value):
    center = value - jnp.mean(value, axis=-1, keepdims=True)
    spread = lax.rsqrt(jnp.mean(center * center, axis=-1, keepdims=True) + epsilon)
    return center * spread, spread


def norm_back(grad, normed, spread, gain):
    scaled = grad * gain
    mean_one = jnp.mean(scaled, axis=-1, keepdims=True)
    mean_two = jnp.mean(scaled * normed, axis=-1, keepdims=True)
    return spread * (scaled - mean_one - normed * mean_two)


def row_sum(value):
    return jnp.sum(value, axis=0, keepdims=True)


def over_rows(total, size, body):
    size = min(size, total)
    if total <= 2 * size:
        for start in range(0, total, size):
            body(start, size)
        return

    def step(i, carry):
        body(pl.multiple_of(i * size, size), size)
        return carry

    lax.fori_loop(0, total // size, step, 0)


def size_of(shape, kind):
    return math.prod(shape) * jnp.dtype(kind).itemsize


RATE = 10**9
COST_SHARE = 1.0
COVER = 40.0
BYTES = 0


class Order:
    def __init__(self, pinned):
        self.pinned = pinned
        self.last = None
        self.near = []
        self.far = []
        self.share = COST_SHARE

    def keep(self, value):
        if self.pinned:
            self.near.append((value, pltpu.VMEM))
        return value

    def leave(self, *values):
        self.far += values

    def placed(self, value):
        for near, space in self.near:
            if value is near:
                return pltpu.with_memory_space_constraint(value, space)
        if any(value is far for far in self.far):
            return pltpu.with_memory_space_constraint(value, pltpu.HBM)
        return value

    def __call__(
        self, kernel, outs, args, specs=None, scratch=(), out_specs=None, final=False, stage=(), cost=1.0, after=()
    ):
        args = tuple(args)
        specs = [VMEM] * len(args) if specs is None else list(specs)
        out_specs = [VMEM] * len(outs) if out_specs is None else list(out_specs)
        count, results_count = len(args), len(outs)
        staged = list(stage) if self.pinned else []
        self.leave(*staged)
        needed = sum(size_of(ref.shape, ref.dtype) for ref in scratch)
        needed += sum(
            size_of(arg.shape, arg.dtype) for arg in args if not any(arg is near for near, _ in self.near)
        )
        shapes = []
        for (shape, kind), spec in zip(outs, out_specs):
            if self.pinned and not final:
                shapes.append((pltpu.SMEM if spec is SMEM else pltpu.VMEM)(shape, kind))
            else:
                shapes.append(jax.ShapeDtypeStruct(shape, kind))
                needed += size_of(shape, kind)
        tail = len(staged)
        args += tuple(staged)
        specs += [ANY] * tail
        unread = tuple(after) if self.last is None else (*after, self.last)
        skipped = len(unread)
        args += unread
        specs += [ANY] * skipped

        def body(*refs):
            own, sources, refs = refs[:count], refs[count : count + tail], refs[count + tail + skipped :]
            results, targets, refs = (
                refs[:results_count], refs[results_count : results_count + tail], refs[results_count + tail :]
            )
            copies = []
            if tail:
                *refs, sems = refs
                copies = [
                    pltpu.make_async_copy(source, target, sems.at[at])
                    for at, (source, target) in enumerate(zip(sources, targets))
                ]
            for copy in copies:
                copy.start()
            kernel(*own, *results, *refs)
            for copy in copies:
                copy.wait()

        results = pl.pallas_call(
            body,
            out_shape=tuple(shapes) + tuple(pltpu.VMEM(array.shape, array.dtype) for array in staged),
            in_specs=specs,
            out_specs=tuple(out_specs) + (VMEM,) * tail,
            scratch_shapes=list(scratch) + ([pltpu.SemaphoreType.DMA((tail,))] if tail else []),
            compiler_params=pltpu.CompilerParams(
                vmem_limit_bytes=min(needed + needed // 4 + 10 * 2**20, 60 * 2**20)
            ),
            cost_estimate=pl.CostEstimate(
                flops=int(cost * RATE * self.share), bytes_accessed=int(cost * BYTES), transcendentals=0
            ),
        )(*(self.placed(arg) for arg in args))
        if self.pinned and not final:
            for result, spec in zip(results, out_specs + [VMEM] * tail):
                self.near.append((result, pltpu.SMEM if spec is SMEM else pltpu.VMEM))
        if not final:
            self.last = results[0]
        if stage and not self.pinned:
            return (*results, *stage)
        return results


class Info:
    def __init__(self, count):
        self.count = count
        self.size = 2 + 5 * count

    def dp(self, ref):
        return ref[0]

    def mp(self, ref):
        return ref[1]

    def owner(self, ref, image):
        return ref[2 + image]

    def live(self, ref, image):
        return ref[2 + self.count + image]

    def source(self, ref, slot):
        return ref[2 + 2 * self.count + slot]

    def cells(self, ref, slot):
        return ref[2 + 3 * self.count + slot]

    def image(self, ref, owner):
        return ref[2 + 4 * self.count + owner]


def fill_info(count, where_ref, owner_ref, patches_ref, info_ref):
    me = where_ref[0]
    info_ref[0] = me
    info_ref[1] = where_ref[1]

    def one(at):
        own = me * count + at
        info_ref[2 + at] = owner_ref[own]
        info_ref[2 + 4 * count + owner_ref[own]] = at
        info_ref[2 + count + at] = patches_ref[own] // 4

        def find(i, found):
            return jnp.where(owner_ref[at * count + i] == me, at * count + i, found)

        source = lax.fori_loop(0, count, find, at * count, unroll=count <= 8)
        info_ref[2 + 2 * count + at] = source
        info_ref[2 + 3 * count + at] = patches_ref[source]

    over_slots(count, one)


def over_slots(count, one_slot):
    if count <= 8:
        for slot in range(count):
            one_slot(slot)
    else:
        lax.fori_loop(0, count, lambda slot, carry: (one_slot(slot), carry)[1], 0)


def side_of(size):
    return (size >= 196).astype(jnp.int32) + (size >= 256).astype(jnp.int32)


def block_at(rest, place, bit):
    low = rest & ((1 << place) - 1)
    return ((rest - low) << 1) + (bit << place) + low


class Exchange:
    def __init__(self, count, bits, block, moved=0, shared=0):
        self.count, self.bits, self.block, self.moved, self.shared = count, bits, block, moved, shared

    def blocks(self, step):
        return self.count >> (step + 1)

    def place(self, step):
        bit = self.bits[step]
        return bit - sum(done < bit for done in self.bits[:step])

    def moved_at(self, step):
        return self.blocks(step) * self.block

    def shared_at(self, step):
        return self.moved_at(step) + self.count // 2 * self.moved

    def rows(self, step):
        return self.shared_at(step) + self.shared

    def own_bit(self, step, info_ref):
        return (info_ref[0] >> self.bits[step]) & 1

    def targets(self, step, info_ref, keep_ref, sent_ref):
        own = self.own_bit(step, info_ref)
        place = self.place(step)
        for ref, which in ((sent_ref, 1 - own), (keep_ref, own)):
            yield ref, [block_at(block, place, which) for block in range(self.blocks(step))]

    def kernel(self, step, parts, info_ref, *refs):
        *from_refs, next_keep_ref, next_sent_ref = refs
        pairs = list(zip(parts, from_refs[::2], from_refs[1::2]))
        sources = 1 << (step - 1)
        rests = self.blocks(step - 1)
        for ref, indices in self.targets(step, info_ref, next_keep_ref, next_sent_ref):
            first, moved_at, shared_at = 0, self.moved_at(step), self.shared_at(step)
            for part, keep_ref, other_ref in pairs:
                for block, index in enumerate(indices if part.block else ()):
                    rows = pl.ds(pl.multiple_of(index * part.block, 16), part.block)
                    at = block * self.block + first
                    ref[at : at + part.block, :] = (
                        keep_ref[rows, :].astype(wide_type) + other_ref[rows, :].astype(wide_type)
                    ).astype(low_type)
                first += part.block
                for from_ref in (keep_ref, other_ref) if part.moved else ():
                    for source in range(sources):
                        for index in indices:
                            rows = part.moved_at(step - 1) + (source * rests + index) * part.moved
                            ref[moved_at : moved_at + part.moved, :] = from_ref[
                                pl.ds(pl.multiple_of(rows, 16), part.moved), :
                            ]
                            moved_at += part.moved
                if part.shared:
                    at = part.shared_at(step - 1)
                    rows = slice(at, at + part.shared)
                    ref[shared_at : shared_at + part.shared, :] = (
                        keep_ref[rows, :].astype(wide_type) + other_ref[rows, :].astype(wide_type)
                    ).astype(low_type)

    def arrived(self, keep_ref, other_ref):
        last = len(self.bits) - 1
        sources = 1 << last
        for half, ref in enumerate((keep_ref, other_ref)):
            for source in range(sources):
                relative = 0
                for step, bit in enumerate(self.bits):
                    relative |= (((source + half * sources) >> step) & 1) << bit
                yield relative, ref, self.moved_at(last) + source * self.moved

    def total(self, keep_ref, other_ref, start, size):
        rows = slice(start, start + size)
        return keep_ref[rows, :].astype(wide_type) + other_ref[rows, :].astype(wide_type)

    def shared_total(self, keep_ref, other_ref):
        return self.total(keep_ref, other_ref, self.shared_at(len(self.bits) - 1), self.shared)


def cotangent_kernel(
    info, exchange, where_ref, owner_ref, patches_ref, visible_ref, cot_ref, keep_ref, sent_ref, info_ref, seen_ref,
    turned_ref,
):
    count = info.count
    fill_info(count, where_ref, owner_ref, patches_ref, info_ref)

    def take(slot):
        seen_ref[pl.ds(slot, 1), :] = visible_ref[pl.ds(info.source(info_ref, slot), 1), :]

    over_slots(count, take)
    turned_ref[...] = seen_ref[...].astype(wide_type).T
    cells = lax.broadcasted_iota(jnp.int32, (VIS, GRID), 1).astype(wide_type)
    own = exchange.own_bit(0, info_ref)
    place = exchange.place(0)
    for slot in range(count):
        onehot = (turned_ref[:, slot : slot + 1] == cells).astype(wide_type).astype(low_type)
        rows = dot(onehot, cot_ref[slot]).astype(low_type)
        rest = (slot & ((1 << place) - 1)) | ((slot >> (place + 1)) << place)
        kept = ((slot >> place) & 1) == own

        @pl.when(kept)
        def _(rest=rest, rows=rows):
            keep_ref[rest * VIS : (rest + 1) * VIS, :] = rows

        @pl.when(jnp.logical_not(kept))
        def _(rest=rest, rows=rows):
            sent_ref[rest * VIS : (rest + 1) * VIS, :] = rows


def position_kernel(
    info, info_ref, visible_ref, cot_ref, turned_high_ref, turned_low_ref, table_high_ref, table_low_ref, pos_ref,
    grad_ref, mask_ref, layout_ref, sums_ref,
):
    cells = lax.broadcasted_iota(jnp.int32, (GRID, VIS), 0)
    cell_column = lax.broadcasted_iota(jnp.int32, (GRID, 1), 0)
    sums_ref[...] = jnp.zeros_like(sums_ref)
    mask_ref[...] = jnp.zeros_like(mask_ref)

    def one_slot(slot):
        size = info.cells(info_ref, slot)
        seen = visible_ref[pl.ds(slot, 1), :] == cells
        fill = (cell_column < size).astype(wide_type) - jnp.sum(
            seen.astype(wide_type), axis=1, keepdims=True
        )
        wide = cot_ref[slot].astype(wide_type)
        mask_ref[...] += row_sum(fill * wide)
        sums_ref[side_of(size)] += wide

    over_slots(info.count, one_slot)
    total = sums_ref[2]
    for side in range(2):
        high, low = split_low(sums_ref[side])
        total += (
            dot(turned_high_ref[side], high) + dot(turned_high_ref[side], low) + dot(turned_low_ref[side], high)
        )
    grad_ref[...] = total
    table = pos_ref[...]
    for side in range(2):
        layout_ref[side] = dot(table_high_ref[side], table) + dot(table_low_ref[side], table)
    layout_ref[2] = table.astype(wide_type)


def wide_row(ref):
    return ref[...].astype(wide_type).reshape(1, ref.shape[0])


def enter_kernel(
    rows_ref, gain_ref, shift_ref, weight_ref, query_ref, value_ref, act_ref, qkv_ref
):
    gain, shift = wide_row(gain_ref), wide_row(shift_ref)
    query, value = wide_row(query_ref), wide_row(value_ref)
    nothing = jnp.zeros((1, HEAD_DIM), wide_type)
    pieces = []
    for start in range(0, query.shape[1], HEAD_DIM):
        pieces += [query[:, start : start + HEAD_DIM], nothing, value[:, start : start + HEAD_DIM]]
    bias = jnp.concatenate(pieces, axis=1)

    def body(start, size):
        rows = pl.ds(start, size)
        normed, _ = normalized(rows_ref[rows, :].astype(wide_type))
        act = (normed * gain + shift).astype(low_type)
        act_ref[rows, :] = act
        qkv_ref[rows, :] = (dot_right_t(act, weight_ref[...]) + bias).astype(low_type)

    over_rows(rows_ref.shape[0], CHUNK, body)


BLOCK = 4 * VIS


def attention_kernel(info, heads, first, info_ref, qkv_ref, packed_ref, prob_ref, attended_ref):
    key_image = lax.broadcasted_iota(jnp.int32, (BLOCK, BLOCK), 0) // VIS
    key_slot = lax.broadcasted_iota(jnp.int32, (BLOCK, BLOCK), 0) % VIS
    own_image = key_image == lax.broadcasted_iota(jnp.int32, (BLOCK, BLOCK), 1) // VIS
    columns = heads * HEAD_DIM
    full = columns // LANES * LANES
    rest = BLOCK * (columns - full) // LANES

    def body(start, size):
        rows = pl.ds(start, size)
        from_rows = pl.ds(first + start, size)
        limit = jnp.zeros((size, size), jnp.int32)
        for image in range(size // VIS):
            limit = jnp.where(key_image == image, info.live(info_ref, (first + start) // VIS + image), limit)
        live = jnp.logical_and(own_image, key_slot < limit)
        for head in range(heads):
            base = head * 3 * HEAD_DIM
            queries = qkv_ref[from_rows, base : base + HEAD_DIM]
            key_rows = qkv_ref[from_rows, base + HEAD_DIM : base + 2 * HEAD_DIM]
            value_rows = qkv_ref[from_rows, base + 2 * HEAD_DIM : base + 3 * HEAD_DIM]
            scores = jnp.where(live, dot_right_t(key_rows, queries) * scale_factor, -1e30)
            raised = jnp.exp(scores - jnp.max(scores, axis=0, keepdims=True))
            probs = (raised / jnp.sum(raised, axis=0, keepdims=True)).astype(low_type)
            prob_ref[rows, head * BLOCK : (head + 1) * BLOCK] = probs
            attended_ref[rows, head * HEAD_DIM : (head + 1) * HEAD_DIM] = dot_left_t(
                probs, value_rows
            ).astype(low_type)
        at = start // BLOCK * (full // LANES * BLOCK + rest)
        for tile in range(full // LANES):
            packed_ref[pl.ds(at, BLOCK), :] = attended_ref[rows, tile * LANES : (tile + 1) * LANES]
            at += BLOCK
        pieces = [
            attended_ref[pl.ds(start + piece * rest, rest), full:].astype(wide_type)
            for piece in range(BLOCK // rest)
        ]
        packed_ref[pl.ds(at, rest), :] = jnp.concatenate(pieces, axis=1).astype(low_type)

    over_rows(prob_ref.shape[0], BLOCK, body)


def unpack(own, packed_refs, start, columns, out_ref):
    full = columns // LANES * LANES
    width = columns - full
    rest = BLOCK * width // LANES
    at = start // BLOCK * (full // LANES * BLOCK + rest)
    count = len(packed_refs)
    for tile in range(full // LANES):
        for relative, ref in enumerate(packed_refs):
            lane = (tile * count + (own ^ relative)) * LANES
            out_ref[:, pl.ds(pl.multiple_of(lane, LANES), LANES)] = ref[pl.ds(at, BLOCK), :]
        at += BLOCK
    lane = full * count
    for other in range(0, count, LANES // width):
        pieces = []
        for part in range(other, other + LANES // width):
            rows = None
            for relative, ref in enumerate(packed_refs):
                here = ref[pl.ds(at, rest), :].astype(wide_type)
                rows = here if rows is None else jnp.where((own ^ relative) == part, here, rows)
            pieces.append(
                jnp.concatenate(
                    [rows[:, piece * width : (piece + 1) * width] for piece in range(BLOCK // rest)], axis=0
                )
            )
        out_ref[:, lane : lane + LANES] = jnp.concatenate(pieces, axis=1).astype(low_type)
        lane += LANES


def weights_kernel(parts, info_ref, *refs):
    out_refs, proj_refs, (out_ref, proj_ref) = refs[:parts], refs[parts : 2 * parts], refs[2 * parts :]
    own = info_ref[1]
    columns = out_refs[0].shape[0]
    full = columns // LANES * LANES
    width = columns - full
    for relative, (out_part_ref, proj_part_ref) in enumerate(zip(out_refs, proj_refs)):
        part = own ^ relative
        for tile in range(full // LANES):
            at = pl.multiple_of((tile * parts + part) * LANES, LANES)
            out_ref[pl.ds(at, LANES), :] = out_part_ref[tile * LANES : (tile + 1) * LANES, :]
        at = pl.multiple_of(full * parts + part * width, 16)
        out_ref[pl.ds(at, width), :] = out_part_ref[full:, :]
        size = proj_part_ref.shape[1]
        proj_ref[:, pl.ds(pl.multiple_of(part * size, LANES), size)] = proj_part_ref[...]


def halves(upper, left_ref, weight_ref, keep_ref, sent_ref, product):
    half = keep_ref.shape[0]
    for out_ref, which in ((sent_ref, 1 - upper), (keep_ref, upper)):

        def body(start, size, out_ref=out_ref, which=which):
            rows = pl.ds(pl.multiple_of(which * half + start, size), size)
            out_ref[pl.ds(start, size), :] = product(left_ref[rows, :], weight_ref[...]).astype(
                out_ref.dtype
            )

        over_rows(half, CHUNK, body)


def both_halves(upper, half, body):
    for source, which in enumerate((upper, 1 - upper)):

        def one(start, size, source=source, which=which):
            body(source, pl.ds(pl.multiple_of(which * half + start, size), size), pl.ds(start, size), size)

        over_rows(half, 256, one)


def back_kernel(info, exchange, info_ref, back_ref, back_other_ref, enc_ref):
    for relative, ref, start in exchange.arrived(back_ref, back_other_ref):
        image = info.image(info_ref, info_ref[0] ^ relative)
        enc_ref[pl.ds(pl.multiple_of(image * VIS, VIS), VIS), :] = ref[start : start + VIS, :]


def add_kernel(left_ref, right_ref, out_ref):
    out_ref[...] = (left_ref[...].astype(wide_type) + right_ref[...].astype(wide_type)).astype(low_type)


def forward_kernel(
    parts, columns, info_ref, rows_ref, out_bias_ref, gain_ref, shift_ref, up_ref, up_bias_ref, weight_ref, *refs
):
    attended_refs = (refs[:parts], refs[parts : 2 * parts])
    hidden_ref, act_ref, acted_ref, slope_ref, all_ref = refs[2 * parts :]
    half = rows_ref.shape[0] // 2
    out_bias, gain, shift, up_bias = (
        wide_row(ref) for ref in (out_bias_ref, gain_ref, shift_ref, up_bias_ref)
    )

    def body(which, start, size):
        rows = pl.ds(which * half + start, size)
        unpack(info_ref[1], attended_refs[which], start, columns, all_ref)
        total = dot(all_ref[...], weight_ref[...])
        hidden = rows_ref[rows, :].astype(wide_type) + total + out_bias
        hidden_ref[rows, :] = hidden
        normed, _ = normalized(hidden)
        act = (normed * gain + shift).astype(low_type)
        act_ref[rows, :] = act
        up_pre = dot(act, up_ref[...]) + up_bias
        cdf = 0.5 + 0.5 * lax.erf(up_pre * math.sqrt(0.5))
        acted_ref[rows, :] = (up_pre * cdf).astype(low_type)
        slope_ref[rows, :] = cdf + up_pre * jnp.exp(-0.5 * up_pre * up_pre) * (
            1.0 / math.sqrt(2.0 * math.pi)
        )

    for which in range(2):
        over_rows(half, BLOCK, lambda start, size, which=which: body(which, start, size))


def forward_part_kernel(info_ref, acted_ref, down_ref, keep_ref, sent_ref):
    halves(info_ref[1] & 1, acted_ref, down_ref, keep_ref, sent_ref, dot)


def forward_grad_kernel(
    parts, own, info_ref, slope_ref, up_ref, down_ref, weight_ref, *refs
):
    enc_refs = refs[:parts]
    part_ref, up_low_ref, down_low_ref, bias_ref, all_ref = refs[parts:]
    upper = info_ref[1] & 1
    half = part_ref.shape[0]
    first = (upper if own else 1 - upper) * half
    bias_ref[...] = jnp.zeros_like(bias_ref)

    def body(start, size):
        from_rows = pl.ds(pl.multiple_of(first + start, size), size)
        rows = pl.ds(start, size)
        for relative, enc_ref in enumerate(enc_refs):
            columns = enc_ref.shape[1]
            lane = pl.multiple_of((info_ref[1] ^ relative) * columns, LANES)
            all_ref[:, pl.ds(lane, columns)] = enc_ref[from_rows, :]
        out_grad = dot_right_t(all_ref[...], weight_ref[...])
        down_low = out_grad.astype(low_type)
        down_low_ref[rows, :] = down_low
        up_low = dot_right_t(down_low, down_ref[...]) * slope_ref[from_rows, :]
        up_low_ref[rows, :] = up_low.astype(low_type)
        bias_ref[0:1, :] += row_sum(out_grad)
        bias_ref[1:2, :] += row_sum(up_low_ref[rows, :].astype(wide_type))
        part_ref[rows, :] = dot_right_t(up_low_ref[rows, :], up_ref[...]).astype(low_type)

    over_rows(half, BLOCK, body)


def put_blocks(exchange, info_ref, keep_ref, sent_ref, wide_ref, pad, first=0):
    share = wide_ref.shape[0] // exchange.count
    for ref, indices in exchange.targets(0, info_ref, keep_ref, sent_ref):
        for block, index in enumerate(indices):
            rows = pl.ds(pl.multiple_of(index * share, 8), share)
            for tile in range(wide_ref.shape[1] // LANES):
                at = block * exchange.block + first + tile * pad
                ref[at : at + share, :] = wide_ref[rows, tile * LANES : (tile + 1) * LANES].astype(low_type)


def halves_of(info_ref, refs):
    if len(refs) == 2:
        return refs[0][...], refs[1][...]
    half = refs[0].shape[0] // 2
    upper = info_ref[1] & 1
    return tuple(
        refs[0][pl.ds(pl.multiple_of(which * half, half), half), :] for which in (upper, 1 - upper)
    )


def early_grads_kernel(
    exchanges, pad, info_ref, low_ref, low_other_ref, acted_ref, act_ref, up_ref, up_other_ref, down_keep_ref,
    down_sent_ref, up_keep_ref, up_sent_ref, wide_ref,
):
    left, right = halves_of(info_ref, (low_ref, low_other_ref)), halves_of(info_ref, (acted_ref,))
    wide_ref[...] = dot_left_t(left[0], right[0]) + dot_left_t(left[1], right[1])
    put_blocks(exchanges[0], info_ref, down_keep_ref, down_sent_ref, wide_ref, pad)
    left, right = halves_of(info_ref, (act_ref,)), halves_of(info_ref, (up_ref, up_other_ref))
    wide_ref[...] = dot_left_t(left[0], right[0]) + dot_left_t(left[1], right[1])
    put_blocks(exchanges[1], info_ref, up_keep_ref, up_sent_ref, wide_ref, pad)


def attention_back_kernel(
    heads, own, info_ref, sum_ref, hidden_ref, low_ref, gain_ref, weight_ref, qkv_ref, prob_ref, prob_last_ref,
    grads_ref, attn_low_ref, grad_ref, bias_ref, probs_ref,
):
    gain = wide_row(gain_ref)
    bias_ref[...] = jnp.zeros_like(bias_ref)
    half = sum_ref.shape[0]
    upper = info_ref[1] & 1
    which = upper if own else 1 - upper

    @pl.when(which == 0)
    def _():
        probs_ref[...] = prob_ref[...]

    @pl.when(which == 1)
    def _():
        probs_ref[...] = prob_last_ref[...]

    def body(start, size):
        part = pl.ds(start, size)
        rows = pl.ds(pl.multiple_of(which * half + start, size), size)
        normed, spread = normalized(hidden_ref[rows, :])
        grad = sum_ref[part, :].astype(wide_type)
        bias_ref[0:1, :] += row_sum(grad * normed)
        bias_ref[1:2, :] += row_sum(grad)
        hidden_grad = low_ref[part, :].astype(wide_type) + norm_back(grad, normed, spread, gain)
        grad_ref[part, :] = hidden_grad
        bias_ref[2:3, :] += row_sum(hidden_grad)
        attn_low = hidden_grad.astype(low_type)
        attn_low_ref[part, :] = attn_low
        attended_grad = dot_right_t(attn_low, weight_ref[...]).astype(low_type)
        for head in range(heads):
            base = head * 3 * HEAD_DIM
            queries = qkv_ref[rows, base : base + HEAD_DIM]
            key_rows = qkv_ref[rows, base + HEAD_DIM : base + 2 * HEAD_DIM]
            value_rows = qkv_ref[rows, base + 2 * HEAD_DIM : base + 3 * HEAD_DIM]
            probs = probs_ref[part, head * BLOCK : (head + 1) * BLOCK]
            grad_rows = attended_grad[:, head * HEAD_DIM : (head + 1) * HEAD_DIM]
            value_low = dot(probs, grad_rows).astype(low_type)
            prob_grad = dot_right_t(value_rows, grad_rows)
            wide_probs = probs.astype(wide_type)
            weighted = wide_probs * prob_grad
            score_low = (
                weighted - wide_probs * jnp.sum(weighted, axis=0, keepdims=True)
            ).astype(low_type)
            query_low = (dot_left_t(score_low, key_rows) * scale_factor).astype(low_type)
            key_low = (dot(score_low, queries) * scale_factor).astype(low_type)
            grads_ref[part, base : base + HEAD_DIM] = query_low
            grads_ref[part, base + HEAD_DIM : base + 2 * HEAD_DIM] = key_low
            grads_ref[part, base + 2 * HEAD_DIM : base + 3 * HEAD_DIM] = value_low

    over_rows(half, BLOCK, body)


def views(ref, sizes):
    starts = [sum(sizes[:at]) for at in range(len(sizes))]
    return [ref.at[pl.ds(start, size), :] for start, size in zip(starts, sizes)]


def step_kernel(moves, sizes, info_ref, *refs):
    parted = [None if size is None else views(ref, size) for ref, size in zip(refs, sizes)]
    for exchange, step, sources, kept, (sent, place) in moves:
        pairs = []
        for _, keep, (came, at) in sources:
            pairs += [refs[keep], parted[came][at]]
        exchange.kernel(step, [part for part, _, _ in sources], info_ref, *pairs, refs[kept], parted[sent][place])


def late_grads_kernel(
    exchanges, pad, middle, info_ref, act_ref, grads_ref, grads_other_ref, low_ref, low_other_ref, first_ref, last_ref,
    keep_ref, sent_ref, turned_keep_ref, turned_sent_ref, bias_ref, wide_ref,
):
    columns = grads_ref.shape[1]
    first = first_ref.shape[1]
    lower = (info_ref[1] & 1) == 0
    attended = (first_ref[...].astype(wide_type), last_ref[...].astype(wide_type))
    attended_own = jnp.where(lower, attended[0], attended[1]).astype(low_type)
    attended_other = jnp.where(lower, attended[1], attended[0]).astype(low_type)
    act_own, act_other = halves_of(info_ref, (act_ref,))
    wide_ref[:, :first] = dot_left_t(low_ref[...], attended_own) + dot_left_t(
        low_other_ref[...], attended_other
    )
    wide_ref[:, first : first + columns] = dot_left_t(act_own, grads_ref[...]) + dot_left_t(
        act_other, grads_other_ref[...]
    )
    put_blocks(exchanges[0], info_ref, keep_ref, sent_ref, wide_ref.at[:, pl.ds(0, middle)], pad)
    put_blocks(
        exchanges[1], info_ref, turned_keep_ref, turned_sent_ref,
        wide_ref.at[:, pl.ds(middle, wide_ref.shape[1] - middle)], pad,
    )
    bias_ref[...] = row_sum(grads_ref[...].astype(wide_type)) + row_sum(grads_other_ref[...].astype(wide_type))


EXTRA = 16


def put_extra(ref, start, gain, shift):
    rows = []
    for value in (gain, shift):
        rows += list(split_low(value))
    rows.append(jnp.zeros((EXTRA - 4, gain.shape[1]), low_type))
    ref[start : start + EXTRA, :] = jnp.concatenate(rows, axis=0)


def get_extra(ref, start):
    rows = ref[start : start + EXTRA, :].astype(wide_type)
    return rows[0:1] + rows[1:2], rows[2:3] + rows[3:4]


def norm_kernel(rows_ref, normed_ref):
    def body(start, size):
        rows = pl.ds(start, size)
        normed_ref[rows, :] = normalized(rows_ref[rows, :].astype(wide_type))[0].astype(low_type)

    over_rows(rows_ref.shape[0], CHUNK, body)


def input_part_kernel(
    info_ref, normed_ref, grads_ref, grads_other_ref, weight_ref, keep_ref, sent_ref, part_ref, bias_ref
):
    lower_bit = info_ref[1] & 1
    bias_ref[...] = jnp.zeros_like(bias_ref)

    def body(source, rows, part, size):
        grad = dot((grads_ref, grads_other_ref)[source][part, :], weight_ref[...])
        part_ref[rows, :] = grad
        bias_ref[0:1, :] += row_sum(grad * normed_ref[rows, :].astype(wide_type))
        bias_ref[1:2, :] += row_sum(grad)

    both_halves(lower_bit, grads_ref.shape[0], body)
    size = keep_ref.shape[0] - EXTRA
    share = size // (lax.axis_size("mp") // 2)
    for out_ref, which in ((sent_ref, 1 - lower_bit), (keep_ref, lower_bit)):
        for block in range(size // share):
            rows = pl.ds(pl.multiple_of((2 * block + which) * share, share), share)
            out_ref[block * share : (block + 1) * share, :] = part_ref[rows, :].astype(low_type)
        put_extra(out_ref, size, bias_ref[0:1, :], bias_ref[1:2, :])


def input_halve_kernel(bit, info_ref, keep_ref, other_ref, next_keep_ref, next_sent_ref, total_ref):
    upper = (info_ref[1] >> bit) & 1
    half = next_keep_ref.shape[0] - EXTRA
    size = 2 * half
    share = total_ref.shape[0] - size
    total_ref[:size, :] = keep_ref[:size, :].astype(wide_type) + other_ref[:size, :].astype(wide_type)
    own, other = get_extra(keep_ref, size), get_extra(other_ref, size)
    for out_ref, which in ((next_sent_ref, 1 - upper), (next_keep_ref, upper)):
        for block in range(half // share):
            rows = pl.ds(pl.multiple_of((2 * block + which) * share, share), share)
            out_ref[block * share : (block + 1) * share, :] = total_ref[rows, :].astype(low_type)
        put_extra(out_ref, half, own[0] + other[0], own[1] + other[1])


def input_grad_kernel(info_ref, rows_ref, keep_ref, other_ref, grad_ref, grad_other_ref, gain_ref, out_ref):
    share = out_ref.shape[0]
    half = grad_ref.shape[0]
    start = info_ref[1] * share
    rows = pl.ds(pl.multiple_of(start, share), share)
    part = pl.ds(pl.multiple_of(start % half, share), share)
    own = start // half == (info_ref[1] & 1)
    normed, spread = normalized(rows_ref[rows, :].astype(wide_type))
    grad = keep_ref[:share, :].astype(wide_type) + other_ref[:share, :].astype(wide_type)
    hidden_grad = jnp.where(own, grad_ref[part, :], grad_other_ref[part, :])
    out_ref[...] = (hidden_grad + norm_back(grad, normed, spread, wide_row(gain_ref))).astype(low_type)


VECTOR_ROWS = 48


def put_rows(values, rows_ref):
    row = 0
    for value in values:
        for tile in range(value.shape[1] // LANES):
            rows_ref[row : row + 1, :] = value[:, tile * LANES : (tile + 1) * LANES]
            row += 1


def take_rows(rows_ref, refs):
    row = 0
    for ref in refs:
        size = ref.shape[0]
        for tile in range(-(-size // LANES)):
            width = min(LANES, size - tile * LANES)
            ref[tile * LANES : tile * LANES + width] = rows_ref[row, :width]
            row += 1


def encoded_kernel(
    info_ref, hidden_ref, sum_ref, sum_other_ref, down_bias_ref, weight_ref, bias_ref, enc_ref, encoded_ref, wide_ref,
    low_ref,
):
    down_bias, bias = wide_row(down_bias_ref), wide_row(bias_ref)

    def body(source, rows, part, size):
        total = (sum_ref, sum_other_ref)[source][part, :].astype(wide_type)
        out_low = (hidden_ref[rows, :] + total + down_bias).astype(low_type)
        low_ref[rows, :] = out_low
        encoded_ref[rows, :] = (dot(out_low, weight_ref[...]) + bias).astype(low_type)

    both_halves(info_ref[1] & 1, sum_ref.shape[0], body)
    wide_ref[...] = dot_left_t(low_ref[...], enc_ref[...])


def last_kernel(
    info, exchange, heads, pad, info_ref, encoded_ref, wide_ref, enc_ref, pos_ref, mask_ref, grads_ref, grads_other_ref,
    second_ref, second_other_ref, qkv_ref, first_ref, first_other_ref, keep_ref, sent_ref, rows_ref,
):
    put_blocks(exchange, info_ref, keep_ref, sent_ref, wide_ref, 0)
    put_blocks(exchange, info_ref, keep_ref, sent_ref, pos_ref, 0, pad)
    for ref, indices in exchange.targets(0, info_ref, keep_ref, sent_ref):
        at = exchange.moved_at(0)
        for index in indices:
            image = info.image(info_ref, index)
            ref[at : at + VIS, :] = encoded_ref[pl.ds(pl.multiple_of(image * VIS, VIS), VIS), :]
            at += VIS
    qkv, early = qkv_ref[...], grads_ref[...] + grads_other_ref[...]
    second = second_ref[...] + second_other_ref[...]
    empty = jnp.zeros((1, 2 * LANES - heads * HEAD_DIM), wide_type)
    spread = []
    for part in (0, 2):
        spread += [
            qkv[:, (3 * head + part) * HEAD_DIM : (3 * head + part + 1) * HEAD_DIM] for head in range(heads)
        ] + [empty]
    own = get_extra(first_ref, first_ref.shape[0] - EXTRA)
    other = get_extra(first_other_ref, first_ref.shape[0] - EXTRA)
    put_rows(
        (
            jnp.concatenate(spread, axis=1), early[1:2], row_sum(enc_ref[...].astype(wide_type)), mask_ref[...],
            own[0] + other[0], own[1] + other[1], second[0:1], second[1:2], second[2:3],
            early[0:1],
        ),
        rows_ref,
    )
    for ref in (keep_ref, sent_ref):
        ref[exchange.shared_at(0) :, :] = rows_ref[...].astype(low_type)


def base_kernel(info, info_ref, seen_ref, mask_ref, layout_ref, base_ref, chosen_ref):
    cells = lax.broadcasted_iota(jnp.int32, (GRID, VIS), 0)
    cell_column = lax.broadcasted_iota(jnp.int32, (GRID, 1), 0)
    mask_row = wide_row(mask_ref)

    def one_slot(slot):
        size = info.cells(info_ref, slot)
        seen = (seen_ref[pl.ds(slot, 1), :] == cells).astype(wide_type)
        fill = (cell_column < size).astype(wide_type) - jnp.sum(seen, axis=1, keepdims=True)
        base_ref[slot] = fill * mask_row + layout_ref[side_of(size)]
        chosen_ref[slot] = seen.astype(low_type)

    over_slots(info.count, one_slot)


def late_out_kernel(
    info, exchange, turned_exchange, pad, middle, sizes, info_ref, chosen_ref, keep_ref, turned_ref, came_ref, base_ref,
    grids_ref, out_ref, qkv_ref, proj_ref, pos_ref, *refs
):
    *vector_refs, wide_ref, rows_ref = refs
    other_ref, turned_other_ref = views(came_ref, sizes)
    for relative, ref, start in exchange.arrived(keep_ref, other_ref):
        slot = info_ref[0] ^ relative
        placed = dot(chosen_ref[slot], ref[start : start + VIS, :])
        grids_ref[slot] = (placed + base_ref[slot]).astype(low_type)
    share = proj_ref.shape[0]
    tiles = wide_ref.shape[1] // LANES
    for tile in range(tiles):
        here = (exchange, keep_ref, other_ref, tile) if tile < middle else (
            turned_exchange, turned_ref, turned_other_ref, tile - middle
        )
        wide_ref[:, tile * LANES : (tile + 1) * LANES] = here[0].total(here[1], here[2], here[3] * pad, share)
    columns = out_ref.shape[0]
    wide_out = -(-columns // LANES) * LANES
    out_ref[...] = wide_ref[:, :wide_out].T[:columns]
    qkv_ref[...] = wide_ref[:, columns:]
    proj_ref[...] = exchange.total(keep_ref, other_ref, middle * pad, share)
    pos_ref[...] = exchange.total(keep_ref, other_ref, (middle + 1) * pad, pos_ref.shape[0])
    rows_ref[...] = exchange.shared_total(keep_ref, other_ref)
    take_rows(rows_ref, vector_refs)


def early_out_kernel(exchanges, pad, *refs):
    for exchange, keep_ref, other_ref, out_ref in zip(exchanges, refs[:2], refs[2:4], refs[4:]):
        for tile in range(out_ref.shape[1] // LANES):
            out_ref[:, tile * LANES : (tile + 1) * LANES] = exchange.total(
                keep_ref, other_ref, tile * pad, out_ref.shape[0]
            )


def swap(value, axis, bit):
    count = lax.axis_size(axis)
    return lax.ppermute(value, axis, [(i, i ^ bit) for i in range(count)])


def local(
    patch_rows, patches, visible, owner, qkv_weight, query_bias, value_bias, out_weight, out_bias, first_gain,
    first_shift, second_gain, second_shift, up_weight, up_bias, down_weight, down_bias, proj_weight, proj_bias,
    mask_token, decoder_pos, grid_cotangent,
):
    count = lax.axis_size("dp")
    parts = lax.axis_size("mp")
    where = jnp.stack([lax.axis_index("dp"), lax.axis_index("mp")]).astype(jnp.int32)
    rows, width = patch_rows.shape
    images = rows // VIS
    heads = qkv_weight.shape[1] // (3 * HEAD_DIM)
    head_columns = heads * HEAD_DIM
    qkv_columns = qkv_weight.shape[1]
    units = up_weight.shape[1]
    columns = proj_weight.shape[1]
    share = width // count
    pos_share = GRID // count
    half = rows // 2
    own_rows = rows // parts
    pads = (-(-share // 16) * 16, -(-pos_share // 16) * 16)
    run = Order(rows <= PINNED_ROWS)

    tables = grid_tables()
    table_high = tables.astype(low_type)
    table_low = (tables - table_high.astype(np.float32)).astype(low_type)
    turned_high = jnp.asarray(np.ascontiguousarray(table_high.transpose(0, 2, 1)))
    turned_low = jnp.asarray(np.ascontiguousarray(table_low.transpose(0, 2, 1)))
    table_high, table_low = jnp.asarray(table_high), jnp.asarray(table_low)
    qkv_weight_t = qkv_weight.T
    run.leave(owner, visible, patches, grid_cotangent, turned_high, turned_low, table_high, table_low, decoder_pos)
    info = Info(count)
    bits = tuple(range(count.bit_length() - 1))
    late_columns = qkv_columns + head_columns
    turned = (1, 0) + bits[2:]
    back_exchange = Exchange(count, bits, 0, moved=VIS)
    far = bits
    up_exchange = Exchange(count, far, units // LANES * pads[0])
    down_exchange = Exchange(count, turned, units // LANES * pads[0])
    tiles = late_columns // LANES
    middle = 3 * tiles // 6
    late_exchange = Exchange(count, bits, middle * pads[0])
    turned_exchange = Exchange(count, turned, (tiles - middle) * pads[0])
    last_exchange = Exchange(count, bits, sum(pads), moved=VIS, shared=VECTOR_ROWS)
    joint_exchange = Exchange(
        count, bits, late_exchange.block + last_exchange.block, moved=VIS, shared=VECTOR_ROWS
    )

    def low(*shape):
        return (shape, low_type)

    def wide(*shape):
        return (shape, wide_type)

    def moved(value, axis, bit):
        return run.keep(swap(value, axis, bit))

    def model_steps(keep, received):
        (total,) = run(add_kernel, [low(half, width)], (keep, received), cost=0.6)
        bit = 2
        while bit < parts:
            received = moved(total, "mp", bit)
            yield
            (total,) = run(add_kernel, [low(half, width)], (total, received), cost=0.6)
            bit *= 2
        other = moved(total, "mp", 1)
        yield
        return total, other

    def model_gather(value):
        values = {0: value}
        bit = parts // 2
        while bit:
            values.update({other | bit: moved(values[other], "mp", bit) for other in tuple(values)})
            bit //= 2
        return tuple(values[at] for at in range(parts))

    def data_step(step, exchange, pairs):
        keep, sent = run(
            lambda *refs: exchange.kernel(step, [part for part, _, _ in pairs], *refs),
            [low(exchange.rows(step), LANES)] * 2,
            (facts,) + tuple(array for _, *arrays in pairs for array in arrays),
            (SMEM,) + (VMEM,) * (2 * len(pairs)),
            cost=1.2,
        )
        return keep, moved(sent, "dp", 2 ** exchange.bits[step])

    def data_steps(exchange, keep, sent):
        received = moved(sent, "dp", 2 ** exchange.bits[0])
        yield keep, received
        for step in range(1, len(exchange.bits)):
            keep, received = data_step(step, exchange, [(exchange, keep, received)])
            yield keep, received

    def steps(kept, arrays, moves, sends, cost=1.0):
        first = len(kept) + len(arrays)
        sizes = [None] * len(kept) + [size for _, size in arrays] + [None] * len(moves)
        sizes += [size for _, size in sends]
        placed = [
            (exchange, step, sources, first + at, (first + len(moves) + to[0], to[1]))
            for at, (exchange, step, sources, to) in enumerate(moves)
        ]
        results = run(
            lambda *refs: step_kernel(placed, sizes, *refs),
            [low(exchange.rows(step), LANES) for exchange, step, _, _ in moves]
            + [low(sum(size), LANES) for _, size in sends],
            (facts, *kept) + tuple(array for array, _ in arrays),
            (SMEM,) + (VMEM,) * first,
            cost=cost,
        )
        return results[: len(moves)], [
            moved(sent, "dp", 2**bit) for sent, (bit, _) in zip(results[len(moves) :], sends)
        ]

    def finish_pair(steps):
        *_, last = steps
        return last

    def finish(steps):
        while True:
            try:
                next(steps)
            except StopIteration as stop:
                return stop.value

    out_all = model_gather(out_weight)
    proj_all = model_gather(proj_weight)
    (
        back_keep, back_sent, facts, seen, patch_rows, qkv_weight_t, first_gain, first_shift, query_bias, value_bias,
    ) = run(
        lambda *refs: cotangent_kernel(info, back_exchange, *refs),
        [
            low(back_exchange.rows(0), columns), low(back_exchange.rows(0), columns), ((info.size,), jnp.int32),
            ((count, VIS), jnp.int32),
        ],
        (where, owner, patches, visible, grid_cotangent),
        (SMEM, SMEM, SMEM, VMEM, VMEM),
        out_specs=(VMEM, VMEM, SMEM, VMEM),
        scratch=[pltpu.VMEM((VIS, count), wide_type)],
        stage=(patch_rows, qkv_weight_t, first_gain, first_shift, query_bias, value_bias),
        cost=3.0,
    )
    back_steps = data_steps(back_exchange, back_keep, back_sent)
    next(back_steps)
    act_one, qkv = run(
        enter_kernel,
        [low(rows, width), low(rows, qkv_columns)],
        (patch_rows, first_gain, first_shift, qkv_weight_t, query_bias, value_bias),
        cost=1.2,
        after=(out_all[1], proj_all[1]),
    )
    next(back_steps)
    packed_rows = half * head_columns // LANES
    packed, first_probs, first_attended, out_bias, second_gain, second_shift, up_weight, up_bias = run(
        lambda *refs: attention_kernel(info, heads, 0, *refs),
        [low(packed_rows, LANES), low(half, heads * BLOCK), low(half, head_columns)],
        (facts, qkv),
        (SMEM, VMEM),
        stage=(out_bias, second_gain, second_shift, up_weight, up_bias),
        cost=2.8,
    )
    first_all = model_gather(packed)
    back_own, back_other = finish_pair(back_steps)
    (
        packed, last_probs, last_attended, down_weight, down_bias, proj_bias, out_near, proj_near, out_core, proj_core
    ) = run(
        lambda *refs: attention_kernel(info, heads, half, *refs),
        [low(packed_rows, LANES), low(half, heads * BLOCK), low(half, head_columns)],
        (facts, qkv),
        (SMEM, VMEM),
        stage=(down_weight, down_bias, proj_bias, out_weight, proj_weight, out_all[1], proj_all[1]),
        cost=2.5,
        after=(out_all[parts // 2], proj_all[parts // 2]),
    )
    last_all = model_gather(packed)
    out_whole, proj_whole = run(
        lambda *refs: weights_kernel(parts, *refs),
        [low(parts * head_columns, width), low(width, parts * columns)],
        (facts, out_near, out_core) + out_all[2:] + (proj_near, proj_core) + proj_all[2:],
        (SMEM,) + (VMEM,) * (2 * parts),
        cost=0.0,
    )
    (enc_grad,) = run(
        lambda *refs: back_kernel(info, back_exchange, *refs),
        [low(rows, columns)],
        (facts, back_own, back_other),
        (SMEM, VMEM, VMEM),
        cost=0.4,
    )
    enc_all = model_gather(enc_grad)
    hidden, act_two, acted, slope = run(
        lambda *refs: forward_kernel(parts, head_columns, *refs),
        [wide(rows, width), low(rows, width), low(rows, units), wide(rows, units)],
        (facts, patch_rows, out_bias, second_gain, second_shift, up_weight, up_bias, out_whole)
        + first_all
        + last_all,
        (SMEM,) + (VMEM,) * (7 + 2 * parts),
        scratch=[pltpu.VMEM((BLOCK, parts * head_columns), low_type)],
        cost=2.6,
    )

    def forward_grad(own):
        return run(
            lambda *refs: forward_grad_kernel(parts, own, *refs),
            [low(half, width), low(half, units), low(half, width), wide(2, width)],
            (facts, slope, up_weight, down_weight, proj_whole) + enc_all,
            (SMEM,) + (VMEM,) * (4 + parts),
            scratch=[pltpu.VMEM((BLOCK, parts * columns), low_type)],
            cost=1.2,
        )

    sent, up_low_other, down_low_other, bias_grads_other = forward_grad(False)
    second_other = moved(sent, "mp", 1)
    keep, up_low, down_low, bias_grads = forward_grad(True)
    second_steps = model_steps(keep, second_other)
    next(second_steps)
    down_keep, down_sent, up_keep, up_sent = run(
        lambda *refs: early_grads_kernel((down_exchange, up_exchange), pads[0], *refs),
        [low(down_exchange.rows(0), LANES)] * 2 + [low(up_exchange.rows(0), LANES)] * 2,
        (facts, down_low, down_low_other, acted, act_two, up_low, up_low_other),
        (SMEM,) + (VMEM,) * 6,
        scratch=[pltpu.VMEM((width, units), wide_type)],
        cost=2.2,
    )
    down_pair = (down_keep, moved(down_sent, "dp", 2 ** turned[0]))
    up_pair = (up_keep, moved(up_sent, "dp", 2 ** bits[0]))
    keep, sent = run(
        forward_part_kernel,
        [low(half, width), low(half, width)],
        (facts, acted, down_weight),
        (SMEM, VMEM, VMEM),
        cost=0.7,
    )
    out_steps = model_steps(keep, moved(sent, "mp", 1))

    pos_grad_own, mask_grad, layouts = run(
        lambda *refs: position_kernel(info, *refs),
        [wide(GRID, columns), wide(1, columns), wide(3, GRID, columns)],
        (facts, seen, grid_cotangent, turned_high, turned_low, table_high, table_low, decoder_pos),
        (SMEM,) + (VMEM,) * 7,
        scratch=[pltpu.VMEM((3, GRID, columns), wide_type)],
        cost=20.0,
    )
    next(out_steps)
    (normed_low,) = run(norm_kernel, [low(rows, width)], (patch_rows,), cost=0.6)
    next(second_steps)
    second_sum, second_other = finish(second_steps)

    def attention_back(own, total, down_part, cost):
        return run(
            lambda *refs: attention_back_kernel(heads, own, *refs),
            [low(half, qkv_columns), low(half, width), wide(half, width), wide(3, width)],
            (facts, total, hidden, down_part, second_gain, out_near, qkv, first_probs, last_probs),
            (SMEM,) + (VMEM,) * 8,
            scratch=[pltpu.VMEM((half, heads * BLOCK), low_type)],
            cost=cost,
        )

    grads, attn_low, hidden_grad, second_grads = attention_back(True, second_sum, down_low, COVER)
    run.share = 2.0
    grads_other, attn_low_other, hidden_grad_other, second_grads_other = attention_back(
        False, second_other, down_low_other, 2.0
    )
    in_keep, in_sent = run(
        input_part_kernel,
        [low(half + EXTRA, width)] * 2,
        (facts, normed_low, grads, grads_other, qkv_weight_t),
        (SMEM,) + (VMEM,) * 4,
        scratch=[pltpu.VMEM((rows, width), wide_type), pltpu.VMEM((2, width), wide_type)],
        cost=2.0,
    )
    in_other = moved(in_sent, "mp", 1)
    in_other = moved(in_sent, "mp", 1)
    late_keep, late_sent, turned_keep, turned_sent, qkv_bias_grad = run(
        lambda *refs: late_grads_kernel((late_exchange, turned_exchange), pads[0], middle * LANES, *refs),
        [low(late_exchange.rows(0), LANES)] * 2
        + [low(turned_exchange.rows(0), LANES)] * 2
        + [wide(1, qkv_columns)],
        (facts, act_one, grads, grads_other, attn_low, attn_low_other, first_attended, last_attended),
        (SMEM,) + (VMEM,) * 7,
        scratch=[pltpu.VMEM((width, late_columns), wide_type)],
        cost=40.0,
    )
    turned_came = moved(turned_sent, "dp", 2 ** turned[0])
    late_came = moved(late_sent, "dp", 2 ** bits[0])
    bit = 1
    size = half
    while 2**bit < parts:
        in_keep, in_sent = run(
            lambda *refs, bit=bit: input_halve_kernel(bit, *refs),
            [low(size // 2 + EXTRA, width)] * 2,
            (facts, in_keep, in_other),
            (SMEM, VMEM, VMEM),
            scratch=[pltpu.VMEM((size + own_rows, width), wide_type)],
            cost=1.1,
            after=(up_pair[1], down_pair[1]),
        )
        in_other = moved(in_sent, "mp", 2**bit)
        size //= 2
        bit += 1
    next(out_steps)
    early_sizes = [[exchange.rows(1)] for exchange in (up_exchange, down_exchange)]
    (up_keep,), (up_came,) = steps(
        (up_pair[0],),
        ((up_pair[1], [up_exchange.rows(0)]),),
        [(up_exchange, 1, [(up_exchange, 0, (1, 0))], (0, 0))],
        [(far[1], early_sizes[0])],
        cost=40.0,
    )
    out_sum, out_other = finish(out_steps)
    encoded, proj_grad = run(
        encoded_kernel,
        [low(rows, columns), wide(width, columns)],
        (facts, hidden, out_sum, out_other, down_bias, proj_near, proj_bias, enc_grad),
        (SMEM,) + (VMEM,) * 7,
        scratch=[pltpu.VMEM((rows, width), low_type)],
        cost=1.0,
    )
    last_keep, last_sent = run(
        lambda *refs: last_kernel(info, last_exchange, heads, pads[0], *refs),
        [low(last_exchange.rows(0), LANES)] * 2,
        (
            facts, encoded, proj_grad, enc_grad, pos_grad_own, mask_grad, bias_grads, bias_grads_other, second_grads,
            second_grads_other, qkv_bias_grad, in_keep, in_other,
        ),
        (SMEM,) + (VMEM,) * 12,
        scratch=[pltpu.VMEM((VECTOR_ROWS, LANES), wide_type)],
        cost=0.6,
    )
    last_came = moved(last_sent, "dp", 2 ** bits[0])
    (down_keep,), (down_came,) = steps(
        (down_pair[0],),
        ((down_pair[1], [down_exchange.rows(0)]),),
        [(down_exchange, 1, [(down_exchange, 0, (1, 0))], (0, 0))],
        [(turned[1], early_sizes[1])],
    )
    (input_grad,) = run(
        input_grad_kernel,
        [low(own_rows, width)],
        (facts, patch_rows, in_keep, in_other, hidden_grad, hidden_grad_other, first_gain),
        (SMEM,) + (VMEM,) * 6,
        final=True,
        cost=0.8,
    )

    early = (up_exchange, down_exchange)
    late = (joint_exchange, turned_exchange)
    base, chosen = run(
        lambda *refs: base_kernel(info, *refs),
        [wide(count, GRID, columns), low(count, GRID, VIS)],
        (facts, seen, mask_token, layouts),
        (SMEM,) + (VMEM,) * 3,
        cost=0.8,
    )
    joint_sizes = [[exchange.rows(1)] for exchange in late]
    (late_keep, turned_keep), late_came = steps(
        (late_keep, last_keep, turned_keep),
        (
            (late_came, [late_exchange.rows(0)]), (last_came, [last_exchange.rows(0)]),
            (turned_came, [turned_exchange.rows(0)]),
        ),
        [
            (joint_exchange, 1, [(late_exchange, 0, (3, 0)), (last_exchange, 1, (4, 0))], (0, 0)),
            (turned_exchange, 1, [(turned_exchange, 2, (5, 0))], (1, 0)),
        ],
        [(bits[1], joint_sizes[0]), (turned[1], joint_sizes[1])],
    )
    (up_keep,), (up_came,) = steps(
        (up_keep,),
        ((up_came, early_sizes[0]),),
        [(up_exchange, 2, [(up_exchange, 0, (1, 0))], (0, 0))],
        [(far[2], [up_exchange.rows(2)])],
    )
    (down_keep,), (down_came,) = steps(
        (down_keep,),
        ((down_came, early_sizes[1]),),
        [(down_exchange, 2, [(down_exchange, 0, (1, 0))], (0, 0))],
        [(turned[2], [down_exchange.rows(2)])],
    )
    early_came = (up_came, down_came)
    early_sizes = [[exchange.rows(2)] for exchange in early]
    last_sizes = [exchange.rows(2) for exchange in late]
    (late_keep, turned_keep), (late_came,) = steps(
        (late_keep, turned_keep),
        ((late_came[0], joint_sizes[0]), (late_came[1], joint_sizes[1])),
        [
            (joint_exchange, 2, [(joint_exchange, 0, (2, 0))], (0, 0)),
            (turned_exchange, 2, [(turned_exchange, 1, (3, 0))], (0, 1)),
        ],
        [(2, last_sizes)],
    )
    for step in range(3, len(bits)):
        old_sizes, early_sizes = early_sizes, [[exchange.rows(step)] for exchange in early]
        (up_keep, down_keep), early_came = steps(
            (up_keep, down_keep),
            ((early_came[0], old_sizes[0]), (early_came[1], old_sizes[1])),
            [(exchange, step, [(exchange, at, (2 + at, 0))], (at, 0)) for at, exchange in enumerate(early)],
            [(step, early_sizes[0]), (step, early_sizes[1])],
        )
        old_sizes, last_sizes = last_sizes, [exchange.rows(step) for exchange in late]
        (late_keep, turned_keep), (late_came,) = steps(
            (late_keep, turned_keep),
            ((late_came, old_sizes),),
            [(exchange, step, [(exchange, at, (2, at))], (0, at)) for at, exchange in enumerate(late)],
            [(step, last_sizes)],
        )
    up_weight_grad, down_weight_grad = run(
        lambda *refs: early_out_kernel(early, pads[0], *refs),
        [wide(share, units)] * 2,
        (up_keep, down_keep, *early_came),
        final=True,
        cost=1.0,
    )
    (
        grids, out_weight_grad, qkv_weight_grad, proj_weight_grad, pos_grad, query_bias_grad, value_bias_grad,
        up_bias_grad, proj_bias_grad, mask_token_grad, first_gain_grad, first_shift_grad, second_gain_grad,
        second_shift_grad, out_bias_grad, down_bias_grad,
    ) = run(
        lambda *refs: late_out_kernel(info, joint_exchange, turned_exchange, pads[0], middle, last_sizes, *refs),
        [
            low(count, GRID, columns), wide(head_columns, share), wide(share, qkv_columns), wide(share, columns),
            wide(pos_share, columns),
        ]
        + [wide(size) for size in (head_columns, head_columns, units, columns, columns) + (width,) * 6],
        (facts, chosen, late_keep, turned_keep, late_came, base),
        (SMEM,) + (VMEM,) * 5,
        scratch=[pltpu.VMEM((share, late_columns), wide_type), pltpu.VMEM((VECTOR_ROWS, LANES), wide_type)],
        final=True,
        cost=2.5,
    )
    return (
        grids, input_grad, qkv_weight_grad, query_bias_grad, value_bias_grad, out_weight_grad, out_bias_grad,
        first_gain_grad, first_shift_grad, second_gain_grad, second_shift_grad, up_weight_grad, up_bias_grad,
        down_weight_grad.T, down_bias_grad, proj_weight_grad, proj_bias_grad, mask_token_grad, pos_grad,
    )


def solution(mesh):
    return jax.shard_map(
        local,
        mesh=mesh,
        in_specs=(
            P("dp", None), P(), P(), P(), P(None, "mp"), P("mp"), P("mp"), P("mp", None), P(), P(), P(), P(), P(),
            P(None, "mp"), P("mp"), P("mp", None), P(), P(None, "mp"), P("mp"), P("mp"), P(None, "mp"),
            P("dp", None, "mp"),
        ),
        out_specs=(
            P("dp", None, "mp"), P(("dp", "mp"), None), P("dp", "mp"), P("mp"), P("mp"), P("mp", "dp"), P(), P(),
            P(), P(), P(), P("dp", "mp"), P("mp"), P("mp", "dp"), P(), P("dp", "mp"), P("mp"), P("mp"),
            P("dp", "mp"),
        ),
        check_vma=False,
    )
```
